32 devices in a mesh: dp: 4 (over x, core), ctx: 8 (over z, y).
Axes of the slice: x: 2, y: 2, z: 4, core: 2. Of those that a mesh axis runs over, the one named last changes fastest.
Arguments:
- tokens: bfloat16 [4096, 1536], P(('dp', 'ctx')), may hold values from -6 to 6
- cotangent: bfloat16 [4096, 1536], P(('dp', 'ctx')), may hold values from -6 to 6
- gain_attn: bfloat16 [1536], P(('dp', 'ctx')), may hold values from 0.5 to 1.5
- w_query: bfloat16 [1536, 1536], P(('dp', 'ctx')), may hold values from -0.1875 to 0.1875
- key_weight: bfloat16 [1536, 768], P(('dp', 'ctx')), may hold values from -0.1875 to 0.1875
- value_weight: bfloat16 [1536, 768], P(('dp', 'ctx')), may hold values from -0.15625 to 0.15625
- w_out: bfloat16 [1536, 1536], P(('dp', 'ctx')), may hold values from -2.5 to 2.5
- gain_ffn: bfloat16 [1536], P(('dp', 'ctx')), may hold values from 0.29882812 to 3
- w_gate: bfloat16 [1536, 4096], P(('dp', 'ctx')), may hold values from -0.15625 to 0.15625
- w_up: bfloat16 [1536, 4096], P(('dp', 'ctx')), may hold values from -0.15625 to 0.15625
- w_down: bfloat16 [4096, 1536], P(('dp', 'ctx')), may hold values from -0.1875 to 0.1875
Outputs:
- output: bfloat16 [4096, 1536], P(('dp', 'ctx'))
- grad_tokens: float32 [4096, 1536], P(('dp', 'ctx'))
- grad_gain_attn: float32 [1536], P(('dp', 'ctx'))
- grad_w_query: float32 [1536, 1536], P(('dp', 'ctx'))
- grad_w_key: float32 [1536, 768], P(('dp', 'ctx'))
- grad_w_value: float32 [1536, 768], P(('dp', 'ctx'))
- grad_w_out: float32 [1536, 1536], P(('dp', 'ctx'))
- grad_gain_ffn: float32 [1536], P(('dp', 'ctx'))
- grad_w_gate: float32 [1536, 4096], P(('dp', 'ctx'))
- grad_w_up: float32 [1536, 4096], P(('dp', 'ctx'))
- grad_w_down: float32 [4096, 1536], P(('dp', 'ctx'))
The draws below stay inside these ranges and needn't reach their ends.
All inputs are finite; a program needn't handle non-finite values.
Results may differ from the reference program's by a relative error of at most 0.028.
Values may be sent and summed in bfloat16 or wider, within the bound.
A program may use at most 320 MiB of HBM per device.

```python
import math
import jax
import jax.numpy as jnp
from jax import lax

MODEL_WIDTH = 1536
QUERY_HEADS = 16
KEY_VALUE_HEADS = 8
HEAD_SIZE = 96
FF = 4096
SEQUENCE_TOKENS = 1024
TOKENS = 4096
N_DP = 4


def shard_levels(rng, shape, pieces, low, largest):
    factor_of = 1.0
    for position, shards_of in pieces:
        heights = jax.random.uniform(jax.random.fold_in(jax.random.fold_in(rng, 6), position), (shards_of,), jnp.float32, low / len(pieces), largest / len(pieces))
        factor_of = factor_of * jnp.repeat(jnp.exp(heights), shape[position] // shards_of).reshape((-1,) + (1,) * (len(shape) - 1 - position))
    return factor_of


def gaussian(rng, shape, deviation, bound, pieces=(), held_as=jnp.bfloat16):
    drawn = jax.random.normal(rng, shape, jnp.float32) * deviation
    if len(pieces) > 0:
        drawn = shard_levels(rng, shape, pieces, -0.22, 0.18) * drawn
    return jnp.clip(drawn, min=-bound, max=bound).astype(held_as)


def setup_inputs(seed: int = 0) -> dict:
    streams_of = jax.random.split(jax.random.key(seed), 12)
    return {
        "tokens": gaussian(streams_of[0], (TOKENS, MODEL_WIDTH), 1.0, 6.0, ((0, 32),)),
        "cotangent": gaussian(streams_of[1], (TOKENS, MODEL_WIDTH), 1.0, 6.0, ((0, 32),)),
        "gain_attn": jnp.clip(1.0 + 0.1 * jax.random.normal(streams_of[2], (MODEL_WIDTH,), jnp.float32), 0.5, 1.5).astype(jnp.bfloat16),
        "w_query": gaussian(streams_of[3], (MODEL_WIDTH, QUERY_HEADS * HEAD_SIZE), (MODEL_WIDTH * 2 // 3) ** -0.5, 0.1875, ((0, 32),)),
        "key_weight": gaussian(streams_of[4], (MODEL_WIDTH, KEY_VALUE_HEADS * HEAD_SIZE), (MODEL_WIDTH * 2 // 3) ** -0.5, 0.1875, ((0, 32),)),
        "value_weight": gaussian(streams_of[5], (MODEL_WIDTH, KEY_VALUE_HEADS * HEAD_SIZE), MODEL_WIDTH ** -0.5, 0.15625, ((0, 32),)),
        "w_out": gaussian(streams_of[6], (QUERY_HEADS * HEAD_SIZE, MODEL_WIDTH), (max(1, MODEL_WIDTH // 256)) ** -0.5, 2.5, ((0, 32),)),
        "gain_ffn": jnp.clip(jnp.exp(math.log(3.0) - 2.306499 * jax.random.uniform(streams_of[7], (MODEL_WIDTH,), jnp.float32) ** shard_levels(streams_of[7], (MODEL_WIDTH,), ((0, 32),), -0.2, 0.2)), 0.29882812, 3.0).astype(jnp.bfloat16),
        "w_gate": gaussian(streams_of[8], (MODEL_WIDTH, FF), MODEL_WIDTH ** -0.5, 0.15625, ((0, 32),)),
        "w_up": gaussian(streams_of[9], (MODEL_WIDTH, FF), MODEL_WIDTH ** -0.5, 0.15625, ((0, 32),)),
        "w_down": gaussian(streams_of[10], (FF, MODEL_WIDTH), (FF // 4) ** -0.5, 0.1875, ((0, 32),)),
    }


NORM_EPS = 1e-05
ROPE_THETA = 100000.0
MASK_FILL = -1e+30

@jax.custom_vjp
def lower_precision(v):
    return lax.optimization_barrier(v.astype(jnp.bfloat16)).astype(jnp.float32)

@jax.custom_vjp
def lower_precision_backward(v):
    return v

def low_keep(v):
    return (lower_precision(v), None)

def low_pass(kept, grad):
    return (grad,)

def back_keep(v):
    return (v, None)

def back_low(kept, grad):
    return (lower_precision(grad),)
lower_precision.defvjp(low_keep, low_pass)
lower_precision_backward.defvjp(back_keep, back_low)

def product_exact(left, right):
    return jnp.dot(left, right, precision=lax.Precision.HIGHEST)

def rms_norm(value_rows, gain):
    return value_rows * lax.rsqrt(lax.optimization_barrier(jnp.mean(value_rows * value_rows, axis=-1, keepdims=True)) + NORM_EPS) * gain

def rope_tables(block_count):
    half_dim = HEAD_SIZE // 2
    positions = jnp.arange(block_count, dtype=jnp.float32)
    frequency = ROPE_THETA ** (-jnp.arange(half_dim, dtype=jnp.float32) * 2.0 / HEAD_SIZE)
    angles = positions[:, None] * frequency[None, :]
    return (jnp.cos(angles)[:, None, :], jnp.sin(angles)[:, None, :])

def apply_rotary(value_rows, cosine_table, sine_values):
    half_dim = HEAD_SIZE // 2
    first_half = value_rows[..., :half_dim]
    second_half = value_rows[..., half_dim:]
    return jnp.concatenate([first_half * cosine_table - second_half * sine_values, second_half * cosine_table + first_half * sine_values], axis=-1)

def attend(query_rows, keys_rot, value_rows):
    block_rows = min(512, SEQUENCE_TOKENS)
    score_scale = HEAD_SIZE ** (-0.5)
    key_pos = jnp.arange(SEQUENCE_TOKENS, dtype=jnp.int32)

    def attend_block(block_index):
        first_row = (block_index * block_rows).astype(jnp.int32)
        query_block = lax.dynamic_slice_in_dim(query_rows, first_row, block_rows, 0)
        scores = jnp.einsum('tkgd,skd->kgts', query_block, keys_rot, precision=lax.Precision.HIGHEST) * score_scale
        query_pos = first_row + jnp.arange(block_rows, dtype=jnp.int32)
        allowed = key_pos[None, :] <= query_pos[:, None]
        scores = lower_precision_backward(jnp.where(allowed, scores, MASK_FILL))
        row_max = lax.optimization_barrier(jnp.max(scores, axis=-1, keepdims=True))
        expo = jnp.exp(scores - row_max)
        probs = expo / lax.optimization_barrier(jnp.sum(expo, axis=-1, keepdims=True))
        result = jnp.einsum('kgts,skd->tkgd', lower_precision(probs), value_rows, precision=lax.Precision.HIGHEST)
        return result.reshape(block_rows, QUERY_HEADS * HEAD_SIZE)
    blocks = lax.map(jax.checkpoint(attend_block), jnp.arange(SEQUENCE_TOKENS // block_rows, dtype=jnp.int32))
    return blocks.reshape(SEQUENCE_TOKENS, QUERY_HEADS * HEAD_SIZE)

def forward(inputs, gain_attn, w_query, key_weight, value_weight, w_out, gain_ffn, w_gate, w_up, w_down):
    head_group = QUERY_HEADS // KEY_VALUE_HEADS
    first_normed = lower_precision(rms_norm(inputs, gain_attn))
    query_unrotated = lower_precision_backward(product_exact(first_normed, w_query)).reshape(SEQUENCE_TOKENS, QUERY_HEADS, HEAD_SIZE)
    key_unrotated = lower_precision_backward(product_exact(first_normed, key_weight)).reshape(SEQUENCE_TOKENS, KEY_VALUE_HEADS, HEAD_SIZE)
    value_rows = lower_precision(lower_precision_backward(product_exact(first_normed, value_weight))).reshape(SEQUENCE_TOKENS, KEY_VALUE_HEADS, HEAD_SIZE)
    cosine_table, sine_values = rope_tables(SEQUENCE_TOKENS)
    query_rows = lower_precision(apply_rotary(query_unrotated, cosine_table, sine_values)).reshape(SEQUENCE_TOKENS, KEY_VALUE_HEADS, head_group, HEAD_SIZE)
    keys_rot = lower_precision(apply_rotary(key_unrotated, cosine_table, sine_values))
    attn_out = lower_precision(lower_precision_backward(attend(query_rows, keys_rot, value_rows)))
    middle = inputs + lower_precision_backward(product_exact(attn_out, w_out))
    normed_two = lower_precision(rms_norm(middle, gain_ffn))
    gate_value = lower_precision_backward(product_exact(normed_two, w_gate))
    up_value = lower_precision_backward(product_exact(normed_two, w_up))
    hidden = lower_precision(gate_value * jax.nn.sigmoid(gate_value) * up_value)
    return middle + lower_precision_backward(product_exact(hidden, w_down))

def reference(tokens, cotangent, gain_attn, w_query, key_weight, value_weight, w_out, gain_ffn, w_gate, w_up, w_down):
    weights = (gain_attn.astype(jnp.float32), w_query.astype(jnp.float32), key_weight.astype(jnp.float32), value_weight.astype(jnp.float32), w_out.astype(jnp.float32), gain_ffn.astype(jnp.float32), w_gate.astype(jnp.float32), w_up.astype(jnp.float32), w_down.astype(jnp.float32))
    sequences = tokens.astype(jnp.float32).reshape(N_DP, SEQUENCE_TOKENS, MODEL_WIDTH)
    seq_grads = cotangent.astype(jnp.float32).reshape(N_DP, SEQUENCE_TOKENS, MODEL_WIDTH)

    def one_sequence(totals, seq_pair):
        inputs, grad_output = seq_pair
        result, pullback = jax.vjp(forward, inputs, *weights)
        gradients = pullback(grad_output)
        totals = tuple((total + grad for total, grad in zip(totals, gradients[1:])))
        return (totals, (result.astype(jnp.bfloat16), gradients[0]))
    starting = tuple((jnp.zeros_like(weight) for weight in weights))
    totals, (results, input_grads) = lax.scan(one_sequence, starting, (sequences, seq_grads))
    return (results.reshape(TOKENS, MODEL_WIDTH), input_grads.reshape(TOKENS, MODEL_WIDTH), totals[0], totals[1], totals[2], totals[3], totals[4], totals[5], totals[6], totals[7], totals[8])
```

```python
import jax
import jax.numpy as jnp
from jax import lax
from jax.sharding import PartitionSpec as P

QUERY_HEADS = 16
KEY_VALUE_HEADS = 8
HEAD_SIZE = 96


NORM_EPS = 1e-05
ROPE_THETA = 100000.0
MASK_FILL = -1e30


def passed_along(value, axis, by):
    peers = lax.axis_size(axis)
    pairs = [(i, i + by) for i in range(peers) if 0 <= i + by < peers]
    return lax.ppermute(value, axis, pairs)


def shifted(block, axis, distance):
    devices = range(lax.axis_size(axis))
    route = [((i - distance) % len(devices), i) for i in devices]
    return lax.ppermute(block, axis, route)


def rope_tables(first_row, block_count):
    half_dim = HEAD_SIZE // 2
    positions = (first_row + jnp.arange(block_count, dtype=jnp.int32)).astype(jnp.float32)
    frequency = ROPE_THETA ** (-jnp.arange(half_dim, dtype=jnp.float32) * 2.0 / HEAD_SIZE)
    angles = positions[:, None] * frequency[None, :]
    return (jnp.cos(angles)[:, None, :], jnp.sin(angles)[:, None, :])


def apply_rotary(value_rows, cosine_table, sine_values, direction):
    half_dim = HEAD_SIZE // 2
    first_half = value_rows[..., :half_dim]
    second_half = value_rows[..., half_dim:]
    return jnp.concatenate(
        [
            first_half * cosine_table - direction * second_half * sine_values,
            second_half * cosine_table + direction * first_half * sine_values,
        ],
        axis=-1,
    )


def norm_back(grad_normed, inputs, inv_root, gain):
    grad_gain = jnp.sum(grad_normed * inputs * inv_root, axis=0)
    scaled = grad_normed * gain.astype(jnp.float32)
    grad_inputs = inv_root * (
        scaled - inputs * inv_root * inv_root * jnp.mean(scaled * inputs, axis=-1, keepdims=True)
    )
    return (grad_gain, grad_inputs)


def row_product(left, right):
    return jnp.einsum("tc,tf->cf", left, right, preferred_element_type=jnp.float32)


def blockwise_layer(
    tokens,
    cotangent,
    gain_attn,
    w_query,
    key_weight,
    value_weight,
    w_out,
    gain_ffn,
    w_gate,
    w_up,
    w_down,
):
    token_rows = tokens.shape[0]
    head_group = QUERY_HEADS // KEY_VALUE_HEADS
    key_value_width = KEY_VALUE_HEADS * HEAD_SIZE
    query_width = QUERY_HEADS * HEAD_SIZE
    score_scale = HEAD_SIZE ** (-0.5)
    ctx_count = lax.axis_size("ctx")
    ctx_rank = lax.axis_index("ctx")
    first_row = ctx_rank * token_rows
    query_pos = first_row + jnp.arange(token_rows, dtype=jnp.int32)
    attn_full = (
        lax.all_gather(gain_attn, ("dp", "ctx"), axis=0, tiled=True),
        lax.all_gather(w_query, ("dp", "ctx"), axis=0, tiled=True),
        lax.all_gather(key_weight, ("dp", "ctx"), axis=0, tiled=True),
        lax.all_gather(value_weight, ("dp", "ctx"), axis=0, tiled=True),
        lax.all_gather(w_out, ("dp", "ctx"), axis=0, tiled=True),
    )
    gain_one, query_full, key_full, value_full, out_full = attn_full
    inputs = tokens.astype(jnp.float32)
    inv_one = lax.rsqrt(jnp.mean(inputs * inputs, axis=-1, keepdims=True) + NORM_EPS)
    first_normed = (inputs * inv_one * gain_one.astype(jnp.float32)).astype(jnp.bfloat16)
    query_unrotated = jnp.dot(first_normed, query_full, preferred_element_type=jnp.float32).reshape(
        token_rows, QUERY_HEADS, HEAD_SIZE
    )
    key_unrotated = jnp.dot(first_normed, key_full, preferred_element_type=jnp.float32).reshape(
        token_rows, KEY_VALUE_HEADS, HEAD_SIZE
    )
    value_raw = jnp.dot(first_normed, value_full, preferred_element_type=jnp.float32)
    cosine_table, sine_values = rope_tables(first_row, token_rows)
    query_rows = (
        apply_rotary(query_unrotated, cosine_table, sine_values, 1.0)
        .astype(jnp.bfloat16)
        .reshape(token_rows, KEY_VALUE_HEADS, head_group, HEAD_SIZE)
    )
    keys_rot = (
        apply_rotary(key_unrotated, cosine_table, sine_values, 1.0)
        .astype(jnp.bfloat16)
        .reshape(token_rows, key_value_width)
    )
    kv_local = jnp.concatenate([keys_rot, value_raw.astype(jnp.bfloat16)], axis=1)
    starting = (
        jnp.full((KEY_VALUE_HEADS, head_group, token_rows), MASK_FILL, jnp.float32),
        jnp.zeros((KEY_VALUE_HEADS, head_group, token_rows), jnp.float32),
        jnp.zeros((token_rows, KEY_VALUE_HEADS, head_group, HEAD_SIZE), jnp.float32),
    )
    sequence_portion = lax.all_gather(kv_local, "ctx", axis=0, tiled=True)

    def update(state):
        run_max, run_sum, run_acc = state
        block_count = sequence_portion.shape[0]
        key_portion = sequence_portion[:, :key_value_width].reshape(
            block_count, KEY_VALUE_HEADS, HEAD_SIZE
        )
        value_portion = sequence_portion[:, key_value_width:].reshape(
            block_count, KEY_VALUE_HEADS, HEAD_SIZE
        )
        scores = (
            jnp.einsum(
                "tkgd,skd->kgts", query_rows, key_portion, preferred_element_type=jnp.float32
            )
            * score_scale
        )
        key_pos = jnp.arange(block_count, dtype=jnp.int32)
        allowed = key_pos[None, :] <= query_pos[:, None]
        scores = jnp.where(allowed, scores, MASK_FILL)
        new_max = jnp.maximum(run_max, jnp.max(scores, axis=-1))
        expo = jnp.exp(scores - new_max[..., None])
        new_sum = jnp.sum(expo, axis=-1)
        added = jnp.einsum(
            "kgts,skd->tkgd",
            expo.astype(jnp.bfloat16),
            value_portion,
            preferred_element_type=jnp.float32,
        )
        return (new_max, new_sum, added)

    def unchanged(state):
        return state

    run_max, run_sum, run_acc = lax.cond(
        jnp.int32(0) <= first_row + token_rows - 1, update, unchanged, starting
    )
    attn_four = run_acc / jnp.transpose(run_sum, (2, 0, 1))[..., None]
    log_total = run_max + jnp.log(run_sum)
    attn_out = attn_four.reshape(token_rows, query_width)
    attn_low = attn_out.astype(jnp.bfloat16)
    middle = inputs + jnp.dot(attn_low, out_full, preferred_element_type=jnp.float32)
    mlp_full = (
        lax.all_gather(gain_ffn, ("dp", "ctx"), axis=0, tiled=True),
        lax.all_gather(w_gate, ("dp", "ctx"), axis=0, tiled=True),
        lax.all_gather(w_up, ("dp", "ctx"), axis=0, tiled=True),
        lax.all_gather(w_down, ("dp", "ctx"), axis=0, tiled=True),
    )
    gain_two, gate_full, up_full, down_full = mlp_full
    inv_two = lax.rsqrt(jnp.mean(middle * middle, axis=-1, keepdims=True) + NORM_EPS)
    normed_two = (middle * inv_two * gain_two.astype(jnp.float32)).astype(jnp.bfloat16)
    gate_value = jnp.dot(normed_two, gate_full, preferred_element_type=jnp.float32)
    up_value = jnp.dot(normed_two, up_full, preferred_element_type=jnp.float32)
    sigmoid_gate = jax.nn.sigmoid(gate_value)
    silu_gate = gate_value * sigmoid_gate
    hidden = (silu_gate * up_value).astype(jnp.bfloat16)
    output = (middle + jnp.dot(hidden, down_full, preferred_element_type=jnp.float32)).astype(
        jnp.bfloat16
    )
    mlp_back = (
        lax.all_gather(gain_ffn, ("dp", "ctx"), axis=0, tiled=True),
        lax.all_gather(w_gate, ("dp", "ctx"), axis=0, tiled=True),
        lax.all_gather(w_up, ("dp", "ctx"), axis=0, tiled=True),
        lax.all_gather(w_down, ("dp", "ctx"), axis=0, tiled=True),
    )
    gain_two_back, gate_back, up_back, down_back = mlp_back
    grad_out = cotangent.astype(jnp.float32)
    grad_hidden = jnp.einsum("td,fd->tf", cotangent, down_back, preferred_element_type=jnp.float32)
    grad_gate = (
        grad_hidden * up_value * sigmoid_gate * (1.0 + gate_value * (1.0 - sigmoid_gate))
    ).astype(jnp.bfloat16)
    grad_up = (grad_hidden * silu_gate).astype(jnp.bfloat16)
    grad_normed_two = jnp.einsum(
        "tf,cf->tc", grad_gate, gate_back, preferred_element_type=jnp.float32
    ) + jnp.einsum("tf,cf->tc", grad_up, up_back, preferred_element_type=jnp.float32)
    grad_gain_two, grad_middle_norm = norm_back(grad_normed_two, middle, inv_two, gain_two_back)
    grad_middle = grad_out + grad_middle_norm
    gate_up_pair = jnp.concatenate([grad_gate, grad_up], axis=1)
    gate_up_sum = lax.psum_scatter(
        row_product(normed_two, gate_up_pair), ("dp", "ctx"), scatter_dimension=0, tiled=True
    )
    grad_down_sum = lax.psum_scatter(
        row_product(hidden, cotangent), ("dp", "ctx"), scatter_dimension=0, tiled=True
    )
    attn_back = (
        lax.all_gather(gain_attn, ("dp", "ctx"), axis=0, tiled=True),
        lax.all_gather(w_query, ("dp", "ctx"), axis=0, tiled=True),
        lax.all_gather(key_weight, ("dp", "ctx"), axis=0, tiled=True),
        lax.all_gather(value_weight, ("dp", "ctx"), axis=0, tiled=True),
        lax.all_gather(w_out, ("dp", "ctx"), axis=0, tiled=True),
    )
    gain_one_back, query_back, key_back, value_back, out_back = attn_back
    grad_branch = grad_middle.astype(jnp.bfloat16)
    attention_gradient = jnp.einsum(
        "td,cd->tc", grad_branch, out_back, preferred_element_type=jnp.float32
    ).astype(jnp.bfloat16)
    gradient_quad = attention_gradient.reshape(token_rows, KEY_VALUE_HEADS, head_group, HEAD_SIZE)
    delta_rows = jnp.transpose(
        jnp.sum(gradient_quad.astype(jnp.float32) * attn_four, axis=-1), (1, 2, 0)
    )

    def pair_terms(key_value_block, key_first):
        block_count = key_value_block.shape[0]
        key_portion = key_value_block[:, :key_value_width].reshape(
            block_count, KEY_VALUE_HEADS, HEAD_SIZE
        )
        value_portion = key_value_block[:, key_value_width:].reshape(
            block_count, KEY_VALUE_HEADS, HEAD_SIZE
        )
        scores = (
            jnp.einsum(
                "tkgd,skd->kgts", query_rows, key_portion, preferred_element_type=jnp.float32
            )
            * score_scale
        )
        key_pos = key_first + jnp.arange(block_count, dtype=jnp.int32)
        allowed = key_pos[None, :] <= query_pos[:, None]
        scores = jnp.where(allowed, scores, MASK_FILL)
        probs = jnp.exp(scores - log_total[..., None])
        grad_probs = jnp.einsum(
            "tkgd,skd->kgts", gradient_quad, value_portion, preferred_element_type=jnp.float32
        )
        grad_scores = (probs * (grad_probs - delta_rows[..., None])).astype(jnp.bfloat16)
        grad_query = (
            jnp.einsum(
                "kgts,skd->tkgd", grad_scores, key_portion, preferred_element_type=jnp.float32
            )
            * score_scale
        )
        grad_keys = (
            jnp.einsum(
                "kgts,tkgd->skd", grad_scores, query_rows, preferred_element_type=jnp.float32
            )
            * score_scale
        )
        grad_values = jnp.einsum(
            "kgts,tkgd->skd",
            probs.astype(jnp.bfloat16),
            gradient_quad,
            preferred_element_type=jnp.float32,
        )
        return (
            grad_query,
            jnp.concatenate(
                [
                    grad_keys.reshape(block_count, key_value_width),
                    grad_values.reshape(block_count, key_value_width),
                ],
                axis=1,
            ),
        )

    def add_pair(operands):
        kv_use, key_first, grad_query, grad_now = operands
        more_query, more_kv = pair_terms(kv_use, key_first)
        return (grad_query + more_query, grad_now + more_kv)

    def keep_pair(operands):
        return (operands[2], operands[3])

    def cycle_step(step, state):
        kv_now, grad_now, grad_query = state
        owner = (ctx_rank - step + ctx_count) % ctx_count
        kv_next = passed_along(kv_now, "ctx", 1)
        grad_query, grad_now = lax.cond(
            owner <= ctx_rank,
            add_pair,
            keep_pair,
            (kv_now, owner * token_rows, grad_query, grad_now),
        )
        grad_next = shifted(grad_now.astype(jnp.bfloat16), "ctx", 1).astype(grad_now.dtype)
        return (kv_next, grad_next, grad_query)

    cycle_start = (
        kv_local,
        jnp.zeros((token_rows, 2 * key_value_width), jnp.float32),
        jnp.zeros((token_rows, KEY_VALUE_HEADS, head_group, HEAD_SIZE), jnp.float32),
    )
    kv_final, key_value_gradient, grad_query = lax.fori_loop(0, ctx_count, cycle_step, cycle_start)
    grad_query_raw = (
        apply_rotary(
            grad_query.reshape(token_rows, QUERY_HEADS, HEAD_SIZE), cosine_table, sine_values, -1.0
        )
        .reshape(token_rows, query_width)
        .astype(jnp.bfloat16)
    )
    grad_key_raw = (
        apply_rotary(
            key_value_gradient[:, :key_value_width].reshape(token_rows, KEY_VALUE_HEADS, HEAD_SIZE),
            cosine_table,
            sine_values,
            -1.0,
        )
        .reshape(token_rows, key_value_width)
        .astype(jnp.bfloat16)
    )
    grad_value_raw = key_value_gradient[:, key_value_width:].astype(jnp.bfloat16)
    grad_normed_one = (
        jnp.einsum("tq,cq->tc", grad_query_raw, query_back, preferred_element_type=jnp.float32)
        + jnp.einsum("tq,cq->tc", grad_key_raw, key_back, preferred_element_type=jnp.float32)
        + jnp.einsum("tq,cq->tc", grad_value_raw, value_back, preferred_element_type=jnp.float32)
    )
    grad_gain_one, grad_input_norm = norm_back(grad_normed_one, inputs, inv_one, gain_one_back)
    grad_tokens = grad_middle + grad_input_norm
    projection_grads = jnp.concatenate([grad_query_raw, grad_key_raw, grad_value_raw], axis=1)
    qkv_sum = lax.psum_scatter(
        row_product(first_normed, projection_grads), ("dp", "ctx"), scatter_dimension=0, tiled=True
    )
    grad_out_sum = lax.psum_scatter(
        row_product(attn_low, grad_branch), ("dp", "ctx"), scatter_dimension=0, tiled=True
    )
    gain_sums = (
        lax.psum_scatter(grad_gain_one, ("dp", "ctx"), scatter_dimension=0, tiled=True),
        lax.psum_scatter(grad_gain_two, ("dp", "ctx"), scatter_dimension=0, tiled=True),
    )
    ff_width = w_gate.shape[1]
    return (
        output,
        grad_tokens,
        gain_sums[0],
        qkv_sum[:, :query_width],
        qkv_sum[:, query_width : query_width + key_value_width],
        qkv_sum[:, query_width + key_value_width :],
        grad_out_sum,
        gain_sums[1],
        gate_up_sum[:, :ff_width],
        gate_up_sum[:, ff_width:],
        grad_down_sum,
    )


def weight_columns(weight, chunk_of, row_count):
    by_share = lax.all_to_all(chunk_of(weight), "ctx", split_axis=0, concat_axis=0, tiled=True)
    rows = by_share.reshape(-1, by_share.shape[-1])
    return lax.all_gather(rows, "dp", axis=0, tiled=True)


def gradient_rows(partial, ctx_count):
    mine = lax.psum_scatter(partial.astype(jnp.bfloat16), "dp", scatter_dimension=0, tiled=True)
    blocks = mine.reshape(ctx_count, -1, mine.shape[-1])
    return lax.all_to_all(blocks, "ctx", split_axis=0, concat_axis=0, tiled=True).astype(jnp.float32)


def normed(rows, gain):
    inv_root = lax.rsqrt(jnp.mean(rows * rows, axis=-1, keepdims=True) + NORM_EPS)
    return inv_root, (rows * inv_root * gain.astype(jnp.float32)).astype(jnp.bfloat16)


def split_layer(
    tokens,
    cotangent,
    gain_attn,
    w_query,
    key_weight,
    value_weight,
    w_out,
    gain_ffn,
    w_gate,
    w_up,
    w_down,
):
    ctx_count = lax.axis_size("ctx")
    dp_count = lax.axis_size("dp")
    ctx_rank = lax.axis_index("ctx")
    block_rows, width = tokens.shape
    weight_rows = w_query.shape[0]
    head_group = QUERY_HEADS // KEY_VALUE_HEADS
    score_scale = HEAD_SIZE ** (-0.5)
    query_share = head_group * HEAD_SIZE
    first_row = ctx_rank * block_rows
    seq_rows = block_rows * ctx_count
    ff_width = w_gate.shape[1]
    down_rows = w_down.shape[0]
    ff_share = dp_count * down_rows

    def own(rows):
        return lax.dynamic_slice_in_dim(rows, first_row, block_rows, 0)

    gain_one = lax.all_gather(gain_attn, ("dp", "ctx"), axis=0, tiled=True)
    gain_two = lax.all_gather(gain_ffn, ("dp", "ctx"), axis=0, tiled=True)
    x_all = lax.all_gather(tokens, "ctx", axis=0, tiled=True)
    ct_all = lax.all_gather(cotangent, "ctx", axis=0, tiled=True)

    def qkv_chunks(_):
        q = w_query.reshape(weight_rows, ctx_count, -1)
        k = key_weight.reshape(weight_rows, ctx_count, -1)
        v = value_weight.reshape(weight_rows, ctx_count, -1)
        return jnp.transpose(jnp.concatenate([q, k, v], axis=2), (1, 0, 2))

    def ff_chunks(weight):
        cut = weight.reshape(weight_rows, dp_count, ctx_count, down_rows)
        return jnp.transpose(cut, (2, 0, 1, 3)).reshape(ctx_count, weight_rows, ff_share)

    w_qkv = weight_columns(None, qkv_chunks, width)
    out_full = lax.all_gather(w_out, ("dp", "ctx"), axis=0, tiled=True)
    w_g = weight_columns(w_gate, ff_chunks, width)
    w_u = weight_columns(w_up, ff_chunks, width)
    w_d = lax.all_gather(w_down, "dp", axis=0, tiled=True)

    inputs = x_all.astype(jnp.float32)
    inv_one, h1 = normed(inputs, gain_one)
    qkv = jnp.dot(h1, w_qkv, preferred_element_type=jnp.float32)
    cosine_table, sine_values = rope_tables(0, seq_rows)
    q = apply_rotary(
        qkv[:, :query_share].reshape(seq_rows, head_group, HEAD_SIZE), cosine_table, sine_values, 1.0
    ).astype(jnp.bfloat16)
    k = apply_rotary(
        qkv[:, query_share : query_share + HEAD_SIZE].reshape(seq_rows, 1, HEAD_SIZE),
        cosine_table,
        sine_values,
        1.0,
    ).astype(jnp.bfloat16)[:, 0]
    v = qkv[:, query_share + HEAD_SIZE :].astype(jnp.bfloat16)
    scores = jnp.einsum("tgd,sd->gts", q, k, preferred_element_type=jnp.float32) * score_scale
    positions = jnp.arange(seq_rows, dtype=jnp.int32)
    allowed = positions[None, :] <= positions[:, None]
    scores = jnp.where(allowed, scores, MASK_FILL)
    top = jnp.max(scores, axis=-1)
    expo = jnp.exp(scores - top[..., None])
    total = jnp.sum(expo, axis=-1)
    attn = jnp.einsum("gts,sd->tgd", expo.astype(jnp.bfloat16), v, preferred_element_type=jnp.float32)
    attn = attn / jnp.transpose(total)[..., None]
    log_total = top + jnp.log(total)
    ob = attn.reshape(seq_rows, query_share).astype(jnp.bfloat16)
    ob_all = lax.all_gather(ob, "ctx", axis=1, tiled=True)

    middle = inputs + jnp.dot(ob_all, out_full, preferred_element_type=jnp.float32)
    inv_two, h2 = normed(middle, gain_two)
    gate = jnp.dot(h2, w_g, preferred_element_type=jnp.float32)
    up = jnp.dot(h2, w_u, preferred_element_type=jnp.float32)
    sig = jax.nn.sigmoid(gate)
    silu = gate * sig
    hidden = (silu * up).astype(jnp.bfloat16)
    out_part = jnp.dot(hidden, w_d, preferred_element_type=jnp.float32).astype(jnp.bfloat16)
    out_sum = lax.psum_scatter(out_part, "ctx", scatter_dimension=0, tiled=True)
    middle_own = own(middle)
    output = (middle_own + out_sum.astype(jnp.float32)).astype(jnp.bfloat16)

    d_hidden = jnp.einsum("td,fd->tf", ct_all, w_d, preferred_element_type=jnp.float32)
    d_gate = (d_hidden * up * sig * (1.0 + gate * (1.0 - sig))).astype(jnp.bfloat16)
    d_up = (d_hidden * silu).astype(jnp.bfloat16)
    dh2_part = jnp.einsum("tf,cf->tc", d_gate, w_g, preferred_element_type=jnp.float32) + jnp.einsum(
        "tf,cf->tc", d_up, w_u, preferred_element_type=jnp.float32
    )
    dh2 = lax.psum_scatter(
        dh2_part.astype(jnp.bfloat16), "ctx", scatter_dimension=0, tiled=True
    ).astype(jnp.float32)
    grad_gain_two, back = norm_back(dh2, middle_own, own(inv_two), gain_two)
    d_middle = cotangent.astype(jnp.float32) + back

    grad_down = lax.psum_scatter(
        row_product(hidden, ct_all).astype(jnp.bfloat16), "dp", scatter_dimension=0, tiled=True
    ).astype(jnp.float32)
    gate_rows = gradient_rows(row_product(h2, d_gate), ctx_count)
    up_rows = gradient_rows(row_product(h2, d_up), ctx_count)

    da = d_middle.astype(jnp.bfloat16)
    do_rows = jnp.einsum("td,cd->tc", da, out_full, preferred_element_type=jnp.float32).astype(
        jnp.bfloat16
    )

    def to_columns(rows):
        blocks = jnp.transpose(rows.reshape(block_rows, ctx_count, -1), (1, 0, 2))
        return lax.all_to_all(blocks, "ctx", split_axis=0, concat_axis=0, tiled=True).reshape(
            seq_rows, -1
        )

    do = to_columns(do_rows).reshape(seq_rows, head_group, HEAD_SIZE)
    da_columns = to_columns(da)
    out_rows = gradient_rows(row_product(ob_all, da_columns), ctx_count)

    delta = jnp.transpose(jnp.sum(do.astype(jnp.float32) * attn, axis=-1))
    probs = jnp.exp(scores - log_total[..., None])
    d_probs = jnp.einsum("tgd,sd->gts", do, v, preferred_element_type=jnp.float32)
    d_scores = (probs * (d_probs - delta[..., None])).astype(jnp.bfloat16)
    dq = jnp.einsum("gts,sd->tgd", d_scores, k, preferred_element_type=jnp.float32) * score_scale
    dk = jnp.einsum("gts,tgd->sd", d_scores, q, preferred_element_type=jnp.float32) * score_scale
    dv = jnp.einsum("gts,tgd->sd", probs.astype(jnp.bfloat16), do, preferred_element_type=jnp.float32)
    dq = apply_rotary(dq, cosine_table, sine_values, -1.0).reshape(seq_rows, query_share)
    dk = apply_rotary(dk[:, None], cosine_table, sine_values, -1.0)[:, 0]
    d_qkv = jnp.concatenate([dq, dk, dv], axis=1).astype(jnp.bfloat16)
    qkv_rows = gradient_rows(row_product(h1, d_qkv), ctx_count)
    dh1_part = jnp.einsum("tq,cq->tc", d_qkv, w_qkv, preferred_element_type=jnp.float32)
    dh1 = lax.psum_scatter(
        dh1_part.astype(jnp.bfloat16), "ctx", scatter_dimension=0, tiled=True
    ).astype(jnp.float32)
    grad_gain_one, back = norm_back(dh1, own(inputs), own(inv_one), gain_one)
    grad_tokens = d_middle + back

    def joined(blocks):
        return jnp.transpose(blocks, (1, 0, 2)).reshape(blocks.shape[1], -1)

    def ff_joined(blocks):
        cut = blocks.reshape(ctx_count, weight_rows, dp_count, down_rows)
        return jnp.transpose(cut, (1, 2, 0, 3)).reshape(weight_rows, ff_width)

    return (
        output,
        grad_tokens,
        lax.psum_scatter(grad_gain_one, ("dp", "ctx"), scatter_dimension=0, tiled=True),
        joined(qkv_rows[:, :, :query_share]),
        joined(qkv_rows[:, :, query_share : query_share + HEAD_SIZE]),
        joined(qkv_rows[:, :, query_share + HEAD_SIZE :]),
        joined(out_rows),
        lax.psum_scatter(grad_gain_two, ("dp", "ctx"), scatter_dimension=0, tiled=True),
        ff_joined(gate_rows),
        ff_joined(up_rows),
        grad_down,
    )


def solution(mesh):
    heads_split = mesh.shape["ctx"] == KEY_VALUE_HEADS
    return jax.shard_map(
        split_layer if heads_split else blockwise_layer,
        mesh=mesh,
        in_specs=(
            P(("dp", "ctx"), None),
            P(("dp", "ctx"), None),
            P(("dp", "ctx")),
            P(("dp", "ctx"), None),
            P(("dp", "ctx"), None),
            P(("dp", "ctx"), None),
            P(("dp", "ctx"), None),
            P(("dp", "ctx")),
            P(("dp", "ctx"), None),
            P(("dp", "ctx"), None),
            P(("dp", "ctx"), None),
        ),
        out_specs=(
            P(("dp", "ctx"), None),
            P(("dp", "ctx"), None),
            P(("dp", "ctx")),
            P(("dp", "ctx"), None),
            P(("dp", "ctx"), None),
            P(("dp", "ctx"), None),
            P(("dp", "ctx"), None),
            P(("dp", "ctx")),
            P(("dp", "ctx"), None),
            P(("dp", "ctx"), None),
            P(("dp", "ctx"), None),
        ),
        check_vma=False,
    )
```

```python
import functools

import jax
import jax.numpy as jnp
from jax import lax
from jax.experimental import pallas as pl
from jax.experimental.pallas import tpu as pltpu
from jax.sharding import PartitionSpec as P

QUERY_HEADS = 16
KEY_VALUE_HEADS = 8
HEAD_SIZE = 96


NORM_EPS = 1e-05
ROPE_THETA = 100000.0
MASK_FILL = -1e30


def passed_along(value, axis, by):
    peers = lax.axis_size(axis)
    pairs = [(i, i + by) for i in range(peers) if 0 <= i + by < peers]
    return lax.ppermute(value, axis, pairs)


def shifted(block, axis, distance):
    devices = range(lax.axis_size(axis))
    route = [((i - distance) % len(devices), i) for i in devices]
    return lax.ppermute(block, axis, route)


def rope_tables(first_row, block_count):
    half_dim = HEAD_SIZE // 2
    positions = (first_row + jnp.arange(block_count, dtype=jnp.int32)).astype(jnp.float32)
    frequency = ROPE_THETA ** (-jnp.arange(half_dim, dtype=jnp.float32) * 2.0 / HEAD_SIZE)
    angles = positions[:, None] * frequency[None, :]
    return (jnp.cos(angles)[:, None, :], jnp.sin(angles)[:, None, :])


def apply_rotary(value_rows, cosine_table, sine_values, direction):
    half_dim = HEAD_SIZE // 2
    first_half = value_rows[..., :half_dim]
    second_half = value_rows[..., half_dim:]
    return jnp.concatenate(
        [
            first_half * cosine_table - direction * second_half * sine_values,
            second_half * cosine_table + direction * first_half * sine_values,
        ],
        axis=-1,
    )


def norm_back(grad_normed, inputs, inv_root, gain):
    grad_gain = jnp.sum(grad_normed * inputs * inv_root, axis=0)
    scaled = grad_normed * gain.astype(jnp.float32)
    grad_inputs = inv_root * (
        scaled - inputs * inv_root * inv_root * jnp.mean(scaled * inputs, axis=-1, keepdims=True)
    )
    return (grad_gain, grad_inputs)


def row_product(left, right):
    return jnp.einsum("tc,tf->cf", left, right, preferred_element_type=jnp.float32)


def blockwise_layer(
    tokens,
    cotangent,
    gain_attn,
    w_query,
    key_weight,
    value_weight,
    w_out,
    gain_ffn,
    w_gate,
    w_up,
    w_down,
):
    token_rows = tokens.shape[0]
    head_group = QUERY_HEADS // KEY_VALUE_HEADS
    key_value_width = KEY_VALUE_HEADS * HEAD_SIZE
    query_width = QUERY_HEADS * HEAD_SIZE
    score_scale = HEAD_SIZE ** (-0.5)
    ctx_count = lax.axis_size("ctx")
    ctx_rank = lax.axis_index("ctx")
    first_row = ctx_rank * token_rows
    query_pos = first_row + jnp.arange(token_rows, dtype=jnp.int32)
    attn_full = (
        lax.all_gather(gain_attn, ("dp", "ctx"), axis=0, tiled=True),
        lax.all_gather(w_query, ("dp", "ctx"), axis=0, tiled=True),
        lax.all_gather(key_weight, ("dp", "ctx"), axis=0, tiled=True),
        lax.all_gather(value_weight, ("dp", "ctx"), axis=0, tiled=True),
        lax.all_gather(w_out, ("dp", "ctx"), axis=0, tiled=True),
    )
    gain_one, query_full, key_full, value_full, out_full = attn_full
    inputs = tokens.astype(jnp.float32)
    inv_one = lax.rsqrt(jnp.mean(inputs * inputs, axis=-1, keepdims=True) + NORM_EPS)
    first_normed = (inputs * inv_one * gain_one.astype(jnp.float32)).astype(jnp.bfloat16)
    query_unrotated = jnp.dot(first_normed, query_full, preferred_element_type=jnp.float32).reshape(
        token_rows, QUERY_HEADS, HEAD_SIZE
    )
    key_unrotated = jnp.dot(first_normed, key_full, preferred_element_type=jnp.float32).reshape(
        token_rows, KEY_VALUE_HEADS, HEAD_SIZE
    )
    value_raw = jnp.dot(first_normed, value_full, preferred_element_type=jnp.float32)
    cosine_table, sine_values = rope_tables(first_row, token_rows)
    query_rows = (
        apply_rotary(query_unrotated, cosine_table, sine_values, 1.0)
        .astype(jnp.bfloat16)
        .reshape(token_rows, KEY_VALUE_HEADS, head_group, HEAD_SIZE)
    )
    keys_rot = (
        apply_rotary(key_unrotated, cosine_table, sine_values, 1.0)
        .astype(jnp.bfloat16)
        .reshape(token_rows, key_value_width)
    )
    kv_local = jnp.concatenate([keys_rot, value_raw.astype(jnp.bfloat16)], axis=1)
    starting = (
        jnp.full((KEY_VALUE_HEADS, head_group, token_rows), MASK_FILL, jnp.float32),
        jnp.zeros((KEY_VALUE_HEADS, head_group, token_rows), jnp.float32),
        jnp.zeros((token_rows, KEY_VALUE_HEADS, head_group, HEAD_SIZE), jnp.float32),
    )
    sequence_portion = lax.all_gather(kv_local, "ctx", axis=0, tiled=True)

    def update(state):
        run_max, run_sum, run_acc = state
        block_count = sequence_portion.shape[0]
        key_portion = sequence_portion[:, :key_value_width].reshape(
            block_count, KEY_VALUE_HEADS, HEAD_SIZE
        )
        value_portion = sequence_portion[:, key_value_width:].reshape(
            block_count, KEY_VALUE_HEADS, HEAD_SIZE
        )
        scores = (
            jnp.einsum(
                "tkgd,skd->kgts", query_rows, key_portion, preferred_element_type=jnp.float32
            )
            * score_scale
        )
        key_pos = jnp.arange(block_count, dtype=jnp.int32)
        allowed = key_pos[None, :] <= query_pos[:, None]
        scores = jnp.where(allowed, scores, MASK_FILL)
        new_max = jnp.maximum(run_max, jnp.max(scores, axis=-1))
        expo = jnp.exp(scores - new_max[..., None])
        new_sum = jnp.sum(expo, axis=-1)
        added = jnp.einsum(
            "kgts,skd->tkgd",
            expo.astype(jnp.bfloat16),
            value_portion,
            preferred_element_type=jnp.float32,
        )
        return (new_max, new_sum, added)

    def unchanged(state):
        return state

    run_max, run_sum, run_acc = lax.cond(
        jnp.int32(0) <= first_row + token_rows - 1, update, unchanged, starting
    )
    attn_four = run_acc / jnp.transpose(run_sum, (2, 0, 1))[..., None]
    log_total = run_max + jnp.log(run_sum)
    attn_out = attn_four.reshape(token_rows, query_width)
    attn_low = attn_out.astype(jnp.bfloat16)
    middle = inputs + jnp.dot(attn_low, out_full, preferred_element_type=jnp.float32)
    mlp_full = (
        lax.all_gather(gain_ffn, ("dp", "ctx"), axis=0, tiled=True),
        lax.all_gather(w_gate, ("dp", "ctx"), axis=0, tiled=True),
        lax.all_gather(w_up, ("dp", "ctx"), axis=0, tiled=True),
        lax.all_gather(w_down, ("dp", "ctx"), axis=0, tiled=True),
    )
    gain_two, gate_full, up_full, down_full = mlp_full
    inv_two = lax.rsqrt(jnp.mean(middle * middle, axis=-1, keepdims=True) + NORM_EPS)
    normed_two = (middle * inv_two * gain_two.astype(jnp.float32)).astype(jnp.bfloat16)
    gate_value = jnp.dot(normed_two, gate_full, preferred_element_type=jnp.float32)
    up_value = jnp.dot(normed_two, up_full, preferred_element_type=jnp.float32)
    sigmoid_gate = jax.nn.sigmoid(gate_value)
    silu_gate = gate_value * sigmoid_gate
    hidden = (silu_gate * up_value).astype(jnp.bfloat16)
    output = (middle + jnp.dot(hidden, down_full, preferred_element_type=jnp.float32)).astype(
        jnp.bfloat16
    )
    mlp_back = (
        lax.all_gather(gain_ffn, ("dp", "ctx"), axis=0, tiled=True),
        lax.all_gather(w_gate, ("dp", "ctx"), axis=0, tiled=True),
        lax.all_gather(w_up, ("dp", "ctx"), axis=0, tiled=True),
        lax.all_gather(w_down, ("dp", "ctx"), axis=0, tiled=True),
    )
    gain_two_back, gate_back, up_back, down_back = mlp_back
    grad_out = cotangent.astype(jnp.float32)
    grad_hidden = jnp.einsum("td,fd->tf", cotangent, down_back, preferred_element_type=jnp.float32)
    grad_gate = (
        grad_hidden * up_value * sigmoid_gate * (1.0 + gate_value * (1.0 - sigmoid_gate))
    ).astype(jnp.bfloat16)
    grad_up = (grad_hidden * silu_gate).astype(jnp.bfloat16)
    grad_normed_two = jnp.einsum(
        "tf,cf->tc", grad_gate, gate_back, preferred_element_type=jnp.float32
    ) + jnp.einsum("tf,cf->tc", grad_up, up_back, preferred_element_type=jnp.float32)
    grad_gain_two, grad_middle_norm = norm_back(grad_normed_two, middle, inv_two, gain_two_back)
    grad_middle = grad_out + grad_middle_norm
    gate_up_pair = jnp.concatenate([grad_gate, grad_up], axis=1)
    gate_up_sum = lax.psum_scatter(
        row_product(normed_two, gate_up_pair), ("dp", "ctx"), scatter_dimension=0, tiled=True
    )
    grad_down_sum = lax.psum_scatter(
        row_product(hidden, cotangent), ("dp", "ctx"), scatter_dimension=0, tiled=True
    )
    attn_back = (
        lax.all_gather(gain_attn, ("dp", "ctx"), axis=0, tiled=True),
        lax.all_gather(w_query, ("dp", "ctx"), axis=0, tiled=True),
        lax.all_gather(key_weight, ("dp", "ctx"), axis=0, tiled=True),
        lax.all_gather(value_weight, ("dp", "ctx"), axis=0, tiled=True),
        lax.all_gather(w_out, ("dp", "ctx"), axis=0, tiled=True),
    )
    gain_one_back, query_back, key_back, value_back, out_back = attn_back
    grad_branch = grad_middle.astype(jnp.bfloat16)
    attention_gradient = jnp.einsum(
        "td,cd->tc", grad_branch, out_back, preferred_element_type=jnp.float32
    ).astype(jnp.bfloat16)
    gradient_quad = attention_gradient.reshape(token_rows, KEY_VALUE_HEADS, head_group, HEAD_SIZE)
    delta_rows = jnp.transpose(
        jnp.sum(gradient_quad.astype(jnp.float32) * attn_four, axis=-1), (1, 2, 0)
    )

    def pair_terms(key_value_block, key_first):
        block_count = key_value_block.shape[0]
        key_portion = key_value_block[:, :key_value_width].reshape(
            block_count, KEY_VALUE_HEADS, HEAD_SIZE
        )
        value_portion = key_value_block[:, key_value_width:].reshape(
            block_count, KEY_VALUE_HEADS, HEAD_SIZE
        )
        scores = (
            jnp.einsum(
                "tkgd,skd->kgts", query_rows, key_portion, preferred_element_type=jnp.float32
            )
            * score_scale
        )
        key_pos = key_first + jnp.arange(block_count, dtype=jnp.int32)
        allowed = key_pos[None, :] <= query_pos[:, None]
        scores = jnp.where(allowed, scores, MASK_FILL)
        probs = jnp.exp(scores - log_total[..., None])
        grad_probs = jnp.einsum(
            "tkgd,skd->kgts", gradient_quad, value_portion, preferred_element_type=jnp.float32
        )
        grad_scores = (probs * (grad_probs - delta_rows[..., None])).astype(jnp.bfloat16)
        grad_query = (
            jnp.einsum(
                "kgts,skd->tkgd", grad_scores, key_portion, preferred_element_type=jnp.float32
            )
            * score_scale
        )
        grad_keys = (
            jnp.einsum(
                "kgts,tkgd->skd", grad_scores, query_rows, preferred_element_type=jnp.float32
            )
            * score_scale
        )
        grad_values = jnp.einsum(
            "kgts,tkgd->skd",
            probs.astype(jnp.bfloat16),
            gradient_quad,
            preferred_element_type=jnp.float32,
        )
        return (
            grad_query,
            jnp.concatenate(
                [
                    grad_keys.reshape(block_count, key_value_width),
                    grad_values.reshape(block_count, key_value_width),
                ],
                axis=1,
            ),
        )

    def add_pair(operands):
        kv_use, key_first, grad_query, grad_now = operands
        more_query, more_kv = pair_terms(kv_use, key_first)
        return (grad_query + more_query, grad_now + more_kv)

    def keep_pair(operands):
        return (operands[2], operands[3])

    def cycle_step(step, state):
        kv_now, grad_now, grad_query = state
        owner = (ctx_rank - step + ctx_count) % ctx_count
        kv_next = passed_along(kv_now, "ctx", 1)
        grad_query, grad_now = lax.cond(
            owner <= ctx_rank,
            add_pair,
            keep_pair,
            (kv_now, owner * token_rows, grad_query, grad_now),
        )
        grad_next = shifted(grad_now.astype(jnp.bfloat16), "ctx", 1).astype(grad_now.dtype)
        return (kv_next, grad_next, grad_query)

    cycle_start = (
        kv_local,
        jnp.zeros((token_rows, 2 * key_value_width), jnp.float32),
        jnp.zeros((token_rows, KEY_VALUE_HEADS, head_group, HEAD_SIZE), jnp.float32),
    )
    kv_final, key_value_gradient, grad_query = lax.fori_loop(0, ctx_count, cycle_step, cycle_start)
    grad_query_raw = (
        apply_rotary(
            grad_query.reshape(token_rows, QUERY_HEADS, HEAD_SIZE), cosine_table, sine_values, -1.0
        )
        .reshape(token_rows, query_width)
        .astype(jnp.bfloat16)
    )
    grad_key_raw = (
        apply_rotary(
            key_value_gradient[:, :key_value_width].reshape(token_rows, KEY_VALUE_HEADS, HEAD_SIZE),
            cosine_table,
            sine_values,
            -1.0,
        )
        .reshape(token_rows, key_value_width)
        .astype(jnp.bfloat16)
    )
    grad_value_raw = key_value_gradient[:, key_value_width:].astype(jnp.bfloat16)
    grad_normed_one = (
        jnp.einsum("tq,cq->tc", grad_query_raw, query_back, preferred_element_type=jnp.float32)
        + jnp.einsum("tq,cq->tc", grad_key_raw, key_back, preferred_element_type=jnp.float32)
        + jnp.einsum("tq,cq->tc", grad_value_raw, value_back, preferred_element_type=jnp.float32)
    )
    grad_gain_one, grad_input_norm = norm_back(grad_normed_one, inputs, inv_one, gain_one_back)
    grad_tokens = grad_middle + grad_input_norm
    projection_grads = jnp.concatenate([grad_query_raw, grad_key_raw, grad_value_raw], axis=1)
    qkv_sum = lax.psum_scatter(
        row_product(first_normed, projection_grads), ("dp", "ctx"), scatter_dimension=0, tiled=True
    )
    grad_out_sum = lax.psum_scatter(
        row_product(attn_low, grad_branch), ("dp", "ctx"), scatter_dimension=0, tiled=True
    )
    gain_sums = (
        lax.psum_scatter(grad_gain_one, ("dp", "ctx"), scatter_dimension=0, tiled=True),
        lax.psum_scatter(grad_gain_two, ("dp", "ctx"), scatter_dimension=0, tiled=True),
    )
    ff_width = w_gate.shape[1]
    return (
        output,
        grad_tokens,
        gain_sums[0],
        qkv_sum[:, :query_width],
        qkv_sum[:, query_width : query_width + key_value_width],
        qkv_sum[:, query_width + key_value_width :],
        grad_out_sum,
        gain_sums[1],
        gate_up_sum[:, :ff_width],
        gate_up_sum[:, ff_width:],
        grad_down_sum,
    )


DP = 4
CTX = 8
STEPS = CTX - 1
HEAD_LANES = 128
HALF_LANES = 64
SHARE = 4 * HEAD_LANES
RIGHT, LEFT = 1, -1
F32 = jnp.float32
BF16 = jnp.bfloat16


def ring_place(rank):
    return jnp.where(lax.rem(rank, 2) == 0, rank // 2, CTX - 1 - rank // 2)


def ring_rank(place):
    place = lax.rem(place + 2 * CTX, CTX)
    return jnp.where(place < CTX // 2, 2 * place, 2 * CTX - 1 - 2 * place)


class Here:
    def __init__(self):
        self.dp = lax.axis_index("dp")
        self.ctx = lax.axis_index("ctx")
        self.place = ring_place(self.ctx)
        self.row = self.dp // 2
        self.core = lax.rem(self.dp, 2)
        self.next = {
            RIGHT: (self.dp, ring_rank(self.place + 1)),
            LEFT: (self.dp, ring_rank(self.place - 1)),
        }
        self.sibling_dp = self.row * 2 + 1 - self.core
        self.across_dp = (1 - self.row) * 2 + self.core
        self.sibling = (self.sibling_dp, self.ctx)
        self.across = (self.across_dp, self.ctx)

    def peer(self, ahead):
        return lax.rem(self.ctx + ahead, CTX)

    def greet(self, partners):
        barrier = pltpu.get_barrier_semaphore()
        for partner in partners:
            pl.semaphore_signal(
                barrier, inc=1, device_id=partner, device_id_type=pl.DeviceIdType.MESH
            )
        pl.semaphore_wait(barrier, len(partners))

    def peers(self):
        return [(self.dp, self.peer(ahead)) for ahead in range(1, CTX)]


def send(source, target, sems, device):
    copy = pltpu.make_async_remote_copy(
        src_ref=source,
        dst_ref=target,
        send_sem=sems[0],
        recv_sem=sems[1],
        device_id=device,
        device_id_type=pl.DeviceIdType.MESH,
    )
    copy.start()
    return copy


class Sems:
    def __init__(self, sent, received):
        self.sent, self.received, self.used = sent, received, 0

    def __call__(self):
        pair = (self.sent.at[self.used], self.received.at[self.used])
        self.used += 1
        return pair


def gather_ring(here, streams, sems):
    flying = [[] for _ in streams]
    for step in range(STEPS):
        for index, (own, place_of, way) in enumerate(streams):
            rank = ring_rank(here.place - way * step)
            if step > 0:
                flying[index][-1].wait_recv()
            source = own if step == 0 else place_of(rank)
            flying[index].append(send(source, place_of(rank), sems(), here.next[way]))
        yield
    for copies in flying:
        copies[-1].wait_recv()
    yield
    for copies in flying:
        for copy in copies:
            copy.wait_send()


def run_all(*generators):
    live = list(generators)
    while live:
        for one in list(live):
            try:
                next(one)
            except StopIteration:
                live.remove(one)


def spread_over_dp(here, place_of, sems, ready=()):
    for copy in ready:
        copy.wait()
    first = send(place_of(here.dp), place_of(here.dp), sems(), here.across)
    beside = send(place_of(here.dp), place_of(here.dp), sems(), here.sibling)
    yield
    first.wait_recv()
    last = send(place_of(here.across_dp), place_of(here.across_dp), sems(), here.sibling)
    yield
    beside.wait_recv()
    last.wait_recv()
    for copy in (first, beside, last):
        copy.wait_send()


def gather_columns(here, chunks, target, local_sem, sems):
    mine = here.dp * CTX + here.ctx
    local = pltpu.make_async_copy(chunks.at[here.ctx], target.at[mine], local_sem)
    local.start()
    copies = []
    for ahead in range(1, CTX):
        peer = here.peer(ahead)
        copies.append(send(chunks.at[peer], target.at[mine], sems(), (here.dp, peer)))
    yield
    yield
    yield
    yield from spread_over_dp(
        here, lambda dp: target.at[pl.ds(dp * CTX, CTX)], sems, copies + [local]
    )


def gather_kernel(
    tokens, cotangent, qkv, gate_up, down, out, x_all, ct_all, w_qkv, w_gu, w_d, w_o, local, sent, got
):
    here = Here()
    sems = Sems(sent, got)
    here.greet(here.peers() + [here.sibling, here.across])
    kept = [
        pltpu.make_async_copy(tokens, x_all.at[here.ctx], local.at[0]),
        pltpu.make_async_copy(cotangent, ct_all.at[here.ctx], local.at[1]),
        pltpu.make_async_copy(down, w_d.at[here.dp], local.at[2]),
        pltpu.make_async_copy(out, w_o.at[here.dp * CTX + here.ctx], local.at[3]),
    ]
    for copy in kept:
        copy.start()

    def rings(own, target, count, base=0):
        width = own.shape[1] // count
        for index in range(count):
            columns = pl.ds(index * width, width)
            yield (
                own.at[:, columns],
                lambda rank, columns=columns: target.at[base + rank, :, columns],
                RIGHT if index < count // 2 else LEFT,
            )

    def out_gather():
        yield from gather_ring(here, list(rings(out, w_o, 2, here.dp * CTX)), sems)
        kept[3].wait()
        yield from spread_over_dp(here, lambda dp: w_o.at[pl.ds(dp * CTX, CTX)], sems)

    run_all(
        gather_ring(here, list(rings(tokens, x_all, 4)), sems),
        gather_columns(here, qkv, w_qkv, local.at[4], sems),
        gather_columns(here, gate_up, w_gu, local.at[5], sems),
        out_gather(),
        gather_ring(here, list(rings(cotangent, ct_all, 4)), sems),
        spread_over_dp(here, lambda dp: w_d.at[dp], sems, [kept[2]]),
    )
    for copy in kept[:2]:
        copy.wait()


ANY = pl.BlockSpec(memory_space=pltpu.MemorySpace.HBM)
VMEM = pl.BlockSpec(memory_space=pltpu.MemorySpace.VMEM)
VMEM_BYTES = 56 * 2**20


def params(collective_id):
    return pltpu.CompilerParams(
        collective_id=collective_id, has_side_effects=True, vmem_limit_bytes=VMEM_BYTES
    )


def dma_sems(count):
    return [pltpu.SemaphoreType.DMA((count,)), pltpu.SemaphoreType.DMA((count,))]


def gather_all(tokens, cotangent, qkv, gate_up, down, out):
    rows, width = tokens.shape
    shape = lambda *dims: jax.ShapeDtypeStruct(dims, BF16)
    return pl.pallas_call(
        gather_kernel,
        out_shape=(
            shape(CTX, rows, width),
            shape(CTX, rows, width),
            shape(DP * CTX, *qkv.shape[1:]),
            shape(DP * CTX, *gate_up.shape[1:]),
            shape(DP, *down.shape),
            shape(DP * CTX, *out.shape),
        ),
        in_specs=[ANY] * 6,
        out_specs=(ANY,) * 6,
        scratch_shapes=[pltpu.SemaphoreType.DMA((6,))] + dma_sems(96),
        compiler_params=params(1),
        name="gather_inputs",
    )(tokens, cotangent, qkv, gate_up, down, out)


def heads_kernel(mine, every, local, sent, got):
    here = Here()
    sems = Sems(sent, got)
    here.greet([here.next[RIGHT], here.next[LEFT]])
    kept = pltpu.make_async_copy(mine, every.at[here.ctx], local)
    kept.start()
    width = mine.shape[1] // 4
    streams = []
    for index in range(4):
        lanes = pl.ds(index * width, width)
        streams.append(
            (
                mine.at[:, lanes],
                lambda rank, lanes=lanes: every.at[rank, :, lanes],
                RIGHT if index < 2 else LEFT,
            )
        )
    run_all(gather_ring(here, streams, sems))
    kept.wait()


def gather_heads(mine):
    return pl.pallas_call(
        heads_kernel,
        out_shape=jax.ShapeDtypeStruct((CTX, *mine.shape), BF16),
        in_specs=[ANY],
        out_specs=ANY,
        scratch_shapes=[pltpu.SemaphoreType.DMA] + dma_sems(4 * STEPS),
        compiler_params=params(2),
        name="gather_heads",
    )(mine)


def reduce_ring(here, part, slots, out, sems):
    width = part.shape[2] // 4
    flying = [[] for _ in range(4)]
    for step in range(STEPS):
        for index in range(4):
            columns = pl.ds(index * width, width)
            way = RIGHT if index < 2 else LEFT
            rank = ring_rank(here.place - way * (1 + step))
            if step == 0:
                source = part.at[rank, :, columns]
            else:
                flying[index][-1].wait_recv()
                source = slots.at[step - 1, :, columns]
                source[...] = (source[...].astype(F32) + part[rank, :, columns].astype(F32)).astype(
                    BF16
                )
            flying[index].append(
                send(source, slots.at[step, :, columns], sems(), here.next[way])
            )
        yield
    for index in range(4):
        columns = pl.ds(index * width, width)
        flying[index][-1].wait_recv()
        out[:, columns] = slots[STEPS - 1, :, columns].astype(F32) + part[
            here.ctx, :, columns
        ].astype(F32)
    yield
    for copies in flying:
        for copy in copies:
            copy.wait_send()


def add_rows(total, more, piece):
    def body(index, carry):
        rows = pl.ds(pl.multiple_of(index * piece, piece), piece)
        total[rows, :] = (total[rows, :].astype(F32) + more[rows, :].astype(F32)).astype(BF16)
        return carry

    lax.fori_loop(0, total.shape[0] // piece, body, 0)


def reduce_over_dp(here, part, beside, across, sems, piece):
    row, far = here.row, 1 - here.row
    first = send(part.at[far * 2 + 1 - here.core], beside.at[0], sems(), here.sibling)
    second = send(part.at[row * 2 + 1 - here.core], beside.at[1], sems(), here.sibling)
    yield
    first.wait_recv()
    add_rows(part.at[here.across_dp], beside.at[0], piece)
    third = send(part.at[here.across_dp], across, sems(), here.across)
    second.wait_recv()
    add_rows(part.at[here.dp], beside.at[1], piece)
    yield
    yield
    yield
    third.wait_recv()
    add_rows(part.at[here.dp], across, piece)
    for copy in (first, second, third):
        copy.wait_send()


def scatter_columns(here, part, beside, across, out, local_sem, sems, rows):
    yield from reduce_over_dp(here, part, beside, across, sems, rows)
    source = lambda rank: part.at[here.dp, pl.ds(rank * rows, rows), :]
    local = pltpu.make_async_copy(source(here.ctx), out.at[here.ctx], local_sem)
    local.start()
    copies = []
    for ahead in range(1, CTX):
        peer = here.peer(ahead)
        copies.append(send(source(peer), out.at[here.ctx], sems(), (here.dp, peer)))
    yield
    for copy in copies + [local]:
        copy.wait()


def ff_back_kernel(
    dh2_part, out_part, gu_part, down_part,
    dh2, out, gu_rows, down_sum,
    dh2_slots, out_slots, gu_beside, gu_across, down_beside, down_across, local, sent, got,
):
    here = Here()
    sems = Sems(sent, got)
    here.greet(here.peers() + [here.sibling, here.across])

    def down_reduce():
        yield from reduce_over_dp(here, down_part, down_beside, down_across, sems, 32)
        down_sum[...] = down_part[here.dp].astype(F32)

    run_all(
        reduce_ring(here, dh2_part, dh2_slots, dh2, sems),
        scatter_columns(
            here, gu_part, gu_beside, gu_across, gu_rows, local, sems, gu_rows.shape[1]
        ),
        down_reduce(),
        reduce_ring(here, out_part, out_slots, out, sems),
    )


def ff_back(dh2_part, out_part, gu_part, down_part):
    rows, width = dh2_part.shape[1:]
    gu_block, down_block = gu_part.shape[1:], down_part.shape[1:]
    own = jax.ShapeDtypeStruct((rows, width), F32)
    return pl.pallas_call(
        ff_back_kernel,
        out_shape=(
            own,
            own,
            jax.ShapeDtypeStruct((CTX, gu_block[0] // CTX, gu_block[1]), BF16),
            jax.ShapeDtypeStruct(down_block, F32),
        ),
        in_specs=[VMEM] * 4,
        out_specs=(VMEM,) * 4,
        scratch_shapes=[
            pltpu.VMEM((STEPS, rows, width), BF16),
            pltpu.VMEM((STEPS, rows, width), BF16),
            pltpu.VMEM((2, *gu_block), BF16),
            pltpu.VMEM(gu_block, BF16),
            pltpu.VMEM((2, *down_block), BF16),
            pltpu.VMEM(down_block, BF16),
            pltpu.SemaphoreType.DMA,
        ]
        + dma_sems(80),
        compiler_params=params(3),
        name="ff_back",
    )(dh2_part, out_part, gu_part, down_part)


def columns_kernel(blocks, every, local, sent, got):
    here = Here()
    sems = Sems(sent, got)
    here.greet(here.peers())
    rows = blocks.shape[3]
    place = lambda rank: every.at[:, :, pl.ds(pl.multiple_of(rank * rows, rows), rows)]
    kept = pltpu.make_async_copy(blocks.at[here.ctx], place(here.ctx), local)
    kept.start()
    copies = []
    for ahead in range(1, CTX):
        peer = here.peer(ahead)
        copies.append(send(blocks.at[peer], place(here.ctx), sems(), (here.dp, peer)))
    for copy in copies:
        copy.wait()
    kept.wait()


def to_columns(blocks):
    _, pair, share, rows = blocks.shape
    return pl.pallas_call(
        columns_kernel,
        out_shape=jax.ShapeDtypeStruct((pair, share, CTX * rows), BF16),
        in_specs=[ANY],
        out_specs=ANY,
        scratch_shapes=[pltpu.SemaphoreType.DMA] + dma_sems(STEPS),
        compiler_params=params(4),
        name="to_columns",
    )(blocks)


def attn_back_kernel(
    dh1_part, qkv_part, out_part,
    dh1, qkv_rows, out_rows,
    slots, qkv_beside, qkv_across, out_beside, out_across, local, sent, got,
):
    here = Here()
    sems = Sems(sent, got)
    here.greet(here.peers() + [here.sibling, here.across])
    rows = qkv_rows.shape[1]
    run_all(
        reduce_ring(here, dh1_part, slots, dh1, sems),
        scatter_columns(
            here, out_part, out_beside, out_across, out_rows, local.at[0], sems, rows
        ),
        scatter_columns(
            here, qkv_part, qkv_beside, qkv_across, qkv_rows, local.at[1], sems, rows
        ),
    )


def attn_back(dh1_part, qkv_part, out_part):
    rows, width = dh1_part.shape[1:]
    qkv_block, out_block = qkv_part.shape[1:], out_part.shape[1:]
    by_owner = lambda block: jax.ShapeDtypeStruct((CTX, block[0] // CTX, block[1]), BF16)
    return pl.pallas_call(
        attn_back_kernel,
        out_shape=(
            jax.ShapeDtypeStruct((rows, width), F32),
            by_owner(qkv_block),
            by_owner(out_block),
        ),
        in_specs=[VMEM] * 3,
        out_specs=(VMEM,) * 3,
        scratch_shapes=[
            pltpu.VMEM((STEPS, rows, width), BF16),
            pltpu.VMEM((2, *qkv_block), BF16),
            pltpu.VMEM(qkv_block, BF16),
            pltpu.VMEM((2, *out_block), BF16),
            pltpu.VMEM(out_block, BF16),
            pltpu.SemaphoreType.DMA((2,)),
        ]
        + dma_sems(60),
        compiler_params=params(5),
        name="attn_back",
    )(dh1_part, qkv_part, out_part)


def gains_kernel(parts, total, every, sent, got):
    here = Here()
    sems = Sems(sent, got)
    mine = here.dp * CTX + here.ctx
    others = []
    for ahead in range(1, DP * CTX):
        rank = lax.rem(mine + ahead, DP * CTX)
        others.append((rank // CTX, lax.rem(rank, CTX)))
    here.greet(others)
    every[mine] = parts[mine]
    copies = []
    for other in others:
        copies.append(send(parts.at[other[0] * CTX + other[1]], every.at[mine], sems(), other))
    for copy in copies:
        copy.wait()
    total[...] = jnp.sum(every[...], axis=0)


def sum_gains(parts):
    return pl.pallas_call(
        gains_kernel,
        out_shape=jax.ShapeDtypeStruct(parts.shape[1:], F32),
        in_specs=[VMEM],
        out_specs=VMEM,
        scratch_shapes=[pltpu.VMEM(parts.shape, F32)] + dma_sems(DP * CTX - 1),
        compiler_params=params(6),
        name="sum_gains",
    )(parts)


def normed(rows, gain):
    inv_root = lax.rsqrt(jnp.mean(rows * rows, axis=-1, keepdims=True) + NORM_EPS)
    return inv_root, (rows * inv_root * gain.astype(F32)).astype(BF16)


def spaced_head(weight):
    half = HEAD_SIZE // 2
    cut = weight.reshape(*weight.shape[:-1], 2, half)
    cut = jnp.pad(cut, [(0, 0)] * (cut.ndim - 1) + [(0, HALF_LANES - half)])
    return cut.reshape(*weight.shape[:-1], HEAD_LANES)


def packed_head(spaced):
    half = HEAD_SIZE // 2
    cut = spaced.reshape(*spaced.shape[:-1], 2, HALF_LANES)[..., :half]
    return cut.reshape(*spaced.shape[:-1], HEAD_SIZE)


def spaced_tables(row_count):
    half = HEAD_SIZE // 2
    cosine, sine = rope_tables(0, row_count)
    pad = ((0, 0), (0, HALF_LANES - half))
    cosine = jnp.pad(cosine[:, 0], pad)
    sine = jnp.pad(sine[:, 0], pad)
    return jnp.concatenate([cosine, cosine], axis=1), jnp.concatenate([-sine, sine], axis=1)


def split_layer(
    tokens,
    cotangent,
    gain_attn,
    w_query,
    key_weight,
    value_weight,
    w_out,
    gain_ffn,
    w_gate,
    w_up,
    w_down,
):
    ctx_rank = lax.axis_index("ctx")
    block_rows, width = tokens.shape
    weight_rows = w_query.shape[0]
    head_group = QUERY_HEADS // KEY_VALUE_HEADS
    score_scale = HEAD_SIZE ** (-0.5)
    query_share = head_group * HEAD_SIZE
    seq_rows = block_rows * CTX
    ff_width = w_gate.shape[1]
    down_rows = w_down.shape[0]
    ff_share = DP * down_rows

    def own(rows):
        return lax.dynamic_slice_in_dim(rows, ctx_rank * block_rows, block_rows, 0)

    q_cut = spaced_head(w_query.reshape(weight_rows, CTX, head_group, HEAD_SIZE))
    k_cut = spaced_head(key_weight.reshape(weight_rows, CTX, HEAD_SIZE))
    gains = jnp.stack([gain_attn, gain_ffn], axis=1)[:, None, :]
    v_cut = jnp.concatenate(
        [
            value_weight.reshape(weight_rows, CTX, HEAD_SIZE),
            jnp.broadcast_to(gains, (weight_rows, CTX, 2)),
            jnp.zeros((weight_rows, CTX, HEAD_LANES - HEAD_SIZE - 2), BF16),
        ],
        axis=2,
    )
    qkv_chunks = jnp.transpose(
        jnp.concatenate([q_cut.reshape(weight_rows, CTX, -1), k_cut, v_cut], axis=2), (1, 0, 2)
    )

    def ff_chunks(weight):
        cut = weight.reshape(weight_rows, DP, CTX, down_rows)
        return jnp.transpose(cut, (2, 0, 1, 3)).reshape(CTX, weight_rows, ff_share)

    gu_chunks = jnp.concatenate([ff_chunks(w_gate), ff_chunks(w_up)], axis=2)
    x_all, ct_all, w_qkv, w_gu, w_d, w_o = gather_all(
        tokens, cotangent, qkv_chunks, gu_chunks, w_down, w_out
    )
    x_all = x_all.reshape(seq_rows, width)
    ct_all = ct_all.reshape(seq_rows, width)
    w_qkv = w_qkv.reshape(width, SHARE)
    w_gu = w_gu.reshape(width, 2 * ff_share)
    w_d = w_d.reshape(ff_share, width)
    w_o = w_o.reshape(width, width)
    gain_lane = 3 * HEAD_LANES + HEAD_SIZE
    gain_one = w_qkv[:, gain_lane]
    gain_two = w_qkv[:, gain_lane + 1]

    inputs = x_all.astype(F32)
    inv_one, h1 = normed(inputs, gain_one)
    qkv = jnp.dot(h1, w_qkv, preferred_element_type=F32).reshape(seq_rows, 4, HEAD_LANES)
    cosine, sine = spaced_tables(seq_rows)
    rotated = qkv[:, :3] * cosine[:, None] + jnp.roll(qkv[:, :3], HALF_LANES, axis=-1) * sine[:, None]
    rotated = rotated.astype(BF16)
    q, k = rotated[:, :head_group], rotated[:, head_group]
    v = qkv[:, 3].astype(BF16)
    scores = jnp.einsum("tgd,sd->gts", q, k, preferred_element_type=F32) * score_scale
    positions = jnp.arange(seq_rows, dtype=jnp.int32)
    allowed = positions[None, :] <= positions[:, None]
    scores = jnp.where(allowed, scores, MASK_FILL)
    top = jnp.max(scores, axis=-1)
    expo = jnp.exp(scores - top[..., None])
    total = jnp.sum(expo, axis=-1)
    attn = jnp.einsum("gts,sd->tgd", expo.astype(BF16), v, preferred_element_type=F32)
    attn = (attn / jnp.transpose(total)[..., None])[..., :HEAD_SIZE]
    log_total = top + jnp.log(total)
    ob_t = jnp.transpose(attn.reshape(seq_rows, query_share).astype(BF16))
    ob_all = gather_heads(ob_t).reshape(width, seq_rows)

    middle = inputs + jnp.einsum("ct,cd->td", ob_all, w_o, preferred_element_type=F32)
    inv_two, h2 = normed(middle, gain_two)
    gate_up = jnp.dot(h2, w_gu, preferred_element_type=F32)
    gate, up = gate_up[:, :ff_share], gate_up[:, ff_share:]
    sig = jax.nn.sigmoid(gate)
    silu = gate * sig
    hidden = (silu * up).astype(BF16)
    out_part = jnp.dot(hidden, w_d, preferred_element_type=F32).astype(BF16)
    d_hidden = jnp.einsum("td,fd->tf", ct_all, w_d, preferred_element_type=F32)
    d_gate = (d_hidden * up * sig * (1.0 + gate * (1.0 - sig))).astype(BF16)
    d_up = (d_hidden * silu).astype(BF16)
    d_gu = jnp.concatenate([d_gate, d_up], axis=1)
    dh2_part = jnp.einsum("tf,cf->tc", d_gu, w_gu, preferred_element_type=F32).astype(BF16)
    gu_part = row_product(h2, d_gu).astype(BF16)
    down_part = row_product(hidden, ct_all).astype(BF16)
    dh2, out_sum, gu_rows, grad_down = ff_back(
        dh2_part.reshape(CTX, block_rows, width),
        out_part.reshape(CTX, block_rows, width),
        gu_part.reshape(DP, CTX * weight_rows, 2 * ff_share),
        down_part.reshape(DP, down_rows, width),
    )
    middle_own = own(middle)
    output = (middle_own + out_sum).astype(BF16)
    grad_gain_two, back = norm_back(dh2, middle_own, own(inv_two), gain_two)
    d_middle = cotangent.astype(F32) + back

    da = d_middle.astype(BF16)
    do_t = jnp.einsum("cd,td->ct", w_o, da, preferred_element_type=F32).astype(BF16)
    pair = jnp.stack(
        [
            do_t.reshape(CTX, query_share, block_rows),
            jnp.transpose(da).reshape(CTX, query_share, block_rows),
        ],
        axis=1,
    )
    do_da = to_columns(pair)
    do = jnp.transpose(do_da[0]).reshape(seq_rows, head_group, HEAD_SIZE)
    out_part = jnp.einsum("ct,et->ce", ob_all, do_da[1], preferred_element_type=F32).astype(BF16)
    out_part = jnp.pad(out_part, ((0, 0), (0, 2 * HEAD_LANES - query_share)))

    delta = jnp.transpose(jnp.sum(do.astype(F32) * attn, axis=-1))
    do = jnp.pad(do, ((0, 0), (0, 0), (0, HEAD_LANES - HEAD_SIZE)))
    probs = jnp.exp(scores - log_total[..., None])
    d_probs = jnp.einsum("tgd,sd->gts", do, v, preferred_element_type=F32)
    d_scores = (probs * (d_probs - delta[..., None])).astype(BF16)
    dq = jnp.einsum("gts,sd->tgd", d_scores, k, preferred_element_type=F32) * score_scale
    dk = jnp.einsum("gts,tgd->sd", d_scores, q, preferred_element_type=F32) * score_scale
    dv = jnp.einsum("gts,tgd->sd", probs.astype(BF16), do, preferred_element_type=F32)
    d_qk = jnp.concatenate([dq, dk[:, None]], axis=1)
    d_qk = d_qk * cosine[:, None] - jnp.roll(d_qk, HALF_LANES, axis=-1) * sine[:, None]
    d_qkv = jnp.concatenate([d_qk.reshape(seq_rows, -1), dv], axis=1).astype(BF16)
    qkv_part = row_product(h1, d_qkv).astype(BF16)
    dh1_part = jnp.einsum("tq,cq->tc", d_qkv, w_qkv, preferred_element_type=F32).astype(BF16)
    dh1, qkv_rows, out_rows = attn_back(
        dh1_part.reshape(CTX, block_rows, width),
        qkv_part.reshape(DP, CTX * weight_rows, SHARE),
        out_part.reshape(DP, CTX * weight_rows, 2 * HEAD_LANES),
    )
    grad_gain_one, back = norm_back(dh1, own(inputs), own(inv_one), gain_one)
    grad_tokens = d_middle + back
    gain_parts = jnp.stack([grad_gain_one, grad_gain_two]).reshape(2, DP * CTX, weight_rows)
    gain_parts = jnp.pad(
        jnp.transpose(gain_parts, (1, 0, 2)), ((0, 0), (0, 6), (0, HEAD_LANES - weight_rows))
    )
    gain_sums = sum_gains(gain_parts)[:2, :weight_rows]

    qkv_rows = jnp.transpose(qkv_rows.astype(F32), (1, 0, 2)).reshape(weight_rows, CTX, 4, HEAD_LANES)
    out_rows = jnp.transpose(out_rows.astype(F32), (1, 0, 2))[..., :query_share]

    def ff_joined(blocks):
        cut = blocks.astype(F32).reshape(CTX, weight_rows, DP, down_rows)
        return jnp.transpose(cut, (1, 2, 0, 3)).reshape(weight_rows, ff_width)

    return (
        output,
        grad_tokens,
        gain_sums[0],
        packed_head(qkv_rows[:, :, :head_group]).reshape(weight_rows, -1),
        packed_head(qkv_rows[:, :, head_group]).reshape(weight_rows, -1),
        qkv_rows[:, :, 3, :HEAD_SIZE].reshape(weight_rows, -1),
        out_rows.reshape(weight_rows, width),
        gain_sums[1],
        ff_joined(gu_rows[:, :, :ff_share]),
        ff_joined(gu_rows[:, :, ff_share:]),
        grad_down,
    )


def solution(mesh):
    heads_split = mesh.shape["dp"] == 4 and mesh.shape["ctx"] == KEY_VALUE_HEADS
    return jax.shard_map(
        split_layer if heads_split else blockwise_layer,
        mesh=mesh,
        in_specs=(
            P(("dp", "ctx"), None),
            P(("dp", "ctx"), None),
            P(("dp", "ctx")),
            P(("dp", "ctx"), None),
            P(("dp", "ctx"), None),
            P(("dp", "ctx"), None),
            P(("dp", "ctx"), None),
            P(("dp", "ctx")),
            P(("dp", "ctx"), None),
            P(("dp", "ctx"), None),
            P(("dp", "ctx"), None),
        ),
        out_specs=(
            P(("dp", "ctx"), None),
            P(("dp", "ctx"), None),
            P(("dp", "ctx")),
            P(("dp", "ctx"), None),
            P(("dp", "ctx"), None),
            P(("dp", "ctx"), None),
            P(("dp", "ctx"), None),
            P(("dp", "ctx")),
            P(("dp", "ctx"), None),
            P(("dp", "ctx"), None),
            P(("dp", "ctx"), None),
        ),
        check_vma=False,
    )
```

```python
import functools

import jax
import jax.numpy as jnp
from jax import lax
from jax.experimental import pallas as pl
from jax.experimental.pallas import tpu as pltpu
from jax.sharding import PartitionSpec as P

QUERY_HEADS = 16
KEY_VALUE_HEADS = 8
HEAD_SIZE = 96


NORM_EPS = 1e-05
ROPE_THETA = 100000.0
MASK_FILL = -1e30


def passed_along(value, axis, by):
    peers = lax.axis_size(axis)
    pairs = [(i, i + by) for i in range(peers) if 0 <= i + by < peers]
    return lax.ppermute(value, axis, pairs)


def shifted(block, axis, distance):
    devices = range(lax.axis_size(axis))
    route = [((i - distance) % len(devices), i) for i in devices]
    return lax.ppermute(block, axis, route)


def rope_tables(first_row, block_count):
    half_dim = HEAD_SIZE // 2
    positions = (first_row + jnp.arange(block_count, dtype=jnp.int32)).astype(jnp.float32)
    frequency = ROPE_THETA ** (-jnp.arange(half_dim, dtype=jnp.float32) * 2.0 / HEAD_SIZE)
    angles = positions[:, None] * frequency[None, :]
    return (jnp.cos(angles)[:, None, :], jnp.sin(angles)[:, None, :])


def apply_rotary(value_rows, cosine_table, sine_values, direction):
    half_dim = HEAD_SIZE // 2
    first_half = value_rows[..., :half_dim]
    second_half = value_rows[..., half_dim:]
    return jnp.concatenate(
        [
            first_half * cosine_table - direction * second_half * sine_values,
            second_half * cosine_table + direction * first_half * sine_values,
        ],
        axis=-1,
    )


def norm_back(grad_normed, inputs, inv_root, gain):
    grad_gain = jnp.sum(grad_normed * inputs * inv_root, axis=0)
    scaled = grad_normed * gain.astype(jnp.float32)
    grad_inputs = inv_root * (
        scaled - inputs * inv_root * inv_root * jnp.mean(scaled * inputs, axis=-1, keepdims=True)
    )
    return (grad_gain, grad_inputs)


def row_product(left, right):
    return jnp.einsum("tc,tf->cf", left, right, preferred_element_type=jnp.float32)


def blockwise_layer(
    tokens,
    cotangent,
    gain_attn,
    w_query,
    key_weight,
    value_weight,
    w_out,
    gain_ffn,
    w_gate,
    w_up,
    w_down,
):
    token_rows = tokens.shape[0]
    head_group = QUERY_HEADS // KEY_VALUE_HEADS
    key_value_width = KEY_VALUE_HEADS * HEAD_SIZE
    query_width = QUERY_HEADS * HEAD_SIZE
    score_scale = HEAD_SIZE ** (-0.5)
    ctx_count = lax.axis_size("ctx")
    ctx_rank = lax.axis_index("ctx")
    first_row = ctx_rank * token_rows
    query_pos = first_row + jnp.arange(token_rows, dtype=jnp.int32)
    attn_full = (
        lax.all_gather(gain_attn, ("dp", "ctx"), axis=0, tiled=True),
        lax.all_gather(w_query, ("dp", "ctx"), axis=0, tiled=True),
        lax.all_gather(key_weight, ("dp", "ctx"), axis=0, tiled=True),
        lax.all_gather(value_weight, ("dp", "ctx"), axis=0, tiled=True),
        lax.all_gather(w_out, ("dp", "ctx"), axis=0, tiled=True),
    )
    gain_one, query_full, key_full, value_full, out_full = attn_full
    inputs = tokens.astype(jnp.float32)
    inv_one = lax.rsqrt(jnp.mean(inputs * inputs, axis=-1, keepdims=True) + NORM_EPS)
    first_normed = (inputs * inv_one * gain_one.astype(jnp.float32)).astype(jnp.bfloat16)
    query_unrotated = jnp.dot(first_normed, query_full, preferred_element_type=jnp.float32).reshape(
        token_rows, QUERY_HEADS, HEAD_SIZE
    )
    key_unrotated = jnp.dot(first_normed, key_full, preferred_element_type=jnp.float32).reshape(
        token_rows, KEY_VALUE_HEADS, HEAD_SIZE
    )
    value_raw = jnp.dot(first_normed, value_full, preferred_element_type=jnp.float32)
    cosine_table, sine_values = rope_tables(first_row, token_rows)
    query_rows = (
        apply_rotary(query_unrotated, cosine_table, sine_values, 1.0)
        .astype(jnp.bfloat16)
        .reshape(token_rows, KEY_VALUE_HEADS, head_group, HEAD_SIZE)
    )
    keys_rot = (
        apply_rotary(key_unrotated, cosine_table, sine_values, 1.0)
        .astype(jnp.bfloat16)
        .reshape(token_rows, key_value_width)
    )
    kv_local = jnp.concatenate([keys_rot, value_raw.astype(jnp.bfloat16)], axis=1)
    starting = (
        jnp.full((KEY_VALUE_HEADS, head_group, token_rows), MASK_FILL, jnp.float32),
        jnp.zeros((KEY_VALUE_HEADS, head_group, token_rows), jnp.float32),
        jnp.zeros((token_rows, KEY_VALUE_HEADS, head_group, HEAD_SIZE), jnp.float32),
    )
    sequence_portion = lax.all_gather(kv_local, "ctx", axis=0, tiled=True)

    def update(state):
        run_max, run_sum, run_acc = state
        block_count = sequence_portion.shape[0]
        key_portion = sequence_portion[:, :key_value_width].reshape(
            block_count, KEY_VALUE_HEADS, HEAD_SIZE
        )
        value_portion = sequence_portion[:, key_value_width:].reshape(
            block_count, KEY_VALUE_HEADS, HEAD_SIZE
        )
        scores = (
            jnp.einsum(
                "tkgd,skd->kgts", query_rows, key_portion, preferred_element_type=jnp.float32
            )
            * score_scale
        )
        key_pos = jnp.arange(block_count, dtype=jnp.int32)
        allowed = key_pos[None, :] <= query_pos[:, None]
        scores = jnp.where(allowed, scores, MASK_FILL)
        new_max = jnp.maximum(run_max, jnp.max(scores, axis=-1))
        expo = jnp.exp(scores - new_max[..., None])
        new_sum = jnp.sum(expo, axis=-1)
        added = jnp.einsum(
            "kgts,skd->tkgd",
            expo.astype(jnp.bfloat16),
            value_portion,
            preferred_element_type=jnp.float32,
        )
        return (new_max, new_sum, added)

    def unchanged(state):
        return state

    run_max, run_sum, run_acc = lax.cond(
        jnp.int32(0) <= first_row + token_rows - 1, update, unchanged, starting
    )
    attn_four = run_acc / jnp.transpose(run_sum, (2, 0, 1))[..., None]
    log_total = run_max + jnp.log(run_sum)
    attn_out = attn_four.reshape(token_rows, query_width)
    attn_low = attn_out.astype(jnp.bfloat16)
    middle = inputs + jnp.dot(attn_low, out_full, preferred_element_type=jnp.float32)
    mlp_full = (
        lax.all_gather(gain_ffn, ("dp", "ctx"), axis=0, tiled=True),
        lax.all_gather(w_gate, ("dp", "ctx"), axis=0, tiled=True),
        lax.all_gather(w_up, ("dp", "ctx"), axis=0, tiled=True),
        lax.all_gather(w_down, ("dp", "ctx"), axis=0, tiled=True),
    )
    gain_two, gate_full, up_full, down_full = mlp_full
    inv_two = lax.rsqrt(jnp.mean(middle * middle, axis=-1, keepdims=True) + NORM_EPS)
    normed_two = (middle * inv_two * gain_two.astype(jnp.float32)).astype(jnp.bfloat16)
    gate_value = jnp.dot(normed_two, gate_full, preferred_element_type=jnp.float32)
    up_value = jnp.dot(normed_two, up_full, preferred_element_type=jnp.float32)
    sigmoid_gate = jax.nn.sigmoid(gate_value)
    silu_gate = gate_value * sigmoid_gate
    hidden = (silu_gate * up_value).astype(jnp.bfloat16)
    output = (middle + jnp.dot(hidden, down_full, preferred_element_type=jnp.float32)).astype(
        jnp.bfloat16
    )
    mlp_back = (
        lax.all_gather(gain_ffn, ("dp", "ctx"), axis=0, tiled=True),
        lax.all_gather(w_gate, ("dp", "ctx"), axis=0, tiled=True),
        lax.all_gather(w_up, ("dp", "ctx"), axis=0, tiled=True),
        lax.all_gather(w_down, ("dp", "ctx"), axis=0, tiled=True),
    )
    gain_two_back, gate_back, up_back, down_back = mlp_back
    grad_out = cotangent.astype(jnp.float32)
    grad_hidden = jnp.einsum("td,fd->tf", cotangent, down_back, preferred_element_type=jnp.float32)
    grad_gate = (
        grad_hidden * up_value * sigmoid_gate * (1.0 + gate_value * (1.0 - sigmoid_gate))
    ).astype(jnp.bfloat16)
    grad_up = (grad_hidden * silu_gate).astype(jnp.bfloat16)
    grad_normed_two = jnp.einsum(
        "tf,cf->tc", grad_gate, gate_back, preferred_element_type=jnp.float32
    ) + jnp.einsum("tf,cf->tc", grad_up, up_back, preferred_element_type=jnp.float32)
    grad_gain_two, grad_middle_norm = norm_back(grad_normed_two, middle, inv_two, gain_two_back)
    grad_middle = grad_out + grad_middle_norm
    gate_up_pair = jnp.concatenate([grad_gate, grad_up], axis=1)
    gate_up_sum = lax.psum_scatter(
        row_product(normed_two, gate_up_pair), ("dp", "ctx"), scatter_dimension=0, tiled=True
    )
    grad_down_sum = lax.psum_scatter(
        row_product(hidden, cotangent), ("dp", "ctx"), scatter_dimension=0, tiled=True
    )
    attn_back = (
        lax.all_gather(gain_attn, ("dp", "ctx"), axis=0, tiled=True),
        lax.all_gather(w_query, ("dp", "ctx"), axis=0, tiled=True),
        lax.all_gather(key_weight, ("dp", "ctx"), axis=0, tiled=True),
        lax.all_gather(value_weight, ("dp", "ctx"), axis=0, tiled=True),
        lax.all_gather(w_out, ("dp", "ctx"), axis=0, tiled=True),
    )
    gain_one_back, query_back, key_back, value_back, out_back = attn_back
    grad_branch = grad_middle.astype(jnp.bfloat16)
    attention_gradient = jnp.einsum(
        "td,cd->tc", grad_branch, out_back, preferred_element_type=jnp.float32
    ).astype(jnp.bfloat16)
    gradient_quad = attention_gradient.reshape(token_rows, KEY_VALUE_HEADS, head_group, HEAD_SIZE)
    delta_rows = jnp.transpose(
        jnp.sum(gradient_quad.astype(jnp.float32) * attn_four, axis=-1), (1, 2, 0)
    )

    def pair_terms(key_value_block, key_first):
        block_count = key_value_block.shape[0]
        key_portion = key_value_block[:, :key_value_width].reshape(
            block_count, KEY_VALUE_HEADS, HEAD_SIZE
        )
        value_portion = key_value_block[:, key_value_width:].reshape(
            block_count, KEY_VALUE_HEADS, HEAD_SIZE
        )
        scores = (
            jnp.einsum(
                "tkgd,skd->kgts", query_rows, key_portion, preferred_element_type=jnp.float32
            )
            * score_scale
        )
        key_pos = key_first + jnp.arange(block_count, dtype=jnp.int32)
        allowed = key_pos[None, :] <= query_pos[:, None]
        scores = jnp.where(allowed, scores, MASK_FILL)
        probs = jnp.exp(scores - log_total[..., None])
        grad_probs = jnp.einsum(
            "tkgd,skd->kgts", gradient_quad, value_portion, preferred_element_type=jnp.float32
        )
        grad_scores = (probs * (grad_probs - delta_rows[..., None])).astype(jnp.bfloat16)
        grad_query = (
            jnp.einsum(
                "kgts,skd->tkgd", grad_scores, key_portion, preferred_element_type=jnp.float32
            )
            * score_scale
        )
        grad_keys = (
            jnp.einsum(
                "kgts,tkgd->skd", grad_scores, query_rows, preferred_element_type=jnp.float32
            )
            * score_scale
        )
        grad_values = jnp.einsum(
            "kgts,tkgd->skd",
            probs.astype(jnp.bfloat16),
            gradient_quad,
            preferred_element_type=jnp.float32,
        )
        return (
            grad_query,
            jnp.concatenate(
                [
                    grad_keys.reshape(block_count, key_value_width),
                    grad_values.reshape(block_count, key_value_width),
                ],
                axis=1,
            ),
        )

    def add_pair(operands):
        kv_use, key_first, grad_query, grad_now = operands
        more_query, more_kv = pair_terms(kv_use, key_first)
        return (grad_query + more_query, grad_now + more_kv)

    def keep_pair(operands):
        return (operands[2], operands[3])

    def cycle_step(step, state):
        kv_now, grad_now, grad_query = state
        owner = (ctx_rank - step + ctx_count) % ctx_count
        kv_next = passed_along(kv_now, "ctx", 1)
        grad_query, grad_now = lax.cond(
            owner <= ctx_rank,
            add_pair,
            keep_pair,
            (kv_now, owner * token_rows, grad_query, grad_now),
        )
        grad_next = shifted(grad_now.astype(jnp.bfloat16), "ctx", 1).astype(grad_now.dtype)
        return (kv_next, grad_next, grad_query)

    cycle_start = (
        kv_local,
        jnp.zeros((token_rows, 2 * key_value_width), jnp.float32),
        jnp.zeros((token_rows, KEY_VALUE_HEADS, head_group, HEAD_SIZE), jnp.float32),
    )
    kv_final, key_value_gradient, grad_query = lax.fori_loop(0, ctx_count, cycle_step, cycle_start)
    grad_query_raw = (
        apply_rotary(
            grad_query.reshape(token_rows, QUERY_HEADS, HEAD_SIZE), cosine_table, sine_values, -1.0
        )
        .reshape(token_rows, query_width)
        .astype(jnp.bfloat16)
    )
    grad_key_raw = (
        apply_rotary(
            key_value_gradient[:, :key_value_width].reshape(token_rows, KEY_VALUE_HEADS, HEAD_SIZE),
            cosine_table,
            sine_values,
            -1.0,
        )
        .reshape(token_rows, key_value_width)
        .astype(jnp.bfloat16)
    )
    grad_value_raw = key_value_gradient[:, key_value_width:].astype(jnp.bfloat16)
    grad_normed_one = (
        jnp.einsum("tq,cq->tc", grad_query_raw, query_back, preferred_element_type=jnp.float32)
        + jnp.einsum("tq,cq->tc", grad_key_raw, key_back, preferred_element_type=jnp.float32)
        + jnp.einsum("tq,cq->tc", grad_value_raw, value_back, preferred_element_type=jnp.float32)
    )
    grad_gain_one, grad_input_norm = norm_back(grad_normed_one, inputs, inv_one, gain_one_back)
    grad_tokens = grad_middle + grad_input_norm
    projection_grads = jnp.concatenate([grad_query_raw, grad_key_raw, grad_value_raw], axis=1)
    qkv_sum = lax.psum_scatter(
        row_product(first_normed, projection_grads), ("dp", "ctx"), scatter_dimension=0, tiled=True
    )
    grad_out_sum = lax.psum_scatter(
        row_product(attn_low, grad_branch), ("dp", "ctx"), scatter_dimension=0, tiled=True
    )
    gain_sums = (
        lax.psum_scatter(grad_gain_one, ("dp", "ctx"), scatter_dimension=0, tiled=True),
        lax.psum_scatter(grad_gain_two, ("dp", "ctx"), scatter_dimension=0, tiled=True),
    )
    ff_width = w_gate.shape[1]
    return (
        output,
        grad_tokens,
        gain_sums[0],
        qkv_sum[:, :query_width],
        qkv_sum[:, query_width : query_width + key_value_width],
        qkv_sum[:, query_width + key_value_width :],
        grad_out_sum,
        gain_sums[1],
        gate_up_sum[:, :ff_width],
        gate_up_sum[:, ff_width:],
        grad_down_sum,
    )


CUBE = 8
BITS = (0, 1, 2)
HEAD_LANES = 128
HALF_LANES = 64
SHARE = 4 * HEAD_LANES
F32 = jnp.float32
BF16 = jnp.bfloat16


class Here:
    def __init__(self):
        dp = lax.axis_index("dp")
        ctx = lax.axis_index("ctx")
        self.core = lax.rem(dp, 2)
        self.far = ctx // 4
        self.own = (dp // 2, lax.rem(ctx // 2, 2), lax.rem(ctx, 2))
        self.shard = self.shard_of(self.own)
        self.at_home = self.own[0] == self.far
        self.sibling = self.device(self.own, core=1 - self.core)
        self.across = self.device(self.own, far=1 - self.far)

    def shard_of(self, bits):
        return bits[0] * 4 + bits[1] * 2 + bits[2]

    def device(self, bits, core=None, far=None):
        core = self.core if core is None else core
        far = self.far if far is None else far
        return (bits[0] * 2 + core, far * 4 + bits[1] * 2 + bits[2])

    def flip(self, *turned, of=None):
        bits = self.own if of is None else of
        return tuple(1 - bit if index in turned else bit for index, bit in enumerate(bits))

    def next(self, bit):
        return self.device(self.flip(bit))

    def others(self):
        return [
            self.flip(*[bit for bit in BITS if code >> (2 - bit) & 1]) for code in range(1, CUBE)
        ]

    def greet(self, partners):
        barrier = pltpu.get_barrier_semaphore()
        for partner in partners:
            pl.semaphore_signal(
                barrier, inc=1, device_id=partner, device_id_type=pl.DeviceIdType.MESH
            )
        pl.semaphore_wait(barrier, len(partners))

    def peers(self):
        return [self.device(bits) for bits in self.others()]


def make_send(source, target, sems, device):
    return pltpu.make_async_remote_copy(
        src_ref=source,
        dst_ref=target,
        send_sem=sems[0],
        recv_sem=sems[1],
        device_id=device,
        device_id_type=pl.DeviceIdType.MESH,
    )


def send(*operands):
    copy = make_send(*operands)
    copy.start()
    return copy


class Sems:
    def __init__(self, sent, received):
        self.sent, self.received, self.used = sent, received, 0

    def __call__(self):
        pair = (self.sent.at[self.used], self.received.at[self.used])
        self.used += 1
        return pair


def run_all(*generators):
    live = list(generators)
    while live:
        for one in list(live):
            try:
                next(one)
            except StopIteration:
                live.remove(one)


ORDERS = ((0, 1, 2), (1, 2, 0), (2, 0, 1))


def gather_cube(here, place_of, order, sems):
    a, b, c = order
    to = lambda bits, bit: send(place_of(bits), place_of(bits), sems(), here.next(bit))
    from_a, from_b = here.flip(a), here.flip(b)
    a0, b0, c0 = to(here.own, a), to(here.own, b), to(here.own, c)
    yield
    a0.wait_recv()
    b1, c1 = to(from_a, b), to(from_a, c)
    yield
    b0.wait_recv()
    c2 = to(from_b, c)
    yield
    b1.wait_recv()
    c3 = to(here.flip(a, b), c)
    yield
    for copy in (c0, c1, c2, c3):
        copy.wait_recv()
    for copy in (a0, b0, b1, c0, c1, c2, c3):
        copy.wait_send()


def gather_cube_thirds(here, place_of, sems):
    return [
        gather_cube(here, functools.partial(place_of, third=third), order, sems)
        for third, order in enumerate(ORDERS)
    ]


def total_of(*refs):
    total = refs[0][...].astype(F32)
    for ref in refs[1:]:
        total = total + ref[...].astype(F32)
    return total


def reduce_cube(here, part_of, slots, out, order, sems):
    c, b, a = order
    own = here.own
    sends = []

    def to(bits, slot, bit):
        sends.append(send(part_of(bits), slots(slot), sems(), here.next(bit)))
        return sends[-1]

    c0 = to(here.flip(c, b, a), 0, c)
    c1 = to(here.flip(c, b), 1, c)
    c2 = to(here.flip(c, a), 2, c)
    c3 = to(here.flip(c), 3, c)
    yield
    c0.wait_recv()
    spot = part_of(here.flip(b, a))
    spot[...] = total_of(spot, slots(0)).astype(BF16)
    b0 = to(here.flip(b, a), 4, b)
    yield
    c1.wait_recv()
    spot = part_of(here.flip(b))
    spot[...] = total_of(spot, slots(1)).astype(BF16)
    b1 = to(here.flip(b), 5, b)
    yield
    c2.wait_recv()
    b0.wait_recv()
    spot = part_of(here.flip(a))
    spot[...] = total_of(spot, slots(2), slots(4)).astype(BF16)
    a0 = to(here.flip(a), 6, a)
    yield
    c3.wait_recv()
    b1.wait_recv()
    a0.wait_recv()
    out[...] = total_of(part_of(own), slots(3), slots(5), slots(6))
    yield
    for copy in sends:
        copy.wait_send()


def reduce_cube_all(here, part, slots, out, sems):
    width = out.shape[1] // 6
    streams = []
    for index in range(6):
        columns = pl.ds(index * width, width)
        streams.append(
            reduce_cube(
                here,
                lambda bits, columns=columns: part.at[bits[0], bits[1], bits[2], :, columns],
                lambda slot, columns=columns: slots.at[slot, :, columns],
                out.at[:, columns],
                ORDERS[index // 2],
                sems,
            )
        )
    return streams


def swap_home(here, source, target, relay, local_sem, sems, beyond=None):
    beyond = target if beyond is None else beyond
    half = source.shape[1] // 2
    left, right = pl.ds(0, half), pl.ds(half, half)
    by_x = here.next(0)
    local = pltpu.make_async_copy(source, target, local_sem)
    out_left = make_send(source.at[:, left], relay.at[0], sems(), here.across)
    out_right = make_send(source.at[:, right], relay.at[1], sems(), by_x)
    on_left = make_send(relay.at[0], beyond.at[:, left], sems(), by_x)
    on_right = make_send(relay.at[1], target.at[:, right], sems(), here.across)

    @pl.when(here.at_home)
    def _():
        local.start()

    @pl.when(jnp.logical_not(here.at_home))
    def _():
        out_left.start()
        out_right.start()

    yield

    @pl.when(here.at_home)
    def _():
        out_left.wait_recv()
        on_left.start()
        out_right.wait_recv()
        on_right.start()
        local.wait()

    @pl.when(jnp.logical_not(here.at_home))
    def _():
        on_left.wait_recv()
        on_right.wait_recv()

    yield

    @pl.when(here.at_home)
    def _():
        on_left.wait_send()
        on_right.wait_send()

    @pl.when(jnp.logical_not(here.at_home))
    def _():
        out_left.wait_send()
        out_right.wait_send()


def spread(here, place_of, sems, ready=()):
    for copy in ready:
        copy.wait()
    over = send(place_of(here.far), place_of(here.far), sems(), here.across)
    beside = send(place_of(here.far), place_of(here.far), sems(), here.sibling)
    yield
    yield
    yield
    over.wait_recv()
    last = send(place_of(1 - here.far), place_of(1 - here.far), sems(), here.sibling)
    yield
    beside.wait_recv()
    last.wait_recv()
    for copy in (over, beside, last):
        copy.wait_send()


def gather_columns(here, chunks, target, local_sem, sems):
    x, z, y = here.own
    place = target.at[x, here.core, here.far, z, y]
    local = pltpu.make_async_copy(chunks.at[here.shard], place, local_sem)
    local.start()
    copies = [
        send(chunks.at[here.shard_of(bits)], place, sems(), here.device(bits))
        for bits in here.others()
    ]
    yield
    yield
    yield from spread(
        here, lambda far: target.at[:, here.core, far], sems, copies + [local]
    )


def in_step(live):
    live = list(live)
    while live:
        for one in list(live):
            try:
                next(one)
            except StopIteration:
                live.remove(one)
        yield


ANY = pl.BlockSpec(memory_space=pltpu.MemorySpace.HBM)
VMEM = pl.BlockSpec(memory_space=pltpu.MemorySpace.VMEM)
VMEM_BYTES = 56 * 2**20


def params(collective_id):
    return pltpu.CompilerParams(
        collective_id=collective_id, has_side_effects=True, vmem_limit_bytes=VMEM_BYTES
    )


def dma_sems(count):
    return [pltpu.SemaphoreType.DMA((count,)), pltpu.SemaphoreType.DMA((count,))]


def half_blocks(block):
    return pltpu.VMEM((2, block[0], block[1] // 2), BF16)


QUERY_TILE = 256
NT = (((1,), (1,)), ((), ()))


def dot(left, right):
    return jnp.dot(left, right, preferred_element_type=F32)


def dot_nt(left, right):
    return lax.dot_general(left, right, NT, preferred_element_type=F32)


def rotate(head, cosine, sine):
    return head * cosine + pltpu.roll(head, HALF_LANES, 1) * sine


def scores_of(keys, queries):
    count = keys.shape[0] - QUERY_TILE
    parts = []
    if count > 0:
        parts.append(dot_nt(keys[:count], queries) * HEAD_SIZE**-0.5)
    last = dot_nt(keys[count:], queries) * HEAD_SIZE**-0.5
    key = lax.broadcasted_iota(jnp.int32, last.shape, 0)
    query = lax.broadcasted_iota(jnp.int32, last.shape, 1)
    parts.append(jnp.where(key <= query, last, MASK_FILL))
    return parts


def attend_tile(q, k, v_t, o_t, ob, lse, group, tile):
    rows = pl.ds(tile * QUERY_TILE, QUERY_TILE)
    count = (tile + 1) * QUERY_TILE
    parts = scores_of(k[:count, :], q[group, rows, :])
    top = jnp.max(parts[-1], axis=0, keepdims=True)
    for part in parts[:-1]:
        top = jnp.maximum(top, jnp.max(part, axis=0, keepdims=True))
    total = jnp.zeros_like(top)
    result = None
    first = 0
    for part in parts:
        expo = jnp.exp(part - top)
        total = total + jnp.sum(expo, axis=0, keepdims=True)
        added = dot(v_t[:, first : first + part.shape[0]], expo.astype(BF16))
        result = added if result is None else result + added
        first += part.shape[0]
    result = result / total
    o_t[group, :, rows] = result
    ob[group * HEAD_SIZE : (group + 1) * HEAD_SIZE, rows] = result[:HEAD_SIZE].astype(BF16)
    lse[group, :, rows] = top + jnp.log(total)


def front_kernel(
    tokens, cotangent, qkv, gate_up, down, out, cosine, sine,
    x_all, ct_all, w_qkv, w_gu, w_d, w_o, ob_all, h1, q, k, v, o_t, lse, gains,
    v_t, x_relay, ct_relay, local, sent, got,
):
    here = Here()
    sems = Sems(sent, got)
    here.greet(here.peers() + [here.sibling, here.across])
    x, z, y = here.own
    width = tokens.shape[1]
    block_rows = tokens.shape[0]
    seq_rows = CUBE * block_rows

    def swapped(source, target, relay, local_sem):
        third_width = width // 3
        yield from swap_home(
            here,
            source,
            target.at[here.shard],
            relay,
            local_sem,
            sems,
            target.at[here.shard_of(here.flip(0))],
        )
        yield from in_step(
            gather_cube_thirds(
                here,
                lambda bits, third: target.at[
                    here.shard_of(bits), :, pl.ds(third * third_width, third_width)
                ],
                sems,
            )
        )

    def out_gather():
        third_width = width // 3
        mine = w_o.at[x, here.core, here.far, z, y]
        kept = pltpu.make_async_copy(out, mine, local.at[3])
        kept.start()
        over = send(out, mine, sems(), here.across)
        yield
        kept.wait()
        over.wait()
        yield from in_step(
            gather_cube_thirds(
                here,
                lambda bits, third: w_o.at[
                    bits[0],
                    here.core,
                    :,
                    bits[1],
                    bits[2],
                    :,
                    pl.ds(third * third_width, third_width),
                ],
                sems,
            )
        )
        beside = send(w_o.at[:, here.core], w_o.at[:, here.core], sems(), here.sibling)
        yield
        beside.wait()

    def down_gather():
        kept = pltpu.make_async_copy(down, w_d.at[here.core, here.far], local.at[2])
        kept.start()
        yield from spread(here, lambda far: w_d.at[here.core, far], sems, [kept])

    get_x = swapped(tokens, x_all, x_relay, local.at[0])
    get_qkv = gather_columns(here, qkv, w_qkv, local.at[4], sems)
    get_gu = gather_columns(here, gate_up, w_gu, local.at[5], sems)
    get_out = out_gather()
    get_down = down_gather()
    get_ct = swapped(cotangent, ct_all, ct_relay, local.at[1])
    next(get_x)
    next(get_qkv)
    next(get_out)
    next(get_x)
    next(get_x)
    next(get_qkv)
    next(get_down)
    next(get_gu)
    next(get_ct)
    run_all(get_x, get_qkv)
    later = in_step([get_ct, get_gu, get_out, get_down])

    turned = jnp.transpose(
        w_qkv[:, :, :, :, :, :, 3 * HEAD_LANES :].astype(F32).reshape(width, HEAD_LANES)
    )
    gains[...] = turned[HEAD_SIZE : HEAD_SIZE + 8]
    next(later)

    def norm_block(index, carry):
        rows = x_all[index].astype(F32)
        inv_root = lax.rsqrt(jnp.mean(rows * rows, axis=-1, keepdims=True) + NORM_EPS)
        place = pl.ds(pl.multiple_of(index * block_rows, block_rows), block_rows)
        h1[place, :] = (rows * inv_root * gains[0:1, :]).astype(BF16)
        return carry

    lax.fori_loop(0, CUBE, norm_block, 0)
    next(later)

    def project(index, carry):
        rows = pl.ds(pl.multiple_of(index * QUERY_TILE, QUERY_TILE), QUERY_TILE)
        raw = dot(h1[rows, :], w_qkv[...].reshape(width, SHARE))
        cos_rows, sin_rows = cosine[rows, :], sine[rows, :]
        heads = [raw[:, lane : lane + HEAD_LANES] for lane in range(0, SHARE, HEAD_LANES)]
        q[0, rows, :] = rotate(heads[0], cos_rows, sin_rows).astype(BF16)
        q[1, rows, :] = rotate(heads[1], cos_rows, sin_rows).astype(BF16)
        k[rows, :] = rotate(heads[2], cos_rows, sin_rows).astype(BF16)
        v[rows, :] = heads[3].astype(BF16)
        v_t[:, rows] = jnp.transpose(heads[3]).astype(BF16)
        return carry

    lax.fori_loop(0, seq_rows // QUERY_TILE, project, 0)
    next(later)

    ob = ob_all.at[here.shard]
    row_third = ob.shape[0] // 3
    streams = []
    tiles = seq_rows // QUERY_TILE
    for tile in range(tiles):
        for group in range(2):
            attend_tile(q, k, v_t, o_t, ob, lse, group, tile)
        if tile % 2 == 1:
            lanes = pl.ds((tile - 1) * QUERY_TILE, 2 * QUERY_TILE)
            half = in_step(
                gather_cube_thirds(
                    here,
                    lambda bits, third, lanes=lanes: ob_all.at[
                        here.shard_of(bits), pl.ds(third * row_third, row_third), lanes
                    ],
                    sems,
                )
            )
            next(half)
            streams.append(half)
        next(later)
    run_all(*streams, later)


def front(tokens, cotangent, qkv, gate_up, down, out, cosine, sine):
    slots = (2, 2, 2, 2, 2)
    shape = lambda *dims: jax.ShapeDtypeStruct(dims, BF16)
    wide = lambda *dims: jax.ShapeDtypeStruct(dims, F32)
    rows, width = tokens.shape
    seq_rows = CUBE * rows
    share = 2 * HEAD_SIZE
    outs = (
        shape(CUBE, rows, width),
        shape(CUBE, rows, width),
        shape(*slots, *qkv.shape[1:]),
        shape(*slots, *gate_up.shape[1:]),
        shape(2, 2, *down.shape),
        shape(*slots, *out.shape),
        shape(CUBE, share, seq_rows),
        shape(seq_rows, width),
        shape(2, seq_rows, HEAD_LANES),
        shape(seq_rows, HEAD_LANES),
        shape(seq_rows, HEAD_LANES),
        wide(2, HEAD_LANES, seq_rows),
        wide(2, 1, seq_rows),
        wide(8, width),
    )
    return pl.pallas_call(
        front_kernel,
        out_shape=outs,
        in_specs=[VMEM] * 8,
        out_specs=(VMEM,) * len(outs),
        scratch_shapes=[
            pltpu.VMEM((HEAD_LANES, seq_rows), BF16),
            half_blocks(tokens.shape),
            half_blocks(tokens.shape),
            pltpu.SemaphoreType.DMA((6,)),
        ]
        + dma_sems(140),
        compiler_params=params(1),
        name="front",
    )(tokens, cotangent, qkv, gate_up, down, out, cosine, sine)


def attend_back_tile(q, k, k_t, v, do_t, o_t, lse, dk, dv, group, tile):
    rows = pl.ds(tile * QUERY_TILE, QUERY_TILE)
    count = (tile + 1) * QUERY_TILE
    q_rows = q[group, rows, :]
    do_rows = do_t[group * HEAD_SIZE : (group + 1) * HEAD_SIZE, rows]
    do_rows = jnp.concatenate(
        [do_rows, jnp.zeros((HEAD_LANES - HEAD_SIZE, QUERY_TILE), BF16)], axis=0
    )
    delta = jnp.sum(do_rows.astype(F32) * o_t[group, :, rows], axis=0, keepdims=True)
    log_total = lse[group, :, rows]
    dq_t = None
    first = 0
    for part in scores_of(k[:count, :], q_rows):
        keys = slice(first, first + part.shape[0])
        probs = jnp.exp(part - log_total)
        d_probs = dot(v[keys, :], do_rows)
        d_scores = (probs * (d_probs - delta)).astype(BF16)
        dv[keys, :] += dot_nt(probs.astype(BF16), do_rows)
        dk[keys, :] += dot(d_scores, q_rows)
        added = dot(k_t[:, keys], d_scores)
        dq_t = added if dq_t is None else dq_t + added
        first += part.shape[0]
    return jnp.transpose(dq_t) * HEAD_SIZE**-0.5


def attn_grads_kernel(q, k, v, do_t, o_t, lse, cosine, sine, d_qkv, k_t, dk, dv):
    seq_rows = k.shape[0]
    k_t[...] = jnp.transpose(k[...].astype(F32)).astype(BF16)
    dk[...] = jnp.zeros_like(dk)
    dv[...] = jnp.zeros_like(dv)
    for tile in range(seq_rows // QUERY_TILE):
        rows = pl.ds(tile * QUERY_TILE, QUERY_TILE)
        for group in range(2):
            dq = attend_back_tile(q, k, k_t, v, do_t, o_t, lse, dk, dv, group, tile)
            d_qkv[rows, group * HEAD_LANES : (group + 1) * HEAD_LANES] = rotate(
                dq, cosine[rows, :], -sine[rows, :]
            ).astype(BF16)
    d_qkv[:, 2 * HEAD_LANES : 3 * HEAD_LANES] = rotate(
        dk[...] * HEAD_SIZE**-0.5, cosine[...], -sine[...]
    ).astype(BF16)
    d_qkv[:, 3 * HEAD_LANES :] = dv[...].astype(BF16)


def attn_grads(q, k, v, do_t, o_t, lse, cosine, sine):
    seq_rows = k.shape[0]
    return pl.pallas_call(
        attn_grads_kernel,
        out_shape=jax.ShapeDtypeStruct((seq_rows, SHARE), BF16),
        in_specs=[VMEM] * 8,
        out_specs=VMEM,
        scratch_shapes=[
            pltpu.VMEM((HEAD_LANES, seq_rows), BF16),
            pltpu.VMEM((seq_rows, HEAD_LANES), F32),
            pltpu.VMEM((seq_rows, HEAD_LANES), F32),
        ],
        compiler_params=pltpu.CompilerParams(vmem_limit_bytes=VMEM_BYTES),
        name="attn_grads",
    )(q, k, v, do_t, o_t, lse, cosine, sine)


def add_rows(total, more, piece):
    def body(index, carry):
        rows = pl.ds(pl.multiple_of(index * piece, piece), piece)
        for block in range(total.shape[0]):
            total[block, rows, :] = total_of(
                total.at[block, rows, :], more.at[block, rows, :]
            ).astype(BF16)
        return carry

    lax.fori_loop(0, total.shape[1] // piece, body, 0)


def reduce_copies(here, part, beside, over, sems, piece):
    core, far = here.core, here.far
    first = send(part.at[:, 1 - core, 1 - far], beside.at[0], sems(), here.sibling)
    second = send(part.at[:, 1 - core, far], beside.at[1], sems(), here.sibling)
    yield
    first.wait_recv()
    add_rows(part.at[:, core, 1 - far], beside.at[0], piece)
    third = send(part.at[:, core, 1 - far], over, sems(), here.across)
    second.wait_recv()
    add_rows(part.at[:, core, far], beside.at[1], piece)
    yield
    yield
    yield
    third.wait_recv()
    add_rows(part.at[:, core, far], over, piece)
    for copy in (first, second, third):
        copy.wait_send()


def scatter_columns(here, part, beside, over, out, local_sem, sems):
    rows = out.shape[1]
    yield from reduce_copies(here, part, beside, over, sems, rows)

    def source(bits):
        place = pl.ds((bits[1] * 2 + bits[2]) * rows, rows)
        return part.at[bits[0], here.core, here.far, place, :]

    local = pltpu.make_async_copy(source(here.own), out.at[here.shard], local_sem)
    local.start()
    copies = [
        send(source(bits), out.at[here.shard], sems(), here.device(bits)) for bits in here.others()
    ]
    yield
    for copy in copies + [local]:
        copy.wait()


def ff_back_kernel(
    dh2_part, out_part, gu_part, down_part,
    dh2, out, gu_rows, down_sum,
    dh2_slots, out_slots, gu_beside, gu_over, down_beside, down_over, local, sent, got,
):
    here = Here()
    sems = Sems(sent, got)
    here.greet(here.peers() + [here.sibling, here.across])

    def down_reduce():
        yield from reduce_copies(here, down_part, down_beside, down_over, sems, 32)
        down_sum[...] = down_part[0, here.core, here.far].astype(F32)

    run_all(
        *reduce_cube_all(here, dh2_part, dh2_slots, dh2, sems),
        scatter_columns(here, gu_part, gu_beside, gu_over, gu_rows, local, sems),
        down_reduce(),
        *reduce_cube_all(here, out_part, out_slots, out, sems),
    )


def copy_slots(part):
    blocks, _, _, rows, share = part.shape
    return [pltpu.VMEM((2, blocks, rows, share), BF16), pltpu.VMEM((blocks, rows, share), BF16)]


def by_owner(part):
    rows, share = part.shape[3:]
    return jax.ShapeDtypeStruct((CUBE, rows // 4, share), BF16)


def ff_back(dh2_part, out_part, gu_part, down_part):
    rows, width = dh2_part.shape[3:]
    own = jax.ShapeDtypeStruct((rows, width), F32)
    return pl.pallas_call(
        ff_back_kernel,
        out_shape=(
            own,
            own,
            by_owner(gu_part),
            jax.ShapeDtypeStruct(down_part.shape[3:], F32),
        ),
        in_specs=[VMEM] * 4,
        out_specs=(VMEM,) * 4,
        scratch_shapes=[
            pltpu.VMEM((CUBE - 1, rows, width), BF16),
            pltpu.VMEM((CUBE - 1, rows, width), BF16),
            *copy_slots(gu_part),
            *copy_slots(down_part),
            pltpu.SemaphoreType.DMA,
        ]
        + dma_sems(100),
        compiler_params=params(3),
        name="ff_back",
    )(dh2_part, out_part, gu_part, down_part)


def columns_kernel(blocks, every, local, sent, got):
    here = Here()
    sems = Sems(sent, got)
    here.greet(here.peers())
    rows = blocks.shape[3]
    place = every.at[:, :, pl.ds(pl.multiple_of(here.shard * rows, rows), rows)]
    kept = pltpu.make_async_copy(blocks.at[here.shard], place, local)
    kept.start()
    copies = [
        send(blocks.at[here.shard_of(bits)], place, sems(), here.device(bits))
        for bits in here.others()
    ]
    for copy in copies:
        copy.wait()
    kept.wait()


def to_columns(blocks):
    _, pair, share, rows = blocks.shape
    return pl.pallas_call(
        columns_kernel,
        out_shape=jax.ShapeDtypeStruct((pair, share, CUBE * rows), BF16),
        in_specs=[VMEM],
        out_specs=VMEM,
        scratch_shapes=[pltpu.SemaphoreType.DMA] + dma_sems(CUBE - 1),
        compiler_params=params(4),
        name="to_columns",
    )(blocks)


def attn_back_kernel(
    dh1_part, qkv_part, out_part, output,
    dh1, qkv_rows, out_rows, output_home,
    slots, qkv_beside, qkv_over, out_beside, out_over, relay, local, sent, got,
):
    here = Here()
    sems = Sems(sent, got)
    here.greet(here.peers() + [here.sibling, here.across])
    run_all(
        *reduce_cube_all(here, dh1_part, slots, dh1, sems),
        scatter_columns(here, out_part, out_beside, out_over, out_rows, local.at[0], sems),
        scatter_columns(here, qkv_part, qkv_beside, qkv_over, qkv_rows, local.at[1], sems),
        swap_home(here, output, output_home, relay, local.at[2], sems),
    )


def attn_back(dh1_part, qkv_part, out_part, output):
    rows, width = dh1_part.shape[3:]
    return pl.pallas_call(
        attn_back_kernel,
        out_shape=(
            jax.ShapeDtypeStruct((rows, width), F32),
            by_owner(qkv_part),
            by_owner(out_part),
            jax.ShapeDtypeStruct((rows, width), BF16),
        ),
        in_specs=[VMEM] * 4,
        out_specs=(VMEM,) * 4,
        scratch_shapes=[
            pltpu.VMEM((CUBE - 1, rows, width), BF16),
            *copy_slots(qkv_part),
            *copy_slots(out_part),
            half_blocks((rows, width)),
            pltpu.SemaphoreType.DMA((3,)),
        ]
        + dma_sems(80),
        compiler_params=params(5),
        name="attn_back",
    )(dh1_part, qkv_part, out_part, output)


def finish_kernel(parts, grad, total, grad_home, every, relay, local, sent, got):
    here = Here()
    sems = Sems(sent, got)
    own = here.device(here.own)
    mine = own[0] * CUBE + own[1]
    count = parts.shape[0]
    others = []
    for ahead in range(1, count):
        rank = lax.rem(mine + ahead, count)
        others.append((rank // CUBE, lax.rem(rank, CUBE)))
    here.greet(others)
    every[mine] = parts[mine]
    swap = swap_home(here, grad, grad_home, relay, local, sems)
    next(swap)
    copies = []
    for other in others:
        copies.append(send(parts.at[other[0] * CUBE + other[1]], every.at[mine], sems(), other))
    for _ in swap:
        pass
    for copy in copies:
        copy.wait()
    total[...] = jnp.sum(every[...], axis=0)


def finish(parts, grad):
    return pl.pallas_call(
        finish_kernel,
        out_shape=(
            jax.ShapeDtypeStruct(parts.shape[1:], F32),
            jax.ShapeDtypeStruct(grad.shape, BF16),
        ),
        in_specs=[VMEM] * 2,
        out_specs=(VMEM,) * 2,
        scratch_shapes=[
            pltpu.VMEM(parts.shape, F32),
            half_blocks(grad.shape),
            pltpu.SemaphoreType.DMA,
        ]
        + dma_sems(parts.shape[0] + 3),
        compiler_params=params(6),
        name="finish",
    )(parts, grad)


def normed(rows, gain):
    inv_root = lax.rsqrt(jnp.mean(rows * rows, axis=-1, keepdims=True) + NORM_EPS)
    return inv_root, (rows * inv_root * gain.astype(F32)).astype(BF16)


def spaced_head(weight):
    half = HEAD_SIZE // 2
    cut = weight.reshape(*weight.shape[:-1], 2, half)
    cut = jnp.pad(cut, [(0, 0)] * (cut.ndim - 1) + [(0, HALF_LANES - half)])
    return cut.reshape(*weight.shape[:-1], HEAD_LANES)


def packed_head(spaced):
    half = HEAD_SIZE // 2
    cut = spaced.reshape(*spaced.shape[:-1], 2, HALF_LANES)[..., :half]
    return cut.reshape(*spaced.shape[:-1], HEAD_SIZE)


def spaced_tables(row_count):
    half = HEAD_SIZE // 2
    cosine, sine = rope_tables(0, row_count)
    pad = ((0, 0), (0, HALF_LANES - half))
    cosine = jnp.pad(cosine[:, 0], pad)
    sine = jnp.pad(sine[:, 0], pad)
    return jnp.concatenate([cosine, cosine], axis=1), jnp.concatenate([-sine, sine], axis=1)


def split_layer(
    tokens,
    cotangent,
    gain_attn,
    w_query,
    key_weight,
    value_weight,
    w_out,
    gain_ffn,
    w_gate,
    w_up,
    w_down,
):
    here = Here()
    block_rows, width = tokens.shape
    weight_rows = w_query.shape[0]
    head_group = QUERY_HEADS // KEY_VALUE_HEADS
    score_scale = HEAD_SIZE ** (-0.5)
    query_share = head_group * HEAD_SIZE
    seq_rows = block_rows * CUBE
    ff_width = w_gate.shape[1]
    down_rows = w_down.shape[0]
    ff_share = 4 * down_rows

    def own(rows):
        return lax.dynamic_slice_in_dim(rows, here.shard * block_rows, block_rows, 0)

    q_cut = spaced_head(w_query.reshape(weight_rows, CUBE, head_group, HEAD_SIZE))
    k_cut = spaced_head(key_weight.reshape(weight_rows, CUBE, HEAD_SIZE))
    gains = jnp.stack([gain_attn, gain_ffn], axis=1)[:, None, :]
    v_cut = jnp.concatenate(
        [
            value_weight.reshape(weight_rows, CUBE, HEAD_SIZE),
            jnp.broadcast_to(gains, (weight_rows, CUBE, 2)),
            jnp.zeros((weight_rows, CUBE, HEAD_LANES - HEAD_SIZE - 2), BF16),
        ],
        axis=2,
    )
    qkv_chunks = jnp.transpose(
        jnp.concatenate([q_cut.reshape(weight_rows, CUBE, -1), k_cut, v_cut], axis=2), (1, 0, 2)
    )

    def ff_chunks(weight):
        cut = weight.reshape(weight_rows, 2, 4, 4, down_rows)
        return jnp.transpose(cut, (1, 3, 0, 2, 4)).reshape(CUBE, weight_rows, ff_share)

    gu_chunks = jnp.concatenate([ff_chunks(w_gate), ff_chunks(w_up)], axis=2)
    cosine, sine = spaced_tables(seq_rows)
    x_all, ct_all, w_qkv, w_gu, w_d, w_o, ob_all, h1, q, k, v, o_t, lse, gains = front(
        tokens, cotangent, qkv_chunks, gu_chunks, w_down, w_out, cosine, sine
    )
    gain_one, gain_two = gains[0], gains[1]
    x_all = x_all.reshape(seq_rows, width)
    ct_all = ct_all.reshape(seq_rows, width)
    w_qkv = w_qkv.reshape(width, SHARE)
    w_gu = w_gu.reshape(width, 2 * ff_share)
    w_d = w_d.reshape(ff_share, width)
    w_o = w_o.reshape(width, width)
    ob_all = ob_all.reshape(width, seq_rows)
    inputs = x_all.astype(F32)

    middle = inputs + jnp.einsum("ct,cd->td", ob_all, w_o, preferred_element_type=F32)
    inv_two, h2 = normed(middle, gain_two)
    gate_up = jnp.dot(h2, w_gu, preferred_element_type=F32)
    gate, up = gate_up[:, :ff_share], gate_up[:, ff_share:]
    sig = jax.nn.sigmoid(gate)
    silu = gate * sig
    hidden = (silu * up).astype(BF16)
    out_part = jnp.dot(hidden, w_d, preferred_element_type=F32).astype(BF16)
    d_hidden = jnp.einsum("td,fd->tf", ct_all, w_d, preferred_element_type=F32)
    d_gate = (d_hidden * up * sig * (1.0 + gate * (1.0 - sig))).astype(BF16)
    d_up = (d_hidden * silu).astype(BF16)
    d_gu = jnp.concatenate([d_gate, d_up], axis=1)
    dh2_part = jnp.einsum("tf,cf->tc", d_gu, w_gu, preferred_element_type=F32).astype(BF16)
    gu_part = row_product(h2, d_gu).astype(BF16)
    down_part = row_product(hidden, ct_all).astype(BF16)
    dh2, out_sum, gu_rows, grad_down = ff_back(
        dh2_part.reshape(2, 2, 2, block_rows, width),
        out_part.reshape(2, 2, 2, block_rows, width),
        gu_part.reshape(2, 2, 2, 4 * weight_rows, 2 * ff_share),
        down_part.reshape(1, 2, 2, down_rows, width),
    )
    middle_own = own(middle)
    output = (middle_own + out_sum).astype(BF16)
    grad_gain_two, back = norm_back(dh2, middle_own, own(inv_two), gain_two)
    d_middle = own(ct_all).astype(F32) + back

    da = d_middle.astype(BF16)
    do_t = jnp.einsum("cd,td->ct", w_o, da, preferred_element_type=F32).astype(BF16)
    pair = jnp.stack(
        [
            do_t.reshape(CUBE, query_share, block_rows),
            jnp.transpose(da).reshape(CUBE, query_share, block_rows),
        ],
        axis=1,
    )
    do_da = to_columns(pair)
    out_part = jnp.einsum("ct,et->ce", ob_all, do_da[1], preferred_element_type=F32).astype(BF16)
    out_part = jnp.pad(out_part, ((0, 0), (0, 2 * HEAD_LANES - query_share)))

    d_qkv = attn_grads(q, k, v, do_da[0], o_t, lse, cosine, sine)
    qkv_part = row_product(h1, d_qkv).astype(BF16)
    dh1_part = jnp.einsum("tq,cq->tc", d_qkv, w_qkv, preferred_element_type=F32).astype(BF16)
    dh1, qkv_rows, out_rows, output = attn_back(
        dh1_part.reshape(2, 2, 2, block_rows, width),
        qkv_part.reshape(2, 2, 2, 4 * weight_rows, SHARE),
        out_part.reshape(2, 2, 2, 4 * weight_rows, 2 * HEAD_LANES),
        output,
    )
    own_inputs = own(inputs)
    inv_one, _ = normed(own_inputs, gain_one)
    grad_gain_one, back = norm_back(dh1, own_inputs, inv_one, gain_one)
    grad_tokens = d_middle + back
    gain_parts = jnp.stack([grad_gain_one, grad_gain_two]).reshape(2, width // weight_rows, weight_rows)
    gain_parts = jnp.pad(
        jnp.transpose(gain_parts, (1, 0, 2)), ((0, 0), (0, 6), (0, HEAD_LANES - weight_rows))
    )
    gain_sums, grad_tokens = finish(gain_parts, grad_tokens.astype(BF16))

    qkv_rows = jnp.transpose(qkv_rows.astype(F32), (1, 0, 2)).reshape(weight_rows, CUBE, 4, HEAD_LANES)
    out_rows = jnp.transpose(out_rows.astype(F32), (1, 0, 2))[..., :query_share]

    def ff_joined(blocks):
        cut = blocks.astype(F32).reshape(2, 4, weight_rows, 4, down_rows)
        return jnp.transpose(cut, (2, 0, 3, 1, 4)).reshape(weight_rows, ff_width)

    return (
        output,
        grad_tokens.astype(F32),
        gain_sums[0, :weight_rows],
        packed_head(qkv_rows[:, :, :head_group]).reshape(weight_rows, -1),
        packed_head(qkv_rows[:, :, head_group]).reshape(weight_rows, -1),
        qkv_rows[:, :, 3, :HEAD_SIZE].reshape(weight_rows, -1),
        out_rows.reshape(weight_rows, width),
        gain_sums[1, :weight_rows],
        ff_joined(gu_rows[:, :, :ff_share]),
        ff_joined(gu_rows[:, :, ff_share:]),
        grad_down,
    )


def solution(mesh):
    heads_split = mesh.shape["dp"] == 4 and mesh.shape["ctx"] == KEY_VALUE_HEADS
    return jax.shard_map(
        split_layer if heads_split else blockwise_layer,
        mesh=mesh,
        in_specs=(
            P(("dp", "ctx"), None),
            P(("dp", "ctx"), None),
            P(("dp", "ctx")),
            P(("dp", "ctx"), None),
            P(("dp", "ctx"), None),
            P(("dp", "ctx"), None),
            P(("dp", "ctx"), None),
            P(("dp", "ctx")),
            P(("dp", "ctx"), None),
            P(("dp", "ctx"), None),
            P(("dp", "ctx"), None),
        ),
        out_specs=(
            P(("dp", "ctx"), None),
            P(("dp", "ctx"), None),
            P(("dp", "ctx")),
            P(("dp", "ctx"), None),
            P(("dp", "ctx"), None),
            P(("dp", "ctx"), None),
            P(("dp", "ctx"), None),
            P(("dp", "ctx")),
            P(("dp", "ctx"), None),
            P(("dp", "ctx"), None),
            P(("dp", "ctx"), None),
        ),
        check_vma=False,
    )
```

```python
import functools

import jax
import jax.numpy as jnp
from jax import lax
from jax.experimental import pallas as pl
from jax.experimental.pallas import tpu as pltpu
from jax.sharding import PartitionSpec as P

QUERY_HEADS = 16
KEY_VALUE_HEADS = 8
HEAD_SIZE = 96


NORM_EPS = 1e-05
ROPE_THETA = 100000.0
MASK_FILL = -1e30


def passed_along(value, axis, by):
    peers = lax.axis_size(axis)
    pairs = [(i, i + by) for i in range(peers) if 0 <= i + by < peers]
    return lax.ppermute(value, axis, pairs)


def shifted(block, axis, distance):
    devices = range(lax.axis_size(axis))
    route = [((i - distance) % len(devices), i) for i in devices]
    return lax.ppermute(block, axis, route)


def rope_tables(first_row, block_count):
    half_dim = HEAD_SIZE // 2
    positions = (first_row + jnp.arange(block_count, dtype=jnp.int32)).astype(jnp.float32)
    frequency = ROPE_THETA ** (-jnp.arange(half_dim, dtype=jnp.float32) * 2.0 / HEAD_SIZE)
    angles = positions[:, None] * frequency[None, :]
    return (jnp.cos(angles)[:, None, :], jnp.sin(angles)[:, None, :])


def apply_rotary(value_rows, cosine_table, sine_values, direction):
    half_dim = HEAD_SIZE // 2
    first_half = value_rows[..., :half_dim]
    second_half = value_rows[..., half_dim:]
    return jnp.concatenate(
        [
            first_half * cosine_table - direction * second_half * sine_values,
            second_half * cosine_table + direction * first_half * sine_values,
        ],
        axis=-1,
    )


def norm_back(grad_normed, inputs, inv_root, gain):
    grad_gain = jnp.sum(grad_normed * inputs * inv_root, axis=0)
    scaled = grad_normed * gain.astype(jnp.float32)
    grad_inputs = inv_root * (
        scaled - inputs * inv_root * inv_root * jnp.mean(scaled * inputs, axis=-1, keepdims=True)
    )
    return (grad_gain, grad_inputs)


def row_product(left, right):
    return jnp.einsum("tc,tf->cf", left, right, preferred_element_type=jnp.float32)


def blockwise_layer(
    tokens,
    cotangent,
    gain_attn,
    w_query,
    key_weight,
    value_weight,
    w_out,
    gain_ffn,
    w_gate,
    w_up,
    w_down,
):
    token_rows = tokens.shape[0]
    head_group = QUERY_HEADS // KEY_VALUE_HEADS
    key_value_width = KEY_VALUE_HEADS * HEAD_SIZE
    query_width = QUERY_HEADS * HEAD_SIZE
    score_scale = HEAD_SIZE ** (-0.5)
    ctx_count = lax.axis_size("ctx")
    ctx_rank = lax.axis_index("ctx")
    first_row = ctx_rank * token_rows
    query_pos = first_row + jnp.arange(token_rows, dtype=jnp.int32)
    attn_full = (
        lax.all_gather(gain_attn, ("dp", "ctx"), axis=0, tiled=True),
        lax.all_gather(w_query, ("dp", "ctx"), axis=0, tiled=True),
        lax.all_gather(key_weight, ("dp", "ctx"), axis=0, tiled=True),
        lax.all_gather(value_weight, ("dp", "ctx"), axis=0, tiled=True),
        lax.all_gather(w_out, ("dp", "ctx"), axis=0, tiled=True),
    )
    gain_one, query_full, key_full, value_full, out_full = attn_full
    inputs = tokens.astype(jnp.float32)
    inv_one = lax.rsqrt(jnp.mean(inputs * inputs, axis=-1, keepdims=True) + NORM_EPS)
    first_normed = (inputs * inv_one * gain_one.astype(jnp.float32)).astype(jnp.bfloat16)
    query_unrotated = jnp.dot(first_normed, query_full, preferred_element_type=jnp.float32).reshape(
        token_rows, QUERY_HEADS, HEAD_SIZE
    )
    key_unrotated = jnp.dot(first_normed, key_full, preferred_element_type=jnp.float32).reshape(
        token_rows, KEY_VALUE_HEADS, HEAD_SIZE
    )
    value_raw = jnp.dot(first_normed, value_full, preferred_element_type=jnp.float32)
    cosine_table, sine_values = rope_tables(first_row, token_rows)
    query_rows = (
        apply_rotary(query_unrotated, cosine_table, sine_values, 1.0)
        .astype(jnp.bfloat16)
        .reshape(token_rows, KEY_VALUE_HEADS, head_group, HEAD_SIZE)
    )
    keys_rot = (
        apply_rotary(key_unrotated, cosine_table, sine_values, 1.0)
        .astype(jnp.bfloat16)
        .reshape(token_rows, key_value_width)
    )
    kv_local = jnp.concatenate([keys_rot, value_raw.astype(jnp.bfloat16)], axis=1)
    starting = (
        jnp.full((KEY_VALUE_HEADS, head_group, token_rows), MASK_FILL, jnp.float32),
        jnp.zeros((KEY_VALUE_HEADS, head_group, token_rows), jnp.float32),
        jnp.zeros((token_rows, KEY_VALUE_HEADS, head_group, HEAD_SIZE), jnp.float32),
    )
    sequence_portion = lax.all_gather(kv_local, "ctx", axis=0, tiled=True)

    def update(state):
        run_max, run_sum, run_acc = state
        block_count = sequence_portion.shape[0]
        key_portion = sequence_portion[:, :key_value_width].reshape(
            block_count, KEY_VALUE_HEADS, HEAD_SIZE
        )
        value_portion = sequence_portion[:, key_value_width:].reshape(
            block_count, KEY_VALUE_HEADS, HEAD_SIZE
        )
        scores = (
            jnp.einsum(
                "tkgd,skd->kgts", query_rows, key_portion, preferred_element_type=jnp.float32
            )
            * score_scale
        )
        key_pos = jnp.arange(block_count, dtype=jnp.int32)
        allowed = key_pos[None, :] <= query_pos[:, None]
        scores = jnp.where(allowed, scores, MASK_FILL)
        new_max = jnp.maximum(run_max, jnp.max(scores, axis=-1))
        expo = jnp.exp(scores - new_max[..., None])
        new_sum = jnp.sum(expo, axis=-1)
        added = jnp.einsum(
            "kgts,skd->tkgd",
            expo.astype(jnp.bfloat16),
            value_portion,
            preferred_element_type=jnp.float32,
        )
        return (new_max, new_sum, added)

    def unchanged(state):
        return state

    run_max, run_sum, run_acc = lax.cond(
        jnp.int32(0) <= first_row + token_rows - 1, update, unchanged, starting
    )
    attn_four = run_acc / jnp.transpose(run_sum, (2, 0, 1))[..., None]
    log_total = run_max + jnp.log(run_sum)
    attn_out = attn_four.reshape(token_rows, query_width)
    attn_low = attn_out.astype(jnp.bfloat16)
    middle = inputs + jnp.dot(attn_low, out_full, preferred_element_type=jnp.float32)
    mlp_full = (
        lax.all_gather(gain_ffn, ("dp", "ctx"), axis=0, tiled=True),
        lax.all_gather(w_gate, ("dp", "ctx"), axis=0, tiled=True),
        lax.all_gather(w_up, ("dp", "ctx"), axis=0, tiled=True),
        lax.all_gather(w_down, ("dp", "ctx"), axis=0, tiled=True),
    )
    gain_two, gate_full, up_full, down_full = mlp_full
    inv_two = lax.rsqrt(jnp.mean(middle * middle, axis=-1, keepdims=True) + NORM_EPS)
    normed_two = (middle * inv_two * gain_two.astype(jnp.float32)).astype(jnp.bfloat16)
    gate_value = jnp.dot(normed_two, gate_full, preferred_element_type=jnp.float32)
    up_value = jnp.dot(normed_two, up_full, preferred_element_type=jnp.float32)
    sigmoid_gate = jax.nn.sigmoid(gate_value)
    silu_gate = gate_value * sigmoid_gate
    hidden = (silu_gate * up_value).astype(jnp.bfloat16)
    output = (middle + jnp.dot(hidden, down_full, preferred_element_type=jnp.float32)).astype(
        jnp.bfloat16
    )
    mlp_back = (
        lax.all_gather(gain_ffn, ("dp", "ctx"), axis=0, tiled=True),
        lax.all_gather(w_gate, ("dp", "ctx"), axis=0, tiled=True),
        lax.all_gather(w_up, ("dp", "ctx"), axis=0, tiled=True),
        lax.all_gather(w_down, ("dp", "ctx"), axis=0, tiled=True),
    )
    gain_two_back, gate_back, up_back, down_back = mlp_back
    grad_out = cotangent.astype(jnp.float32)
    grad_hidden = jnp.einsum("td,fd->tf", cotangent, down_back, preferred_element_type=jnp.float32)
    grad_gate = (
        grad_hidden * up_value * sigmoid_gate * (1.0 + gate_value * (1.0 - sigmoid_gate))
    ).astype(jnp.bfloat16)
    grad_up = (grad_hidden * silu_gate).astype(jnp.bfloat16)
    grad_normed_two = jnp.einsum(
        "tf,cf->tc", grad_gate, gate_back, preferred_element_type=jnp.float32
    ) + jnp.einsum("tf,cf->tc", grad_up, up_back, preferred_element_type=jnp.float32)
    grad_gain_two, grad_middle_norm = norm_back(grad_normed_two, middle, inv_two, gain_two_back)
    grad_middle = grad_out + grad_middle_norm
    gate_up_pair = jnp.concatenate([grad_gate, grad_up], axis=1)
    gate_up_sum = lax.psum_scatter(
        row_product(normed_two, gate_up_pair), ("dp", "ctx"), scatter_dimension=0, tiled=True
    )
    grad_down_sum = lax.psum_scatter(
        row_product(hidden, cotangent), ("dp", "ctx"), scatter_dimension=0, tiled=True
    )
    attn_back = (
        lax.all_gather(gain_attn, ("dp", "ctx"), axis=0, tiled=True),
        lax.all_gather(w_query, ("dp", "ctx"), axis=0, tiled=True),
        lax.all_gather(key_weight, ("dp", "ctx"), axis=0, tiled=True),
        lax.all_gather(value_weight, ("dp", "ctx"), axis=0, tiled=True),
        lax.all_gather(w_out, ("dp", "ctx"), axis=0, tiled=True),
    )
    gain_one_back, query_back, key_back, value_back, out_back = attn_back
    grad_branch = grad_middle.astype(jnp.bfloat16)
    attention_gradient = jnp.einsum(
        "td,cd->tc", grad_branch, out_back, preferred_element_type=jnp.float32
    ).astype(jnp.bfloat16)
    gradient_quad = attention_gradient.reshape(token_rows, KEY_VALUE_HEADS, head_group, HEAD_SIZE)
    delta_rows = jnp.transpose(
        jnp.sum(gradient_quad.astype(jnp.float32) * attn_four, axis=-1), (1, 2, 0)
    )

    def pair_terms(key_value_block, key_first):
        block_count = key_value_block.shape[0]
        key_portion = key_value_block[:, :key_value_width].reshape(
            block_count, KEY_VALUE_HEADS, HEAD_SIZE
        )
        value_portion = key_value_block[:, key_value_width:].reshape(
            block_count, KEY_VALUE_HEADS, HEAD_SIZE
        )
        scores = (
            jnp.einsum(
                "tkgd,skd->kgts", query_rows, key_portion, preferred_element_type=jnp.float32
            )
            * score_scale
        )
        key_pos = key_first + jnp.arange(block_count, dtype=jnp.int32)
        allowed = key_pos[None, :] <= query_pos[:, None]
        scores = jnp.where(allowed, scores, MASK_FILL)
        probs = jnp.exp(scores - log_total[..., None])
        grad_probs = jnp.einsum(
            "tkgd,skd->kgts", gradient_quad, value_portion, preferred_element_type=jnp.float32
        )
        grad_scores = (probs * (grad_probs - delta_rows[..., None])).astype(jnp.bfloat16)
        grad_query = (
            jnp.einsum(
                "kgts,skd->tkgd", grad_scores, key_portion, preferred_element_type=jnp.float32
            )
            * score_scale
        )
        grad_keys = (
            jnp.einsum(
                "kgts,tkgd->skd", grad_scores, query_rows, preferred_element_type=jnp.float32
            )
            * score_scale
        )
        grad_values = jnp.einsum(
            "kgts,tkgd->skd",
            probs.astype(jnp.bfloat16),
            gradient_quad,
            preferred_element_type=jnp.float32,
        )
        return (
            grad_query,
            jnp.concatenate(
                [
                    grad_keys.reshape(block_count, key_value_width),
                    grad_values.reshape(block_count, key_value_width),
                ],
                axis=1,
            ),
        )

    def add_pair(operands):
        kv_use, key_first, grad_query, grad_now = operands
        more_query, more_kv = pair_terms(kv_use, key_first)
        return (grad_query + more_query, grad_now + more_kv)

    def keep_pair(operands):
        return (operands[2], operands[3])

    def cycle_step(step, state):
        kv_now, grad_now, grad_query = state
        owner = (ctx_rank - step + ctx_count) % ctx_count
        kv_next = passed_along(kv_now, "ctx", 1)
        grad_query, grad_now = lax.cond(
            owner <= ctx_rank,
            add_pair,
            keep_pair,
            (kv_now, owner * token_rows, grad_query, grad_now),
        )
        grad_next = shifted(grad_now.astype(jnp.bfloat16), "ctx", 1).astype(grad_now.dtype)
        return (kv_next, grad_next, grad_query)

    cycle_start = (
        kv_local,
        jnp.zeros((token_rows, 2 * key_value_width), jnp.float32),
        jnp.zeros((token_rows, KEY_VALUE_HEADS, head_group, HEAD_SIZE), jnp.float32),
    )
    kv_final, key_value_gradient, grad_query = lax.fori_loop(0, ctx_count, cycle_step, cycle_start)
    grad_query_raw = (
        apply_rotary(
            grad_query.reshape(token_rows, QUERY_HEADS, HEAD_SIZE), cosine_table, sine_values, -1.0
        )
        .reshape(token_rows, query_width)
        .astype(jnp.bfloat16)
    )
    grad_key_raw = (
        apply_rotary(
            key_value_gradient[:, :key_value_width].reshape(token_rows, KEY_VALUE_HEADS, HEAD_SIZE),
            cosine_table,
            sine_values,
            -1.0,
        )
        .reshape(token_rows, key_value_width)
        .astype(jnp.bfloat16)
    )
    grad_value_raw = key_value_gradient[:, key_value_width:].astype(jnp.bfloat16)
    grad_normed_one = (
        jnp.einsum("tq,cq->tc", grad_query_raw, query_back, preferred_element_type=jnp.float32)
        + jnp.einsum("tq,cq->tc", grad_key_raw, key_back, preferred_element_type=jnp.float32)
        + jnp.einsum("tq,cq->tc", grad_value_raw, value_back, preferred_element_type=jnp.float32)
    )
    grad_gain_one, grad_input_norm = norm_back(grad_normed_one, inputs, inv_one, gain_one_back)
    grad_tokens = grad_middle + grad_input_norm
    projection_grads = jnp.concatenate([grad_query_raw, grad_key_raw, grad_value_raw], axis=1)
    qkv_sum = lax.psum_scatter(
        row_product(first_normed, projection_grads), ("dp", "ctx"), scatter_dimension=0, tiled=True
    )
    grad_out_sum = lax.psum_scatter(
        row_product(attn_low, grad_branch), ("dp", "ctx"), scatter_dimension=0, tiled=True
    )
    gain_sums = (
        lax.psum_scatter(grad_gain_one, ("dp", "ctx"), scatter_dimension=0, tiled=True),
        lax.psum_scatter(grad_gain_two, ("dp", "ctx"), scatter_dimension=0, tiled=True),
    )
    ff_width = w_gate.shape[1]
    return (
        output,
        grad_tokens,
        gain_sums[0],
        qkv_sum[:, :query_width],
        qkv_sum[:, query_width : query_width + key_value_width],
        qkv_sum[:, query_width + key_value_width :],
        grad_out_sum,
        gain_sums[1],
        gate_up_sum[:, :ff_width],
        gate_up_sum[:, ff_width:],
        grad_down_sum,
    )


CUBE = 8
BITS = (0, 1, 2)
HEAD_LANES = 128
HALF_LANES = 64
SHARE = 4 * HEAD_LANES
F32 = jnp.float32
BF16 = jnp.bfloat16


class Here:
    def __init__(self):
        dp = lax.axis_index("dp")
        ctx = lax.axis_index("ctx")
        self.core = lax.rem(dp, 2)
        self.far = ctx // 4
        self.own = (dp // 2, lax.rem(ctx // 2, 2), lax.rem(ctx, 2))
        self.shard = self.shard_of(self.own)
        self.at_home = self.own[0] == self.far
        self.sibling = self.device(self.own, core=1 - self.core)
        self.across = self.device(self.own, far=1 - self.far)

    def shard_of(self, bits):
        return bits[0] * 4 + bits[1] * 2 + bits[2]

    def device(self, bits, core=None, far=None):
        core = self.core if core is None else core
        far = self.far if far is None else far
        return (bits[0] * 2 + core, far * 4 + bits[1] * 2 + bits[2])

    def flip(self, *turned, of=None):
        bits = self.own if of is None else of
        return tuple(1 - bit if index in turned else bit for index, bit in enumerate(bits))

    def next(self, bit):
        return self.device(self.flip(bit))

    def others(self):
        return [
            self.flip(*[bit for bit in BITS if code >> (2 - bit) & 1]) for code in range(1, CUBE)
        ]

    def greet(self, partners):
        barrier = pltpu.get_barrier_semaphore()
        for partner in partners:
            pl.semaphore_signal(
                barrier, inc=1, device_id=partner, device_id_type=pl.DeviceIdType.MESH
            )
        pl.semaphore_wait(barrier, len(partners))

    def peers(self):
        return [self.device(bits) for bits in self.others()]

    def same_core(self):
        beyond = [self.device(bits, far=1 - self.far) for bits in self.others() + [self.own]]
        return self.peers() + beyond


def make_send(source, target, sems, device):
    return pltpu.make_async_remote_copy(
        src_ref=source,
        dst_ref=target,
        send_sem=sems[0],
        recv_sem=sems[1],
        device_id=device,
        device_id_type=pl.DeviceIdType.MESH,
    )


def send(*operands):
    copy = make_send(*operands)
    copy.start()
    return copy


class Sems:
    def __init__(self, sent, received):
        self.sent, self.received, self.used = sent, received, 0

    def __call__(self):
        pair = (self.sent.at[self.used], self.received.at[self.used])
        self.used += 1
        return pair


def run_all(*generators):
    live = list(generators)
    while live:
        for one in list(live):
            try:
                next(one)
            except StopIteration:
                live.remove(one)


def in_step(live):
    live = list(live)
    while live:
        for one in list(live):
            try:
                next(one)
            except StopIteration:
                live.remove(one)
        yield


ORDERS = ((0, 1, 2), (1, 2, 0), (2, 0, 1))
ORDERS_Z_FIRST = ((1, 0, 2), (1, 2, 0))


def gather_cube(here, place_of, order, sems):
    a, b, c = order
    to = lambda bits, bit: send(place_of(bits), place_of(bits), sems(), here.next(bit))
    from_a, from_b = here.flip(a), here.flip(b)
    a0, b0, c0 = to(here.own, a), to(here.own, b), to(here.own, c)
    yield
    a0.wait_recv()
    b1, c1 = to(from_a, b), to(from_a, c)
    yield
    b0.wait_recv()
    c2 = to(from_b, c)
    yield
    b1.wait_recv()
    c3 = to(here.flip(a, b), c)
    yield
    for copy in (c0, c1, c2, c3):
        copy.wait_recv()
    for copy in (a0, b0, b1, c0, c1, c2, c3):
        copy.wait_send()


def gather_cube_parts(here, place_of, size, orders, sems):
    step = size // len(orders)
    return in_step(
        [
            gather_cube(
                here, functools.partial(place_of, part=pl.ds(index * step, step)), order, sems
            )
            for index, order in enumerate(orders)
        ]
    )


def total_of(*refs):
    total = refs[0][...].astype(F32)
    for ref in refs[1:]:
        total = total + ref[...].astype(F32)
    return total


PAIRS = (((0, 1, 2), (0, 1)), ((1, 2), (0, 2)), ((0,), (2,)), ((1,), ()))


class ReduceStream:
    def __init__(self, here, part_of, slots, out, order, sems):
        self.here, self.part_of, self.slots, self.out = here, part_of, slots, out
        c, b, a = self.order = order
        self.first = [(c, b, a), (c, b), (c, a), (c,)]
        self.copies = [None] * (CUBE - 1)
        self.sems = [sems() for _ in range(CUBE - 1)]
        self.made = set()

    def send(self, turned, slot, bit):
        self.copies[slot] = send(
            self.part_of(self.here.flip(*turned)),
            self.slots(slot),
            self.sems[slot],
            self.here.next(bit),
        )

    def add(self, turned, *slots):
        for slot in slots:
            self.copies[slot].wait_recv()
        spot = self.part_of(self.here.flip(*turned))
        spot[...] = total_of(spot, *[self.slots(slot) for slot in slots]).astype(BF16)

    def after(self, pair):
        c, b, a = self.order
        before = set(self.made)
        self.made |= {frozenset(turned) for turned in PAIRS[pair]}
        for slot, turned in enumerate(self.first):
            if frozenset(turned) in self.made - before:
                self.send(turned, slot, c)
        if self.copies[4] is None and self.copies[0] is not None and frozenset((b, a)) in self.made:
            self.add((b, a), 0)
            self.send((b, a), 4, b)
        if self.copies[5] is None and self.copies[1] is not None and frozenset((b,)) in self.made:
            self.add((b,), 1)
            self.send((b,), 5, b)

    def finish(self):
        _, b, a = self.order
        self.add((a,), 2, 4)
        self.send((a,), 6, a)
        yield
        for slot in (3, 5, 6):
            self.copies[slot].wait_recv()
        self.out[...] = total_of(
            self.part_of(self.here.own), self.slots(3), self.slots(5), self.slots(6)
        )
        yield
        for copy in self.copies:
            copy.wait_send()


def reductions(here, part, slots, out, orders, sems):
    width = out.shape[1] // len(orders)
    return [
        ReduceStream(
            here,
            lambda bits, columns=columns: part.at[here.shard_of(bits), :, columns],
            lambda slot, columns=columns: slots.at[slot, :, columns],
            out.at[:, columns],
            order,
            sems,
        )
        for columns, order in [
            (pl.ds(index * width, width), order) for index, order in enumerate(orders)
        ]
    ]


def swap_home(here, source, target, relay, local_sem, sems, beyond=None):
    beyond = target if beyond is None else beyond
    half = source.shape[1] // 2
    left, right = pl.ds(0, half), pl.ds(half, half)
    there = here.device(here.flip(0), far=1 - here.far)
    local = pltpu.make_async_copy(source, target, local_sem)
    straight = make_send(source.at[:, left], beyond.at[:, left], sems(), there)
    aside = make_send(source.at[:, right], relay, sems(), here.next(0))
    onward = make_send(relay, target.at[:, right], sems(), here.across)

    @pl.when(here.at_home)
    def _():
        local.start()

    @pl.when(jnp.logical_not(here.at_home))
    def _():
        aside.start()
        straight.start()

    yield

    @pl.when(here.at_home)
    def _():
        aside.wait_recv()
        onward.start()

    yield

    @pl.when(here.at_home)
    def _():
        local.wait()

    @pl.when(jnp.logical_not(here.at_home))
    def _():
        straight.wait_recv()
        onward.wait_recv()
        straight.wait_send()
        aside.wait_send()

    yield

    @pl.when(here.at_home)
    def _():
        onward.wait_send()


def spread(here, place_of, sems, ready=()):
    for copy in ready:
        copy.wait()
    over = send(place_of(here.far), place_of(here.far), sems(), here.across)
    beside = send(place_of(here.far), place_of(here.far), sems(), here.sibling)
    yield
    over.wait_recv()
    last = send(place_of(1 - here.far), place_of(1 - here.far), sems(), here.sibling)
    yield
    beside.wait_recv()
    last.wait_recv()
    for copy in (over, beside, last):
        copy.wait_send()


def gather_columns(here, chunks, target, local_sem, sems):
    x, z, y = here.own
    place = target.at[x, here.core, here.far, z, y]
    local = pltpu.make_async_copy(chunks.at[here.shard], place, local_sem)
    local.start()
    copies = [
        send(chunks.at[here.shard_of(bits)], place, sems(), here.device(bits))
        for bits in here.others()
    ]
    yield
    yield from spread(
        here, lambda far: target.at[:, here.core, far], sems, copies + [local]
    )


ANY = pl.BlockSpec(memory_space=pltpu.MemorySpace.HBM)
VMEM = pl.BlockSpec(memory_space=pltpu.MemorySpace.VMEM)
VMEM_BYTES = 56 * 2**20


def params(collective_id):
    return pltpu.CompilerParams(
        collective_id=collective_id, has_side_effects=True, vmem_limit_bytes=VMEM_BYTES
    )


def dma_sems(count):
    return [pltpu.SemaphoreType.DMA((count,)), pltpu.SemaphoreType.DMA((count,))]


def half_blocks(block):
    return pltpu.VMEM((block[0], block[1] // 2), BF16)


QUERY_TILE = 256
NT = (((1,), (1,)), ((), ()))
TN = (((0,), (0,)), ((), ()))


def dot(left, right):
    return jnp.dot(left, right, preferred_element_type=F32)


def dot_nt(left, right):
    return lax.dot_general(left, right, NT, preferred_element_type=F32)


def dot_tn(left, right):
    return lax.dot_general(left, right, TN, preferred_element_type=F32)


def rotate(head, cosine, sine):
    return head * cosine + pltpu.roll(head, HALF_LANES, 1) * sine


def scores_of(keys, queries):
    count = keys.shape[0] - QUERY_TILE
    parts = []
    if count > 0:
        parts.append(dot_nt(keys[:count], queries) * HEAD_SIZE**-0.5)
    last = dot_nt(keys[count:], queries) * HEAD_SIZE**-0.5
    key = lax.broadcasted_iota(jnp.int32, last.shape, 0)
    query = lax.broadcasted_iota(jnp.int32, last.shape, 1)
    parts.append(jnp.where(key <= query, last, MASK_FILL))
    return parts


def attend_tile(q, k, v_t, o_t, ob, lse, group, tile):
    rows = pl.ds(tile * QUERY_TILE, QUERY_TILE)
    count = (tile + 1) * QUERY_TILE
    parts = scores_of(k[:count, :], q[group, rows, :])
    top = jnp.max(parts[-1], axis=0, keepdims=True)
    for part in parts[:-1]:
        top = jnp.maximum(top, jnp.max(part, axis=0, keepdims=True))
    total = jnp.zeros_like(top)
    result = None
    first = 0
    for part in parts:
        expo = jnp.exp(part - top)
        total = total + jnp.sum(expo, axis=0, keepdims=True)
        added = dot(v_t[:, first : first + part.shape[0]], expo.astype(BF16))
        result = added if result is None else result + added
        first += part.shape[0]
    result = result / total
    o_t[group, :, rows] = result
    ob[group * HEAD_SIZE : (group + 1) * HEAD_SIZE, rows] = result[:HEAD_SIZE].astype(BF16)
    lse[group, :, rows] = top + jnp.log(total)


def front_kernel(
    tokens, cotangent, qkv, gate_up, down, out, cosine, sine,
    w_qkv, w_gu, w_d, w_o, ob_all, h1, q, k, v, o_t, lse, gains, out_part, dh2, x_own, ct_own, y1_own,
    x_all, ct_all, v_t, hidden, d_gu, dh2_part, slots, x_relay, ct_relay, local, sent, got,
):
    here = Here()
    sems = Sems(sent, got)
    here.greet(here.same_core() + [here.sibling])
    x, z, y = here.own
    width = tokens.shape[1]
    block_rows = tokens.shape[0]
    seq_rows = CUBE * block_rows

    def swapped(source, target, relay, local_sem, orders):
        yield from swap_home(
            here,
            source,
            target.at[here.shard],
            relay,
            local_sem,
            sems,
            target.at[here.shard_of(here.flip(0))],
        )
        yield from gather_cube_parts(
            here, lambda bits, part: target.at[here.shard_of(bits), :, part], width, orders, sems
        )

    def out_gather():
        mine = w_o.at[x, here.core, here.far, z, y]
        kept = pltpu.make_async_copy(out, mine, local.at[3])
        kept.start()
        over = send(out, mine, sems(), here.across)
        yield
        kept.wait()
        over.wait()
        yield from gather_cube_parts(
            here,
            lambda bits, part: w_o.at[bits[0], here.core, :, bits[1], bits[2], :, part],
            width,
            ORDERS_Z_FIRST,
            sems,
        )
        beside = send(w_o.at[:, here.core], w_o.at[:, here.core], sems(), here.sibling)
        yield
        beside.wait()

    def down_gather():
        kept = pltpu.make_async_copy(down, w_d.at[here.core, here.far], local.at[2])
        kept.start()
        yield from spread(here, lambda far: w_d.at[here.core, far], sems, [kept])

    get_x = swapped(tokens, x_all, x_relay, local.at[0], ORDERS)
    get_qkv = gather_columns(here, qkv, w_qkv, local.at[4], sems)
    get_gu = gather_columns(here, gate_up, w_gu, local.at[5], sems)
    get_out = out_gather()
    get_down = down_gather()
    get_ct = swapped(cotangent, ct_all, ct_relay, local.at[1], ORDERS_Z_FIRST)
    for step in (
        get_x,
        get_qkv,
        get_out,
        get_x,
        get_qkv,
        get_gu,
        get_x,
        get_x,
        get_ct,
        get_x,
        get_ct,
        get_gu,
        get_x,
        get_down,
        get_x,
        get_qkv,
        get_ct,
        get_out,
        get_ct,
    ):
        next(step)
    run_all(get_x, get_qkv)
    later = in_step([get_ct, get_out, get_gu, get_down])

    turned = jnp.transpose(
        w_qkv[:, :, :, :, :, :, 3 * HEAD_LANES :].astype(F32).reshape(width, HEAD_LANES)
    )
    gains[...] = turned[HEAD_SIZE : HEAD_SIZE + 8]
    next(later, None)

    def norm_block(index, carry):
        rows = x_all[index].astype(F32)
        inv_root = lax.rsqrt(jnp.mean(rows * rows, axis=-1, keepdims=True) + NORM_EPS)
        place = pl.ds(pl.multiple_of(index * block_rows, block_rows), block_rows)
        h1[place, :] = (rows * inv_root * gains[0:1, :]).astype(BF16)
        return carry

    lax.fori_loop(0, CUBE, norm_block, 0)
    next(later, None)

    def project(index, carry):
        rows = pl.ds(pl.multiple_of(index * QUERY_TILE, QUERY_TILE), QUERY_TILE)
        raw = dot(h1[rows, :], w_qkv[...].reshape(width, SHARE))
        cos_rows, sin_rows = cosine[rows, :], sine[rows, :]
        heads = [raw[:, lane : lane + HEAD_LANES] for lane in range(0, SHARE, HEAD_LANES)]
        q[0, rows, :] = rotate(heads[0], cos_rows, sin_rows).astype(BF16)
        q[1, rows, :] = rotate(heads[1], cos_rows, sin_rows).astype(BF16)
        k[rows, :] = rotate(heads[2], cos_rows, sin_rows).astype(BF16)
        v[rows, :] = heads[3].astype(BF16)
        v_t[:, rows] = jnp.transpose(heads[3]).astype(BF16)
        return carry

    lax.fori_loop(0, seq_rows // QUERY_TILE, project, 0)
    next(later, None)

    ob = ob_all.at[here.shard]
    streams = []
    tiles = seq_rows // QUERY_TILE
    for tile in range(tiles):
        for group in range(2):
            attend_tile(q, k, v_t, o_t, ob, lse, group, tile)
        if tile % 2 == 1:
            lanes = pl.ds((tile - 1) * QUERY_TILE, 2 * QUERY_TILE)
            half = gather_cube_parts(
                here,
                lambda bits, part, lanes=lanes: ob_all.at[here.shard_of(bits), part, lanes],
                ob.shape[0],
                ORDERS,
                sems,
            )
            next(half, None)
            streams.append(half)
        next(later, None)
    run_all(*streams, later)

    x_own[...] = x_all[here.shard]
    ct_own[...] = ct_all[here.shard]
    streams = reductions(here, dh2_part, slots, dh2, ORDERS, sems)
    for pair, turned in enumerate(PAIRS):
        shards = [here.shard_of(here.flip(*bits)) for bits in turned]
        feed_forward(
            shards, x_all, ct_all, ob_all, w_o, w_gu, w_d, gains, hidden, d_gu, out_part, dh2_part,
            y1_own if turned[-1] == () else None,
        )
        for stream in streams:
            stream.after(pair)
    finish = in_step([stream.finish() for stream in streams])
    next(finish, None)

    def gate_up_grad(index, carry):
        lanes = pl.ds(pl.multiple_of(index * 4 * HEAD_SIZE, 4 * HEAD_SIZE), 4 * HEAD_SIZE)
        left = x_all[:, :, lanes].reshape(seq_rows, 4 * HEAD_SIZE)
        grad = dot_tn(left, d_gu[...]).astype(BF16)
        w_gu[index // 2, lax.rem(index, 2)] = grad.reshape(w_gu.shape[2:])
        return carry

    def down_grad(index, carry):
        lanes = pl.ds(pl.multiple_of(index * HEAD_LANES, HEAD_LANES), HEAD_LANES)
        grad = dot_tn(hidden[:, lanes], ct_all[...].reshape(seq_rows, width)).astype(BF16)
        w_d[index // 2, lax.rem(index, 2)] = grad
        return carry

    lax.fori_loop(0, 4, down_grad, 0)
    next(finish, None)
    lax.fori_loop(0, 4, gate_up_grad, 0)
    for _ in finish:
        pass


def feed_forward(
    shards, x_all, ct_all, ob_all, w_o, w_gu, w_d, gains, hidden, d_gu, out_part, dh2_part, y1_own
):
    _, block_rows, width = x_all.shape
    share = d_gu.shape[1] // 2
    pair = lambda ref: jnp.concatenate([ref[shard] for shard in shards], axis=0)
    rows_of = [
        pl.ds(pl.multiple_of(shard * block_rows, block_rows), block_rows) for shard in shards
    ]
    ob_t = jnp.concatenate([ob_all[:, :, rows].reshape(width, block_rows) for rows in rows_of], axis=1)
    y1 = pair(x_all).astype(F32) + dot_tn(ob_t, w_o[...].reshape(width, width))
    inv_root = lax.rsqrt(jnp.mean(y1 * y1, axis=-1, keepdims=True) + NORM_EPS)
    h2 = (y1 * inv_root * gains[1:2, :]).astype(BF16)
    if y1_own is not None:
        y1_own[...] = y1[block_rows:]
    gate_up = dot(h2, w_gu[...].reshape(width, 2 * share))
    gate, up = gate_up[:, :share], gate_up[:, share:]
    sig = 1.0 / (1.0 + jnp.exp(-gate))
    silu = gate * sig
    kept = (silu * up).astype(BF16)
    down = w_d[...].reshape(share, width)
    d_hidden = dot_nt(pair(ct_all), down)
    d_gate = (d_hidden * up * sig * (1.0 + gate * (1.0 - sig))).astype(BF16)
    d_up = (d_hidden * silu).astype(BF16)
    d_both = jnp.concatenate([d_gate, d_up], axis=1)
    dh2 = dot_nt(d_both, w_gu[...].reshape(width, 2 * share)).astype(BF16)
    out = dot(kept, down).astype(BF16)
    for index, (shard, rows) in enumerate(zip(shards, rows_of)):
        block = slice(index * block_rows, (index + 1) * block_rows)
        x_all[shard] = h2[block]
        hidden[rows, :] = kept[block]
        d_gu[rows, :] = d_both[block]
        dh2_part[shard] = dh2[block]
        out_part[shard] = out[block]


def front(tokens, cotangent, qkv, gate_up, down, out, cosine, sine):
    slots = (2, 2, 2, 2, 2)
    shape = lambda *dims: jax.ShapeDtypeStruct(dims, BF16)
    wide = lambda *dims: jax.ShapeDtypeStruct(dims, F32)
    rows, width = tokens.shape
    seq_rows = CUBE * rows
    share = 2 * HEAD_SIZE
    ff_share = 4 * down.shape[0]
    outs = (
        shape(*slots, *qkv.shape[1:]),
        shape(*slots, *gate_up.shape[1:]),
        shape(2, 2, *down.shape),
        shape(*slots, *out.shape),
        shape(CUBE, share, seq_rows),
        shape(seq_rows, width),
        shape(2, seq_rows, HEAD_LANES),
        shape(seq_rows, HEAD_LANES),
        shape(seq_rows, HEAD_LANES),
        wide(2, HEAD_LANES, seq_rows),
        wide(2, 1, seq_rows),
        wide(8, width),
        shape(CUBE, rows, width),
        wide(rows, width),
        shape(rows, width),
        shape(rows, width),
        wide(rows, width),
    )
    return pl.pallas_call(
        front_kernel,
        out_shape=outs,
        in_specs=[VMEM] * 8,
        out_specs=(VMEM,) * len(outs),
        scratch_shapes=[
            pltpu.VMEM((CUBE, rows, width), BF16),
            pltpu.VMEM((CUBE, rows, width), BF16),
            pltpu.VMEM((HEAD_LANES, seq_rows), BF16),
            pltpu.VMEM((seq_rows, ff_share), BF16),
            pltpu.VMEM((seq_rows, 2 * ff_share), BF16),
            pltpu.VMEM((CUBE, rows, width), BF16),
            pltpu.VMEM((CUBE - 1, rows, width), BF16),
            half_blocks(tokens.shape),
            half_blocks(tokens.shape),
            pltpu.SemaphoreType.DMA((6,)),
        ]
        + dma_sems(162),
        compiler_params=params(1),
        name="front",
    )(tokens, cotangent, qkv, gate_up, down, out, cosine, sine)


def attend_back_tile(q, k, k_t, v, do_t, o_t, lse, dk, dv, group, tile):
    rows = pl.ds(tile * QUERY_TILE, QUERY_TILE)
    count = (tile + 1) * QUERY_TILE
    q_rows = q[group, rows, :]
    do_rows = do_t[group * HEAD_SIZE : (group + 1) * HEAD_SIZE, rows]
    do_rows = jnp.concatenate(
        [do_rows, jnp.zeros((HEAD_LANES - HEAD_SIZE, QUERY_TILE), BF16)], axis=0
    )
    delta = jnp.sum(do_rows.astype(F32) * o_t[group, :, rows], axis=0, keepdims=True)
    log_total = lse[group, :, rows]
    dq_t = None
    first = 0
    for part in scores_of(k[:count, :], q_rows):
        keys = slice(first, first + part.shape[0])
        probs = jnp.exp(part - log_total)
        d_probs = dot(v[keys, :], do_rows)
        d_scores = (probs * (d_probs - delta)).astype(BF16)
        dv[keys, :] += dot_nt(probs.astype(BF16), do_rows)
        dk[keys, :] += dot(d_scores, q_rows)
        added = dot(k_t[:, keys], d_scores)
        dq_t = added if dq_t is None else dq_t + added
        first += part.shape[0]
    return jnp.transpose(dq_t) * HEAD_SIZE**-0.5


def add_rows(total, more, piece):
    def body(index, carry):
        rows = pl.ds(pl.multiple_of(index * piece, piece), piece)
        for block in range(total.shape[0]):
            total[block, rows, :] = total_of(
                total.at[block, rows, :], more.at[block, rows, :]
            ).astype(BF16)
        return carry

    lax.fori_loop(0, total.shape[1] // piece, body, 0)


def reduce_copies(here, part, beside, over, sems, piece):
    core, far = here.core, here.far
    first = send(part.at[:, 1 - core, 1 - far], beside.at[0], sems(), here.sibling)
    second = send(part.at[:, 1 - core, far], beside.at[1], sems(), here.sibling)
    yield
    first.wait_recv()
    add_rows(part.at[:, core, 1 - far], beside.at[0], piece)
    third = send(part.at[:, core, 1 - far], over, sems(), here.across)
    second.wait_recv()
    add_rows(part.at[:, core, far], beside.at[1], piece)
    yield
    third.wait_recv()
    add_rows(part.at[:, core, far], over, piece)
    for copy in (first, second, third):
        copy.wait_send()


def scatter_columns(here, part, beside, over, out, local_sem, sems):
    rows = out.shape[1]
    yield from reduce_copies(here, part, beside, over, sems, rows)

    def source(bits):
        place = pl.ds((bits[1] * 2 + bits[2]) * rows, rows)
        return part.at[bits[0], here.core, here.far, place, :]

    local = pltpu.make_async_copy(source(here.own), out.at[here.shard], local_sem)
    local.start()
    copies = [
        send(source(bits), out.at[here.shard], sems(), here.device(bits)) for bits in here.others()
    ]
    yield
    for copy in copies + [local]:
        copy.wait()


def copy_slots(part):
    blocks, _, _, rows, share = part.shape
    return [pltpu.VMEM((2, blocks, rows, share), BF16), pltpu.VMEM((blocks, rows, share), BF16)]


def by_owner(part):
    rows, share = part.shape[3:]
    return jax.ShapeDtypeStruct((CUBE, rows // 4, share), BF16)


def norm_back_rows(grad_normed, rows, gain):
    inv_root = lax.rsqrt(jnp.mean(rows * rows, axis=-1, keepdims=True) + NORM_EPS)
    grad_gain, grad_rows = norm_back(grad_normed, rows, inv_root, gain)
    return grad_gain.reshape(1, -1), grad_rows


def sum_everywhere(here, total, slots, sems):
    hops = [here.sibling] + [here.next(bit) for bit in BITS] + [here.across]
    for index, device in enumerate(hops):
        copy = send(total, slots.at[index], sems(), device)
        yield
        copy.wait()
        total[...] += slots[index]


def back_kernel(
    dh2, x_own, ct_own, y1_own, gains, out_part, gu_part, down_part,
    w_qkv, w_o, ob_all, h1, q, k, v, o_t, lse, cosine, sine,
    output_home, grad_home, gu_rows, down_sum, qkv_rows, out_rows, gain_sums,
    d_middle, pairs, columns, d_qkv, k_t, dk, dv, dh1_part, dh1, dh1_slots, out_sum, out_slots,
    gu_beside, gu_over, down_beside, down_over, qkv_part, qkv_beside, qkv_over,
    wo_part, wo_beside, wo_over, own_rows, relay, relay_too, gain_slots, local, sent, got,
):
    here = Here()
    sems = Sems(sent, got)
    here.greet(here.same_core() + [here.sibling])
    block_rows, width = dh2.shape
    seq_rows = CUBE * block_rows
    share = 2 * HEAD_SIZE

    def half_gu(index):
        lanes = pl.ds(index * gu_part.shape[4] // 2, gu_part.shape[4] // 2)
        return scatter_columns(
            here,
            gu_part.at[:, :, :, :, lanes],
            gu_beside.at[:, :, :, lanes],
            gu_over.at[:, :, lanes],
            gu_rows.at[:, :, lanes],
            local.at[index],
            sems,
        )

    def down_reduce():
        yield from reduce_copies(here, down_part, down_beside, down_over, sems, 32)
        down_sum[...] = down_part[0, here.core, here.far].astype(F32)

    grads = in_step([half_gu(0), half_gu(1), down_reduce()])
    next(grads, None)

    y1 = y1_own[...]
    grad_gain, back = norm_back_rows(dh2[...], y1, gains[1:2, :])
    gain_sums[...] = jnp.zeros_like(gain_sums)
    gain_sums[1:2, :] = grad_gain
    d_middle[...] = ct_own[...].astype(F32) + back
    da = d_middle[...].astype(BF16)
    pairs[:, 0] = dot_nt(w_o[...], da).astype(BF16).reshape(CUBE, share, block_rows)
    pairs[:, 1] = jnp.transpose(d_middle[...]).astype(BF16).reshape(CUBE, share, block_rows)
    place = columns.at[:, :, pl.ds(pl.multiple_of(here.shard * block_rows, block_rows), block_rows)]
    kept = pltpu.make_async_copy(pairs.at[here.shard], place, local.at[2])
    kept.start()
    copies = [
        send(pairs.at[here.shard_of(bits)], place, sems(), here.device(bits))
        for bits in here.others()
    ]
    next(grads, None)
    k_t[...] = jnp.transpose(k[...].astype(F32)).astype(BF16)
    dk[...] = jnp.zeros_like(dk)
    dv[...] = jnp.zeros_like(dv)
    for copy in copies + [kept]:
        copy.wait()

    sums = reductions(here, out_part, out_slots, out_sum, ORDERS, sems)
    for tile in range(seq_rows // QUERY_TILE):
        for stream in sums:
            stream.after(tile)
        rows = pl.ds(tile * QUERY_TILE, QUERY_TILE)
        for group in range(2):
            dq = attend_back_tile(
                q, k, k_t, v, columns.at[0], o_t, lse, dk, dv, group, tile
            )
            d_qkv[rows, group * HEAD_LANES : (group + 1) * HEAD_LANES] = rotate(
                dq, cosine[rows, :], -sine[rows, :]
            ).astype(BF16)
    d_qkv[:, 2 * HEAD_LANES : 3 * HEAD_LANES] = rotate(
        dk[...] * HEAD_SIZE**-0.5, cosine[...], -sine[...]
    ).astype(BF16)
    d_qkv[:, 3 * HEAD_LANES :] = dv[...].astype(BF16)

    streams = reductions(here, dh1_part, dh1_slots, dh1, ORDERS, sems)
    for pair, turned in enumerate(PAIRS):
        shards = [here.shard_of(here.flip(*bits)) for bits in turned]
        some = jnp.concatenate(
            [
                d_qkv[pl.ds(pl.multiple_of(shard * block_rows, block_rows), block_rows), :]
                for shard in shards
            ],
            axis=0,
        )
        rows = dot_nt(some, w_qkv[...]).astype(BF16)
        for index, shard in enumerate(shards):
            dh1_part[shard] = rows[index * block_rows : (index + 1) * block_rows]
        for stream in streams:
            stream.after(pair)
    finish_out = in_step([stream.finish() for stream in sums])
    finish = in_step([stream.finish() for stream in streams])
    next(finish_out, None)
    next(finish, None)

    def qkv_grad(index, carry):
        lanes = pl.ds(pl.multiple_of(index * 4 * HEAD_SIZE, 4 * HEAD_SIZE), 4 * HEAD_SIZE)
        grad = dot_tn(h1[:, lanes], d_qkv[...]).astype(BF16)
        qkv_part[index // 2, lax.rem(index, 2)] = grad.reshape(qkv_part.shape[2:])
        return carry

    lax.fori_loop(0, 4, qkv_grad, 0)
    grads_too = [
        scatter_columns(here, qkv_part, qkv_beside, qkv_over, qkv_rows, local.at[3], sems)
    ]
    next(grads_too[0], None)
    next(finish_out, None)
    output = (y1_own[...] + out_sum[...]).astype(BF16)
    own_rows[0] = output
    swap_output = swap_home(here, own_rows.at[0], output_home, relay, local.at[4], sems)
    next(swap_output, None)

    for index in range(4):
        left = ob_all[2 * index : 2 * index + 2].reshape(2 * share, seq_rows)
        grad = dot_nt(left, columns[1]).astype(BF16)
        grad = jnp.concatenate(
            [grad, jnp.zeros((2 * share, wo_part.shape[4] - share), BF16)], axis=1
        )
        wo_part[index // 2, index % 2] = grad.reshape(wo_part.shape[2:])
    grads_too.append(scatter_columns(here, wo_part, wo_beside, wo_over, out_rows, local.at[5], sems))
    next(grads_too[1], None)
    next(grads_too[0], None)
    for _ in finish:
        pass

    grad_gain, back = norm_back_rows(dh1[...], x_own[...].astype(F32), gains[0:1, :])
    gain_sums[0:1, :] = grad_gain
    own_rows[1] = (d_middle[...] + back).astype(BF16)
    swap_grad = swap_home(here, own_rows.at[1], grad_home, relay_too, local.at[6], sems)
    next(swap_grad, None)
    gain_sum = sum_everywhere(here, gain_sums, gain_slots, sems)
    next(gain_sum, None)
    run_all(gain_sum, swap_output, swap_grad, *grads_too, grads, finish_out)


def back(*operands):
    dh2, x_own, _, _, _, out_part, gu_part, down_part = operands[:8]
    rows, width = dh2.shape
    seq_rows = CUBE * rows
    share = 2 * HEAD_SIZE
    part = lambda lanes: jax.ShapeDtypeStruct((*gu_part.shape[:4], lanes), BF16)
    qkv_part, wo_part = part(SHARE), part(2 * HEAD_LANES)
    vmem = lambda like: pltpu.VMEM(like.shape, BF16)
    wide = lambda *dims: jax.ShapeDtypeStruct(dims, F32)
    outs = (
        jax.ShapeDtypeStruct((rows, width), BF16),
        jax.ShapeDtypeStruct((rows, width), BF16),
        by_owner(gu_part),
        wide(*down_part.shape[3:]),
        by_owner(qkv_part),
        by_owner(wo_part),
        wide(8, width),
    )
    return pl.pallas_call(
        back_kernel,
        out_shape=outs,
        in_specs=[VMEM] * len(operands),
        out_specs=(VMEM,) * len(outs),
        scratch_shapes=[
            pltpu.VMEM((rows, width), F32),
            pltpu.VMEM((CUBE, 2, share, rows), BF16),
            pltpu.VMEM((2, share, seq_rows), BF16),
            pltpu.VMEM((seq_rows, SHARE), BF16),
            pltpu.VMEM((HEAD_LANES, seq_rows), BF16),
            pltpu.VMEM((seq_rows, HEAD_LANES), F32),
            pltpu.VMEM((seq_rows, HEAD_LANES), F32),
            vmem(out_part),
            pltpu.VMEM((rows, width), F32),
            pltpu.VMEM((CUBE - 1, rows, width), BF16),
            pltpu.VMEM((rows, width), F32),
            pltpu.VMEM((CUBE - 1, rows, width), BF16),
            *copy_slots(gu_part),
            *copy_slots(down_part),
            vmem(qkv_part),
            *copy_slots(qkv_part),
            vmem(wo_part),
            *copy_slots(wo_part),
            pltpu.VMEM((2, rows, width), BF16),
            half_blocks((rows, width)),
            half_blocks((rows, width)),
            pltpu.VMEM((5, 8, width), F32),
            pltpu.SemaphoreType.DMA((7,)),
        ]
        + dma_sems(110),
        compiler_params=params(2),
        name="back",
    )(*operands)


def spaced_head(weight):
    half = HEAD_SIZE // 2
    cut = weight.reshape(*weight.shape[:-1], 2, half)
    cut = jnp.pad(cut, [(0, 0)] * (cut.ndim - 1) + [(0, HALF_LANES - half)])
    return cut.reshape(*weight.shape[:-1], HEAD_LANES)


def packed_head(spaced):
    half = HEAD_SIZE // 2
    cut = spaced.reshape(*spaced.shape[:-1], 2, HALF_LANES)[..., :half]
    return cut.reshape(*spaced.shape[:-1], HEAD_SIZE)


def spaced_tables(row_count):
    half = HEAD_SIZE // 2
    cosine, sine = rope_tables(0, row_count)
    pad = ((0, 0), (0, HALF_LANES - half))
    cosine = jnp.pad(cosine[:, 0], pad)
    sine = jnp.pad(sine[:, 0], pad)
    return jnp.concatenate([cosine, cosine], axis=1), jnp.concatenate([-sine, sine], axis=1)


def split_layer(
    tokens,
    cotangent,
    gain_attn,
    w_query,
    key_weight,
    value_weight,
    w_out,
    gain_ffn,
    w_gate,
    w_up,
    w_down,
):
    block_rows, width = tokens.shape
    weight_rows = w_query.shape[0]
    head_group = QUERY_HEADS // KEY_VALUE_HEADS
    score_scale = HEAD_SIZE ** (-0.5)
    query_share = head_group * HEAD_SIZE
    seq_rows = block_rows * CUBE
    ff_width = w_gate.shape[1]
    down_rows = w_down.shape[0]
    ff_share = 4 * down_rows

    q_cut = spaced_head(w_query.reshape(weight_rows, CUBE, head_group, HEAD_SIZE))
    k_cut = spaced_head(key_weight.reshape(weight_rows, CUBE, HEAD_SIZE))
    gains = jnp.stack([gain_attn, gain_ffn], axis=1)[:, None, :]
    v_cut = jnp.concatenate(
        [
            value_weight.reshape(weight_rows, CUBE, HEAD_SIZE),
            jnp.broadcast_to(gains, (weight_rows, CUBE, 2)),
            jnp.zeros((weight_rows, CUBE, HEAD_LANES - HEAD_SIZE - 2), BF16),
        ],
        axis=2,
    )
    qkv_chunks = jnp.transpose(
        jnp.concatenate([q_cut.reshape(weight_rows, CUBE, -1), k_cut, v_cut], axis=2), (1, 0, 2)
    )

    def ff_chunks(weight):
        cut = weight.reshape(weight_rows, 2, 4, 4, down_rows)
        return jnp.transpose(cut, (1, 3, 0, 2, 4)).reshape(CUBE, weight_rows, ff_share)

    gu_chunks = jnp.concatenate([ff_chunks(w_gate), ff_chunks(w_up)], axis=2)
    cosine, sine = spaced_tables(seq_rows)
    (
        w_qkv, gu_part, down_part, w_o, ob_all, h1, q, k, v, o_t, lse, gains,
        out_part, dh2, x_own, ct_own, y1_own,
    ) = front(tokens, cotangent, qkv_chunks, gu_chunks, w_down, w_out, cosine, sine)
    w_qkv = w_qkv.reshape(width, SHARE)
    w_o = w_o.reshape(width, width)
    cut = lambda part: part.reshape(2, 2, 2, 4 * weight_rows, -1)
    output, grad_tokens, gu_rows, grad_down, qkv_rows, out_rows, gain_sums = back(
        dh2, x_own, ct_own, y1_own, gains, out_part, cut(gu_part),
        down_part.reshape(1, 2, 2, down_rows, width),
        w_qkv, w_o, ob_all, h1, q, k, v, o_t, lse, cosine, sine,
    )
    rank = lax.axis_index("dp") * lax.axis_size("ctx") + lax.axis_index("ctx")
    gain_sums = lax.dynamic_slice_in_dim(gain_sums[:2], rank * weight_rows, weight_rows, 1)

    qkv_rows = jnp.transpose(qkv_rows.astype(F32), (1, 0, 2)).reshape(weight_rows, CUBE, 4, HEAD_LANES)
    out_rows = jnp.transpose(out_rows.astype(F32), (1, 0, 2))[..., :query_share]

    def ff_joined(blocks):
        cut = blocks.astype(F32).reshape(2, 4, weight_rows, 4, down_rows)
        return jnp.transpose(cut, (2, 0, 3, 1, 4)).reshape(weight_rows, ff_width)

    return (
        output,
        grad_tokens.astype(F32),
        gain_sums[0],
        packed_head(qkv_rows[:, :, :head_group]).reshape(weight_rows, -1),
        packed_head(qkv_rows[:, :, head_group]).reshape(weight_rows, -1),
        qkv_rows[:, :, 3, :HEAD_SIZE].reshape(weight_rows, -1),
        out_rows.reshape(weight_rows, width),
        gain_sums[1],
        ff_joined(gu_rows[:, :, :ff_share]),
        ff_joined(gu_rows[:, :, ff_share:]),
        grad_down,
    )


def solution(mesh):
    heads_split = mesh.shape["dp"] == 4 and mesh.shape["ctx"] == KEY_VALUE_HEADS
    return jax.shard_map(
        split_layer if heads_split else blockwise_layer,
        mesh=mesh,
        in_specs=(
            P(("dp", "ctx"), None),
            P(("dp", "ctx"), None),
            P(("dp", "ctx")),
            P(("dp", "ctx"), None),
            P(("dp", "ctx"), None),
            P(("dp", "ctx"), None),
            P(("dp", "ctx"), None),
            P(("dp", "ctx")),
            P(("dp", "ctx"), None),
            P(("dp", "ctx"), None),
            P(("dp", "ctx"), None),
        ),
        out_specs=(
            P(("dp", "ctx"), None),
            P(("dp", "ctx"), None),
            P(("dp", "ctx")),
            P(("dp", "ctx"), None),
            P(("dp", "ctx"), None),
            P(("dp", "ctx"), None),
            P(("dp", "ctx"), None),
            P(("dp", "ctx")),
            P(("dp", "ctx"), None),
            P(("dp", "ctx"), None),
            P(("dp", "ctx"), None),
        ),
        check_vma=False,
    )
```

```python
import functools

import jax
import jax.numpy as jnp
import numpy as np
from jax import lax
from jax.experimental import pallas as pl
from jax.experimental.pallas import tpu as pltpu
from jax.sharding import PartitionSpec as P

QUERY_HEADS = 16
KEY_VALUE_HEADS = 8
HEAD_SIZE = 96


NORM_EPS = 1e-05
ROPE_THETA = 100000.0
MASK_FILL = -1e30


def passed_along(value, axis, by):
    peers = lax.axis_size(axis)
    pairs = [(i, i + by) for i in range(peers) if 0 <= i + by < peers]
    return lax.ppermute(value, axis, pairs)


def shifted(block, axis, distance):
    devices = range(lax.axis_size(axis))
    route = [((i - distance) % len(devices), i) for i in devices]
    return lax.ppermute(block, axis, route)


def rope_tables(first_row, block_count):
    half_dim = HEAD_SIZE // 2
    positions = (first_row + jnp.arange(block_count, dtype=jnp.int32)).astype(jnp.float32)
    frequency = ROPE_THETA ** (-jnp.arange(half_dim, dtype=jnp.float32) * 2.0 / HEAD_SIZE)
    angles = positions[:, None] * frequency[None, :]
    return (jnp.cos(angles)[:, None, :], jnp.sin(angles)[:, None, :])


def apply_rotary(value_rows, cosine_table, sine_values, direction):
    half_dim = HEAD_SIZE // 2
    first_half = value_rows[..., :half_dim]
    second_half = value_rows[..., half_dim:]
    return jnp.concatenate(
        [
            first_half * cosine_table - direction * second_half * sine_values,
            second_half * cosine_table + direction * first_half * sine_values,
        ],
        axis=-1,
    )


def norm_back(grad_normed, inputs, inv_root, gain):
    grad_gain = jnp.sum(grad_normed * inputs * inv_root, axis=0)
    scaled = grad_normed * gain.astype(jnp.float32)
    grad_inputs = inv_root * (
        scaled - inputs * inv_root * inv_root * jnp.mean(scaled * inputs, axis=-1, keepdims=True)
    )
    return (grad_gain, grad_inputs)


def row_product(left, right):
    return jnp.einsum("tc,tf->cf", left, right, preferred_element_type=jnp.float32)


def blockwise_layer(
    tokens,
    cotangent,
    gain_attn,
    w_query,
    key_weight,
    value_weight,
    w_out,
    gain_ffn,
    w_gate,
    w_up,
    w_down,
):
    token_rows = tokens.shape[0]
    head_group = QUERY_HEADS // KEY_VALUE_HEADS
    key_value_width = KEY_VALUE_HEADS * HEAD_SIZE
    query_width = QUERY_HEADS * HEAD_SIZE
    score_scale = HEAD_SIZE ** (-0.5)
    ctx_count = lax.axis_size("ctx")
    ctx_rank = lax.axis_index("ctx")
    first_row = ctx_rank * token_rows
    query_pos = first_row + jnp.arange(token_rows, dtype=jnp.int32)
    attn_full = (
        lax.all_gather(gain_attn, ("dp", "ctx"), axis=0, tiled=True),
        lax.all_gather(w_query, ("dp", "ctx"), axis=0, tiled=True),
        lax.all_gather(key_weight, ("dp", "ctx"), axis=0, tiled=True),
        lax.all_gather(value_weight, ("dp", "ctx"), axis=0, tiled=True),
        lax.all_gather(w_out, ("dp", "ctx"), axis=0, tiled=True),
    )
    gain_one, query_full, key_full, value_full, out_full = attn_full
    inputs = tokens.astype(jnp.float32)
    inv_one = lax.rsqrt(jnp.mean(inputs * inputs, axis=-1, keepdims=True) + NORM_EPS)
    first_normed = (inputs * inv_one * gain_one.astype(jnp.float32)).astype(jnp.bfloat16)
    query_unrotated = jnp.dot(first_normed, query_full, preferred_element_type=jnp.float32).reshape(
        token_rows, QUERY_HEADS, HEAD_SIZE
    )
    key_unrotated = jnp.dot(first_normed, key_full, preferred_element_type=jnp.float32).reshape(
        token_rows, KEY_VALUE_HEADS, HEAD_SIZE
    )
    value_raw = jnp.dot(first_normed, value_full, preferred_element_type=jnp.float32)
    cosine_table, sine_values = rope_tables(first_row, token_rows)
    query_rows = (
        apply_rotary(query_unrotated, cosine_table, sine_values, 1.0)
        .astype(jnp.bfloat16)
        .reshape(token_rows, KEY_VALUE_HEADS, head_group, HEAD_SIZE)
    )
    keys_rot = (
        apply_rotary(key_unrotated, cosine_table, sine_values, 1.0)
        .astype(jnp.bfloat16)
        .reshape(token_rows, key_value_width)
    )
    kv_local = jnp.concatenate([keys_rot, value_raw.astype(jnp.bfloat16)], axis=1)
    starting = (
        jnp.full((KEY_VALUE_HEADS, head_group, token_rows), MASK_FILL, jnp.float32),
        jnp.zeros((KEY_VALUE_HEADS, head_group, token_rows), jnp.float32),
        jnp.zeros((token_rows, KEY_VALUE_HEADS, head_group, HEAD_SIZE), jnp.float32),
    )
    sequence_portion = lax.all_gather(kv_local, "ctx", axis=0, tiled=True)

    def update(state):
        run_max, run_sum, run_acc = state
        block_count = sequence_portion.shape[0]
        key_portion = sequence_portion[:, :key_value_width].reshape(
            block_count, KEY_VALUE_HEADS, HEAD_SIZE
        )
        value_portion = sequence_portion[:, key_value_width:].reshape(
            block_count, KEY_VALUE_HEADS, HEAD_SIZE
        )
        scores = (
            jnp.einsum(
                "tkgd,skd->kgts", query_rows, key_portion, preferred_element_type=jnp.float32
            )
            * score_scale
        )
        key_pos = jnp.arange(block_count, dtype=jnp.int32)
        allowed = key_pos[None, :] <= query_pos[:, None]
        scores = jnp.where(allowed, scores, MASK_FILL)
        new_max = jnp.maximum(run_max, jnp.max(scores, axis=-1))
        expo = jnp.exp(scores - new_max[..., None])
        new_sum = jnp.sum(expo, axis=-1)
        added = jnp.einsum(
            "kgts,skd->tkgd",
            expo.astype(jnp.bfloat16),
            value_portion,
            preferred_element_type=jnp.float32,
        )
        return (new_max, new_sum, added)

    def unchanged(state):
        return state

    run_max, run_sum, run_acc = lax.cond(
        jnp.int32(0) <= first_row + token_rows - 1, update, unchanged, starting
    )
    attn_four = run_acc / jnp.transpose(run_sum, (2, 0, 1))[..., None]
    log_total = run_max + jnp.log(run_sum)
    attn_out = attn_four.reshape(token_rows, query_width)
    attn_low = attn_out.astype(jnp.bfloat16)
    middle = inputs + jnp.dot(attn_low, out_full, preferred_element_type=jnp.float32)
    mlp_full = (
        lax.all_gather(gain_ffn, ("dp", "ctx"), axis=0, tiled=True),
        lax.all_gather(w_gate, ("dp", "ctx"), axis=0, tiled=True),
        lax.all_gather(w_up, ("dp", "ctx"), axis=0, tiled=True),
        lax.all_gather(w_down, ("dp", "ctx"), axis=0, tiled=True),
    )
    gain_two, gate_full, up_full, down_full = mlp_full
    inv_two = lax.rsqrt(jnp.mean(middle * middle, axis=-1, keepdims=True) + NORM_EPS)
    normed_two = (middle * inv_two * gain_two.astype(jnp.float32)).astype(jnp.bfloat16)
    gate_value = jnp.dot(normed_two, gate_full, preferred_element_type=jnp.float32)
    up_value = jnp.dot(normed_two, up_full, preferred_element_type=jnp.float32)
    sigmoid_gate = jax.nn.sigmoid(gate_value)
    silu_gate = gate_value * sigmoid_gate
    hidden = (silu_gate * up_value).astype(jnp.bfloat16)
    output = (middle + jnp.dot(hidden, down_full, preferred_element_type=jnp.float32)).astype(
        jnp.bfloat16
    )
    mlp_back = (
        lax.all_gather(gain_ffn, ("dp", "ctx"), axis=0, tiled=True),
        lax.all_gather(w_gate, ("dp", "ctx"), axis=0, tiled=True),
        lax.all_gather(w_up, ("dp", "ctx"), axis=0, tiled=True),
        lax.all_gather(w_down, ("dp", "ctx"), axis=0, tiled=True),
    )
    gain_two_back, gate_back, up_back, down_back = mlp_back
    grad_out = cotangent.astype(jnp.float32)
    grad_hidden = jnp.einsum("td,fd->tf", cotangent, down_back, preferred_element_type=jnp.float32)
    grad_gate = (
        grad_hidden * up_value * sigmoid_gate * (1.0 + gate_value * (1.0 - sigmoid_gate))
    ).astype(jnp.bfloat16)
    grad_up = (grad_hidden * silu_gate).astype(jnp.bfloat16)
    grad_normed_two = jnp.einsum(
        "tf,cf->tc", grad_gate, gate_back, preferred_element_type=jnp.float32
    ) + jnp.einsum("tf,cf->tc", grad_up, up_back, preferred_element_type=jnp.float32)
    grad_gain_two, grad_middle_norm = norm_back(grad_normed_two, middle, inv_two, gain_two_back)
    grad_middle = grad_out + grad_middle_norm
    gate_up_pair = jnp.concatenate([grad_gate, grad_up], axis=1)
    gate_up_sum = lax.psum_scatter(
        row_product(normed_two, gate_up_pair), ("dp", "ctx"), scatter_dimension=0, tiled=True
    )
    grad_down_sum = lax.psum_scatter(
        row_product(hidden, cotangent), ("dp", "ctx"), scatter_dimension=0, tiled=True
    )
    attn_back = (
        lax.all_gather(gain_attn, ("dp", "ctx"), axis=0, tiled=True),
        lax.all_gather(w_query, ("dp", "ctx"), axis=0, tiled=True),
        lax.all_gather(key_weight, ("dp", "ctx"), axis=0, tiled=True),
        lax.all_gather(value_weight, ("dp", "ctx"), axis=0, tiled=True),
        lax.all_gather(w_out, ("dp", "ctx"), axis=0, tiled=True),
    )
    gain_one_back, query_back, key_back, value_back, out_back = attn_back
    grad_branch = grad_middle.astype(jnp.bfloat16)
    attention_gradient = jnp.einsum(
        "td,cd->tc", grad_branch, out_back, preferred_element_type=jnp.float32
    ).astype(jnp.bfloat16)
    gradient_quad = attention_gradient.reshape(token_rows, KEY_VALUE_HEADS, head_group, HEAD_SIZE)
    delta_rows = jnp.transpose(
        jnp.sum(gradient_quad.astype(jnp.float32) * attn_four, axis=-1), (1, 2, 0)
    )

    def pair_terms(key_value_block, key_first):
        block_count = key_value_block.shape[0]
        key_portion = key_value_block[:, :key_value_width].reshape(
            block_count, KEY_VALUE_HEADS, HEAD_SIZE
        )
        value_portion = key_value_block[:, key_value_width:].reshape(
            block_count, KEY_VALUE_HEADS, HEAD_SIZE
        )
        scores = (
            jnp.einsum(
                "tkgd,skd->kgts", query_rows, key_portion, preferred_element_type=jnp.float32
            )
            * score_scale
        )
        key_pos = key_first + jnp.arange(block_count, dtype=jnp.int32)
        allowed = key_pos[None, :] <= query_pos[:, None]
        scores = jnp.where(allowed, scores, MASK_FILL)
        probs = jnp.exp(scores - log_total[..., None])
        grad_probs = jnp.einsum(
            "tkgd,skd->kgts", gradient_quad, value_portion, preferred_element_type=jnp.float32
        )
        grad_scores = (probs * (grad_probs - delta_rows[..., None])).astype(jnp.bfloat16)
        grad_query = (
            jnp.einsum(
                "kgts,skd->tkgd", grad_scores, key_portion, preferred_element_type=jnp.float32
            )
            * score_scale
        )
        grad_keys = (
            jnp.einsum(
                "kgts,tkgd->skd", grad_scores, query_rows, preferred_element_type=jnp.float32
            )
            * score_scale
        )
        grad_values = jnp.einsum(
            "kgts,tkgd->skd",
            probs.astype(jnp.bfloat16),
            gradient_quad,
            preferred_element_type=jnp.float32,
        )
        return (
            grad_query,
            jnp.concatenate(
                [
                    grad_keys.reshape(block_count, key_value_width),
                    grad_values.reshape(block_count, key_value_width),
                ],
                axis=1,
            ),
        )

    def add_pair(operands):
        kv_use, key_first, grad_query, grad_now = operands
        more_query, more_kv = pair_terms(kv_use, key_first)
        return (grad_query + more_query, grad_now + more_kv)

    def keep_pair(operands):
        return (operands[2], operands[3])

    def cycle_step(step, state):
        kv_now, grad_now, grad_query = state
        owner = (ctx_rank - step + ctx_count) % ctx_count
        kv_next = passed_along(kv_now, "ctx", 1)
        grad_query, grad_now = lax.cond(
            owner <= ctx_rank,
            add_pair,
            keep_pair,
            (kv_now, owner * token_rows, grad_query, grad_now),
        )
        grad_next = shifted(grad_now.astype(jnp.bfloat16), "ctx", 1).astype(grad_now.dtype)
        return (kv_next, grad_next, grad_query)

    cycle_start = (
        kv_local,
        jnp.zeros((token_rows, 2 * key_value_width), jnp.float32),
        jnp.zeros((token_rows, KEY_VALUE_HEADS, head_group, HEAD_SIZE), jnp.float32),
    )
    kv_final, key_value_gradient, grad_query = lax.fori_loop(0, ctx_count, cycle_step, cycle_start)
    grad_query_raw = (
        apply_rotary(
            grad_query.reshape(token_rows, QUERY_HEADS, HEAD_SIZE), cosine_table, sine_values, -1.0
        )
        .reshape(token_rows, query_width)
        .astype(jnp.bfloat16)
    )
    grad_key_raw = (
        apply_rotary(
            key_value_gradient[:, :key_value_width].reshape(token_rows, KEY_VALUE_HEADS, HEAD_SIZE),
            cosine_table,
            sine_values,
            -1.0,
        )
        .reshape(token_rows, key_value_width)
        .astype(jnp.bfloat16)
    )
    grad_value_raw = key_value_gradient[:, key_value_width:].astype(jnp.bfloat16)
    grad_normed_one = (
        jnp.einsum("tq,cq->tc", grad_query_raw, query_back, preferred_element_type=jnp.float32)
        + jnp.einsum("tq,cq->tc", grad_key_raw, key_back, preferred_element_type=jnp.float32)
        + jnp.einsum("tq,cq->tc", grad_value_raw, value_back, preferred_element_type=jnp.float32)
    )
    grad_gain_one, grad_input_norm = norm_back(grad_normed_one, inputs, inv_one, gain_one_back)
    grad_tokens = grad_middle + grad_input_norm
    projection_grads = jnp.concatenate([grad_query_raw, grad_key_raw, grad_value_raw], axis=1)
    qkv_sum = lax.psum_scatter(
        row_product(first_normed, projection_grads), ("dp", "ctx"), scatter_dimension=0, tiled=True
    )
    grad_out_sum = lax.psum_scatter(
        row_product(attn_low, grad_branch), ("dp", "ctx"), scatter_dimension=0, tiled=True
    )
    gain_sums = (
        lax.psum_scatter(grad_gain_one, ("dp", "ctx"), scatter_dimension=0, tiled=True),
        lax.psum_scatter(grad_gain_two, ("dp", "ctx"), scatter_dimension=0, tiled=True),
    )
    ff_width = w_gate.shape[1]
    return (
        output,
        grad_tokens,
        gain_sums[0],
        qkv_sum[:, :query_width],
        qkv_sum[:, query_width : query_width + key_value_width],
        qkv_sum[:, query_width + key_value_width :],
        grad_out_sum,
        gain_sums[1],
        gate_up_sum[:, :ff_width],
        gate_up_sum[:, ff_width:],
        grad_down_sum,
    )


CUBE = 8
BITS = (0, 1, 2)
HEAD_LANES = 128
HALF_LANES = 64
SHARE = 4 * HEAD_LANES
F32 = jnp.float32
BF16 = jnp.bfloat16


class Here:
    def __init__(self):
        dp = lax.axis_index("dp")
        ctx = lax.axis_index("ctx")
        self.core = lax.rem(dp, 2)
        self.far = ctx // 4
        self.own = (dp // 2, lax.rem(ctx // 2, 2), lax.rem(ctx, 2))
        self.shard = self.shard_of(self.own)
        self.at_home = self.own[0] == self.far
        self.sibling = self.device(self.own, core=1 - self.core)
        self.across = self.device(self.own, far=1 - self.far)

    def shard_of(self, bits):
        return bits[0] * 4 + bits[1] * 2 + bits[2]

    def device(self, bits, core=None, far=None):
        core = self.core if core is None else core
        far = self.far if far is None else far
        return (bits[0] * 2 + core, far * 4 + bits[1] * 2 + bits[2])

    def flip(self, *turned, of=None):
        bits = self.own if of is None else of
        return tuple(1 - bit if index in turned else bit for index, bit in enumerate(bits))

    def next(self, bit):
        return self.device(self.flip(bit))

    def others(self):
        return [
            self.flip(*[bit for bit in BITS if code >> (2 - bit) & 1]) for code in range(1, CUBE)
        ]

    def greet(self, partners):
        barrier = pltpu.get_barrier_semaphore()
        for partner in partners:
            pl.semaphore_signal(
                barrier, inc=1, device_id=partner, device_id_type=pl.DeviceIdType.MESH
            )
        pl.semaphore_wait(barrier, len(partners))

    def peers(self):
        return [self.device(bits) for bits in self.others()]

    def same_core(self):
        beyond = [self.device(bits, far=1 - self.far) for bits in self.others() + [self.own]]
        return self.peers() + beyond


def make_send(source, target, sems, device):
    return pltpu.make_async_remote_copy(
        src_ref=source,
        dst_ref=target,
        send_sem=sems[0],
        recv_sem=sems[1],
        device_id=device,
        device_id_type=pl.DeviceIdType.MESH,
    )


def send(*operands):
    copy = make_send(*operands)
    copy.start()
    return copy


class Sems:
    def __init__(self, sent, received):
        self.sent, self.received, self.used = sent, received, 0

    def __call__(self):
        pair = (self.sent.at[self.used], self.received.at[self.used])
        self.used += 1
        return pair


def run_all(*generators):
    live = list(generators)
    while live:
        for one in list(live):
            try:
                next(one)
            except StopIteration:
                live.remove(one)


def play(script, transfers, actions):
    actions = {name: list(some) for name, some in actions.items()}
    for name in script:
        if name in actions:
            actions[name].pop(0)()
        else:
            next(transfers[name], None)
    run_all(*transfers.values())


def in_step(live):
    live = list(live)
    while live:
        for one in list(live):
            try:
                next(one)
            except StopIteration:
                live.remove(one)
        yield


ORDERS = ((0, 1, 2), (1, 2, 0), (2, 0, 1))
ORDERS_Z_FIRST = ((1, 0, 2), (1, 2, 0))


def gather_cube(here, place_of, order, sems):
    a, b, c = order
    to = lambda bits, bit: send(place_of(bits), place_of(bits), sems(), here.next(bit))
    from_a, from_b = here.flip(a), here.flip(b)
    a0, b0, c0 = to(here.own, a), to(here.own, b), to(here.own, c)
    yield
    a0.wait_recv()
    b1, c1 = to(from_a, b), to(from_a, c)
    yield
    b0.wait_recv()
    c2 = to(from_b, c)
    yield
    b1.wait_recv()
    c3 = to(here.flip(a, b), c)
    yield
    for copy in (c0, c1, c2, c3):
        copy.wait_recv()
    for copy in (a0, b0, b1, c0, c1, c2, c3):
        copy.wait_send()


def gather_cube_parts(here, place_of, size, orders, sems):
    step = size // len(orders)
    return in_step(
        [
            gather_cube(
                here, functools.partial(place_of, part=pl.ds(index * step, step)), order, sems
            )
            for index, order in enumerate(orders)
        ]
    )


def total_of(*refs):
    total = refs[0][...].astype(F32)
    for ref in refs[1:]:
        total = total + ref[...].astype(F32)
    return total


PAIRS = (((0, 1, 2), (0, 1)), ((1, 2), (0, 2)), ((0,), (2,)), ((1,), ()))


class ReduceStream:
    def __init__(self, here, part_of, slots, out, order, sems):
        self.here, self.part_of, self.slots, self.out = here, part_of, slots, out
        c, b, a = self.order = order
        self.first = [(c, b, a), (c, b), (c, a), (c,)]
        self.copies = [None] * (CUBE - 1)
        self.sems = [sems() for _ in range(CUBE - 1)]
        self.made = set()

    def send(self, turned, slot, bit):
        self.copies[slot] = send(
            self.part_of(self.here.flip(*turned)),
            self.slots(slot),
            self.sems[slot],
            self.here.next(bit),
        )

    def add(self, turned, *slots):
        for slot in slots:
            self.copies[slot].wait_recv()
        spot = self.part_of(self.here.flip(*turned))
        spot[...] = total_of(spot, *[self.slots(slot) for slot in slots]).astype(BF16)

    def after(self, pair):
        c, b, a = self.order
        before = set(self.made)
        self.made |= {frozenset(turned) for turned in PAIRS[pair]}
        for slot, turned in enumerate(self.first):
            if frozenset(turned) in self.made - before:
                self.send(turned, slot, c)
        if self.copies[4] is None and self.copies[0] is not None and frozenset((b, a)) in self.made:
            self.add((b, a), 0)
            self.send((b, a), 4, b)
        if self.copies[5] is None and self.copies[1] is not None and frozenset((b,)) in self.made:
            self.add((b,), 1)
            self.send((b,), 5, b)

    def finish(self):
        _, b, a = self.order
        self.add((a,), 2, 4)
        self.send((a,), 6, a)
        yield
        for slot in (3, 5, 6):
            self.copies[slot].wait_recv()
        self.out[...] = total_of(
            self.part_of(self.here.own), self.slots(3), self.slots(5), self.slots(6)
        )
        yield
        for copy in self.copies:
            copy.wait_send()


def reductions(here, part, slots, out, orders, sems):
    width = out.shape[1] // len(orders)
    return [
        ReduceStream(
            here,
            lambda bits, columns=columns: part.at[here.shard_of(bits), :, columns],
            lambda slot, columns=columns: slots.at[slot, :, columns],
            out.at[:, columns],
            order,
            sems,
        )
        for columns, order in [
            (pl.ds(index * width, width), order) for index, order in enumerate(orders)
        ]
    ]


def swap_home(here, source, target, relay, local_sem, sems, beyond=None):
    beyond = target if beyond is None else beyond
    half = source.shape[1] // 2
    left, right = pl.ds(0, half), pl.ds(half, half)
    there = here.device(here.flip(0), far=1 - here.far)
    local = pltpu.make_async_copy(source, target, local_sem)
    straight = make_send(source.at[:, left], beyond.at[:, left], sems(), there)
    aside = make_send(source.at[:, right], relay, sems(), here.next(0))
    onward = make_send(relay, target.at[:, right], sems(), here.across)

    @pl.when(here.at_home)
    def _():
        local.start()

    @pl.when(jnp.logical_not(here.at_home))
    def _():
        aside.start()
        straight.start()

    yield

    @pl.when(here.at_home)
    def _():
        aside.wait_recv()
        onward.start()

    yield

    @pl.when(here.at_home)
    def _():
        local.wait()

    @pl.when(jnp.logical_not(here.at_home))
    def _():
        straight.wait_recv()
        onward.wait_recv()
        straight.wait_send()
        aside.wait_send()

    yield

    @pl.when(here.at_home)
    def _():
        onward.wait_send()


def spread(here, place_of, sems, ready=()):
    for copy in ready:
        copy.wait()
    over = send(place_of(here.far), place_of(here.far), sems(), here.across)
    beside = send(place_of(here.far), place_of(here.far), sems(), here.sibling)
    yield
    over.wait_recv()
    last = send(place_of(1 - here.far), place_of(1 - here.far), sems(), here.sibling)
    yield
    beside.wait_recv()
    last.wait_recv()
    for copy in (over, beside, last):
        copy.wait_send()


def gather_columns(here, chunks, target, local_sem, sems):
    x, z, y = here.own
    place = target.at[x, here.core, here.far, z, y]
    local = pltpu.make_async_copy(chunks.at[here.shard], place, local_sem)
    local.start()
    copies = [
        send(chunks.at[here.shard_of(bits)], place, sems(), here.device(bits))
        for bits in here.others()
    ]
    yield
    yield from spread(
        here, lambda far: target.at[:, here.core, far], sems, copies + [local]
    )


ANY = pl.BlockSpec(memory_space=pltpu.MemorySpace.HBM)
VMEM = pl.BlockSpec(memory_space=pltpu.MemorySpace.VMEM)
VMEM_BYTES = 56 * 2**20


def params(collective_id):
    return pltpu.CompilerParams(
        collective_id=collective_id, has_side_effects=True, vmem_limit_bytes=VMEM_BYTES
    )


def dma_sems(count):
    return [pltpu.SemaphoreType.DMA((count,)), pltpu.SemaphoreType.DMA((count,))]


def half_blocks(block):
    return pltpu.VMEM((block[0], block[1] // 2), BF16)


QUERY_TILE = 256
KEPT = 17
FRONT = "oxqgcxcqxxccgxodxxcococoqqx11111bbcbbbooaaaooaaPgPdgPdPd"
FRONT_ORDERS = dict(x=ORDERS, c=ORDERS_Z_FIRST, o=ORDERS, a=ORDERS)
NT = (((1,), (1,)), ((), ()))
TN = (((0,), (0,)), ((), ()))


def dot(left, right):
    return jnp.dot(left, right, preferred_element_type=F32)


def dot_nt(left, right):
    return lax.dot_general(left, right, NT, preferred_element_type=F32)


def dot_tn(left, right):
    return lax.dot_general(left, right, TN, preferred_element_type=F32)


def rotate(head, cosine, sine):
    return head * cosine + pltpu.roll(head, HALF_LANES, 1) * sine


def scores_of(keys, queries):
    count = keys.shape[0] - QUERY_TILE
    parts = []
    if count > 0:
        parts.append(dot_nt(keys[:count], queries) * HEAD_SIZE**-0.5)
    last = dot_nt(keys[count:], queries) * HEAD_SIZE**-0.5
    key = lax.broadcasted_iota(jnp.int32, last.shape, 0)
    query = lax.broadcasted_iota(jnp.int32, last.shape, 1)
    parts.append(jnp.where(key <= query, last, MASK_FILL))
    return parts


def attend_tile(q, k, v_t, o_t, ob, lse, group, tile):
    rows = pl.ds(tile * QUERY_TILE, QUERY_TILE)
    count = (tile + 1) * QUERY_TILE
    parts = scores_of(k[:count, :], q[group, rows, :])
    top = jnp.max(parts[-1], axis=0, keepdims=True)
    for part in parts[:-1]:
        top = jnp.maximum(top, jnp.max(part, axis=0, keepdims=True))
    total = jnp.zeros_like(top)
    result = None
    first = 0
    for part in parts:
        expo = jnp.exp(part - top)
        total = total + jnp.sum(expo, axis=0, keepdims=True)
        added = dot(v_t[:, first : first + part.shape[0]], expo.astype(BF16))
        result = added if result is None else result + added
        first += part.shape[0]
    result = result / total
    o_t[group, :, rows] = result
    ob[group * HEAD_SIZE : (group + 1) * HEAD_SIZE, rows] = result[:HEAD_SIZE].astype(BF16)
    lse[group, :, rows] = top + jnp.log(total)


def spaced(head):
    half = HEAD_SIZE // 2
    gap = jnp.zeros((head.shape[0], HALF_LANES - half), head.dtype)
    return jnp.concatenate([head[:, :half], gap, head[:, half:], gap], axis=1)


def packed(head):
    half = HEAD_SIZE // 2
    return jnp.concatenate([head[:, :half], head[:, HALF_LANES : HALF_LANES + half]], axis=1)


def as_column(row):
    size = row.shape[1]
    same = lax.broadcasted_iota(jnp.int32, (size, size), 0) == lax.broadcasted_iota(
        jnp.int32, (size, size), 1
    )
    return jnp.sum(jnp.where(same, row, 0.0), axis=1, keepdims=True)


def cut_projections(w_query, key_weight, value_weight, gain_attn, gain_ffn, chunks):
    query, key, value = (ref[...].astype(F32) for ref in (w_query, key_weight, value_weight))
    rows = query.shape[0]
    gains = [as_column(ref[...].astype(F32)) for ref in (gain_attn, gain_ffn)]
    gap = jnp.zeros((rows, HEAD_LANES - HEAD_SIZE - 2), F32)
    head = lambda weight, index: weight[:, index * HEAD_SIZE : (index + 1) * HEAD_SIZE]
    for shard in range(CUBE):
        parts = [
            spaced(head(query, 2 * shard)),
            spaced(head(query, 2 * shard + 1)),
            spaced(head(key, shard)),
            jnp.concatenate([head(value, shard), *gains, gap], axis=1),
        ]
        chunks[shard] = jnp.concatenate(parts, axis=1).astype(BF16)


def hidden_lanes(shard, part, lanes):
    x, zy = divmod(shard, 4)
    first = (x * 16 + part * 4 + zy) * lanes
    return slice(first, first + lanes)


def cut_hidden(w_gate, w_up, chunks):
    lanes = chunks.shape[2] // 8
    for shard in range(CUBE):
        for part in range(4):
            place = hidden_lanes(shard, part, lanes)
            chunks[shard, :, part * lanes : (part + 1) * lanes] = w_gate[:, place]
            chunks[shard, :, (4 + part) * lanes : (5 + part) * lanes] = w_up[:, place]


def front_kernel(
    tokens, cotangent, w_query, key_weight, value_weight, gain_attn, gain_ffn, w_gate, w_up, down, out,
    cosine, sine, *refs
):
    kept_here, refs = refs[:KEPT], refs[KEPT:]
    kept, refs = refs[:KEPT], refs[KEPT:]
    (
        w_qkv, w_o, q, k, v, o_t, lse, h1, ob_all, gains, x_own, ct_own,
        y1_own, out_part, dh2, w_d, w_gu,
    ) = kept
    (
        x_all, ct_all, v_t, hidden, d_gu, dh2_part, slots, x_relay, ct_relay, qkv, gate_up,
        local, keep_sems, sent, got,
    ) = refs
    here = Here()
    sems = Sems(sent, got)
    here.greet(here.same_core() + [here.sibling])
    keeps = []

    def keep(*some):
        for ref in some:
            index = [one is ref for one in kept].index(True)
            keeps.append(pltpu.make_async_copy(ref, kept_here[index], keep_sems.at[index]))
            keeps[-1].start()

    x, z, y = here.own
    width = tokens.shape[1]
    block_rows = tokens.shape[0]
    seq_rows = CUBE * block_rows

    def swapped(source, target, relay, local_sem, orders):
        yield from swap_home(
            here,
            source,
            target.at[here.shard],
            relay,
            local_sem,
            sems,
            target.at[here.shard_of(here.flip(0))],
        )
        yield from gather_cube_parts(
            here, lambda bits, part: target.at[here.shard_of(bits), :, part], width, orders, sems
        )

    def out_gather():
        mine = w_o.at[x, here.core, here.far, z, y]
        kept = pltpu.make_async_copy(out, mine, local.at[3])
        kept.start()
        over = send(out, mine, sems(), here.across)
        yield
        kept.wait()
        over.wait()
        yield from gather_cube_parts(
            here,
            lambda bits, part: w_o.at[bits[0], here.core, :, bits[1], bits[2], :, part],
            width,
            FRONT_ORDERS["o"],
            sems,
        )
        beside = send(w_o.at[:, here.core], w_o.at[:, here.core], sems(), here.sibling)
        yield
        beside.wait()

    def down_gather():
        kept = pltpu.make_async_copy(down, w_d.at[here.core, here.far], local.at[2])
        kept.start()
        yield from spread(here, lambda far: w_d.at[here.core, far], sems, [kept])

    def qkv_gather():
        cut_projections(w_query, key_weight, value_weight, gain_attn, gain_ffn, qkv)
        yield from gather_columns(here, qkv, w_qkv, local.at[4], sems)

    def gate_up_gather():
        cut_hidden(w_gate, w_up, gate_up)
        yield from gather_columns(here, gate_up, w_gu, local.at[5], sems)

    transfers = dict(
        x=swapped(tokens, x_all, x_relay, local.at[0], FRONT_ORDERS["x"]),
        q=qkv_gather(),
        g=gate_up_gather(),
        o=out_gather(),
        d=down_gather(),
        c=swapped(cotangent, ct_all, ct_relay, local.at[1], FRONT_ORDERS["c"]),
    )
    ob = ob_all.at[here.shard]
    turns = [[here.shard_of(here.flip(*bits)) for bits in turned] for turned in PAIRS]

    def norm():
        turned = jnp.transpose(
            w_qkv[:, :, :, :, :, :, 3 * HEAD_LANES :].astype(F32).reshape(width, HEAD_LANES)
        )
        gains[...] = turned[HEAD_SIZE : HEAD_SIZE + 8]
        x_own[...] = x_all[here.shard]

        def norm_block(index, carry):
            rows = x_all[index].astype(F32)
            inv_root = lax.rsqrt(jnp.mean(rows * rows, axis=-1, keepdims=True) + NORM_EPS)
            place = pl.ds(pl.multiple_of(index * block_rows, block_rows), block_rows)
            h1[place, :] = (rows * inv_root * gains[0:1, :]).astype(BF16)
            return carry

        lax.fori_loop(0, CUBE, norm_block, 0)

    def project():
        def project_tile(index, carry):
            rows = pl.ds(pl.multiple_of(index * QUERY_TILE, QUERY_TILE), QUERY_TILE)
            raw = dot(h1[rows, :], w_qkv[...].reshape(width, SHARE))
            cos_rows, sin_rows = cosine[rows, :], sine[rows, :]
            heads = [raw[:, lane : lane + HEAD_LANES] for lane in range(0, SHARE, HEAD_LANES)]
            q[0, rows, :] = rotate(heads[0], cos_rows, sin_rows).astype(BF16)
            q[1, rows, :] = rotate(heads[1], cos_rows, sin_rows).astype(BF16)
            k[rows, :] = rotate(heads[2], cos_rows, sin_rows).astype(BF16)
            v[rows, :] = heads[3].astype(BF16)
            v_t[:, rows] = jnp.transpose(heads[3]).astype(BF16)
            return carry

        lax.fori_loop(0, seq_rows // QUERY_TILE, project_tile, 0)
        keep(w_qkv, h1, q, k, v, gains, x_own)

    def attend(*tiles):
        for tile in tiles:
            for group in range(2):
                attend_tile(q, k, v_t, o_t, ob, lse, group, tile)
        if tiles[-1] % 2 == 1:
            lanes = pl.ds((tiles[-1] - 1) * QUERY_TILE, 2 * QUERY_TILE)
            transfers["ab"[tiles[-1] // 2]] = gather_cube_parts(
                here,
                lambda bits, part: ob_all.at[here.shard_of(bits), part, lanes],
                ob.shape[0],
                FRONT_ORDERS["a"],
                sems,
            )

    def normed_pair(pair):
        own = PAIRS[pair][-1] == ()
        if pair == 0:
            keep(o_t, lse, ob_all, w_o)
        norm_after_attention(turns[pair], x_all, ob_all, w_o, gains, y1_own if own else None)
        if own:
            keep(y1_own)

    bind = functools.partial
    play(
        FRONT,
        transfers,
        {
            "1": [norm, project, bind(attend, 0), bind(attend, 1), bind(attend, 2, 3)],
            "P": [bind(normed_pair, pair) for pair in range(len(PAIRS))],
        },
    )
    ct_own[...] = ct_all[here.shard]
    keep(ct_own)
    streams = reductions(here, dh2_part, slots, dh2, ORDERS, sems)
    for pair, shards in enumerate(turns):
        feed_forward(shards, x_all, ct_all, w_gu, w_d, hidden, d_gu, out_part, dh2_part)
        for stream in streams:
            stream.after(pair)
    keep(out_part)
    finish = in_step([stream.finish() for stream in streams])
    next(finish, None)

    def gate_up_grad(index, carry):
        lanes = pl.ds(pl.multiple_of(index * 4 * HEAD_SIZE, 4 * HEAD_SIZE), 4 * HEAD_SIZE)
        left = x_all[:, :, lanes].reshape(seq_rows, 4 * HEAD_SIZE)
        grad = dot_tn(left, d_gu[...]).astype(BF16)
        w_gu[index // 2, lax.rem(index, 2)] = grad.reshape(w_gu.shape[2:])
        return carry

    def down_grad(index, carry):
        lanes = pl.ds(pl.multiple_of(index * HEAD_LANES, HEAD_LANES), HEAD_LANES)
        grad = dot_tn(hidden[:, lanes], ct_all[...].reshape(seq_rows, width)).astype(BF16)
        w_d[index // 2, lax.rem(index, 2)] = grad
        return carry

    lax.fori_loop(0, 4, down_grad, 0)
    keep(w_d)
    next(finish, None)
    lax.fori_loop(0, 4, gate_up_grad, 0)
    keep(w_gu)
    for _ in finish:
        pass
    keep(dh2)
    for copy in keeps:
        copy.wait()


def norm_after_attention(shards, x_all, ob_all, w_o, gains, y1_own):
    _, block_rows, width = x_all.shape
    rows_of = [
        pl.ds(pl.multiple_of(shard * block_rows, block_rows), block_rows) for shard in shards
    ]
    ob_t = jnp.concatenate([ob_all[:, :, rows].reshape(width, block_rows) for rows in rows_of], axis=1)
    x = jnp.concatenate([x_all[shard] for shard in shards], axis=0)
    y1 = x.astype(F32) + dot_tn(ob_t, w_o[...].reshape(width, width))
    inv_root = lax.rsqrt(jnp.mean(y1 * y1, axis=-1, keepdims=True) + NORM_EPS)
    h2 = (y1 * inv_root * gains[1:2, :]).astype(BF16)
    if y1_own is not None:
        y1_own[...] = y1[block_rows:]
    for index, shard in enumerate(shards):
        x_all[shard] = h2[index * block_rows : (index + 1) * block_rows]


def feed_forward(shards, h2_all, ct_all, w_gu, w_d, hidden, d_gu, out_part, dh2_part):
    _, block_rows, width = h2_all.shape
    share = d_gu.shape[1] // 2
    pair = lambda ref: jnp.concatenate([ref[shard] for shard in shards], axis=0)
    rows_of = [
        pl.ds(pl.multiple_of(shard * block_rows, block_rows), block_rows) for shard in shards
    ]
    h2 = pair(h2_all)
    gate_up = dot(h2, w_gu[...].reshape(width, 2 * share))
    gate, up = gate_up[:, :share], gate_up[:, share:]
    sig = 1.0 / (1.0 + jnp.exp(-gate))
    silu = gate * sig
    kept = (silu * up).astype(BF16)
    down = w_d[...].reshape(share, width)
    d_hidden = dot_nt(pair(ct_all), down)
    d_gate = (d_hidden * up * sig * (1.0 + gate * (1.0 - sig))).astype(BF16)
    d_up = (d_hidden * silu).astype(BF16)
    d_both = jnp.concatenate([d_gate, d_up], axis=1)
    dh2 = dot_nt(d_both, w_gu[...].reshape(width, 2 * share)).astype(BF16)
    out = dot(kept, down).astype(BF16)
    for index, (shard, rows) in enumerate(zip(shards, rows_of)):
        block = slice(index * block_rows, (index + 1) * block_rows)
        hidden[rows, :] = kept[block]
        d_gu[rows, :] = d_both[block]
        dh2_part[shard] = dh2[block]
        out_part[shard] = out[block]


def front(tokens, cotangent, w_query, key_weight, value_weight, gain_attn, gain_ffn, w_gate, w_up,
          down, out, cosine, sine):
    slots = (2, 2, 2, 2, 2)
    rows, width = tokens.shape
    weight_rows = out.shape[0]
    seq_rows = CUBE * rows
    share = 2 * HEAD_SIZE
    ff_share = 4 * down.shape[0]
    low = lambda *dims: (dims, BF16)
    wide = lambda *dims: (dims, F32)
    kept = (
        low(*slots, weight_rows, SHARE),
        low(*slots, weight_rows, width),
        low(2, seq_rows, HEAD_LANES),
        low(seq_rows, HEAD_LANES),
        low(seq_rows, HEAD_LANES),
        wide(2, HEAD_LANES, seq_rows),
        wide(2, 1, seq_rows),
        low(seq_rows, width),
        low(CUBE, share, seq_rows),
        wide(8, width),
        low(rows, width),
        low(rows, width),
        wide(rows, width),
        low(CUBE, rows, width),
        wide(rows, width),
        low(2, 2, *down.shape),
        low(*slots, weight_rows, 2 * ff_share),
    )
    return pl.pallas_call(
        front_kernel,
        out_shape=tuple(jax.ShapeDtypeStruct(*one) for one in kept),
        in_specs=[VMEM] * 13,
        out_specs=(ANY,) * KEPT,
        scratch_shapes=[pltpu.VMEM(*one) for one in kept]
        + [
            pltpu.VMEM((CUBE, rows, width), BF16),
            pltpu.VMEM((CUBE, rows, width), BF16),
            pltpu.VMEM((HEAD_LANES, seq_rows), BF16),
            pltpu.VMEM((seq_rows, ff_share), BF16),
            pltpu.VMEM((seq_rows, 2 * ff_share), BF16),
            pltpu.VMEM((CUBE, rows, width), BF16),
            pltpu.VMEM((CUBE - 1, rows, width), BF16),
            half_blocks(tokens.shape),
            half_blocks(tokens.shape),
            pltpu.VMEM((CUBE, weight_rows, SHARE), BF16),
            pltpu.VMEM((CUBE, weight_rows, 2 * ff_share), BF16),
            pltpu.SemaphoreType.DMA((6,)),
            pltpu.SemaphoreType.DMA((KEPT,)),
        ]
        + dma_sems(240),
        compiler_params=params(1),
        name="front",
    )(tokens, cotangent, w_query, key_weight, value_weight, gain_attn, gain_ffn, w_gate, w_up, down,
      out, cosine, sine)


def attend_back_tile(q, k, k_t, v, do_t, o_t, lse, dk, dv, group, tile):
    rows = pl.ds(tile * QUERY_TILE, QUERY_TILE)
    count = (tile + 1) * QUERY_TILE
    q_rows = q[group, rows, :]
    do_rows = do_t[group * HEAD_SIZE : (group + 1) * HEAD_SIZE, rows]
    do_rows = jnp.concatenate(
        [do_rows, jnp.zeros((HEAD_LANES - HEAD_SIZE, QUERY_TILE), BF16)], axis=0
    )
    delta = jnp.sum(do_rows.astype(F32) * o_t[group, :, rows], axis=0, keepdims=True)
    log_total = lse[group, :, rows]
    dq_t = None
    first = 0
    for part in scores_of(k[:count, :], q_rows):
        keys = slice(first, first + part.shape[0])
        probs = jnp.exp(part - log_total)
        d_probs = dot(v[keys, :], do_rows)
        d_scores = (probs * (d_probs - delta)).astype(BF16)
        dv[keys, :] += dot_nt(probs.astype(BF16), do_rows)
        dk[keys, :] += dot(d_scores, q_rows)
        added = dot(k_t[:, keys], d_scores)
        dq_t = added if dq_t is None else dq_t + added
        first += part.shape[0]
    return jnp.transpose(dq_t) * HEAD_SIZE**-0.5


def add_rows(total, more, piece):
    def body(index, carry):
        rows = pl.ds(pl.multiple_of(index * piece, piece), piece)
        for block in range(total.shape[0]):
            total[block, rows, :] = total_of(
                total.at[block, rows, :], more.at[block, rows, :]
            ).astype(BF16)
        return carry

    lax.fori_loop(0, total.shape[1] // piece, body, 0)


def reduce_copies(here, part, beside, over, sems, piece):
    core, far = here.core, here.far
    first = send(part.at[:, 1 - core, 1 - far], beside.at[0], sems(), here.sibling)
    second = send(part.at[:, 1 - core, far], beside.at[1], sems(), here.sibling)
    yield
    first.wait_recv()
    add_rows(part.at[:, core, 1 - far], beside.at[0], piece)
    third = send(part.at[:, core, 1 - far], over, sems(), here.across)
    second.wait_recv()
    add_rows(part.at[:, core, far], beside.at[1], piece)
    yield
    third.wait_recv()
    add_rows(part.at[:, core, far], over, piece)
    for copy in (first, second, third):
        copy.wait_send()


def scatter_columns(here, part, beside, over, out, local_sem, sems):
    rows = out.shape[1]
    yield from reduce_copies(here, part, beside, over, sems, rows)

    def source(bits):
        place = pl.ds((bits[1] * 2 + bits[2]) * rows, rows)
        return part.at[bits[0], here.core, here.far, place, :]

    local = pltpu.make_async_copy(source(here.own), out.at[here.shard], local_sem)
    local.start()
    copies = [
        send(source(bits), out.at[here.shard], sems(), here.device(bits)) for bits in here.others()
    ]
    yield
    for copy in copies + [local]:
        copy.wait()


def copy_slots(part):
    blocks, _, _, rows, share = part.shape
    return [pltpu.VMEM((2, blocks, rows, share), BF16), pltpu.VMEM((blocks, rows, share), BF16)]


def by_owner(part):
    rows, share = part.shape[3:]
    return jax.ShapeDtypeStruct((CUBE, rows // 4, share), BF16)


def norm_back_rows(grad_normed, rows, gain):
    inv_root = lax.rsqrt(jnp.mean(rows * rows, axis=-1, keepdims=True) + NORM_EPS)
    grad_gain, grad_rows = norm_back(grad_normed, rows, inv_root, gain)
    return grad_gain.reshape(1, -1), grad_rows


def sum_everywhere(here, total, slots, sems):
    hops = [here.sibling] + [here.next(bit) for bit in BITS] + [here.across]
    for index, device in enumerate(hops):
        copy = send(total, slots.at[index], sems(), device)
        yield
        copy.wait()
        total[...] += slots[index]


def back_kernel(*refs):
    kept_here, refs = refs[:KEPT], refs[KEPT:]
    (
        cosine, sine, output_home, grad_home, gu_rows, down_sum, qkv_rows, out_rows, gain_out,
    ), refs = refs[:9], refs[9:]
    kept, refs = refs[:KEPT], refs[KEPT:]
    (
        w_qkv, w_o, q, k, v, o_t, lse, h1, ob_all, gains, x_own, ct_own,
        y1_own, out_part, dh2, down_part, gu_part,
    ) = kept
    (
        gain_sums, d_middle, pairs, columns, d_qkv, k_t, dk, dv, dh1_part,
        dh1, dh1_slots, out_sum, out_slots, gu_beside, gu_over, down_beside, down_over, qkv_part,
        qkv_beside, qkv_over, wo_part, wo_beside, wo_over, own_rows, relay, relay_too, gain_slots,
        local, load_sems, sent, got,
    ) = refs
    loads = []
    for index in range(KEPT):
        loads.append(pltpu.make_async_copy(kept_here[index], kept[index], load_sems.at[index]))
    for index in (16, 15, 14, 12, 11, 9, 1, 3, 2, 4, 5, 6, 13, 0, 7, 8, 10):
        loads[index].start()

    def need(*some):
        for ref in some:
            index = [one is ref for one in kept].index(True)
            if loads[index] is not None:
                loads[index].wait()
                loads[index] = None

    here = Here()
    sems = Sems(sent, got)
    here.greet(here.same_core() + [here.sibling])
    block_rows, width = dh2.shape
    weight_rows = gu_rows.shape[1]
    seq_rows = CUBE * block_rows
    share = 2 * HEAD_SIZE

    def half_gu(index):
        need(gu_part)
        lanes = pl.ds(index * gu_part.shape[4] // 2, gu_part.shape[4] // 2)
        yield from scatter_columns(
            here,
            gu_part.at[:, :, :, :, lanes],
            gu_beside.at[:, :, :, lanes],
            gu_over.at[:, :, lanes],
            gu_rows.at[:, :, lanes],
            local.at[index],
            sems,
        )

    def down_reduce():
        need(down_part)
        yield from reduce_copies(here, down_part, down_beside, down_over, sems, 32)
        down_sum[...] = down_part[0, here.core, here.far]

    def to_heads():
        rows = pl.ds(pl.multiple_of(here.shard * block_rows, block_rows), block_rows)
        place = columns.at[:, :, rows]
        mine = pltpu.make_async_copy(pairs.at[here.shard], place, local.at[2])
        mine.start()
        copies = [
            send(pairs.at[here.shard_of(bits)], place, sems(), here.device(bits))
            for bits in here.others()
        ]
        yield
        for copy in copies + [mine]:
            copy.wait()

    def reduce_rows(part, slots, out, orders):
        streams = reductions(here, part, slots, out, orders, sems)
        for pair in range(len(PAIRS)):
            for stream in streams:
                stream.after(pair)
            yield
        yield from in_step([stream.finish() for stream in streams])

    def output_reduce():
        need(out_part)
        yield from reduce_rows(out_part, out_slots, out_sum, BACK_ORDERS["r"])

    def output_swap():
        own_rows[0] = (y1_own[...] + out_sum[...]).astype(BF16)
        yield from swap_home(here, own_rows.at[0], output_home, relay, local.at[4], sems)

    transfers = dict(
        f=half_gu(0),
        g=half_gu(1),
        d=down_reduce(),
        p=to_heads(),
        r=output_reduce(),
        s=reduce_rows(dh1_part, dh1_slots, dh1, BACK_ORDERS["s"]),
        q=scatter_columns(here, qkv_part, qkv_beside, qkv_over, qkv_rows, local.at[3], sems),
        w=scatter_columns(here, wo_part, wo_beside, wo_over, out_rows, local.at[5], sems),
        u=output_swap(),
        v=swap_home(here, own_rows.at[1], grad_home, relay_too, local.at[6], sems),
        n=sum_everywhere(here, gain_sums, gain_slots, sems),
    )

    def norm_two():
        need(dh2, y1_own, ct_own, gains, w_o)
        grad_gain, grad_rows = norm_back_rows(dh2[...], y1_own[...], gains[1:2, :])
        gain_sums[...] = jnp.zeros_like(gain_sums)
        gain_sums[1:2, :] = grad_gain
        d_middle[...] = ct_own[...].astype(F32) + grad_rows
        da = d_middle[...].astype(BF16)
        pairs[:, 0] = dot_nt(w_o[...], da).astype(BF16).reshape(CUBE, share, block_rows)
        pairs[:, 1] = jnp.transpose(d_middle[...]).astype(BF16).reshape(CUBE, share, block_rows)

    def norm_one():
        need(x_own)
        grad_gain, grad_rows = norm_back_rows(dh1[...], x_own[...].astype(F32), gains[0:1, :])
        gain_sums[0:1, :] = grad_gain
        own_rows[1] = (d_middle[...] + grad_rows).astype(BF16)

    def attention(tile):
        if tile == 0:
            need(q, k, v, o_t, lse)
            k_t[...] = jnp.transpose(k[...].astype(F32)).astype(BF16)
            dk[...] = jnp.zeros_like(dk)
            dv[...] = jnp.zeros_like(dv)
        rows = pl.ds(tile * QUERY_TILE, QUERY_TILE)
        for group in range(2):
            dq = attend_back_tile(q, k, k_t, v, columns.at[0], o_t, lse, dk, dv, group, tile)
            d_qkv[rows, group * HEAD_LANES : (group + 1) * HEAD_LANES] = rotate(
                dq, cosine[rows, :], -sine[rows, :]
            ).astype(BF16)
        if rows.start + rows.size == seq_rows:
            d_qkv[:, 2 * HEAD_LANES : 3 * HEAD_LANES] = rotate(
                dk[...] * HEAD_SIZE**-0.5, cosine[...], -sine[...]
            ).astype(BF16)
            d_qkv[:, 3 * HEAD_LANES :] = dv[...].astype(BF16)

    def pair_back(pair):
        need(w_qkv)
        shards = [here.shard_of(here.flip(*bits)) for bits in PAIRS[pair]]
        some = jnp.concatenate(
            [
                d_qkv[pl.ds(pl.multiple_of(shard * block_rows, block_rows), block_rows), :]
                for shard in shards
            ],
            axis=0,
        )
        rows = dot_nt(some, w_qkv[...]).astype(BF16)
        for index, shard in enumerate(shards):
            dh1_part[shard] = rows[index * block_rows : (index + 1) * block_rows]

    def qkv_grad():
        need(h1)

        def quarter(index, carry):
            lanes = pl.ds(pl.multiple_of(index * 4 * HEAD_SIZE, 4 * HEAD_SIZE), 4 * HEAD_SIZE)
            grad = dot_tn(h1[:, lanes], d_qkv[...]).astype(BF16)
            qkv_part[index // 2, lax.rem(index, 2)] = grad.reshape(qkv_part.shape[2:])
            return carry

        lax.fori_loop(0, 4, quarter, 0)

    def out_grad():
        need(ob_all)
        for index in range(4):
            left = ob_all[2 * index : 2 * index + 2].reshape(2 * share, seq_rows)
            grad = dot_nt(left, columns[1]).astype(BF16)
            grad = jnp.concatenate(
                [grad, jnp.zeros((2 * share, wo_part.shape[4] - share), BF16)], axis=1
            )
            wo_part[index // 2, index % 2] = grad.reshape(wo_part.shape[2:])

    bind = functools.partial
    play(
        BACK[0] + BACK[1],
        transfers,
        {
            "1": [norm_two, norm_one],
            "2": [bind(attention, tile) for tile in range(seq_rows // QUERY_TILE)],
            "3": [bind(pair_back, pair) for pair in range(len(PAIRS))],
            "4": [qkv_grad, out_grad],
        },
    )
    rank = here.device(here.own)
    rank = rank[0] * CUBE + rank[1]
    mine = pltpu.roll(gain_sums[...], lax.rem(width - rank * weight_rows, width), 1)
    gain_out[...] = mine[:, :HEAD_LANES]


BACK = ("fgd1pfgdpr2r2r2r23s3s3s3s", "rrr4q4wqwussssu1vnnvnnnvfgdfgdqwqwuuv")
ORDERS_ALL = ORDERS + ((0, 2, 1), (1, 0, 2), (2, 1, 0))
BACK_ORDERS = dict(r=ORDERS_ALL, s=ORDERS_ALL)


def back(kept, cosine, sine, weight_rows):
    dh2, out_part, down_part, gu_part = (kept[index] for index in (14, 13, 15, 16))
    rows, width = dh2.shape
    seq_rows = CUBE * rows
    share = 2 * HEAD_SIZE
    part = lambda lanes: jax.ShapeDtypeStruct((*gu_part.shape[:4], lanes), BF16)
    qkv_part, wo_part = part(SHARE), part(2 * HEAD_LANES)
    low = lambda *dims: pltpu.VMEM(dims, BF16)
    wide = lambda *dims: pltpu.VMEM(dims, F32)
    like = lambda one: pltpu.VMEM(one.shape, one.dtype)
    out = lambda *dims: jax.ShapeDtypeStruct(dims, BF16)
    outs = (
        out(rows, width),
        out(rows, width),
        out(CUBE, weight_rows, gu_part.shape[4]),
        out(*down_part.shape[3:]),
        out(CUBE, weight_rows, SHARE),
        out(CUBE, weight_rows, 2 * HEAD_LANES),
        jax.ShapeDtypeStruct((8, HEAD_LANES), F32),
    )
    return pl.pallas_call(
        back_kernel,
        out_shape=outs,
        in_specs=[ANY] * KEPT + [VMEM] * 2,
        out_specs=(VMEM,) * len(outs),
        scratch_shapes=[like(one) for one in kept]
        + [
            wide(8, width),
            wide(rows, width),
            low(CUBE, 2, share, rows),
            low(2, share, seq_rows),
            low(seq_rows, SHARE),
            low(HEAD_LANES, seq_rows),
            wide(seq_rows, HEAD_LANES),
            wide(seq_rows, HEAD_LANES),
            like(out_part),
            wide(rows, width),
            low(CUBE - 1, rows, width),
            wide(rows, width),
            low(CUBE - 1, rows, width),
            *copy_slots(gu_part),
            *copy_slots(down_part),
            like(qkv_part),
            *copy_slots(qkv_part),
            like(wo_part),
            *copy_slots(wo_part),
            low(2, rows, width),
            half_blocks((rows, width)),
            half_blocks((rows, width)),
            wide(5, 8, width),
            pltpu.SemaphoreType.DMA((7,)),
            pltpu.SemaphoreType.DMA((KEPT,)),
        ]
        + dma_sems(180),
        compiler_params=params(2),
        name="back",
    )(*kept, cosine, sine)


def finish_kernel(
    output_home, grad_home, gu_rows, down_sum, qkv_rows, out_rows, gains,
    output, grad, gate, up, down, query, key, value, out, gain_one, gain_two,
):
    output[...] = output_home[...]
    grad[...] = grad_home[...].astype(F32)
    down[...] = down_sum[...].astype(F32)
    lanes = gu_rows.shape[2] // 8
    for shard in range(CUBE):
        for part in range(4):
            place = hidden_lanes(shard, part, lanes)
            gate[:, place] = gu_rows[shard, :, part * lanes : (part + 1) * lanes].astype(F32)
            up[:, place] = gu_rows[shard, :, (4 + part) * lanes : (5 + part) * lanes].astype(F32)
    heads = [
        [
            qkv_rows[shard, :, index * HEAD_LANES : (index + 1) * HEAD_LANES].astype(F32)
            for index in range(4)
        ]
        for shard in range(CUBE)
    ]
    query[...] = jnp.concatenate([packed(head) for some in heads for head in some[:2]], axis=1)
    key[...] = jnp.concatenate([packed(some[2]) for some in heads], axis=1)
    value[...] = jnp.concatenate([some[3][:, :HEAD_SIZE] for some in heads], axis=1)
    out[...] = jnp.concatenate(
        [out_rows[shard, :, : 2 * HEAD_SIZE].astype(F32) for shard in range(CUBE)], axis=1
    )
    gain_one[...] = gains[0, : gain_one.shape[0]]
    gain_two[...] = gains[1, : gain_two.shape[0]]


def finish(parts, ff_width):
    rows, width = parts[0].shape
    weight_rows = parts[2].shape[1]
    out = lambda *dims: jax.ShapeDtypeStruct(dims, F32)
    outs = (
        jax.ShapeDtypeStruct((rows, width), BF16),
        out(rows, width),
        out(weight_rows, ff_width),
        out(weight_rows, ff_width),
        out(*parts[3].shape),
        out(weight_rows, width),
        out(weight_rows, width // 2),
        out(weight_rows, width // 2),
        out(weight_rows, width),
        out(weight_rows),
        out(weight_rows),
    )
    return pl.pallas_call(
        finish_kernel,
        out_shape=outs,
        in_specs=[VMEM] * len(parts),
        out_specs=(VMEM,) * len(outs),
        compiler_params=pltpu.CompilerParams(vmem_limit_bytes=VMEM_BYTES),
        name="finish",
    )(*parts)


def spaced_tables(row_count):
    half = HEAD_SIZE // 2
    frequency = np.float32(ROPE_THETA) ** (-np.arange(half, dtype=np.float32) * 2.0 / HEAD_SIZE)
    angles = np.arange(row_count, dtype=np.float32)[:, None] * frequency.astype(np.float32)[None, :]
    pad = ((0, 0), (0, HALF_LANES - half))
    cosine, sine = np.pad(np.cos(angles), pad), np.pad(np.sin(angles), pad)
    return (
        jnp.asarray(np.concatenate([cosine, cosine], axis=1), F32),
        jnp.asarray(np.concatenate([-sine, sine], axis=1), F32),
    )


def split_layer(
    tokens,
    cotangent,
    gain_attn,
    w_query,
    key_weight,
    value_weight,
    w_out,
    gain_ffn,
    w_gate,
    w_up,
    w_down,
):
    block_rows, width = tokens.shape
    weight_rows = w_query.shape[0]
    cosine, sine = spaced_tables(block_rows * CUBE)
    kept = list(
        front(
            tokens, cotangent, w_query, key_weight, value_weight, gain_attn[None], gain_ffn[None],
            w_gate, w_up, w_down, w_out, cosine, sine,
        )
    )
    kept[0] = kept[0].reshape(width, SHARE)
    kept[1] = kept[1].reshape(width, width)
    kept[15] = kept[15].reshape(1, 2, 2, *w_down.shape)
    kept[16] = kept[16].reshape(2, 2, 2, 4 * weight_rows, -1)
    parts = back(kept, cosine, sine, weight_rows)
    output, grad, gate, up, down, query, key, value, out, gain_one, gain_two = finish(
        parts, w_gate.shape[1]
    )
    return (output, grad, gain_one, query, key, value, out, gain_two, gate, up, down)


def solution(mesh):
    heads_split = mesh.shape["dp"] == 4 and mesh.shape["ctx"] == KEY_VALUE_HEADS
    return jax.shard_map(
        split_layer if heads_split else blockwise_layer,
        mesh=mesh,
        in_specs=(
            P(("dp", "ctx"), None),
            P(("dp", "ctx"), None),
            P(("dp", "ctx")),
            P(("dp", "ctx"), None),
            P(("dp", "ctx"), None),
            P(("dp", "ctx"), None),
            P(("dp", "ctx"), None),
            P(("dp", "ctx")),
            P(("dp", "ctx"), None),
            P(("dp", "ctx"), None),
            P(("dp", "ctx"), None),
        ),
        out_specs=(
            P(("dp", "ctx"), None),
            P(("dp", "ctx"), None),
            P(("dp", "ctx")),
            P(("dp", "ctx"), None),
            P(("dp", "ctx"), None),
            P(("dp", "ctx"), None),
            P(("dp", "ctx"), None),
            P(("dp", "ctx")),
            P(("dp", "ctx"), None),
            P(("dp", "ctx"), None),
            P(("dp", "ctx"), None),
        ),
        check_vma=False,
    )
```

```python
import functools

import jax
import jax.numpy as jnp
import numpy as np
from jax import lax
from jax.experimental import pallas as pl
from jax.experimental.pallas import tpu as pltpu
from jax.sharding import PartitionSpec as P

QUERY_HEADS = 16
KEY_VALUE_HEADS = 8
HEAD_SIZE = 96


NORM_EPS = 1e-05
ROPE_THETA = 100000.0
MASK_FILL = -1e30


def passed_along(value, axis, by):
    peers = lax.axis_size(axis)
    pairs = [(i, i + by) for i in range(peers) if 0 <= i + by < peers]
    return lax.ppermute(value, axis, pairs)


def shifted(block, axis, distance):
    devices = range(lax.axis_size(axis))
    route = [((i - distance) % len(devices), i) for i in devices]
    return lax.ppermute(block, axis, route)


def rope_tables(first_row, block_count):
    half_dim = HEAD_SIZE // 2
    positions = (first_row + jnp.arange(block_count, dtype=jnp.int32)).astype(jnp.float32)
    frequency = ROPE_THETA ** (-jnp.arange(half_dim, dtype=jnp.float32) * 2.0 / HEAD_SIZE)
    angles = positions[:, None] * frequency[None, :]
    return (jnp.cos(angles)[:, None, :], jnp.sin(angles)[:, None, :])


def apply_rotary(value_rows, cosine_table, sine_values, direction):
    half_dim = HEAD_SIZE // 2
    first_half = value_rows[..., :half_dim]
    second_half = value_rows[..., half_dim:]
    return jnp.concatenate(
        [
            first_half * cosine_table - direction * second_half * sine_values,
            second_half * cosine_table + direction * first_half * sine_values,
        ],
        axis=-1,
    )


def norm_back(grad_normed, inputs, inv_root, gain):
    grad_gain = jnp.sum(grad_normed * inputs * inv_root, axis=0)
    scaled = grad_normed * gain.astype(jnp.float32)
    grad_inputs = inv_root * (
        scaled - inputs * inv_root * inv_root * jnp.mean(scaled * inputs, axis=-1, keepdims=True)
    )
    return (grad_gain, grad_inputs)


def row_product(left, right):
    return jnp.einsum("tc,tf->cf", left, right, preferred_element_type=jnp.float32)


def blockwise_layer(
    tokens,
    cotangent,
    gain_attn,
    w_query,
    key_weight,
    value_weight,
    w_out,
    gain_ffn,
    w_gate,
    w_up,
    w_down,
):
    token_rows = tokens.shape[0]
    head_group = QUERY_HEADS // KEY_VALUE_HEADS
    key_value_width = KEY_VALUE_HEADS * HEAD_SIZE
    query_width = QUERY_HEADS * HEAD_SIZE
    score_scale = HEAD_SIZE ** (-0.5)
    ctx_count = lax.axis_size("ctx")
    ctx_rank = lax.axis_index("ctx")
    first_row = ctx_rank * token_rows
    query_pos = first_row + jnp.arange(token_rows, dtype=jnp.int32)
    attn_full = (
        lax.all_gather(gain_attn, ("dp", "ctx"), axis=0, tiled=True),
        lax.all_gather(w_query, ("dp", "ctx"), axis=0, tiled=True),
        lax.all_gather(key_weight, ("dp", "ctx"), axis=0, tiled=True),
        lax.all_gather(value_weight, ("dp", "ctx"), axis=0, tiled=True),
        lax.all_gather(w_out, ("dp", "ctx"), axis=0, tiled=True),
    )
    gain_one, query_full, key_full, value_full, out_full = attn_full
    inputs = tokens.astype(jnp.float32)
    inv_one = lax.rsqrt(jnp.mean(inputs * inputs, axis=-1, keepdims=True) + NORM_EPS)
    first_normed = (inputs * inv_one * gain_one.astype(jnp.float32)).astype(jnp.bfloat16)
    query_unrotated = jnp.dot(first_normed, query_full, preferred_element_type=jnp.float32).reshape(
        token_rows, QUERY_HEADS, HEAD_SIZE
    )
    key_unrotated = jnp.dot(first_normed, key_full, preferred_element_type=jnp.float32).reshape(
        token_rows, KEY_VALUE_HEADS, HEAD_SIZE
    )
    value_raw = jnp.dot(first_normed, value_full, preferred_element_type=jnp.float32)
    cosine_table, sine_values = rope_tables(first_row, token_rows)
    query_rows = (
        apply_rotary(query_unrotated, cosine_table, sine_values, 1.0)
        .astype(jnp.bfloat16)
        .reshape(token_rows, KEY_VALUE_HEADS, head_group, HEAD_SIZE)
    )
    keys_rot = (
        apply_rotary(key_unrotated, cosine_table, sine_values, 1.0)
        .astype(jnp.bfloat16)
        .reshape(token_rows, key_value_width)
    )
    kv_local = jnp.concatenate([keys_rot, value_raw.astype(jnp.bfloat16)], axis=1)
    starting = (
        jnp.full((KEY_VALUE_HEADS, head_group, token_rows), MASK_FILL, jnp.float32),
        jnp.zeros((KEY_VALUE_HEADS, head_group, token_rows), jnp.float32),
        jnp.zeros((token_rows, KEY_VALUE_HEADS, head_group, HEAD_SIZE), jnp.float32),
    )
    sequence_portion = lax.all_gather(kv_local, "ctx", axis=0, tiled=True)

    def update(state):
        run_max, run_sum, run_acc = state
        block_count = sequence_portion.shape[0]
        key_portion = sequence_portion[:, :key_value_width].reshape(
            block_count, KEY_VALUE_HEADS, HEAD_SIZE
        )
        value_portion = sequence_portion[:, key_value_width:].reshape(
            block_count, KEY_VALUE_HEADS, HEAD_SIZE
        )
        scores = (
            jnp.einsum(
                "tkgd,skd->kgts", query_rows, key_portion, preferred_element_type=jnp.float32
            )
            * score_scale
        )
        key_pos = jnp.arange(block_count, dtype=jnp.int32)
        allowed = key_pos[None, :] <= query_pos[:, None]
        scores = jnp.where(allowed, scores, MASK_FILL)
        new_max = jnp.maximum(run_max, jnp.max(scores, axis=-1))
        expo = jnp.exp(scores - new_max[..., None])
        new_sum = jnp.sum(expo, axis=-1)
        added = jnp.einsum(
            "kgts,skd->tkgd",
            expo.astype(jnp.bfloat16),
            value_portion,
            preferred_element_type=jnp.float32,
        )
        return (new_max, new_sum, added)

    def unchanged(state):
        return state

    run_max, run_sum, run_acc = lax.cond(
        jnp.int32(0) <= first_row + token_rows - 1, update, unchanged, starting
    )
    attn_four = run_acc / jnp.transpose(run_sum, (2, 0, 1))[..., None]
    log_total = run_max + jnp.log(run_sum)
    attn_out = attn_four.reshape(token_rows, query_width)
    attn_low = attn_out.astype(jnp.bfloat16)
    middle = inputs + jnp.dot(attn_low, out_full, preferred_element_type=jnp.float32)
    mlp_full = (
        lax.all_gather(gain_ffn, ("dp", "ctx"), axis=0, tiled=True),
        lax.all_gather(w_gate, ("dp", "ctx"), axis=0, tiled=True),
        lax.all_gather(w_up, ("dp", "ctx"), axis=0, tiled=True),
        lax.all_gather(w_down, ("dp", "ctx"), axis=0, tiled=True),
    )
    gain_two, gate_full, up_full, down_full = mlp_full
    inv_two = lax.rsqrt(jnp.mean(middle * middle, axis=-1, keepdims=True) + NORM_EPS)
    normed_two = (middle * inv_two * gain_two.astype(jnp.float32)).astype(jnp.bfloat16)
    gate_value = jnp.dot(normed_two, gate_full, preferred_element_type=jnp.float32)
    up_value = jnp.dot(normed_two, up_full, preferred_element_type=jnp.float32)
    sigmoid_gate = jax.nn.sigmoid(gate_value)
    silu_gate = gate_value * sigmoid_gate
    hidden = (silu_gate * up_value).astype(jnp.bfloat16)
    output = (middle + jnp.dot(hidden, down_full, preferred_element_type=jnp.float32)).astype(
        jnp.bfloat16
    )
    mlp_back = (
        lax.all_gather(gain_ffn, ("dp", "ctx"), axis=0, tiled=True),
        lax.all_gather(w_gate, ("dp", "ctx"), axis=0, tiled=True),
        lax.all_gather(w_up, ("dp", "ctx"), axis=0, tiled=True),
        lax.all_gather(w_down, ("dp", "ctx"), axis=0, tiled=True),
    )
    gain_two_back, gate_back, up_back, down_back = mlp_back
    grad_out = cotangent.astype(jnp.float32)
    grad_hidden = jnp.einsum("td,fd->tf", cotangent, down_back, preferred_element_type=jnp.float32)
    grad_gate = (
        grad_hidden * up_value * sigmoid_gate * (1.0 + gate_value * (1.0 - sigmoid_gate))
    ).astype(jnp.bfloat16)
    grad_up = (grad_hidden * silu_gate).astype(jnp.bfloat16)
    grad_normed_two = jnp.einsum(
        "tf,cf->tc", grad_gate, gate_back, preferred_element_type=jnp.float32
    ) + jnp.einsum("tf,cf->tc", grad_up, up_back, preferred_element_type=jnp.float32)
    grad_gain_two, grad_middle_norm = norm_back(grad_normed_two, middle, inv_two, gain_two_back)
    grad_middle = grad_out + grad_middle_norm
    gate_up_pair = jnp.concatenate([grad_gate, grad_up], axis=1)
    gate_up_sum = lax.psum_scatter(
        row_product(normed_two, gate_up_pair), ("dp", "ctx"), scatter_dimension=0, tiled=True
    )
    grad_down_sum = lax.psum_scatter(
        row_product(hidden, cotangent), ("dp", "ctx"), scatter_dimension=0, tiled=True
    )
    attn_back = (
        lax.all_gather(gain_attn, ("dp", "ctx"), axis=0, tiled=True),
        lax.all_gather(w_query, ("dp", "ctx"), axis=0, tiled=True),
        lax.all_gather(key_weight, ("dp", "ctx"), axis=0, tiled=True),
        lax.all_gather(value_weight, ("dp", "ctx"), axis=0, tiled=True),
        lax.all_gather(w_out, ("dp", "ctx"), axis=0, tiled=True),
    )
    gain_one_back, query_back, key_back, value_back, out_back = attn_back
    grad_branch = grad_middle.astype(jnp.bfloat16)
    attention_gradient = jnp.einsum(
        "td,cd->tc", grad_branch, out_back, preferred_element_type=jnp.float32
    ).astype(jnp.bfloat16)
    gradient_quad = attention_gradient.reshape(token_rows, KEY_VALUE_HEADS, head_group, HEAD_SIZE)
    delta_rows = jnp.transpose(
        jnp.sum(gradient_quad.astype(jnp.float32) * attn_four, axis=-1), (1, 2, 0)
    )

    def pair_terms(key_value_block, key_first):
        block_count = key_value_block.shape[0]
        key_portion = key_value_block[:, :key_value_width].reshape(
            block_count, KEY_VALUE_HEADS, HEAD_SIZE
        )
        value_portion = key_value_block[:, key_value_width:].reshape(
            block_count, KEY_VALUE_HEADS, HEAD_SIZE
        )
        scores = (
            jnp.einsum(
                "tkgd,skd->kgts", query_rows, key_portion, preferred_element_type=jnp.float32
            )
            * score_scale
        )
        key_pos = key_first + jnp.arange(block_count, dtype=jnp.int32)
        allowed = key_pos[None, :] <= query_pos[:, None]
        scores = jnp.where(allowed, scores, MASK_FILL)
        probs = jnp.exp(scores - log_total[..., None])
        grad_probs = jnp.einsum(
            "tkgd,skd->kgts", gradient_quad, value_portion, preferred_element_type=jnp.float32
        )
        grad_scores = (probs * (grad_probs - delta_rows[..., None])).astype(jnp.bfloat16)
        grad_query = (
            jnp.einsum(
                "kgts,skd->tkgd", grad_scores, key_portion, preferred_element_type=jnp.float32
            )
            * score_scale
        )
        grad_keys = (
            jnp.einsum(
                "kgts,tkgd->skd", grad_scores, query_rows, preferred_element_type=jnp.float32
            )
            * score_scale
        )
        grad_values = jnp.einsum(
            "kgts,tkgd->skd",
            probs.astype(jnp.bfloat16),
            gradient_quad,
            preferred_element_type=jnp.float32,
        )
        return (
            grad_query,
            jnp.concatenate(
                [
                    grad_keys.reshape(block_count, key_value_width),
                    grad_values.reshape(block_count, key_value_width),
                ],
                axis=1,
            ),
        )

    def add_pair(operands):
        kv_use, key_first, grad_query, grad_now = operands
        more_query, more_kv = pair_terms(kv_use, key_first)
        return (grad_query + more_query, grad_now + more_kv)

    def keep_pair(operands):
        return (operands[2], operands[3])

    def cycle_step(step, state):
        kv_now, grad_now, grad_query = state
        owner = (ctx_rank - step + ctx_count) % ctx_count
        kv_next = passed_along(kv_now, "ctx", 1)
        grad_query, grad_now = lax.cond(
            owner <= ctx_rank,
            add_pair,
            keep_pair,
            (kv_now, owner * token_rows, grad_query, grad_now),
        )
        grad_next = shifted(grad_now.astype(jnp.bfloat16), "ctx", 1).astype(grad_now.dtype)
        return (kv_next, grad_next, grad_query)

    cycle_start = (
        kv_local,
        jnp.zeros((token_rows, 2 * key_value_width), jnp.float32),
        jnp.zeros((token_rows, KEY_VALUE_HEADS, head_group, HEAD_SIZE), jnp.float32),
    )
    kv_final, key_value_gradient, grad_query = lax.fori_loop(0, ctx_count, cycle_step, cycle_start)
    grad_query_raw = (
        apply_rotary(
            grad_query.reshape(token_rows, QUERY_HEADS, HEAD_SIZE), cosine_table, sine_values, -1.0
        )
        .reshape(token_rows, query_width)
        .astype(jnp.bfloat16)
    )
    grad_key_raw = (
        apply_rotary(
            key_value_gradient[:, :key_value_width].reshape(token_rows, KEY_VALUE_HEADS, HEAD_SIZE),
            cosine_table,
            sine_values,
            -1.0,
        )
        .reshape(token_rows, key_value_width)
        .astype(jnp.bfloat16)
    )
    grad_value_raw = key_value_gradient[:, key_value_width:].astype(jnp.bfloat16)
    grad_normed_one = (
        jnp.einsum("tq,cq->tc", grad_query_raw, query_back, preferred_element_type=jnp.float32)
        + jnp.einsum("tq,cq->tc", grad_key_raw, key_back, preferred_element_type=jnp.float32)
        + jnp.einsum("tq,cq->tc", grad_value_raw, value_back, preferred_element_type=jnp.float32)
    )
    grad_gain_one, grad_input_norm = norm_back(grad_normed_one, inputs, inv_one, gain_one_back)
    grad_tokens = grad_middle + grad_input_norm
    projection_grads = jnp.concatenate([grad_query_raw, grad_key_raw, grad_value_raw], axis=1)
    qkv_sum = lax.psum_scatter(
        row_product(first_normed, projection_grads), ("dp", "ctx"), scatter_dimension=0, tiled=True
    )
    grad_out_sum = lax.psum_scatter(
        row_product(attn_low, grad_branch), ("dp", "ctx"), scatter_dimension=0, tiled=True
    )
    gain_sums = (
        lax.psum_scatter(grad_gain_one, ("dp", "ctx"), scatter_dimension=0, tiled=True),
        lax.psum_scatter(grad_gain_two, ("dp", "ctx"), scatter_dimension=0, tiled=True),
    )
    ff_width = w_gate.shape[1]
    return (
        output,
        grad_tokens,
        gain_sums[0],
        qkv_sum[:, :query_width],
        qkv_sum[:, query_width : query_width + key_value_width],
        qkv_sum[:, query_width + key_value_width :],
        grad_out_sum,
        gain_sums[1],
        gate_up_sum[:, :ff_width],
        gate_up_sum[:, ff_width:],
        grad_down_sum,
    )


CUBE = 8
BITS = (0, 1, 2)
HEAD_LANES = 128
HALF_LANES = 64
SHARE = 4 * HEAD_LANES
F32 = jnp.float32
BF16 = jnp.bfloat16


class Here:
    def __init__(self):
        dp = lax.axis_index("dp")
        ctx = lax.axis_index("ctx")
        self.core = lax.rem(dp, 2)
        self.far = ctx // 4
        self.own = (dp // 2, lax.rem(ctx // 2, 2), lax.rem(ctx, 2))
        self.shard = self.shard_of(self.own)
        self.at_home = self.own[0] == self.far
        self.sibling = self.device(self.own, core=1 - self.core)
        self.across = self.device(self.own, far=1 - self.far)

    def shard_of(self, bits):
        return bits[0] * 4 + bits[1] * 2 + bits[2]

    def device(self, bits, core=None, far=None):
        core = self.core if core is None else core
        far = self.far if far is None else far
        return (bits[0] * 2 + core, far * 4 + bits[1] * 2 + bits[2])

    def flip(self, *turned, of=None):
        bits = self.own if of is None else of
        return tuple(1 - bit if index in turned else bit for index, bit in enumerate(bits))

    def next(self, bit):
        return self.device(self.flip(bit))

    def others(self):
        return [
            self.flip(*[bit for bit in BITS if code >> (2 - bit) & 1]) for code in range(1, CUBE)
        ]

    def greet(self, partners):
        barrier = pltpu.get_barrier_semaphore()
        for partner in partners:
            pl.semaphore_signal(
                barrier, inc=1, device_id=partner, device_id_type=pl.DeviceIdType.MESH
            )
        pl.semaphore_wait(barrier, len(partners))

    def peers(self):
        return [self.device(bits) for bits in self.others()]

    def same_core(self):
        beyond = [self.device(bits, far=1 - self.far) for bits in self.others() + [self.own]]
        return self.peers() + beyond


def make_send(source, target, sems, device):
    return pltpu.make_async_remote_copy(
        src_ref=source,
        dst_ref=target,
        send_sem=sems[0],
        recv_sem=sems[1],
        device_id=device,
        device_id_type=pl.DeviceIdType.MESH,
    )


def send(*operands):
    copy = make_send(*operands)
    copy.start()
    return copy


class Sems:
    def __init__(self, sent, received):
        self.sent, self.received, self.used = sent, received, 0

    def __call__(self):
        pair = (self.sent.at[self.used], self.received.at[self.used])
        self.used += 1
        return pair


def run_all(*generators):
    live = list(generators)
    while live:
        for one in list(live):
            try:
                next(one)
            except StopIteration:
                live.remove(one)


def play(script, transfers, actions):
    actions = {name: list(some) for name, some in actions.items()}
    for name in script:
        if name in actions:
            actions[name].pop(0)()
        else:
            next(transfers[name], None)
    run_all(*transfers.values())


def in_step(live):
    live = list(live)
    while live:
        for one in list(live):
            try:
                next(one)
            except StopIteration:
                live.remove(one)
        yield


ORDERS = ((0, 1, 2), (1, 2, 0), (2, 0, 1))
ORDERS_Z_FIRST = ((1, 0, 2), (1, 2, 0))


def gather_cube(here, place_of, order, sems, source=None):
    a, b, c = order
    to = lambda bits, bit: send(place_of(bits), place_of(bits), sems(), here.next(bit))
    from_a, from_b = here.flip(a), here.flip(b)
    own = place_of(here.own)
    pairs = [sems() for _ in order]
    first = lambda block: [
        make_send(block, own, pair, here.next(bit)) for pair, bit in zip(pairs, order)
    ]
    a0, b0, c0 = first(own)
    if source is None:
        for copy in (a0, b0, c0):
            copy.start()
    else:

        @pl.when(here.at_home)
        def _():
            for copy in first(source):
                copy.start()

        yield
        yield

        @pl.when(jnp.logical_not(here.at_home))
        def _():
            for copy in (a0, b0, c0):
                copy.start()

    yield
    a0.wait_recv()
    b1, c1 = to(from_a, b), to(from_a, c)
    yield
    b0.wait_recv()
    c2 = to(from_b, c)
    yield
    b1.wait_recv()
    c3 = to(here.flip(a, b), c)
    yield
    for copy in (c0, c1, c2, c3):
        copy.wait_recv()
    for copy in (a0, b0, b1, c0, c1, c2, c3):
        copy.wait_send()


def gather_cube_parts(here, place_of, size, orders, sems, source=None):
    step = size // len(orders)
    live = []
    for index, order in enumerate(orders):
        part = pl.ds(index * step, step)
        live.append(
            gather_cube(
                here,
                functools.partial(place_of, part=part),
                order,
                sems,
                None if source is None else source.at[:, part],
            )
        )
    return in_step(live)


def total_of(*refs):
    total = refs[0][...].astype(F32)
    for ref in refs[1:]:
        total = total + ref[...].astype(F32)
    return total


PAIRS = (((0, 1, 2), (0, 1)), ((1, 2), (0, 2)), ((0,), (2,)), ((1,), ()))


class ReduceStream:
    def __init__(self, here, part_of, slots, out, order, sems):
        self.here, self.part_of, self.slots, self.out = here, part_of, slots, out
        c, b, a = self.order = order
        self.first = [(c, b, a), (c, b), (c, a), (c,)]
        self.copies = [None] * (CUBE - 1)
        self.sems = [sems() for _ in range(CUBE - 1)]
        self.made = set()

    def send(self, turned, slot, bit):
        self.copies[slot] = send(
            self.part_of(self.here.flip(*turned)),
            self.slots(slot),
            self.sems[slot],
            self.here.next(bit),
        )

    def add(self, turned, *slots):
        for slot in slots:
            self.copies[slot].wait_recv()
        spot = self.part_of(self.here.flip(*turned))
        spot[...] = total_of(spot, *[self.slots(slot) for slot in slots]).astype(BF16)

    def after(self, pair):
        c, b, a = self.order
        before = set(self.made)
        self.made |= {frozenset(turned) for turned in PAIRS[pair]}
        for slot, turned in enumerate(self.first):
            if frozenset(turned) in self.made - before:
                self.send(turned, slot, c)
        if self.copies[4] is None and self.copies[0] is not None and frozenset((b, a)) in self.made:
            self.add((b, a), 0)
            self.send((b, a), 4, b)
        if self.copies[5] is None and self.copies[1] is not None and frozenset((b,)) in self.made:
            self.add((b,), 1)
            self.send((b,), 5, b)

    def finish(self):
        _, b, a = self.order
        self.add((a,), 2, 4)
        self.send((a,), 6, a)
        yield
        for slot in (3, 5, 6):
            self.copies[slot].wait_recv()
        self.out[...] = total_of(
            self.part_of(self.here.own), self.slots(3), self.slots(5), self.slots(6)
        )
        yield
        for copy in self.copies:
            copy.wait_send()


def reductions(here, part, slots, out, orders, sems):
    width = out.shape[1] // len(orders)
    return [
        ReduceStream(
            here,
            lambda bits, columns=columns: part.at[here.shard_of(bits), :, columns],
            lambda slot, columns=columns: slots.at[slot, :, columns],
            out.at[:, columns],
            order,
            sems,
        )
        for columns, order in [
            (pl.ds(index * width, width), order) for index, order in enumerate(orders)
        ]
    ]


def swap_home(here, source, target, relay, local_sem, sems, beyond=None):
    beyond = target if beyond is None else beyond
    half = source.shape[1] // 2
    left, right = pl.ds(0, half), pl.ds(half, half)
    there = here.device(here.flip(0), far=1 - here.far)
    local = pltpu.make_async_copy(source, target, local_sem)
    straight = make_send(source.at[:, left], beyond.at[:, left], sems(), there)
    aside = make_send(source.at[:, right], relay, sems(), here.next(0))
    onward = make_send(relay, target.at[:, right], sems(), here.across)

    @pl.when(here.at_home)
    def _():
        local.start()

    @pl.when(jnp.logical_not(here.at_home))
    def _():
        aside.start()
        straight.start()

    yield

    @pl.when(here.at_home)
    def _():
        aside.wait_recv()
        onward.start()

    yield

    @pl.when(here.at_home)
    def _():
        local.wait()

    @pl.when(jnp.logical_not(here.at_home))
    def _():
        straight.wait_recv()
        onward.wait_recv()
        straight.wait_send()
        aside.wait_send()

    yield

    @pl.when(here.at_home)
    def _():
        onward.wait_send()


def spread(here, place_of, sems, ready=()):
    for copy in ready:
        copy.wait()
    over = send(place_of(here.far), place_of(here.far), sems(), here.across)
    beside = send(place_of(here.far), place_of(here.far), sems(), here.sibling)
    yield
    over.wait_recv()
    last = send(place_of(1 - here.far), place_of(1 - here.far), sems(), here.sibling)
    yield
    beside.wait_recv()
    last.wait_recv()
    for copy in (over, beside, last):
        copy.wait_send()


def gather_columns(here, chunks, target, local_sem, sems):
    x, z, y = here.own
    place = target.at[x, here.core, here.far, z, y]
    local = pltpu.make_async_copy(chunks.at[here.shard], place, local_sem)
    local.start()
    copies = [
        send(chunks.at[here.shard_of(bits)], place, sems(), here.device(bits))
        for bits in here.others()
    ]
    yield
    yield from spread(
        here, lambda far: target.at[:, here.core, far], sems, copies + [local]
    )


ANY = pl.BlockSpec(memory_space=pltpu.MemorySpace.HBM)
VMEM = pl.BlockSpec(memory_space=pltpu.MemorySpace.VMEM)
VMEM_BYTES = 62 * 2**20


def params(collective_id):
    return pltpu.CompilerParams(
        collective_id=collective_id, has_side_effects=True, vmem_limit_bytes=VMEM_BYTES
    )


def dma_sems(count):
    return [pltpu.SemaphoreType.DMA((count,)), pltpu.SemaphoreType.DMA((count,))]


def half_blocks(block):
    return pltpu.VMEM((block[0], block[1] // 2), BF16)


QUERY_TILE = 256
SCRIPT = (
    "oxqghxcxcxqxoxcgodocxcocqqx1h11o1g1ocababadbabhabo",
    "PPPPgdgdcchhAAAAGfBfBBBGjGisjiss",
    "Npp2222f3t3t3t3ti4tj4kwktwtNvnvrrrrnrnrnrnvufuijkjwuuu",
)
ORDERS_SPARE_Z = ((1, 0, 2), (1, 2, 0), (0, 1, 2), (2, 1, 0))
ORDERS_Z_LAST = ((0, 2, 1), (2, 0, 1))
ORDERS_ALL = ORDERS + ((0, 2, 1), (1, 0, 2), (2, 1, 0))
FRONT_ORDERS = dict(x=ORDERS_ALL, c=ORDERS_SPARE_Z, o=ORDERS_SPARE_Z, a=ORDERS_ALL)
BACK_ORDERS = dict(r=ORDERS_ALL, t=ORDERS_ALL, s=ORDERS)
NT = (((1,), (1,)), ((), ()))
TN = (((0,), (0,)), ((), ()))


def dot(left, right):
    return jnp.dot(left, right, preferred_element_type=F32)


def dot_nt(left, right):
    return lax.dot_general(left, right, NT, preferred_element_type=F32)


def dot_tn(left, right):
    return lax.dot_general(left, right, TN, preferred_element_type=F32)


def rotate(head, cosine, sine):
    return head * cosine + pltpu.roll(head, HALF_LANES, 1) * sine


def scores_of(keys, queries):
    count = keys.shape[0] - QUERY_TILE
    parts = []
    if count > 0:
        parts.append(dot_nt(keys[:count], queries) * HEAD_SIZE**-0.5)
    last = dot_nt(keys[count:], queries) * HEAD_SIZE**-0.5
    key = lax.broadcasted_iota(jnp.int32, last.shape, 0)
    query = lax.broadcasted_iota(jnp.int32, last.shape, 1)
    parts.append(jnp.where(key <= query, last, MASK_FILL))
    return parts


def attend_tile(q, k, v_t, o_t, ob, lse, group, tile):
    rows = pl.ds(tile * QUERY_TILE, QUERY_TILE)
    count = (tile + 1) * QUERY_TILE
    parts = scores_of(k[:count, :], q[group, rows, :])
    top = jnp.max(parts[-1], axis=0, keepdims=True)
    for part in parts[:-1]:
        top = jnp.maximum(top, jnp.max(part, axis=0, keepdims=True))
    total = jnp.zeros_like(top)
    result = None
    first = 0
    for part in parts:
        expo = jnp.exp(part - top)
        total = total + jnp.sum(expo, axis=0, keepdims=True)
        added = dot(v_t[:, first : first + part.shape[0]], expo.astype(BF16))
        result = added if result is None else result + added
        first += part.shape[0]
    result = result / total
    o_t[group, :, rows] = result
    ob[group * HEAD_SIZE : (group + 1) * HEAD_SIZE, rows] = result[:HEAD_SIZE].astype(BF16)
    lse[group, :, rows] = top + jnp.log(total)


def spaced(head):
    half = HEAD_SIZE // 2
    gap = jnp.zeros((head.shape[0], HALF_LANES - half), head.dtype)
    return jnp.concatenate([head[:, :half], gap, head[:, half:], gap], axis=1)


def packed(head):
    half = HEAD_SIZE // 2
    return jnp.concatenate([head[:, :half], head[:, HALF_LANES : HALF_LANES + half]], axis=1)


def as_column(row):
    size = row.shape[1]
    same = lax.broadcasted_iota(jnp.int32, (size, size), 0) == lax.broadcasted_iota(
        jnp.int32, (size, size), 1
    )
    return jnp.sum(jnp.where(same, row, 0.0), axis=1, keepdims=True)


def cut_projections(w_query, key_weight, value_weight, gain_attn, gain_ffn, chunks):
    query, key, value = (ref[...].astype(F32) for ref in (w_query, key_weight, value_weight))
    rows = query.shape[0]
    gains = [as_column(ref[...].astype(F32)) for ref in (gain_attn, gain_ffn)]
    gap = jnp.zeros((rows, HEAD_LANES - HEAD_SIZE - 2), F32)
    head = lambda weight, index: weight[:, index * HEAD_SIZE : (index + 1) * HEAD_SIZE]
    for shard in range(CUBE):
        parts = [
            spaced(head(query, 2 * shard)),
            spaced(head(query, 2 * shard + 1)),
            spaced(head(key, shard)),
            jnp.concatenate([head(value, shard), *gains, gap], axis=1),
        ]
        chunks[shard] = jnp.concatenate(parts, axis=1).astype(BF16)


def hidden_lanes(shard, part, lanes):
    x, zy = divmod(shard, 4)
    first = (x * 16 + part * 4 + zy) * lanes
    return slice(first, first + lanes)


def chunk_lanes(part, lanes):
    first = (part // 2 * 4 + part % 2) * lanes
    return slice(first, first + lanes), slice(first + 2 * lanes, first + 3 * lanes)


def cut_hidden(w_gate, w_up, chunks, half):
    lanes = chunks.shape[2] // 8
    for shard in range(CUBE):
        for part in (2 * half, 2 * half + 1):
            place = hidden_lanes(shard, part, lanes)
            gate, up = chunk_lanes(part, lanes)
            chunks[shard, :, gate] = w_gate[:, place]
            chunks[shard, :, up] = w_up[:, place]


def norm_after_attention(shards, x_all, ob_all, w_o, gains, y1_own):
    _, block_rows, width = x_all.shape
    rows_of = [
        pl.ds(pl.multiple_of(shard * block_rows, block_rows), block_rows) for shard in shards
    ]
    ob_t = jnp.concatenate([ob_all[:, :, rows].reshape(width, block_rows) for rows in rows_of], axis=1)
    x = jnp.concatenate([x_all[shard] for shard in shards], axis=0)
    y1 = x.astype(F32) + dot_tn(ob_t, w_o[...].reshape(width, width))
    inv_root = lax.rsqrt(jnp.mean(y1 * y1, axis=-1, keepdims=True) + NORM_EPS)
    h2 = (y1 * inv_root * gains[1:2, :]).astype(BF16)
    if y1_own is not None:
        y1_own[...] = y1[block_rows:]
    for index, shard in enumerate(shards):
        x_all[shard] = h2[index * block_rows : (index + 1) * block_rows]


def feed_forward(half, shards, h2_all, ct_all, w_gu, w_d, hidden, d_gu, out_part, dh2_part):
    _, block_rows, width = h2_all.shape
    share = d_gu.shape[1] // 4
    pair = lambda ref: jnp.concatenate([ref[shard] for shard in shards], axis=0)
    rows_of = [
        pl.ds(pl.multiple_of(shard * block_rows, block_rows), block_rows) for shard in shards
    ]
    both = pl.ds(half * 2 * share, 2 * share)
    weight = w_gu[:, :, :, :, :, :, both].reshape(width, 2 * share)
    gate_up = dot(pair(h2_all), weight)
    gate, up = gate_up[:, :share], gate_up[:, share:]
    sig = 1.0 / (1.0 + jnp.exp(-gate))
    silu = gate * sig
    kept = (silu * up).astype(BF16)
    down = w_d[0, half].reshape(share, width)
    d_hidden = dot_nt(pair(ct_all), down)
    d_gate = (d_hidden * up * sig * (1.0 + gate * (1.0 - sig))).astype(BF16)
    d_up = (d_hidden * silu).astype(BF16)
    d_both = jnp.concatenate([d_gate, d_up], axis=1)
    dh2 = dot_nt(d_both, weight)
    out = dot(kept, down)
    for index, (shard, rows) in enumerate(zip(shards, rows_of)):
        block = slice(index * block_rows, (index + 1) * block_rows)
        hidden[rows, pl.ds(half * share, share)] = kept[block]
        d_gu[rows, both] = d_both[block]
        for total, added in ((dh2_part, dh2), (out_part, out)):
            more = added[block]
            if half == 1:
                more = more + total[shard].astype(F32)
            total[shard] = more.astype(BF16)


def attend_back_tile(q, k, k_t, v, do_t, o_t, lse, dk, dv, group, tile):
    rows = pl.ds(tile * QUERY_TILE, QUERY_TILE)
    count = (tile + 1) * QUERY_TILE
    q_rows = q[group, rows, :]
    do_rows = do_t[group * HEAD_SIZE : (group + 1) * HEAD_SIZE, rows]
    do_rows = jnp.concatenate(
        [do_rows, jnp.zeros((HEAD_LANES - HEAD_SIZE, QUERY_TILE), BF16)], axis=0
    )
    delta = jnp.sum(do_rows.astype(F32) * o_t[group, :, rows], axis=0, keepdims=True)
    log_total = lse[group, :, rows]
    dq_t = None
    first = 0
    for part in scores_of(k[:count, :], q_rows):
        keys = slice(first, first + part.shape[0])
        probs = jnp.exp(part - log_total)
        d_probs = dot(v[keys, :], do_rows)
        d_scores = (probs * (d_probs - delta)).astype(BF16)
        dv[keys, :] += dot_nt(probs.astype(BF16), do_rows)
        dk[keys, :] += dot(d_scores, q_rows)
        added = dot(k_t[:, keys], d_scores)
        dq_t = added if dq_t is None else dq_t + added
        first += part.shape[0]
    return jnp.transpose(dq_t) * HEAD_SIZE**-0.5


def add_rows(total, more, piece):
    if len(total.shape) == 5:
        for z in range(2):
            for y in range(2):
                add_rows(total.at[:, z, y], more.at[:, z, y], piece)
        return

    def body(index, carry):
        rows = pl.ds(pl.multiple_of(index * piece, piece), piece)
        for block in range(total.shape[0]):
            total[block, rows, :] = total_of(
                total.at[block, rows, :], more.at[block, rows, :]
            ).astype(BF16)
        return carry

    lax.fori_loop(0, total.shape[1] // piece, body, 0)


def reduce_copies(here, part, beside, over, sems, piece):
    core, far = here.core, here.far
    first = send(part.at[:, 1 - core, 1 - far], beside.at[0], sems(), here.sibling)
    second = send(part.at[:, 1 - core, far], beside.at[1], sems(), here.sibling)
    yield
    first.wait_recv()
    add_rows(part.at[:, core, 1 - far], beside.at[0], piece)
    third = send(part.at[:, core, 1 - far], over, sems(), here.across)
    second.wait_recv()
    add_rows(part.at[:, core, far], beside.at[1], piece)
    yield
    third.wait_recv()
    add_rows(part.at[:, core, far], over, piece)
    for copy in (first, second, third):
        copy.wait_send()


def scatter_columns(here, part, beside, over, out, local_sem, sems):
    rows = out.shape[1]
    yield from reduce_copies(here, part, beside, over, sems, rows)

    def source(bits):
        return part.at[bits[0], here.core, here.far, bits[1], bits[2]]

    local = pltpu.make_async_copy(source(here.own), out.at[here.shard], local_sem)
    local.start()
    copies = [
        send(source(bits), out.at[here.shard], sems(), here.device(bits)) for bits in here.others()
    ]
    yield
    for copy in copies + [local]:
        copy.wait()


def copy_slots(shape):
    rest = (shape[0], *shape[3:])
    return [pltpu.VMEM((2, *rest), BF16), pltpu.VMEM(rest, BF16)]


def norm_back_rows(grad_normed, rows, gain):
    inv_root = lax.rsqrt(jnp.mean(rows * rows, axis=-1, keepdims=True) + NORM_EPS)
    grad_gain, grad_rows = norm_back(grad_normed, rows, inv_root, gain)
    return grad_gain.reshape(1, -1), grad_rows


def sum_everywhere(here, total, slots, sems):
    hops = [here.sibling] + [here.next(bit) for bit in BITS] + [here.across]
    for index, device in enumerate(hops):
        copy = send(total, slots.at[index], sems(), device)
        yield
        copy.wait()
        total[...] += slots[index]


def layer_kernel(
    tokens, cotangent, w_query, key_weight, value_weight, gain_attn, gain_ffn, w_gate, w_up, down, out,
    cosine, sine,
    output_home, grad_home, gu_rows_too, down_sum, qkv_rows, out_rows, gain_out, gu_rows,
    w_qkv, w_gu, w_d, w_o, x_all, ct_all, ob_all, h1, q, k, v, v_t, o_t, lse, gains, x_own, ct_own, y1_own,
    hidden, d_gu, out_part, dh2_part, dh2, slots, x_relay, ct_relay, qkv, gate_up,
    gu_beside, gu_over, gu_beside_too, gu_over_too, down_beside, down_over, qkv_beside, qkv_over,
    wo_part, wo_beside, wo_over, gain_sums, gain_slots, d_middle, pairs, columns, k_t, dk, dv, out_sum,
    own_rows, local, sent, got,
):
    here = Here()
    sems = Sems(sent, got)
    here.greet(here.same_core() + [here.sibling])
    out_slots, dh1_part, dh1, d_qkv = ct_all, x_all, dh2, hidden
    x, z, y = here.own
    width = tokens.shape[1]
    block_rows = tokens.shape[0]
    seq_rows = CUBE * block_rows

    def swapped(source, target, relay, local_sem, orders):
        swap = swap_home(
            here,
            source,
            target.at[here.shard],
            relay,
            local_sem,
            sems,
            target.at[here.shard_of(here.flip(0))],
        )
        gather = gather_cube_parts(
            here,
            lambda bits, part: target.at[here.shard_of(bits), :, part],
            width,
            orders,
            sems,
            source,
        )
        for _ in range(3):
            next(swap)
            next(gather)
            yield
        run_all(swap)
        yield from gather

    def out_gather():
        mine = w_o.at[x, here.core, here.far, z, y]
        kept = pltpu.make_async_copy(out, mine, local.at[3])
        kept.start()
        over = send(out, mine, sems(), here.across)
        yield
        kept.wait()
        over.wait()
        yield from gather_cube_parts(
            here,
            lambda bits, part: w_o.at[bits[0], here.core, :, bits[1], bits[2], :, part],
            width,
            FRONT_ORDERS["o"],
            sems,
        )
        beside = send(w_o.at[:, here.core], w_o.at[:, here.core], sems(), here.sibling)
        yield
        beside.wait()

    def down_gather():
        kept = pltpu.make_async_copy(down, w_d.at[0, here.core, here.far], local.at[2])
        kept.start()
        yield from spread(here, lambda far: w_d.at[0, here.core, far], sems, [kept])

    def qkv_gather():
        cut_projections(w_query, key_weight, value_weight, gain_attn, gain_ffn, qkv)
        yield from gather_columns(here, qkv, w_qkv, local.at[4], sems)

    ff_share = w_gu.shape[6] // 2
    halves = [pl.ds(half * ff_share, ff_share) for half in range(2)]

    def gate_up_gather(half):
        cut_hidden(w_gate, w_up, gate_up, half)
        yield from gather_columns(
            here,
            gate_up.at[:, :, halves[half]],
            w_gu.at[:, :, :, :, :, :, halves[half]],
            local.at[5 + half],
            sems,
        )

    transfers = dict(
        x=swapped(tokens, x_all, x_relay, local.at[0], FRONT_ORDERS["x"]),
        q=qkv_gather(),
        g=gate_up_gather(0),
        h=gate_up_gather(1),
        o=out_gather(),
        d=down_gather(),
        c=swapped(cotangent, ct_all, ct_relay, local.at[1], FRONT_ORDERS["c"]),
    )
    ob = ob_all.at[here.shard]
    turns = [[here.shard_of(here.flip(*bits)) for bits in turned] for turned in PAIRS]

    def norm():
        turned = jnp.transpose(
            w_qkv[:, :, :, :, :, :, 3 * HEAD_LANES :].astype(F32).reshape(width, HEAD_LANES)
        )
        gains[...] = turned[HEAD_SIZE : HEAD_SIZE + 8]
        x_own[...] = x_all[here.shard]

        def norm_block(index, carry):
            rows = x_all[index].astype(F32)
            inv_root = lax.rsqrt(jnp.mean(rows * rows, axis=-1, keepdims=True) + NORM_EPS)
            place = pl.ds(pl.multiple_of(index * block_rows, block_rows), block_rows)
            h1[place, :] = (rows * inv_root * gains[0:1, :]).astype(BF16)
            return carry

        lax.fori_loop(0, CUBE, norm_block, 0)

    def project():
        def project_tile(index, carry):
            rows = pl.ds(pl.multiple_of(index * QUERY_TILE, QUERY_TILE), QUERY_TILE)
            raw = dot(h1[rows, :], w_qkv[...].reshape(width, SHARE))
            cos_rows, sin_rows = cosine[rows, :], sine[rows, :]
            heads = [raw[:, lane : lane + HEAD_LANES] for lane in range(0, SHARE, HEAD_LANES)]
            q[0, rows, :] = rotate(heads[0], cos_rows, sin_rows).astype(BF16)
            q[1, rows, :] = rotate(heads[1], cos_rows, sin_rows).astype(BF16)
            k[rows, :] = rotate(heads[2], cos_rows, sin_rows).astype(BF16)
            v[rows, :] = heads[3].astype(BF16)
            v_t[:, rows] = jnp.transpose(heads[3]).astype(BF16)
            return carry

        lax.fori_loop(0, seq_rows // QUERY_TILE, project_tile, 0)

    def attend(*tiles):
        for tile in tiles:
            for group in range(2):
                attend_tile(q, k, v_t, o_t, ob, lse, group, tile)
        if tiles[-1] % 2 == 1:
            lanes = pl.ds((tiles[-1] - 1) * QUERY_TILE, 2 * QUERY_TILE)
            transfers["ab"[tiles[-1] // 2]] = gather_cube_parts(
                here,
                lambda bits, part: ob_all.at[here.shard_of(bits), part, lanes],
                ob.shape[0],
                FRONT_ORDERS["a"],
                sems,
            )

    def normed_pair(pair):
        own = PAIRS[pair][-1] == ()
        norm_after_attention(turns[pair], x_all, ob_all, w_o, gains, y1_own if own else None)

    bind = functools.partial
    streams = reductions(here, dh2_part, slots, dh2, BACK_ORDERS["s"], sems)

    def feed(half, pair):
        if half == 0 and pair == 0:
            ct_own[...] = ct_all[here.shard]
        feed_forward(
            half, turns[pair], x_all, ct_all, w_gu, w_d, hidden, d_gu, out_part, dh2_part
        )
        if half == 1:
            for stream in streams:
                stream.after(pair)

    def gate_up_grad(half):
        def quarter(index, carry):
            lanes = pl.ds(pl.multiple_of(index * 4 * HEAD_SIZE, 4 * HEAD_SIZE), 4 * HEAD_SIZE)
            left = x_all[:, :, lanes].reshape(seq_rows, 4 * HEAD_SIZE)
            grad = dot_tn(left, d_gu[:, halves[half]]).astype(BF16)
            place = w_gu.at[index // 2, lax.rem(index, 2), :, :, :, :, halves[half]]
            place[...] = grad.reshape(place.shape)
            return carry

        lax.fori_loop(0, 4, quarter, 0)

    def down_grad():
        def quarter(index, carry):
            lanes = pl.ds(pl.multiple_of(index * HEAD_LANES, HEAD_LANES), HEAD_LANES)
            grad = dot_tn(hidden[:, lanes], ct_all[...].reshape(seq_rows, width)).astype(BF16)
            w_d[0, index // 2, lax.rem(index, 2)] = grad
            return carry

        lax.fori_loop(0, 4, quarter, 0)

    weight_rows = out.shape[0]
    share = 2 * HEAD_SIZE

    def gate_up_reduce(half, beside, over, rows):
        yield from scatter_columns(
            here,
            w_gu.at[:, :, :, :, :, :, halves[half]],
            beside,
            over,
            rows,
            local.at[7 + half],
            sems,
        )

    def down_reduce():
        yield from reduce_copies(here, w_d, down_beside, down_over, sems, 32)
        down_sum[...] = w_d[0, here.core, here.far]

    def to_heads():
        rows = pl.ds(pl.multiple_of(here.shard * block_rows, block_rows), block_rows)
        place = columns.at[:, :, rows]
        mine = pltpu.make_async_copy(pairs.at[here.shard], place, local.at[9])
        mine.start()
        copies = [
            send(pairs.at[here.shard_of(bits)], place, sems(), here.device(bits))
            for bits in here.others()
        ]
        yield
        for copy in copies + [mine]:
            copy.wait()

    def reduce_rows(part, slots, out, orders):
        streams = reductions(here, part, slots, out, orders, sems)
        for pair in range(len(PAIRS)):
            for stream in streams:
                stream.after(pair)
            yield
        yield from in_step([stream.finish() for stream in streams])

    def output_reduce():
        yield from reduce_rows(out_part, out_slots, out_sum, BACK_ORDERS["r"])

    def output_swap():
        own_rows[0] = (y1_own[...] + out_sum[...]).astype(BF16)
        yield from swap_home(here, own_rows.at[0], output_home, ct_relay, local.at[12], sems)

    transfers.update(
        f=gate_up_reduce(0, gu_beside, gu_over, gu_rows),
        s=in_step([stream.finish() for stream in streams]),
        i=gate_up_reduce(1, gu_beside_too, gu_over_too, gu_rows_too),
        j=down_reduce(),
        p=to_heads(),
        r=output_reduce(),
        t=reduce_rows(dh1_part, slots, dh1, BACK_ORDERS["t"]),
        k=scatter_columns(here, w_qkv, qkv_beside, qkv_over, qkv_rows, local.at[10], sems),
        w=scatter_columns(here, wo_part, wo_beside, wo_over, out_rows, local.at[11], sems),
        u=output_swap(),
        v=swap_home(here, own_rows.at[1], grad_home, x_relay, local.at[13], sems),
        n=sum_everywhere(here, gain_sums, gain_slots, sems),
    )

    def norm_two():
        grad_gain, grad_rows = norm_back_rows(dh2[...], y1_own[...], gains[1:2, :])
        gain_sums[...] = jnp.zeros_like(gain_sums)
        gain_sums[1:2, :] = grad_gain
        d_middle[...] = ct_own[...].astype(F32) + grad_rows
        da = d_middle[...].astype(BF16)
        pairs[:, 0] = dot_nt(w_o[...].reshape(width, width), da).astype(BF16).reshape(CUBE, share, block_rows)
        pairs[:, 1] = jnp.transpose(d_middle[...]).astype(BF16).reshape(CUBE, share, block_rows)

    def norm_one():
        grad_gain, grad_rows = norm_back_rows(dh1[...], x_own[...].astype(F32), gains[0:1, :])
        gain_sums[0:1, :] = grad_gain
        own_rows[1] = (d_middle[...] + grad_rows).astype(BF16)

    def attention(tile):
        if tile == 0:
            k_t[...] = jnp.transpose(k[...].astype(F32)).astype(BF16)
            dk[...] = jnp.zeros_like(dk)
            dv[...] = jnp.zeros_like(dv)
        rows = pl.ds(tile * QUERY_TILE, QUERY_TILE)
        for group in range(2):
            dq = attend_back_tile(q, k, k_t, v, columns.at[0], o_t, lse, dk, dv, group, tile)
            d_qkv[rows, group * HEAD_LANES : (group + 1) * HEAD_LANES] = rotate(
                dq, cosine[rows, :], -sine[rows, :]
            ).astype(BF16)
        if rows.start + rows.size == seq_rows:
            d_qkv[:, 2 * HEAD_LANES : 3 * HEAD_LANES] = rotate(
                dk[...] * HEAD_SIZE**-0.5, cosine[...], -sine[...]
            ).astype(BF16)
            d_qkv[:, 3 * HEAD_LANES :] = dv[...].astype(BF16)

    def pair_back(pair):
        shards = [here.shard_of(here.flip(*bits)) for bits in PAIRS[pair]]
        some = jnp.concatenate(
            [
                d_qkv[pl.ds(pl.multiple_of(shard * block_rows, block_rows), block_rows), :]
                for shard in shards
            ],
            axis=0,
        )
        rows = dot_nt(some, w_qkv[...].reshape(width, SHARE)).astype(BF16)
        for index, shard in enumerate(shards):
            dh1_part[shard] = rows[index * block_rows : (index + 1) * block_rows]

    def qkv_grad():

        def quarter(index, carry):
            lanes = pl.ds(pl.multiple_of(index * 4 * HEAD_SIZE, 4 * HEAD_SIZE), 4 * HEAD_SIZE)
            grad = dot_tn(h1[:, lanes], d_qkv[...]).astype(BF16)
            w_qkv[index // 2, lax.rem(index, 2)] = grad.reshape(w_qkv.shape[2:])
            return carry

        lax.fori_loop(0, 4, quarter, 0)

    def out_grad():
        for index in range(4):
            left = ob_all[2 * index : 2 * index + 2].reshape(2 * share, seq_rows)
            grad = dot_nt(left, columns[1]).astype(BF16)
            grad = jnp.concatenate(
                [grad, jnp.zeros((2 * share, wo_part.shape[6] - share), BF16)], axis=1
            )
            wo_part[index // 2, index % 2] = grad.reshape(wo_part.shape[2:])

    bind = functools.partial
    everyone = range(len(PAIRS))
    play(
        "".join(SCRIPT),
        transfers,
        {
            "1": [norm, project, bind(attend, 0), bind(attend, 1), bind(attend, 2, 3)],
            "P": [bind(normed_pair, pair) for pair in everyone],
            "A": [bind(feed, 0, pair) for pair in everyone],
            "B": [bind(feed, 1, pair) for pair in everyone],
            "G": [bind(gate_up_grad, 0), down_grad, bind(gate_up_grad, 1)],
            "N": [norm_two, norm_one],
            "2": [bind(attention, tile) for tile in range(seq_rows // QUERY_TILE)],
            "3": [bind(pair_back, pair) for pair in everyone],
            "4": [qkv_grad, out_grad],
        },
    )
    rank = here.device(here.own)
    rank = rank[0] * CUBE + rank[1]
    mine = pltpu.roll(gain_sums[...], lax.rem(width - rank * weight_rows, width), 1)
    gain_out[...] = mine[:, :HEAD_LANES]


def layer(tokens, cotangent, w_query, key_weight, value_weight, gain_attn, gain_ffn, w_gate, w_up, down,
          out, cosine, sine):
    operands = (
        tokens, cotangent, w_query, key_weight, value_weight, gain_attn, gain_ffn, w_gate, w_up, down, out,
        cosine, sine,
    )
    rows, width = tokens.shape
    weight_rows = out.shape[0]
    seq_rows = CUBE * rows
    share = 2 * HEAD_SIZE
    ff_share = 4 * down.shape[0]
    by_row = lambda lanes: (2, 2, 2, 2, 2, weight_rows, lanes)
    low = lambda *dims: pltpu.VMEM(dims, BF16)
    wide = lambda *dims: pltpu.VMEM(dims, F32)
    home = lambda *dims: jax.ShapeDtypeStruct(dims, BF16)
    outs = (
        home(rows, width),
        home(rows, width),
        home(CUBE, weight_rows, ff_share),
        home(*down.shape),
        home(CUBE, weight_rows, SHARE),
        home(CUBE, weight_rows, 2 * HEAD_LANES),
        jax.ShapeDtypeStruct((8, HEAD_LANES), F32),
        home(CUBE, weight_rows, ff_share),
    )
    return pl.pallas_call(
        layer_kernel,
        out_shape=outs,
        in_specs=[VMEM] * len(operands),
        out_specs=(VMEM,) * len(outs),
        scratch_shapes=[
            low(*by_row(SHARE)),
            low(*by_row(2 * ff_share)),
            low(1, 2, 2, *down.shape),
            low(*by_row(width)),
            low(CUBE, rows, width),
            low(CUBE, rows, width),
            low(CUBE, share, seq_rows),
            low(seq_rows, width),
            low(2, seq_rows, HEAD_LANES),
            low(seq_rows, HEAD_LANES),
            low(seq_rows, HEAD_LANES),
            low(HEAD_LANES, seq_rows),
            wide(2, HEAD_LANES, seq_rows),
            wide(2, 1, seq_rows),
            wide(8, width),
            low(rows, width),
            low(rows, width),
            wide(rows, width),
            low(seq_rows, ff_share),
            low(seq_rows, 2 * ff_share),
            low(CUBE, rows, width),
            low(CUBE, rows, width),
            wide(rows, width),
            low(CUBE - 1, rows, width),
            half_blocks(tokens.shape),
            half_blocks(tokens.shape),
            low(CUBE, weight_rows, SHARE),
            low(CUBE, weight_rows, 2 * ff_share),
            *copy_slots(by_row(ff_share)),
            *copy_slots(by_row(ff_share)),
            *copy_slots((1, 2, 2, *down.shape)),
            *copy_slots(by_row(SHARE)),
            low(*by_row(2 * HEAD_LANES)),
            *copy_slots(by_row(2 * HEAD_LANES)),
            wide(8, width),
            wide(5, 8, width),
            wide(rows, width),
            low(CUBE, 2, share, rows),
            low(2, share, seq_rows),
            low(HEAD_LANES, seq_rows),
            wide(seq_rows, HEAD_LANES),
            wide(seq_rows, HEAD_LANES),
            wide(rows, width),
            low(2, rows, width),
            pltpu.SemaphoreType.DMA((14,)),
        ]
        + dma_sems(500),
        compiler_params=params(1),
        name="layer",
    )(*operands)


def finish_kernel(
    output_home, grad_home, gu_rows_too, down_sum, qkv_rows, out_rows, gains, gu_rows,
    output, grad, gate, up, down, query, key, value, out, gain_one, gain_two,
):
    output[...] = output_home[...]
    grad[...] = grad_home[...].astype(F32)
    down[...] = down_sum[...].astype(F32)
    lanes = gu_rows.shape[2] // 4
    for shard in range(CUBE):
        for part in range(4):
            place = hidden_lanes(shard, part, lanes)
            gate_lanes, up_lanes = chunk_lanes(part % 2, lanes)
            rows = (gu_rows, gu_rows_too)[part // 2]
            gate[:, place] = rows[shard, :, gate_lanes].astype(F32)
            up[:, place] = rows[shard, :, up_lanes].astype(F32)
    heads = [
        [
            qkv_rows[shard, :, index * HEAD_LANES : (index + 1) * HEAD_LANES].astype(F32)
            for index in range(4)
        ]
        for shard in range(CUBE)
    ]
    query[...] = jnp.concatenate([packed(head) for some in heads for head in some[:2]], axis=1)
    key[...] = jnp.concatenate([packed(some[2]) for some in heads], axis=1)
    value[...] = jnp.concatenate([some[3][:, :HEAD_SIZE] for some in heads], axis=1)
    out[...] = jnp.concatenate(
        [out_rows[shard, :, : 2 * HEAD_SIZE].astype(F32) for shard in range(CUBE)], axis=1
    )
    gain_one[...] = gains[0, : gain_one.shape[0]]
    gain_two[...] = gains[1, : gain_two.shape[0]]


def finish(parts, ff_width):
    rows, width = parts[0].shape
    weight_rows = parts[2].shape[1]
    out = lambda *dims: jax.ShapeDtypeStruct(dims, F32)
    outs = (
        jax.ShapeDtypeStruct((rows, width), BF16),
        out(rows, width),
        out(weight_rows, ff_width),
        out(weight_rows, ff_width),
        out(*parts[3].shape),
        out(weight_rows, width),
        out(weight_rows, width // 2),
        out(weight_rows, width // 2),
        out(weight_rows, width),
        out(weight_rows),
        out(weight_rows),
    )
    return pl.pallas_call(
        finish_kernel,
        out_shape=outs,
        in_specs=[VMEM] * len(parts),
        out_specs=(VMEM,) * len(outs),
        compiler_params=pltpu.CompilerParams(vmem_limit_bytes=VMEM_BYTES),
        name="finish",
    )(*parts)


def spaced_tables(row_count):
    half = HEAD_SIZE // 2
    frequency = np.float32(ROPE_THETA) ** (-np.arange(half, dtype=np.float32) * 2.0 / HEAD_SIZE)
    angles = np.arange(row_count, dtype=np.float32)[:, None] * frequency.astype(np.float32)[None, :]
    pad = ((0, 0), (0, HALF_LANES - half))
    cosine, sine = np.pad(np.cos(angles), pad), np.pad(np.sin(angles), pad)
    return (
        jnp.asarray(np.concatenate([cosine, cosine], axis=1), F32),
        jnp.asarray(np.concatenate([-sine, sine], axis=1), F32),
    )


def split_layer(
    tokens,
    cotangent,
    gain_attn,
    w_query,
    key_weight,
    value_weight,
    w_out,
    gain_ffn,
    w_gate,
    w_up,
    w_down,
):
    block_rows = tokens.shape[0]
    cosine, sine = spaced_tables(block_rows * CUBE)
    parts = layer(
        tokens, cotangent, w_query, key_weight, value_weight, gain_attn[None], gain_ffn[None], w_gate, w_up,
        w_down, w_out, cosine, sine,
    )
    output, grad, gate, up, down, query, key, value, out, gain_one, gain_two = finish(
        parts, w_gate.shape[1]
    )
    return (output, grad, gain_one, query, key, value, out, gain_two, gate, up, down)


def solution(mesh):
    heads_split = mesh.shape["dp"] == 4 and mesh.shape["ctx"] == KEY_VALUE_HEADS
    return jax.shard_map(
        split_layer if heads_split else blockwise_layer,
        mesh=mesh,
        in_specs=(
            P(("dp", "ctx"), None),
            P(("dp", "ctx"), None),
            P(("dp", "ctx")),
            P(("dp", "ctx"), None),
            P(("dp", "ctx"), None),
            P(("dp", "ctx"), None),
            P(("dp", "ctx"), None),
            P(("dp", "ctx")),
            P(("dp", "ctx"), None),
            P(("dp", "ctx"), None),
            P(("dp", "ctx"), None),
        ),
        out_specs=(
            P(("dp", "ctx"), None),
            P(("dp", "ctx"), None),
            P(("dp", "ctx")),
            P(("dp", "ctx"), None),
            P(("dp", "ctx"), None),
            P(("dp", "ctx"), None),
            P(("dp", "ctx"), None),
            P(("dp", "ctx")),
            P(("dp", "ctx"), None),
            P(("dp", "ctx"), None),
            P(("dp", "ctx"), None),
        ),
        check_vma=False,
    )
```

```python
import functools

import jax
import jax.numpy as jnp
import numpy as np
from jax import lax
from jax.experimental import pallas as pl
from jax.experimental.pallas import tpu as pltpu
from jax.sharding import PartitionSpec as P

QUERY_HEADS = 16
KEY_VALUE_HEADS = 8
HEAD_SIZE = 96


NORM_EPS = 1e-05
ROPE_THETA = 100000.0
MASK_FILL = -1e30


def passed_along(value, axis, by):
    peers = lax.axis_size(axis)
    pairs = [(i, i + by) for i in range(peers) if 0 <= i + by < peers]
    return lax.ppermute(value, axis, pairs)


def shifted(block, axis, distance):
    devices = range(lax.axis_size(axis))
    route = [((i - distance) % len(devices), i) for i in devices]
    return lax.ppermute(block, axis, route)


def rope_tables(first_row, block_count):
    half_dim = HEAD_SIZE // 2
    positions = (first_row + jnp.arange(block_count, dtype=jnp.int32)).astype(jnp.float32)
    frequency = ROPE_THETA ** (-jnp.arange(half_dim, dtype=jnp.float32) * 2.0 / HEAD_SIZE)
    angles = positions[:, None] * frequency[None, :]
    return (jnp.cos(angles)[:, None, :], jnp.sin(angles)[:, None, :])


def apply_rotary(value_rows, cosine_table, sine_values, direction):
    half_dim = HEAD_SIZE // 2
    first_half = value_rows[..., :half_dim]
    second_half = value_rows[..., half_dim:]
    return jnp.concatenate(
        [
            first_half * cosine_table - direction * second_half * sine_values,
            second_half * cosine_table + direction * first_half * sine_values,
        ],
        axis=-1,
    )


def norm_back(grad_normed, inputs, inv_root, gain):
    grad_gain = jnp.sum(grad_normed * inputs * inv_root, axis=0)
    scaled = grad_normed * gain.astype(jnp.float32)
    grad_inputs = inv_root * (
        scaled - inputs * inv_root * inv_root * jnp.mean(scaled * inputs, axis=-1, keepdims=True)
    )
    return (grad_gain, grad_inputs)


def row_product(left, right):
    return jnp.einsum("tc,tf->cf", left, right, preferred_element_type=jnp.float32)


def blockwise_layer(
    tokens,
    cotangent,
    gain_attn,
    w_query,
    key_weight,
    value_weight,
    w_out,
    gain_ffn,
    w_gate,
    w_up,
    w_down,
):
    token_rows = tokens.shape[0]
    head_group = QUERY_HEADS // KEY_VALUE_HEADS
    key_value_width = KEY_VALUE_HEADS * HEAD_SIZE
    query_width = QUERY_HEADS * HEAD_SIZE
    score_scale = HEAD_SIZE ** (-0.5)
    ctx_count = lax.axis_size("ctx")
    ctx_rank = lax.axis_index("ctx")
    first_row = ctx_rank * token_rows
    query_pos = first_row + jnp.arange(token_rows, dtype=jnp.int32)
    attn_full = (
        lax.all_gather(gain_attn, ("dp", "ctx"), axis=0, tiled=True),
        lax.all_gather(w_query, ("dp", "ctx"), axis=0, tiled=True),
        lax.all_gather(key_weight, ("dp", "ctx"), axis=0, tiled=True),
        lax.all_gather(value_weight, ("dp", "ctx"), axis=0, tiled=True),
        lax.all_gather(w_out, ("dp", "ctx"), axis=0, tiled=True),
    )
    gain_one, query_full, key_full, value_full, out_full = attn_full
    inputs = tokens.astype(jnp.float32)
    inv_one = lax.rsqrt(jnp.mean(inputs * inputs, axis=-1, keepdims=True) + NORM_EPS)
    first_normed = (inputs * inv_one * gain_one.astype(jnp.float32)).astype(jnp.bfloat16)
    query_unrotated = jnp.dot(first_normed, query_full, preferred_element_type=jnp.float32).reshape(
        token_rows, QUERY_HEADS, HEAD_SIZE
    )
    key_unrotated = jnp.dot(first_normed, key_full, preferred_element_type=jnp.float32).reshape(
        token_rows, KEY_VALUE_HEADS, HEAD_SIZE
    )
    value_raw = jnp.dot(first_normed, value_full, preferred_element_type=jnp.float32)
    cosine_table, sine_values = rope_tables(first_row, token_rows)
    query_rows = (
        apply_rotary(query_unrotated, cosine_table, sine_values, 1.0)
        .astype(jnp.bfloat16)
        .reshape(token_rows, KEY_VALUE_HEADS, head_group, HEAD_SIZE)
    )
    keys_rot = (
        apply_rotary(key_unrotated, cosine_table, sine_values, 1.0)
        .astype(jnp.bfloat16)
        .reshape(token_rows, key_value_width)
    )
    kv_local = jnp.concatenate([keys_rot, value_raw.astype(jnp.bfloat16)], axis=1)
    starting = (
        jnp.full((KEY_VALUE_HEADS, head_group, token_rows), MASK_FILL, jnp.float32),
        jnp.zeros((KEY_VALUE_HEADS, head_group, token_rows), jnp.float32),
        jnp.zeros((token_rows, KEY_VALUE_HEADS, head_group, HEAD_SIZE), jnp.float32),
    )
    sequence_portion = lax.all_gather(kv_local, "ctx", axis=0, tiled=True)

    def update(state):
        run_max, run_sum, run_acc = state
        block_count = sequence_portion.shape[0]
        key_portion = sequence_portion[:, :key_value_width].reshape(
            block_count, KEY_VALUE_HEADS, HEAD_SIZE
        )
        value_portion = sequence_portion[:, key_value_width:].reshape(
            block_count, KEY_VALUE_HEADS, HEAD_SIZE
        )
        scores = (
            jnp.einsum(
                "tkgd,skd->kgts", query_rows, key_portion, preferred_element_type=jnp.float32
            )
            * score_scale
        )
        key_pos = jnp.arange(block_count, dtype=jnp.int32)
        allowed = key_pos[None, :] <= query_pos[:, None]
        scores = jnp.where(allowed, scores, MASK_FILL)
        new_max = jnp.maximum(run_max, jnp.max(scores, axis=-1))
        expo = jnp.exp(scores - new_max[..., None])
        new_sum = jnp.sum(expo, axis=-1)
        added = jnp.einsum(
            "kgts,skd->tkgd",
            expo.astype(jnp.bfloat16),
            value_portion,
            preferred_element_type=jnp.float32,
        )
        return (new_max, new_sum, added)

    def unchanged(state):
        return state

    run_max, run_sum, run_acc = lax.cond(
        jnp.int32(0) <= first_row + token_rows - 1, update, unchanged, starting
    )
    attn_four = run_acc / jnp.transpose(run_sum, (2, 0, 1))[..., None]
    log_total = run_max + jnp.log(run_sum)
    attn_out = attn_four.reshape(token_rows, query_width)
    attn_low = attn_out.astype(jnp.bfloat16)
    middle = inputs + jnp.dot(attn_low, out_full, preferred_element_type=jnp.float32)
    mlp_full = (
        lax.all_gather(gain_ffn, ("dp", "ctx"), axis=0, tiled=True),
        lax.all_gather(w_gate, ("dp", "ctx"), axis=0, tiled=True),
        lax.all_gather(w_up, ("dp", "ctx"), axis=0, tiled=True),
        lax.all_gather(w_down, ("dp", "ctx"), axis=0, tiled=True),
    )
    gain_two, gate_full, up_full, down_full = mlp_full
    inv_two = lax.rsqrt(jnp.mean(middle * middle, axis=-1, keepdims=True) + NORM_EPS)
    normed_two = (middle * inv_two * gain_two.astype(jnp.float32)).astype(jnp.bfloat16)
    gate_value = jnp.dot(normed_two, gate_full, preferred_element_type=jnp.float32)
    up_value = jnp.dot(normed_two, up_full, preferred_element_type=jnp.float32)
    sigmoid_gate = jax.nn.sigmoid(gate_value)
    silu_gate = gate_value * sigmoid_gate
    hidden = (silu_gate * up_value).astype(jnp.bfloat16)
    output = (middle + jnp.dot(hidden, down_full, preferred_element_type=jnp.float32)).astype(
        jnp.bfloat16
    )
    mlp_back = (
        lax.all_gather(gain_ffn, ("dp", "ctx"), axis=0, tiled=True),
        lax.all_gather(w_gate, ("dp", "ctx"), axis=0, tiled=True),
        lax.all_gather(w_up, ("dp", "ctx"), axis=0, tiled=True),
        lax.all_gather(w_down, ("dp", "ctx"), axis=0, tiled=True),
    )
    gain_two_back, gate_back, up_back, down_back = mlp_back
    grad_out = cotangent.astype(jnp.float32)
    grad_hidden = jnp.einsum("td,fd->tf", cotangent, down_back, preferred_element_type=jnp.float32)
    grad_gate = (
        grad_hidden * up_value * sigmoid_gate * (1.0 + gate_value * (1.0 - sigmoid_gate))
    ).astype(jnp.bfloat16)
    grad_up = (grad_hidden * silu_gate).astype(jnp.bfloat16)
    grad_normed_two = jnp.einsum(
        "tf,cf->tc", grad_gate, gate_back, preferred_element_type=jnp.float32
    ) + jnp.einsum("tf,cf->tc", grad_up, up_back, preferred_element_type=jnp.float32)
    grad_gain_two, grad_middle_norm = norm_back(grad_normed_two, middle, inv_two, gain_two_back)
    grad_middle = grad_out + grad_middle_norm
    gate_up_pair = jnp.concatenate([grad_gate, grad_up], axis=1)
    gate_up_sum = lax.psum_scatter(
        row_product(normed_two, gate_up_pair), ("dp", "ctx"), scatter_dimension=0, tiled=True
    )
    grad_down_sum = lax.psum_scatter(
        row_product(hidden, cotangent), ("dp", "ctx"), scatter_dimension=0, tiled=True
    )
    attn_back = (
        lax.all_gather(gain_attn, ("dp", "ctx"), axis=0, tiled=True),
        lax.all_gather(w_query, ("dp", "ctx"), axis=0, tiled=True),
        lax.all_gather(key_weight, ("dp", "ctx"), axis=0, tiled=True),
        lax.all_gather(value_weight, ("dp", "ctx"), axis=0, tiled=True),
        lax.all_gather(w_out, ("dp", "ctx"), axis=0, tiled=True),
    )
    gain_one_back, query_back, key_back, value_back, out_back = attn_back
    grad_branch = grad_middle.astype(jnp.bfloat16)
    attention_gradient = jnp.einsum(
        "td,cd->tc", grad_branch, out_back, preferred_element_type=jnp.float32
    ).astype(jnp.bfloat16)
    gradient_quad = attention_gradient.reshape(token_rows, KEY_VALUE_HEADS, head_group, HEAD_SIZE)
    delta_rows = jnp.transpose(
        jnp.sum(gradient_quad.astype(jnp.float32) * attn_four, axis=-1), (1, 2, 0)
    )

    def pair_terms(key_value_block, key_first):
        block_count = key_value_block.shape[0]
        key_portion = key_value_block[:, :key_value_width].reshape(
            block_count, KEY_VALUE_HEADS, HEAD_SIZE
        )
        value_portion = key_value_block[:, key_value_width:].reshape(
            block_count, KEY_VALUE_HEADS, HEAD_SIZE
        )
        scores = (
            jnp.einsum(
                "tkgd,skd->kgts", query_rows, key_portion, preferred_element_type=jnp.float32
            )
            * score_scale
        )
        key_pos = key_first + jnp.arange(block_count, dtype=jnp.int32)
        allowed = key_pos[None, :] <= query_pos[:, None]
        scores = jnp.where(allowed, scores, MASK_FILL)
        probs = jnp.exp(scores - log_total[..., None])
        grad_probs = jnp.einsum(
            "tkgd,skd->kgts", gradient_quad, value_portion, preferred_element_type=jnp.float32
        )
        grad_scores = (probs * (grad_probs - delta_rows[..., None])).astype(jnp.bfloat16)
        grad_query = (
            jnp.einsum(
                "kgts,skd->tkgd", grad_scores, key_portion, preferred_element_type=jnp.float32
            )
            * score_scale
        )
        grad_keys = (
            jnp.einsum(
                "kgts,tkgd->skd", grad_scores, query_rows, preferred_element_type=jnp.float32
            )
            * score_scale
        )
        grad_values = jnp.einsum(
            "kgts,tkgd->skd",
            probs.astype(jnp.bfloat16),
            gradient_quad,
            preferred_element_type=jnp.float32,
        )
        return (
            grad_query,
            jnp.concatenate(
                [
                    grad_keys.reshape(block_count, key_value_width),
                    grad_values.reshape(block_count, key_value_width),
                ],
                axis=1,
            ),
        )

    def add_pair(operands):
        kv_use, key_first, grad_query, grad_now = operands
        more_query, more_kv = pair_terms(kv_use, key_first)
        return (grad_query + more_query, grad_now + more_kv)

    def keep_pair(operands):
        return (operands[2], operands[3])

    def cycle_step(step, state):
        kv_now, grad_now, grad_query = state
        owner = (ctx_rank - step + ctx_count) % ctx_count
        kv_next = passed_along(kv_now, "ctx", 1)
        grad_query, grad_now = lax.cond(
            owner <= ctx_rank,
            add_pair,
            keep_pair,
            (kv_now, owner * token_rows, grad_query, grad_now),
        )
        grad_next = shifted(grad_now.astype(jnp.bfloat16), "ctx", 1).astype(grad_now.dtype)
        return (kv_next, grad_next, grad_query)

    cycle_start = (
        kv_local,
        jnp.zeros((token_rows, 2 * key_value_width), jnp.float32),
        jnp.zeros((token_rows, KEY_VALUE_HEADS, head_group, HEAD_SIZE), jnp.float32),
    )
    kv_final, key_value_gradient, grad_query = lax.fori_loop(0, ctx_count, cycle_step, cycle_start)
    grad_query_raw = (
        apply_rotary(
            grad_query.reshape(token_rows, QUERY_HEADS, HEAD_SIZE), cosine_table, sine_values, -1.0
        )
        .reshape(token_rows, query_width)
        .astype(jnp.bfloat16)
    )
    grad_key_raw = (
        apply_rotary(
            key_value_gradient[:, :key_value_width].reshape(token_rows, KEY_VALUE_HEADS, HEAD_SIZE),
            cosine_table,
            sine_values,
            -1.0,
        )
        .reshape(token_rows, key_value_width)
        .astype(jnp.bfloat16)
    )
    grad_value_raw = key_value_gradient[:, key_value_width:].astype(jnp.bfloat16)
    grad_normed_one = (
        jnp.einsum("tq,cq->tc", grad_query_raw, query_back, preferred_element_type=jnp.float32)
        + jnp.einsum("tq,cq->tc", grad_key_raw, key_back, preferred_element_type=jnp.float32)
        + jnp.einsum("tq,cq->tc", grad_value_raw, value_back, preferred_element_type=jnp.float32)
    )
    grad_gain_one, grad_input_norm = norm_back(grad_normed_one, inputs, inv_one, gain_one_back)
    grad_tokens = grad_middle + grad_input_norm
    projection_grads = jnp.concatenate([grad_query_raw, grad_key_raw, grad_value_raw], axis=1)
    qkv_sum = lax.psum_scatter(
        row_product(first_normed, projection_grads), ("dp", "ctx"), scatter_dimension=0, tiled=True
    )
    grad_out_sum = lax.psum_scatter(
        row_product(attn_low, grad_branch), ("dp", "ctx"), scatter_dimension=0, tiled=True
    )
    gain_sums = (
        lax.psum_scatter(grad_gain_one, ("dp", "ctx"), scatter_dimension=0, tiled=True),
        lax.psum_scatter(grad_gain_two, ("dp", "ctx"), scatter_dimension=0, tiled=True),
    )
    ff_width = w_gate.shape[1]
    return (
        output,
        grad_tokens,
        gain_sums[0],
        qkv_sum[:, :query_width],
        qkv_sum[:, query_width : query_width + key_value_width],
        qkv_sum[:, query_width + key_value_width :],
        grad_out_sum,
        gain_sums[1],
        gate_up_sum[:, :ff_width],
        gate_up_sum[:, ff_width:],
        grad_down_sum,
    )


CUBE = 8
BITS = (0, 1, 2)
HEAD_LANES = 128
HALF_LANES = 64
SHARE = 4 * HEAD_LANES
F32 = jnp.float32
BF16 = jnp.bfloat16


class Here:
    def __init__(self):
        dp = lax.axis_index("dp")
        ctx = lax.axis_index("ctx")
        self.core = lax.rem(dp, 2)
        self.far = ctx // 4
        self.own = (dp // 2, lax.rem(ctx // 2, 2), lax.rem(ctx, 2))
        self.shard = self.shard_of(self.own)
        self.at_home = self.own[0] == self.far
        self.sibling = self.device(self.own, core=1 - self.core)
        self.across = self.device(self.own, far=1 - self.far)

    def shard_of(self, bits):
        return bits[0] * 4 + bits[1] * 2 + bits[2]

    def device(self, bits, core=None, far=None):
        core = self.core if core is None else core
        far = self.far if far is None else far
        return (bits[0] * 2 + core, far * 4 + bits[1] * 2 + bits[2])

    def flip(self, *turned, of=None):
        bits = self.own if of is None else of
        return tuple(1 - bit if index in turned else bit for index, bit in enumerate(bits))

    def next(self, bit):
        return self.device(self.flip(bit))

    def others(self):
        return [
            self.flip(*[bit for bit in BITS if code >> (2 - bit) & 1]) for code in range(1, CUBE)
        ]

    def greet(self, partners):
        barrier = pltpu.get_barrier_semaphore()
        for partner in partners:
            pl.semaphore_signal(
                barrier, inc=1, device_id=partner, device_id_type=pl.DeviceIdType.MESH
            )
        pl.semaphore_wait(barrier, len(partners))

    def peers(self):
        return [self.device(bits) for bits in self.others()]

    def same_core(self):
        beyond = [self.device(bits, far=1 - self.far) for bits in self.others() + [self.own]]
        return self.peers() + beyond


def make_send(source, target, sems, device):
    return pltpu.make_async_remote_copy(
        src_ref=source,
        dst_ref=target,
        send_sem=sems[0],
        recv_sem=sems[1],
        device_id=device,
        device_id_type=pl.DeviceIdType.MESH,
    )


def send(*operands):
    copy = make_send(*operands)
    copy.start()
    return copy


class Sems:
    def __init__(self, sent, received):
        self.sent, self.received, self.used = sent, received, 0

    def __call__(self):
        pair = (self.sent.at[self.used], self.received.at[self.used])
        self.used += 1
        return pair


def run_all(*generators):
    live = list(generators)
    while live:
        for one in list(live):
            try:
                next(one)
            except StopIteration:
                live.remove(one)


def play(script, transfers, actions):
    actions = {name: list(some) for name, some in actions.items()}
    for name in script:
        if name in actions:
            actions[name].pop(0)()
        else:
            next(transfers[name], None)
    run_all(*transfers.values())


def in_step(live):
    live = list(live)
    while live:
        for one in list(live):
            try:
                next(one)
            except StopIteration:
                live.remove(one)
        yield


ORDERS = ((0, 1, 2), (1, 2, 0), (2, 0, 1))
ORDERS_Z_FIRST = ((1, 0, 2), (1, 2, 0))


def gather_cube(here, place_of, order, sems, source=None):
    a, b, c = order
    to = lambda bits, bit: send(place_of(bits), place_of(bits), sems(), here.next(bit))
    from_a, from_b = here.flip(a), here.flip(b)
    own = place_of(here.own)
    pairs = [sems() for _ in order]
    first = lambda block: [
        make_send(block, own, pair, here.next(bit)) for pair, bit in zip(pairs, order)
    ]
    a0, b0, c0 = first(own)
    if source is None:
        for copy in (a0, b0, c0):
            copy.start()
    else:

        @pl.when(here.at_home)
        def _():
            for copy in first(source):
                copy.start()

        yield
        yield

        @pl.when(jnp.logical_not(here.at_home))
        def _():
            for copy in (a0, b0, c0):
                copy.start()

    yield
    a0.wait_recv()
    b1, c1 = to(from_a, b), to(from_a, c)
    yield
    b0.wait_recv()
    c2 = to(from_b, c)
    yield
    b1.wait_recv()
    c3 = to(here.flip(a, b), c)
    yield
    for copy in (c0, c1, c2, c3):
        copy.wait_recv()
    for copy in (a0, b0, b1, c0, c1, c2, c3):
        copy.wait_send()


def gather_cube_parts(here, place_of, size, orders, sems, source=None):
    step = size // len(orders)
    live = []
    for index, order in enumerate(orders):
        part = pl.ds(index * step, step)
        live.append(
            gather_cube(
                here,
                functools.partial(place_of, part=part),
                order,
                sems,
                None if source is None else source.at[:, part],
            )
        )
    return in_step(live)


def total_of(*refs):
    total = refs[0][...].astype(F32)
    for ref in refs[1:]:
        total = total + ref[...].astype(F32)
    return total


PAIRS = (((0, 1, 2), (0, 1)), ((1, 2), (0, 2)), ((0,), (2,)), ((1,), ()))


class ReduceStream:
    def __init__(self, here, part_of, slots, out, order, sems):
        self.here, self.part_of, self.slots, self.out = here, part_of, slots, out
        c, b, a = self.order = order
        self.first = [(c, b, a), (c, b), (c, a), (c,)]
        self.copies = [None] * (CUBE - 1)
        self.sems = [sems() for _ in range(CUBE - 1)]
        self.made = set()

    def send(self, turned, slot, bit):
        self.copies[slot] = send(
            self.part_of(self.here.flip(*turned)),
            self.slots(slot),
            self.sems[slot],
            self.here.next(bit),
        )

    def add(self, turned, *slots):
        for slot in slots:
            self.copies[slot].wait_recv()
        spot = self.part_of(self.here.flip(*turned))
        spot[...] = total_of(spot, *[self.slots(slot) for slot in slots]).astype(BF16)

    def after(self, pair):
        c, b, a = self.order
        before = set(self.made)
        self.made |= {frozenset(turned) for turned in PAIRS[pair]}
        for slot, turned in enumerate(self.first):
            if frozenset(turned) in self.made - before:
                self.send(turned, slot, c)
        if self.copies[4] is None and self.copies[0] is not None and frozenset((b, a)) in self.made:
            self.add((b, a), 0)
            self.send((b, a), 4, b)
        if self.copies[5] is None and self.copies[1] is not None and frozenset((b,)) in self.made:
            self.add((b,), 1)
            self.send((b,), 5, b)

    def finish(self):
        _, b, a = self.order
        self.add((a,), 2, 4)
        self.send((a,), 6, a)
        yield
        for slot in (3, 5, 6):
            self.copies[slot].wait_recv()
        self.out[...] = total_of(
            self.part_of(self.here.own), self.slots(3), self.slots(5), self.slots(6)
        )
        yield
        for copy in self.copies:
            copy.wait_send()


def reductions(here, part, slots, out, orders, sems):
    width = out.shape[1] // len(orders)
    return [
        ReduceStream(
            here,
            lambda bits, columns=columns: part.at[here.shard_of(bits), :, columns],
            lambda slot, columns=columns: slots.at[slot, :, columns],
            out.at[:, columns],
            order,
            sems,
        )
        for columns, order in [
            (pl.ds(index * width, width), order) for index, order in enumerate(orders)
        ]
    ]


def swap_home(here, source, target, relay, local_sem, sems, beyond=None):
    beyond = target if beyond is None else beyond
    half = source.shape[1] // 2
    left, right = pl.ds(0, half), pl.ds(half, half)
    there = here.device(here.flip(0), far=1 - here.far)
    local = pltpu.make_async_copy(source, target, local_sem)
    straight = make_send(source.at[:, left], beyond.at[:, left], sems(), there)
    aside = make_send(source.at[:, right], relay, sems(), here.next(0))
    onward = make_send(relay, target.at[:, right], sems(), here.across)

    @pl.when(here.at_home)
    def _():
        local.start()

    @pl.when(jnp.logical_not(here.at_home))
    def _():
        aside.start()
        straight.start()

    yield

    @pl.when(here.at_home)
    def _():
        aside.wait_recv()
        onward.start()

    yield

    @pl.when(here.at_home)
    def _():
        local.wait()

    @pl.when(jnp.logical_not(here.at_home))
    def _():
        straight.wait_recv()
        onward.wait_recv()
        straight.wait_send()
        aside.wait_send()

    yield

    @pl.when(here.at_home)
    def _():
        onward.wait_send()


def spread(here, place_of, sems, ready=()):
    for copy in ready:
        copy.wait()
    over = send(place_of(here.far), place_of(here.far), sems(), here.across)
    beside = send(place_of(here.far), place_of(here.far), sems(), here.sibling)
    yield
    over.wait_recv()
    last = send(place_of(1 - here.far), place_of(1 - here.far), sems(), here.sibling)
    yield
    beside.wait_recv()
    last.wait_recv()
    for copy in (over, beside, last):
        copy.wait_send()


def gather_columns(here, chunks, target, local_sem, sems):
    x, z, y = here.own
    place = target.at[x, here.core, here.far, z, y]
    local = pltpu.make_async_copy(chunks.at[here.shard], place, local_sem)
    local.start()
    copies = [
        send(chunks.at[here.shard_of(bits)], place, sems(), here.device(bits))
        for bits in here.others()
    ]
    yield
    yield from spread(
        here, lambda far: target.at[:, here.core, far], sems, copies + [local]
    )


ANY = pl.BlockSpec(memory_space=pltpu.MemorySpace.HBM)
VMEM = pl.BlockSpec(memory_space=pltpu.MemorySpace.VMEM)
VMEM_BYTES = 62 * 2**20


def params(collective_id):
    return pltpu.CompilerParams(
        collective_id=collective_id, has_side_effects=True, vmem_limit_bytes=VMEM_BYTES
    )


def dma_sems(count):
    return [pltpu.SemaphoreType.DMA((count,)), pltpu.SemaphoreType.DMA((count,))]


def half_blocks(block):
    return pltpu.VMEM((block[0], block[1] // 2), BF16)


QUERY_TILE = 256
SCRIPT = (
    "xqgxhxqxcoxdxqcxogcqxo1c1o1chgo1c1oababadogbabhaboc",
    "PPPPgdgdhhAAAAGfBfBBBGjGisjiss",
    "Npp2222f3t3t3t3t4kitj4wktwtrrNvnvrrnrnrrvuijfukwjuuu",
)
ORDERS_SPARE_Z = ((1, 0, 2), (1, 2, 0), (0, 1, 2), (2, 1, 0))
ORDERS_Z_LAST = ((0, 2, 1), (2, 0, 1))
ORDERS_ALL = ORDERS + ((0, 2, 1), (1, 0, 2), (2, 1, 0))
FRONT_ORDERS = dict(x=ORDERS_ALL, c=ORDERS_SPARE_Z, o=ORDERS_SPARE_Z, a=ORDERS_ALL)
BACK_ORDERS = dict(r=ORDERS_ALL, t=ORDERS_ALL, s=ORDERS)
NT = (((1,), (1,)), ((), ()))
TN = (((0,), (0,)), ((), ()))


def dot(left, right):
    return jnp.dot(left, right, preferred_element_type=F32)


def dot_nt(left, right):
    return lax.dot_general(left, right, NT, preferred_element_type=F32)


def dot_tn(left, right):
    return lax.dot_general(left, right, TN, preferred_element_type=F32)


def rotate(head, cosine, sine):
    return head * cosine + pltpu.roll(head, HALF_LANES, 1) * sine


def scores_of(keys, queries):
    count = keys.shape[0] - QUERY_TILE
    parts = []
    if count > 0:
        parts.append(dot_nt(keys[:count], queries) * HEAD_SIZE**-0.5)
    last = dot_nt(keys[count:], queries) * HEAD_SIZE**-0.5
    key = lax.broadcasted_iota(jnp.int32, last.shape, 0)
    query = lax.broadcasted_iota(jnp.int32, last.shape, 1)
    parts.append(jnp.where(key <= query, last, MASK_FILL))
    return parts


def attend_tile(q, k, v_t, o_t, ob, lse, group, tile):
    rows = pl.ds(tile * QUERY_TILE, QUERY_TILE)
    count = (tile + 1) * QUERY_TILE
    parts = scores_of(k[:count, :], q[group, rows, :])
    top = jnp.max(parts[-1], axis=0, keepdims=True)
    for part in parts[:-1]:
        top = jnp.maximum(top, jnp.max(part, axis=0, keepdims=True))
    total = jnp.zeros_like(top)
    result = None
    first = 0
    for part in parts:
        expo = jnp.exp(part - top)
        total = total + jnp.sum(expo, axis=0, keepdims=True)
        added = dot(v_t[:, first : first + part.shape[0]], expo.astype(BF16))
        result = added if result is None else result + added
        first += part.shape[0]
    result = result / total
    o_t[group, :, rows] = result
    ob[group * HEAD_SIZE : (group + 1) * HEAD_SIZE, rows] = result[:HEAD_SIZE].astype(BF16)
    lse[group, :, rows] = top + jnp.log(total)


def spaced(head):
    half = HEAD_SIZE // 2
    gap = jnp.zeros((head.shape[0], HALF_LANES - half), head.dtype)
    return jnp.concatenate([head[:, :half], gap, head[:, half:], gap], axis=1)


def packed(head):
    half = HEAD_SIZE // 2
    return jnp.concatenate([head[:, :half], head[:, HALF_LANES : HALF_LANES + half]], axis=1)


def as_column(row):
    size = row.shape[1]
    same = lax.broadcasted_iota(jnp.int32, (size, size), 0) == lax.broadcasted_iota(
        jnp.int32, (size, size), 1
    )
    return jnp.sum(jnp.where(same, row, 0.0), axis=1, keepdims=True)


def cut_projections(w_query, key_weight, value_weight, gain_attn, gain_ffn, chunks):
    query, key, value = (ref[...].astype(F32) for ref in (w_query, key_weight, value_weight))
    rows = query.shape[0]
    gains = [as_column(ref[...].astype(F32)) for ref in (gain_attn, gain_ffn)]
    gap = jnp.zeros((rows, HEAD_LANES - HEAD_SIZE - 2), F32)
    head = lambda weight, index: weight[:, index * HEAD_SIZE : (index + 1) * HEAD_SIZE]
    for shard in range(CUBE):
        parts = [
            spaced(head(query, 2 * shard)),
            spaced(head(query, 2 * shard + 1)),
            spaced(head(key, shard)),
            jnp.concatenate([head(value, shard), *gains, gap], axis=1),
        ]
        chunks[shard] = jnp.concatenate(parts, axis=1).astype(BF16)


def hidden_lanes(shard, part, lanes):
    x, zy = divmod(shard, 4)
    first = (x * 16 + part * 4 + zy) * lanes
    return slice(first, first + lanes)


def chunk_lanes(part, lanes):
    first = (part // 2 * 4 + part % 2) * lanes
    return slice(first, first + lanes), slice(first + 2 * lanes, first + 3 * lanes)


def cut_hidden(w_gate, w_up, chunks, half):
    lanes = chunks.shape[2] // 8
    for shard in range(CUBE):
        for part in (2 * half, 2 * half + 1):
            place = hidden_lanes(shard, part, lanes)
            gate, up = chunk_lanes(part, lanes)
            chunks[shard, :, gate] = w_gate[:, place]
            chunks[shard, :, up] = w_up[:, place]


def norm_after_attention(shards, own, x_all, ob_all, w_o, gains, y1_own):
    _, block_rows, width = x_all.shape
    rows = pl.ds(shards[0] * block_rows, len(shards) * block_rows)
    ob_t = ob_all[:, :, rows].reshape(width, len(shards) * block_rows)
    x = x_all[pl.ds(shards[0], len(shards))].reshape(len(shards) * block_rows, width)
    y1 = x.astype(F32) + dot_tn(ob_t, w_o[...].reshape(width, width))
    inv_root = lax.rsqrt(jnp.mean(y1 * y1, axis=-1, keepdims=True) + NORM_EPS)
    h2 = (y1 * inv_root * gains[1:2, :]).astype(BF16)
    for index, shard in enumerate(shards):
        block = slice(index * block_rows, (index + 1) * block_rows)
        x_all[shard] = h2[block]

        @pl.when(own == shard)
        def _():
            y1_own[...] = y1[block]


def feed_forward(half, shards, h2_all, ct_all, w_gu, w_d, hidden, d_gu, out_part, dh2_part):
    _, block_rows, width = h2_all.shape
    share = d_gu.shape[1] // 4
    pair = lambda ref: jnp.concatenate([ref[shard] for shard in shards], axis=0)
    rows_of = [
        pl.ds(pl.multiple_of(shard * block_rows, block_rows), block_rows) for shard in shards
    ]
    both = pl.ds(half * 2 * share, 2 * share)
    weight = w_gu[:, :, :, :, :, :, both].reshape(width, 2 * share)
    gate_up = dot(pair(h2_all), weight)
    gate, up = gate_up[:, :share], gate_up[:, share:]
    sig = 1.0 / (1.0 + jnp.exp(-gate))
    silu = gate * sig
    kept = (silu * up).astype(BF16)
    down = w_d[0, half].reshape(share, width)
    d_hidden = dot_nt(pair(ct_all), down)
    d_gate = (d_hidden * up * sig * (1.0 + gate * (1.0 - sig))).astype(BF16)
    d_up = (d_hidden * silu).astype(BF16)
    d_both = jnp.concatenate([d_gate, d_up], axis=1)
    dh2 = dot_nt(d_both, weight)
    out = dot(kept, down)
    for index, (shard, rows) in enumerate(zip(shards, rows_of)):
        block = slice(index * block_rows, (index + 1) * block_rows)
        hidden[rows, pl.ds(half * share, share)] = kept[block]
        d_gu[rows, both] = d_both[block]
        for total, added in ((dh2_part, dh2), (out_part, out)):
            more = added[block]
            if half == 1:
                more = more + total[shard].astype(F32)
            total[shard] = more.astype(BF16)


def attend_back_tile(q, k, k_t, v, do_t, o_t, lse, dk, dv, group, tile):
    rows = pl.ds(tile * QUERY_TILE, QUERY_TILE)
    count = (tile + 1) * QUERY_TILE
    q_rows = q[group, rows, :]
    do_rows = do_t[group * HEAD_SIZE : (group + 1) * HEAD_SIZE, rows]
    do_rows = jnp.concatenate(
        [do_rows, jnp.zeros((HEAD_LANES - HEAD_SIZE, QUERY_TILE), BF16)], axis=0
    )
    delta = jnp.sum(do_rows.astype(F32) * o_t[group, :, rows], axis=0, keepdims=True)
    log_total = lse[group, :, rows]
    dq_t = None
    first = 0
    for part in scores_of(k[:count, :], q_rows):
        keys = slice(first, first + part.shape[0])
        probs = jnp.exp(part - log_total)
        d_probs = dot(v[keys, :], do_rows)
        d_scores = (probs * (d_probs - delta)).astype(BF16)
        dv[keys, :] += dot_nt(probs.astype(BF16), do_rows)
        dk[keys, :] += dot(d_scores, q_rows)
        added = dot(k_t[:, keys], d_scores)
        dq_t = added if dq_t is None else dq_t + added
        first += part.shape[0]
    return jnp.transpose(dq_t) * HEAD_SIZE**-0.5


def add_rows(total, more, piece):
    if len(total.shape) == 5:
        for z in range(2):
            for y in range(2):
                add_rows(total.at[:, z, y], more.at[:, z, y], piece)
        return

    def body(index, carry):
        rows = pl.ds(pl.multiple_of(index * piece, piece), piece)
        for block in range(total.shape[0]):
            total[block, rows, :] = total_of(
                total.at[block, rows, :], more.at[block, rows, :]
            ).astype(BF16)
        return carry

    lax.fori_loop(0, total.shape[1] // piece, body, 0)


def reduce_copies(here, part, beside, over, sems, piece):
    core, far = here.core, here.far
    first = send(part.at[:, 1 - core, 1 - far], beside.at[0], sems(), here.sibling)
    second = send(part.at[:, 1 - core, far], beside.at[1], sems(), here.sibling)
    yield
    first.wait_recv()
    add_rows(part.at[:, core, 1 - far], beside.at[0], piece)
    third = send(part.at[:, core, 1 - far], over, sems(), here.across)
    second.wait_recv()
    add_rows(part.at[:, core, far], beside.at[1], piece)
    yield
    third.wait_recv()
    add_rows(part.at[:, core, far], over, piece)
    for copy in (first, second, third):
        copy.wait_send()


def scatter_columns(here, part, beside, over, out, local_sem, sems):
    rows = out.shape[1]
    yield from reduce_copies(here, part, beside, over, sems, rows)

    def source(bits):
        return part.at[bits[0], here.core, here.far, bits[1], bits[2]]

    local = pltpu.make_async_copy(source(here.own), out.at[here.shard], local_sem)
    local.start()
    copies = [
        send(source(bits), out.at[here.shard], sems(), here.device(bits)) for bits in here.others()
    ]
    yield
    for copy in copies + [local]:
        copy.wait()


def copy_slots(shape):
    rest = (shape[0], *shape[3:])
    return [pltpu.VMEM((2, *rest), BF16), pltpu.VMEM(rest, BF16)]


def norm_back_rows(grad_normed, rows, gain):
    inv_root = lax.rsqrt(jnp.mean(rows * rows, axis=-1, keepdims=True) + NORM_EPS)
    grad_gain, grad_rows = norm_back(grad_normed, rows, inv_root, gain)
    return grad_gain.reshape(1, -1), grad_rows


def sum_everywhere(here, total, slots, sems):
    peers = here.same_core()
    copies = [send(total, slots.at[index], sems(), device) for index, device in enumerate(peers)]
    yield
    for copy in copies:
        copy.wait()
    total[...] += jnp.sum(slots[: len(peers)], axis=0)
    beside = send(total, slots.at[len(peers)], sems(), here.sibling)
    yield
    beside.wait()
    total[...] += slots[len(peers)]


def layer_kernel(
    tokens, cotangent, w_query, key_weight, value_weight, gain_attn, gain_ffn, w_gate, w_up, down, out,
    cosine, sine,
    output_home, grad_home, gu_rows_too, down_sum, qkv_rows, out_rows, gain_out, gu_rows,
    w_qkv, w_gu, w_d, w_o, x_all, ct_all, ob_all, h1, q, k, v, v_t, o_t, lse, gains, x_own, ct_own, y1_own,
    hidden, d_gu, out_part, dh2_part, dh2, slots, x_relay, ct_relay, qkv, gate_up,
    gu_beside, gu_over, gu_beside_too, gu_over_too, down_beside, down_over, qkv_beside, qkv_over,
    wo_part, wo_beside, wo_over, gain_sums, gain_slots, d_middle, pairs, columns, k_t, dk, dv, out_sum,
    own_rows, local, sent, got,
):
    here = Here()
    sems = Sems(sent, got)
    here.greet(here.same_core() + [here.sibling])
    out_slots, dh1_part, dh1, d_qkv = ct_all, x_all, dh2, hidden
    x, z, y = here.own
    width = tokens.shape[1]
    block_rows = tokens.shape[0]
    seq_rows = CUBE * block_rows

    def swapped(source, target, relay, local_sem, orders):
        swap = swap_home(
            here,
            source,
            target.at[here.shard],
            relay,
            local_sem,
            sems,
            target.at[here.shard_of(here.flip(0))],
        )
        gather = gather_cube_parts(
            here,
            lambda bits, part: target.at[here.shard_of(bits), :, part],
            width,
            orders,
            sems,
            source,
        )
        for _ in range(3):
            next(swap)
            next(gather)
            yield
        run_all(swap)
        yield from gather

    def out_gather():
        mine = w_o.at[x, here.core, here.far, z, y]
        kept = pltpu.make_async_copy(out, mine, local.at[3])
        kept.start()
        over = send(out, mine, sems(), here.across)
        yield
        kept.wait()
        over.wait()
        yield from gather_cube_parts(
            here,
            lambda bits, part: w_o.at[bits[0], here.core, :, bits[1], bits[2], :, part],
            width,
            FRONT_ORDERS["o"],
            sems,
        )
        beside = send(w_o.at[:, here.core], w_o.at[:, here.core], sems(), here.sibling)
        yield
        beside.wait()

    def down_gather():
        kept = pltpu.make_async_copy(down, w_d.at[0, here.core, here.far], local.at[2])
        kept.start()
        yield from spread(here, lambda far: w_d.at[0, here.core, far], sems, [kept])

    def qkv_gather():
        cut_projections(w_query, key_weight, value_weight, gain_attn, gain_ffn, qkv)
        yield from gather_columns(here, qkv, w_qkv, local.at[4], sems)

    ff_share = w_gu.shape[6] // 2
    halves = [pl.ds(half * ff_share, ff_share) for half in range(2)]

    def gate_up_gather(half):
        cut_hidden(w_gate, w_up, gate_up, half)
        yield from gather_columns(
            here,
            gate_up.at[:, :, halves[half]],
            w_gu.at[:, :, :, :, :, :, halves[half]],
            local.at[5 + half],
            sems,
        )

    transfers = dict(
        x=swapped(tokens, x_all, x_relay, local.at[0], FRONT_ORDERS["x"]),
        q=qkv_gather(),
        g=gate_up_gather(0),
        h=gate_up_gather(1),
        o=out_gather(),
        d=down_gather(),
        c=swapped(cotangent, ct_all, ct_relay, local.at[1], FRONT_ORDERS["c"]),
    )
    ob = ob_all.at[here.shard]
    turns = [[here.shard_of(here.flip(*bits)) for bits in turned] for turned in PAIRS]

    def norm():
        turned = jnp.transpose(
            w_qkv[:, :, :, :, :, :, 3 * HEAD_LANES :].astype(F32).reshape(width, HEAD_LANES)
        )
        gains[...] = turned[HEAD_SIZE : HEAD_SIZE + 8]
        x_own[...] = x_all[here.shard]

        def norm_block(index, carry):
            rows = x_all[index].astype(F32)
            inv_root = lax.rsqrt(jnp.mean(rows * rows, axis=-1, keepdims=True) + NORM_EPS)
            place = pl.ds(pl.multiple_of(index * block_rows, block_rows), block_rows)
            h1[place, :] = (rows * inv_root * gains[0:1, :]).astype(BF16)
            return carry

        lax.fori_loop(0, CUBE, norm_block, 0)

    def project():
        def project_tile(index, carry):
            rows = pl.ds(pl.multiple_of(index * QUERY_TILE, QUERY_TILE), QUERY_TILE)
            raw = dot(h1[rows, :], w_qkv[...].reshape(width, SHARE))
            cos_rows, sin_rows = cosine[rows, :], sine[rows, :]
            heads = [raw[:, lane : lane + HEAD_LANES] for lane in range(0, SHARE, HEAD_LANES)]
            q[0, rows, :] = rotate(heads[0], cos_rows, sin_rows).astype(BF16)
            q[1, rows, :] = rotate(heads[1], cos_rows, sin_rows).astype(BF16)
            k[rows, :] = rotate(heads[2], cos_rows, sin_rows).astype(BF16)
            v[rows, :] = heads[3].astype(BF16)
            v_t[:, rows] = jnp.transpose(heads[3]).astype(BF16)
            return carry

        lax.fori_loop(0, seq_rows // QUERY_TILE, project_tile, 0)

    def attend(*tiles):
        for tile in tiles:
            for group in range(2):
                attend_tile(q, k, v_t, o_t, ob, lse, group, tile)
        if tiles[-1] % 2 == 1:
            lanes = pl.ds((tiles[-1] - 1) * QUERY_TILE, 2 * QUERY_TILE)
            transfers["ab"[tiles[-1] // 2]] = gather_cube_parts(
                here,
                lambda bits, part: ob_all.at[here.shard_of(bits), part, lanes],
                ob.shape[0],
                FRONT_ORDERS["a"],
                sems,
            )

    def normed_pair(pair):
        norm_after_attention(
            (2 * pair, 2 * pair + 1), here.shard, x_all, ob_all, w_o, gains, y1_own
        )

    bind = functools.partial
    streams = reductions(here, dh2_part, slots, dh2, BACK_ORDERS["s"], sems)

    def feed(half, pair):
        if half == 0 and pair == 0:
            ct_own[...] = ct_all[here.shard]
        feed_forward(
            half, turns[pair], x_all, ct_all, w_gu, w_d, hidden, d_gu, out_part, dh2_part
        )
        if half == 1:
            for stream in streams:
                stream.after(pair)

    def gate_up_grad(half):
        def quarter(index, carry):
            lanes = pl.ds(pl.multiple_of(index * 4 * HEAD_SIZE, 4 * HEAD_SIZE), 4 * HEAD_SIZE)
            left = x_all[:, :, lanes].reshape(seq_rows, 4 * HEAD_SIZE)
            grad = dot_tn(left, d_gu[:, halves[half]]).astype(BF16)
            place = w_gu.at[index // 2, lax.rem(index, 2), :, :, :, :, halves[half]]
            place[...] = grad.reshape(place.shape)
            return carry

        lax.fori_loop(0, 4, quarter, 0)

    def down_grad():
        def quarter(index, carry):
            lanes = pl.ds(pl.multiple_of(index * HEAD_LANES, HEAD_LANES), HEAD_LANES)
            grad = dot_tn(hidden[:, lanes], ct_all[...].reshape(seq_rows, width)).astype(BF16)
            w_d[0, index // 2, lax.rem(index, 2)] = grad
            return carry

        lax.fori_loop(0, 4, quarter, 0)

    weight_rows = out.shape[0]
    share = 2 * HEAD_SIZE

    def gate_up_reduce(half, beside, over, rows):
        yield from scatter_columns(
            here,
            w_gu.at[:, :, :, :, :, :, halves[half]],
            beside,
            over,
            rows,
            local.at[7 + half],
            sems,
        )

    def down_reduce():
        yield from reduce_copies(here, w_d, down_beside, down_over, sems, 32)
        down_sum[...] = w_d[0, here.core, here.far]

    def to_heads():
        rows = pl.ds(pl.multiple_of(here.shard * block_rows, block_rows), block_rows)
        place = columns.at[:, :, rows]
        mine = pltpu.make_async_copy(pairs.at[here.shard], place, local.at[9])
        mine.start()
        copies = [
            send(pairs.at[here.shard_of(bits)], place, sems(), here.device(bits))
            for bits in here.others()
        ]
        yield
        for copy in copies + [mine]:
            copy.wait()

    def reduce_rows(part, slots, out, orders):
        streams = reductions(here, part, slots, out, orders, sems)
        for pair in range(len(PAIRS)):
            for stream in streams:
                stream.after(pair)
            yield
        yield from in_step([stream.finish() for stream in streams])

    def output_reduce():
        yield from reduce_rows(out_part, out_slots, out_sum, BACK_ORDERS["r"])

    def output_swap():
        own_rows[0] = (y1_own[...] + out_sum[...]).astype(BF16)
        yield from swap_home(here, own_rows.at[0], output_home, ct_relay, local.at[12], sems)

    transfers.update(
        f=gate_up_reduce(0, gu_beside, gu_over, gu_rows),
        s=in_step([stream.finish() for stream in streams]),
        i=gate_up_reduce(1, gu_beside_too, gu_over_too, gu_rows_too),
        j=down_reduce(),
        p=to_heads(),
        r=output_reduce(),
        t=reduce_rows(dh1_part, slots, dh1, BACK_ORDERS["t"]),
        k=scatter_columns(here, w_qkv, qkv_beside, qkv_over, qkv_rows, local.at[10], sems),
        w=scatter_columns(here, wo_part, wo_beside, wo_over, out_rows, local.at[11], sems),
        u=output_swap(),
        v=swap_home(here, own_rows.at[1], grad_home, x_relay, local.at[13], sems),
        n=sum_everywhere(here, gain_sums, gain_slots, sems),
    )

    def norm_two():
        grad_gain, grad_rows = norm_back_rows(dh2[...], y1_own[...], gains[1:2, :])
        gain_sums[...] = jnp.zeros_like(gain_sums)
        gain_sums[1:2, :] = grad_gain
        d_middle[...] = ct_own[...].astype(F32) + grad_rows
        da = d_middle[...].astype(BF16)
        pairs[:, 0] = dot_nt(w_o[...].reshape(width, width), da).astype(BF16).reshape(CUBE, share, block_rows)
        pairs[:, 1] = jnp.transpose(d_middle[...]).astype(BF16).reshape(CUBE, share, block_rows)

    def norm_one():
        grad_gain, grad_rows = norm_back_rows(dh1[...], x_own[...].astype(F32), gains[0:1, :])
        gain_sums[0:1, :] = grad_gain
        own_rows[1] = (d_middle[...] + grad_rows).astype(BF16)

    def attention(tile):
        if tile == 0:
            k_t[...] = jnp.transpose(k[...].astype(F32)).astype(BF16)
            dk[...] = jnp.zeros_like(dk)
            dv[...] = jnp.zeros_like(dv)
        rows = pl.ds(tile * QUERY_TILE, QUERY_TILE)
        for group in range(2):
            dq = attend_back_tile(q, k, k_t, v, columns.at[0], o_t, lse, dk, dv, group, tile)
            d_qkv[rows, group * HEAD_LANES : (group + 1) * HEAD_LANES] = rotate(
                dq, cosine[rows, :], -sine[rows, :]
            ).astype(BF16)
        if rows.start + rows.size == seq_rows:
            d_qkv[:, 2 * HEAD_LANES : 3 * HEAD_LANES] = rotate(
                dk[...] * HEAD_SIZE**-0.5, cosine[...], -sine[...]
            ).astype(BF16)
            d_qkv[:, 3 * HEAD_LANES :] = dv[...].astype(BF16)

    def pair_back(pair):
        shards = [here.shard_of(here.flip(*bits)) for bits in PAIRS[pair]]
        some = jnp.concatenate(
            [
                d_qkv[pl.ds(pl.multiple_of(shard * block_rows, block_rows), block_rows), :]
                for shard in shards
            ],
            axis=0,
        )
        rows = dot_nt(some, w_qkv[...].reshape(width, SHARE)).astype(BF16)
        for index, shard in enumerate(shards):
            dh1_part[shard] = rows[index * block_rows : (index + 1) * block_rows]

    def qkv_grad():

        def quarter(index, carry):
            lanes = pl.ds(pl.multiple_of(index * 4 * HEAD_SIZE, 4 * HEAD_SIZE), 4 * HEAD_SIZE)
            grad = dot_tn(h1[:, lanes], d_qkv[...]).astype(BF16)
            w_qkv[index // 2, lax.rem(index, 2)] = grad.reshape(w_qkv.shape[2:])
            return carry

        lax.fori_loop(0, 4, quarter, 0)

    def out_grad():
        for index in range(4):
            left = ob_all[2 * index : 2 * index + 2].reshape(2 * share, seq_rows)
            grad = dot_nt(left, columns[1]).astype(BF16)
            grad = jnp.concatenate(
                [grad, jnp.zeros((2 * share, wo_part.shape[6] - share), BF16)], axis=1
            )
            wo_part[index // 2, index % 2] = grad.reshape(wo_part.shape[2:])

    bind = functools.partial
    everyone = range(len(PAIRS))
    play(
        "".join(SCRIPT),
        transfers,
        {
            "1": [norm, project, bind(attend, 0), bind(attend, 1), bind(attend, 2, 3)],
            "P": [bind(normed_pair, pair) for pair in everyone],
            "A": [bind(feed, 0, pair) for pair in everyone],
            "B": [bind(feed, 1, pair) for pair in everyone],
            "G": [bind(gate_up_grad, 0), down_grad, bind(gate_up_grad, 1)],
            "N": [norm_two, norm_one],
            "2": [bind(attention, tile) for tile in range(seq_rows // QUERY_TILE)],
            "3": [bind(pair_back, pair) for pair in everyone],
            "4": [qkv_grad, out_grad],
        },
    )
    rank = here.device(here.own)
    rank = rank[0] * CUBE + rank[1]
    sums = jnp.concatenate([gain_sums[...], jnp.zeros((6, width), F32)], axis=0)
    gain_out[...] = pltpu.roll(sums, lax.rem(width - rank * weight_rows, width), 1)[:, :HEAD_LANES]


def layer(tokens, cotangent, w_query, key_weight, value_weight, gain_attn, gain_ffn, w_gate, w_up, down,
          out, cosine, sine):
    operands = (
        tokens, cotangent, w_query, key_weight, value_weight, gain_attn, gain_ffn, w_gate, w_up, down, out,
        cosine, sine,
    )
    rows, width = tokens.shape
    weight_rows = out.shape[0]
    seq_rows = CUBE * rows
    share = 2 * HEAD_SIZE
    ff_share = 4 * down.shape[0]
    by_row = lambda lanes: (2, 2, 2, 2, 2, weight_rows, lanes)
    low = lambda *dims: pltpu.VMEM(dims, BF16)
    wide = lambda *dims: pltpu.VMEM(dims, F32)
    home = lambda *dims: jax.ShapeDtypeStruct(dims, BF16)
    outs = (
        home(rows, width),
        home(rows, width),
        home(CUBE, weight_rows, ff_share),
        home(*down.shape),
        home(CUBE, weight_rows, SHARE),
        home(CUBE, weight_rows, 2 * HEAD_LANES),
        jax.ShapeDtypeStruct((8, HEAD_LANES), F32),
        home(CUBE, weight_rows, ff_share),
    )
    return pl.pallas_call(
        layer_kernel,
        out_shape=outs,
        in_specs=[VMEM] * len(operands),
        out_specs=(VMEM,) * len(outs),
        scratch_shapes=[
            low(*by_row(SHARE)),
            low(*by_row(2 * ff_share)),
            low(1, 2, 2, *down.shape),
            low(*by_row(width)),
            low(CUBE, rows, width),
            low(CUBE, rows, width),
            low(CUBE, share, seq_rows),
            low(seq_rows, width),
            low(2, seq_rows, HEAD_LANES),
            low(seq_rows, HEAD_LANES),
            low(seq_rows, HEAD_LANES),
            low(HEAD_LANES, seq_rows),
            wide(2, HEAD_LANES, seq_rows),
            wide(2, 1, seq_rows),
            wide(8, width),
            low(rows, width),
            low(rows, width),
            wide(rows, width),
            low(seq_rows, ff_share),
            low(seq_rows, 2 * ff_share),
            low(CUBE, rows, width),
            low(CUBE, rows, width),
            wide(rows, width),
            low(CUBE - 1, rows, width),
            half_blocks(tokens.shape),
            half_blocks(tokens.shape),
            low(CUBE, weight_rows, SHARE),
            low(CUBE, weight_rows, 2 * ff_share),
            *copy_slots(by_row(ff_share)),
            *copy_slots(by_row(ff_share)),
            *copy_slots((1, 2, 2, *down.shape)),
            *copy_slots(by_row(SHARE)),
            low(*by_row(2 * HEAD_LANES)),
            *copy_slots(by_row(2 * HEAD_LANES)),
            wide(2, width),
            wide(2 * CUBE, 2, width),
            wide(rows, width),
            low(CUBE, 2, share, rows),
            low(2, share, seq_rows),
            low(HEAD_LANES, seq_rows),
            wide(seq_rows, HEAD_LANES),
            wide(seq_rows, HEAD_LANES),
            wide(rows, width),
            low(2, rows, width),
            pltpu.SemaphoreType.DMA((14,)),
        ]
        + dma_sems(500),
        compiler_params=params(1),
        name="layer",
    )(*operands)


def finish_kernel(
    output_home, grad_home, gu_rows_too, down_sum, qkv_rows, out_rows, gains, gu_rows,
    output, grad, gate, up, down, query, key, value, out, gain_one, gain_two,
):
    output[...] = output_home[...]
    grad[...] = grad_home[...].astype(F32)
    down[...] = down_sum[...].astype(F32)
    lanes = gu_rows.shape[2] // 4
    for shard in range(CUBE):
        for part in range(4):
            place = hidden_lanes(shard, part, lanes)
            gate_lanes, up_lanes = chunk_lanes(part % 2, lanes)
            rows = (gu_rows, gu_rows_too)[part // 2]
            gate[:, place] = rows[shard, :, gate_lanes].astype(F32)
            up[:, place] = rows[shard, :, up_lanes].astype(F32)
    heads = [
        [
            qkv_rows[shard, :, index * HEAD_LANES : (index + 1) * HEAD_LANES].astype(F32)
            for index in range(4)
        ]
        for shard in range(CUBE)
    ]
    query[...] = jnp.concatenate([packed(head) for some in heads for head in some[:2]], axis=1)
    key[...] = jnp.concatenate([packed(some[2]) for some in heads], axis=1)
    value[...] = jnp.concatenate([some[3][:, :HEAD_SIZE] for some in heads], axis=1)
    out[...] = jnp.concatenate(
        [out_rows[shard, :, : 2 * HEAD_SIZE].astype(F32) for shard in range(CUBE)], axis=1
    )
    gain_one[...] = gains[0, : gain_one.shape[0]]
    gain_two[...] = gains[1, : gain_two.shape[0]]


def finish(parts, ff_width):
    rows, width = parts[0].shape
    weight_rows = parts[2].shape[1]
    out = lambda *dims: jax.ShapeDtypeStruct(dims, F32)
    outs = (
        jax.ShapeDtypeStruct((rows, width), BF16),
        out(rows, width),
        out(weight_rows, ff_width),
        out(weight_rows, ff_width),
        out(*parts[3].shape),
        out(weight_rows, width),
        out(weight_rows, width // 2),
        out(weight_rows, width // 2),
        out(weight_rows, width),
        out(weight_rows),
        out(weight_rows),
    )
    return pl.pallas_call(
        finish_kernel,
        out_shape=outs,
        in_specs=[VMEM] * len(parts),
        out_specs=(VMEM,) * len(outs),
        compiler_params=pltpu.CompilerParams(vmem_limit_bytes=VMEM_BYTES),
        name="finish",
    )(*parts)


def spaced_tables(row_count):
    half = HEAD_SIZE // 2
    frequency = np.float32(ROPE_THETA) ** (-np.arange(half, dtype=np.float32) * 2.0 / HEAD_SIZE)
    angles = np.arange(row_count, dtype=np.float32)[:, None] * frequency.astype(np.float32)[None, :]
    pad = ((0, 0), (0, HALF_LANES - half))
    cosine, sine = np.pad(np.cos(angles), pad), np.pad(np.sin(angles), pad)
    return (
        jnp.asarray(np.concatenate([cosine, cosine], axis=1), F32),
        jnp.asarray(np.concatenate([-sine, sine], axis=1), F32),
    )


def split_layer(
    tokens,
    cotangent,
    gain_attn,
    w_query,
    key_weight,
    value_weight,
    w_out,
    gain_ffn,
    w_gate,
    w_up,
    w_down,
):
    block_rows = tokens.shape[0]
    cosine, sine = spaced_tables(block_rows * CUBE)
    parts = layer(
        tokens, cotangent, w_query, key_weight, value_weight, gain_attn[None], gain_ffn[None], w_gate, w_up,
        w_down, w_out, cosine, sine,
    )
    output, grad, gate, up, down, query, key, value, out, gain_one, gain_two = finish(
        parts, w_gate.shape[1]
    )
    return (output, grad, gain_one, query, key, value, out, gain_two, gate, up, down)


def solution(mesh):
    heads_split = mesh.shape["dp"] == 4 and mesh.shape["ctx"] == KEY_VALUE_HEADS
    return jax.shard_map(
        split_layer if heads_split else blockwise_layer,
        mesh=mesh,
        in_specs=(
            P(("dp", "ctx"), None),
            P(("dp", "ctx"), None),
            P(("dp", "ctx")),
            P(("dp", "ctx"), None),
            P(("dp", "ctx"), None),
            P(("dp", "ctx"), None),
            P(("dp", "ctx"), None),
            P(("dp", "ctx")),
            P(("dp", "ctx"), None),
            P(("dp", "ctx"), None),
            P(("dp", "ctx"), None),
        ),
        out_specs=(
            P(("dp", "ctx"), None),
            P(("dp", "ctx"), None),
            P(("dp", "ctx")),
            P(("dp", "ctx"), None),
            P(("dp", "ctx"), None),
            P(("dp", "ctx"), None),
            P(("dp", "ctx"), None),
            P(("dp", "ctx")),
            P(("dp", "ctx"), None),
            P(("dp", "ctx"), None),
            P(("dp", "ctx"), None),
        ),
        check_vma=False,
    )
```

```python
import functools

import jax
import jax.numpy as jnp
import numpy as np
from jax import lax
from jax.experimental import pallas as pl
from jax.experimental.pallas import tpu as pltpu
from jax.sharding import PartitionSpec as P

QUERY_HEADS = 16
KEY_VALUE_HEADS = 8
HEAD_SIZE = 96


NORM_EPS = 1e-05
ROPE_THETA = 100000.0
MASK_FILL = -1e30


def passed_along(value, axis, by):
    peers = lax.axis_size(axis)
    pairs = [(i, i + by) for i in range(peers) if 0 <= i + by < peers]
    return lax.ppermute(value, axis, pairs)


def shifted(block, axis, distance):
    devices = range(lax.axis_size(axis))
    route = [((i - distance) % len(devices), i) for i in devices]
    return lax.ppermute(block, axis, route)


def rope_tables(first_row, block_count):
    half_dim = HEAD_SIZE // 2
    positions = (first_row + jnp.arange(block_count, dtype=jnp.int32)).astype(jnp.float32)
    frequency = ROPE_THETA ** (-jnp.arange(half_dim, dtype=jnp.float32) * 2.0 / HEAD_SIZE)
    angles = positions[:, None] * frequency[None, :]
    return (jnp.cos(angles)[:, None, :], jnp.sin(angles)[:, None, :])


def apply_rotary(value_rows, cosine_table, sine_values, direction):
    half_dim = HEAD_SIZE // 2
    first_half = value_rows[..., :half_dim]
    second_half = value_rows[..., half_dim:]
    return jnp.concatenate(
        [
            first_half * cosine_table - direction * second_half * sine_values,
            second_half * cosine_table + direction * first_half * sine_values,
        ],
        axis=-1,
    )


def norm_back(grad_normed, inputs, inv_root, gain):
    grad_gain = jnp.sum(grad_normed * inputs * inv_root, axis=0)
    scaled = grad_normed * gain.astype(jnp.float32)
    grad_inputs = inv_root * (
        scaled - inputs * inv_root * inv_root * jnp.mean(scaled * inputs, axis=-1, keepdims=True)
    )
    return (grad_gain, grad_inputs)


def row_product(left, right):
    return jnp.einsum("tc,tf->cf", left, right, preferred_element_type=jnp.float32)


def blockwise_layer(
    tokens,
    cotangent,
    gain_attn,
    w_query,
    key_weight,
    value_weight,
    w_out,
    gain_ffn,
    w_gate,
    w_up,
    w_down,
):
    token_rows = tokens.shape[0]
    head_group = QUERY_HEADS // KEY_VALUE_HEADS
    key_value_width = KEY_VALUE_HEADS * HEAD_SIZE
    query_width = QUERY_HEADS * HEAD_SIZE
    score_scale = HEAD_SIZE ** (-0.5)
    ctx_count = lax.axis_size("ctx")
    ctx_rank = lax.axis_index("ctx")
    first_row = ctx_rank * token_rows
    query_pos = first_row + jnp.arange(token_rows, dtype=jnp.int32)
    attn_full = (
        lax.all_gather(gain_attn, ("dp", "ctx"), axis=0, tiled=True),
        lax.all_gather(w_query, ("dp", "ctx"), axis=0, tiled=True),
        lax.all_gather(key_weight, ("dp", "ctx"), axis=0, tiled=True),
        lax.all_gather(value_weight, ("dp", "ctx"), axis=0, tiled=True),
        lax.all_gather(w_out, ("dp", "ctx"), axis=0, tiled=True),
    )
    gain_one, query_full, key_full, value_full, out_full = attn_full
    inputs = tokens.astype(jnp.float32)
    inv_one = lax.rsqrt(jnp.mean(inputs * inputs, axis=-1, keepdims=True) + NORM_EPS)
    first_normed = (inputs * inv_one * gain_one.astype(jnp.float32)).astype(jnp.bfloat16)
    query_unrotated = jnp.dot(first_normed, query_full, preferred_element_type=jnp.float32).reshape(
        token_rows, QUERY_HEADS, HEAD_SIZE
    )
    key_unrotated = jnp.dot(first_normed, key_full, preferred_element_type=jnp.float32).reshape(
        token_rows, KEY_VALUE_HEADS, HEAD_SIZE
    )
    value_raw = jnp.dot(first_normed, value_full, preferred_element_type=jnp.float32)
    cosine_table, sine_values = rope_tables(first_row, token_rows)
    query_rows = (
        apply_rotary(query_unrotated, cosine_table, sine_values, 1.0)
        .astype(jnp.bfloat16)
        .reshape(token_rows, KEY_VALUE_HEADS, head_group, HEAD_SIZE)
    )
    keys_rot = (
        apply_rotary(key_unrotated, cosine_table, sine_values, 1.0)
        .astype(jnp.bfloat16)
        .reshape(token_rows, key_value_width)
    )
    kv_local = jnp.concatenate([keys_rot, value_raw.astype(jnp.bfloat16)], axis=1)
    starting = (
        jnp.full((KEY_VALUE_HEADS, head_group, token_rows), MASK_FILL, jnp.float32),
        jnp.zeros((KEY_VALUE_HEADS, head_group, token_rows), jnp.float32),
        jnp.zeros((token_rows, KEY_VALUE_HEADS, head_group, HEAD_SIZE), jnp.float32),
    )
    sequence_portion = lax.all_gather(kv_local, "ctx", axis=0, tiled=True)

    def update(state):
        run_max, run_sum, run_acc = state
        block_count = sequence_portion.shape[0]
        key_portion = sequence_portion[:, :key_value_width].reshape(
            block_count, KEY_VALUE_HEADS, HEAD_SIZE
        )
        value_portion = sequence_portion[:, key_value_width:].reshape(
            block_count, KEY_VALUE_HEADS, HEAD_SIZE
        )
        scores = (
            jnp.einsum(
                "tkgd,skd->kgts", query_rows, key_portion, preferred_element_type=jnp.float32
            )
            * score_scale
        )
        key_pos = jnp.arange(block_count, dtype=jnp.int32)
        allowed = key_pos[None, :] <= query_pos[:, None]
        scores = jnp.where(allowed, scores, MASK_FILL)
        new_max = jnp.maximum(run_max, jnp.max(scores, axis=-1))
        expo = jnp.exp(scores - new_max[..., None])
        new_sum = jnp.sum(expo, axis=-1)
        added = jnp.einsum(
            "kgts,skd->tkgd",
            expo.astype(jnp.bfloat16),
            value_portion,
            preferred_element_type=jnp.float32,
        )
        return (new_max, new_sum, added)

    def unchanged(state):
        return state

    run_max, run_sum, run_acc = lax.cond(
        jnp.int32(0) <= first_row + token_rows - 1, update, unchanged, starting
    )
    attn_four = run_acc / jnp.transpose(run_sum, (2, 0, 1))[..., None]
    log_total = run_max + jnp.log(run_sum)
    attn_out = attn_four.reshape(token_rows, query_width)
    attn_low = attn_out.astype(jnp.bfloat16)
    middle = inputs + jnp.dot(attn_low, out_full, preferred_element_type=jnp.float32)
    mlp_full = (
        lax.all_gather(gain_ffn, ("dp", "ctx"), axis=0, tiled=True),
        lax.all_gather(w_gate, ("dp", "ctx"), axis=0, tiled=True),
        lax.all_gather(w_up, ("dp", "ctx"), axis=0, tiled=True),
        lax.all_gather(w_down, ("dp", "ctx"), axis=0, tiled=True),
    )
    gain_two, gate_full, up_full, down_full = mlp_full
    inv_two = lax.rsqrt(jnp.mean(middle * middle, axis=-1, keepdims=True) + NORM_EPS)
    normed_two = (middle * inv_two * gain_two.astype(jnp.float32)).astype(jnp.bfloat16)
    gate_value = jnp.dot(normed_two, gate_full, preferred_element_type=jnp.float32)
    up_value = jnp.dot(normed_two, up_full, preferred_element_type=jnp.float32)
    sigmoid_gate = jax.nn.sigmoid(gate_value)
    silu_gate = gate_value * sigmoid_gate
    hidden = (silu_gate * up_value).astype(jnp.bfloat16)
    output = (middle + jnp.dot(hidden, down_full, preferred_element_type=jnp.float32)).astype(
        jnp.bfloat16
    )
    mlp_back = (
        lax.all_gather(gain_ffn, ("dp", "ctx"), axis=0, tiled=True),
        lax.all_gather(w_gate, ("dp", "ctx"), axis=0, tiled=True),
        lax.all_gather(w_up, ("dp", "ctx"), axis=0, tiled=True),
        lax.all_gather(w_down, ("dp", "ctx"), axis=0, tiled=True),
    )
    gain_two_back, gate_back, up_back, down_back = mlp_back
    grad_out = cotangent.astype(jnp.float32)
    grad_hidden = jnp.einsum("td,fd->tf", cotangent, down_back, preferred_element_type=jnp.float32)
    grad_gate = (
        grad_hidden * up_value * sigmoid_gate * (1.0 + gate_value * (1.0 - sigmoid_gate))
    ).astype(jnp.bfloat16)
    grad_up = (grad_hidden * silu_gate).astype(jnp.bfloat16)
    grad_normed_two = jnp.einsum(
        "tf,cf->tc", grad_gate, gate_back, preferred_element_type=jnp.float32
    ) + jnp.einsum("tf,cf->tc", grad_up, up_back, preferred_element_type=jnp.float32)
    grad_gain_two, grad_middle_norm = norm_back(grad_normed_two, middle, inv_two, gain_two_back)
    grad_middle = grad_out + grad_middle_norm
    gate_up_pair = jnp.concatenate([grad_gate, grad_up], axis=1)
    gate_up_sum = lax.psum_scatter(
        row_product(normed_two, gate_up_pair), ("dp", "ctx"), scatter_dimension=0, tiled=True
    )
    grad_down_sum = lax.psum_scatter(
        row_product(hidden, cotangent), ("dp", "ctx"), scatter_dimension=0, tiled=True
    )
    attn_back = (
        lax.all_gather(gain_attn, ("dp", "ctx"), axis=0, tiled=True),
        lax.all_gather(w_query, ("dp", "ctx"), axis=0, tiled=True),
        lax.all_gather(key_weight, ("dp", "ctx"), axis=0, tiled=True),
        lax.all_gather(value_weight, ("dp", "ctx"), axis=0, tiled=True),
        lax.all_gather(w_out, ("dp", "ctx"), axis=0, tiled=True),
    )
    gain_one_back, query_back, key_back, value_back, out_back = attn_back
    grad_branch = grad_middle.astype(jnp.bfloat16)
    attention_gradient = jnp.einsum(
        "td,cd->tc", grad_branch, out_back, preferred_element_type=jnp.float32
    ).astype(jnp.bfloat16)
    gradient_quad = attention_gradient.reshape(token_rows, KEY_VALUE_HEADS, head_group, HEAD_SIZE)
    delta_rows = jnp.transpose(
        jnp.sum(gradient_quad.astype(jnp.float32) * attn_four, axis=-1), (1, 2, 0)
    )

    def pair_terms(key_value_block, key_first):
        block_count = key_value_block.shape[0]
        key_portion = key_value_block[:, :key_value_width].reshape(
            block_count, KEY_VALUE_HEADS, HEAD_SIZE
        )
        value_portion = key_value_block[:, key_value_width:].reshape(
            block_count, KEY_VALUE_HEADS, HEAD_SIZE
        )
        scores = (
            jnp.einsum(
                "tkgd,skd->kgts", query_rows, key_portion, preferred_element_type=jnp.float32
            )
            * score_scale
        )
        key_pos = key_first + jnp.arange(block_count, dtype=jnp.int32)
        allowed = key_pos[None, :] <= query_pos[:, None]
        scores = jnp.where(allowed, scores, MASK_FILL)
        probs = jnp.exp(scores - log_total[..., None])
        grad_probs = jnp.einsum(
            "tkgd,skd->kgts", gradient_quad, value_portion, preferred_element_type=jnp.float32
        )
        grad_scores = (probs * (grad_probs - delta_rows[..., None])).astype(jnp.bfloat16)
        grad_query = (
            jnp.einsum(
                "kgts,skd->tkgd", grad_scores, key_portion, preferred_element_type=jnp.float32
            )
            * score_scale
        )
        grad_keys = (
            jnp.einsum(
                "kgts,tkgd->skd", grad_scores, query_rows, preferred_element_type=jnp.float32
            )
            * score_scale
        )
        grad_values = jnp.einsum(
            "kgts,tkgd->skd",
            probs.astype(jnp.bfloat16),
            gradient_quad,
            preferred_element_type=jnp.float32,
        )
        return (
            grad_query,
            jnp.concatenate(
                [
                    grad_keys.reshape(block_count, key_value_width),
                    grad_values.reshape(block_count, key_value_width),
                ],
                axis=1,
            ),
        )

    def add_pair(operands):
        kv_use, key_first, grad_query, grad_now = operands
        more_query, more_kv = pair_terms(kv_use, key_first)
        return (grad_query + more_query, grad_now + more_kv)

    def keep_pair(operands):
        return (operands[2], operands[3])

    def cycle_step(step, state):
        kv_now, grad_now, grad_query = state
        owner = (ctx_rank - step + ctx_count) % ctx_count
        kv_next = passed_along(kv_now, "ctx", 1)
        grad_query, grad_now = lax.cond(
            owner <= ctx_rank,
            add_pair,
            keep_pair,
            (kv_now, owner * token_rows, grad_query, grad_now),
        )
        grad_next = shifted(grad_now.astype(jnp.bfloat16), "ctx", 1).astype(grad_now.dtype)
        return (kv_next, grad_next, grad_query)

    cycle_start = (
        kv_local,
        jnp.zeros((token_rows, 2 * key_value_width), jnp.float32),
        jnp.zeros((token_rows, KEY_VALUE_HEADS, head_group, HEAD_SIZE), jnp.float32),
    )
    kv_final, key_value_gradient, grad_query = lax.fori_loop(0, ctx_count, cycle_step, cycle_start)
    grad_query_raw = (
        apply_rotary(
            grad_query.reshape(token_rows, QUERY_HEADS, HEAD_SIZE), cosine_table, sine_values, -1.0
        )
        .reshape(token_rows, query_width)
        .astype(jnp.bfloat16)
    )
    grad_key_raw = (
        apply_rotary(
            key_value_gradient[:, :key_value_width].reshape(token_rows, KEY_VALUE_HEADS, HEAD_SIZE),
            cosine_table,
            sine_values,
            -1.0,
        )
        .reshape(token_rows, key_value_width)
        .astype(jnp.bfloat16)
    )
    grad_value_raw = key_value_gradient[:, key_value_width:].astype(jnp.bfloat16)
    grad_normed_one = (
        jnp.einsum("tq,cq->tc", grad_query_raw, query_back, preferred_element_type=jnp.float32)
        + jnp.einsum("tq,cq->tc", grad_key_raw, key_back, preferred_element_type=jnp.float32)
        + jnp.einsum("tq,cq->tc", grad_value_raw, value_back, preferred_element_type=jnp.float32)
    )
    grad_gain_one, grad_input_norm = norm_back(grad_normed_one, inputs, inv_one, gain_one_back)
    grad_tokens = grad_middle + grad_input_norm
    projection_grads = jnp.concatenate([grad_query_raw, grad_key_raw, grad_value_raw], axis=1)
    qkv_sum = lax.psum_scatter(
        row_product(first_normed, projection_grads), ("dp", "ctx"), scatter_dimension=0, tiled=True
    )
    grad_out_sum = lax.psum_scatter(
        row_product(attn_low, grad_branch), ("dp", "ctx"), scatter_dimension=0, tiled=True
    )
    gain_sums = (
        lax.psum_scatter(grad_gain_one, ("dp", "ctx"), scatter_dimension=0, tiled=True),
        lax.psum_scatter(grad_gain_two, ("dp", "ctx"), scatter_dimension=0, tiled=True),
    )
    ff_width = w_gate.shape[1]
    return (
        output,
        grad_tokens,
        gain_sums[0],
        qkv_sum[:, :query_width],
        qkv_sum[:, query_width : query_width + key_value_width],
        qkv_sum[:, query_width + key_value_width :],
        grad_out_sum,
        gain_sums[1],
        gate_up_sum[:, :ff_width],
        gate_up_sum[:, ff_width:],
        grad_down_sum,
    )


CUBE = 8
BITS = (0, 1, 2)
HEAD_LANES = 128
HALF_LANES = 64
SHARE = 4 * HEAD_LANES
F32 = jnp.float32
BF16 = jnp.bfloat16


class Here:
    def __init__(self):
        dp = lax.axis_index("dp")
        ctx = lax.axis_index("ctx")
        self.core = lax.rem(dp, 2)
        self.far = ctx // 4
        self.own = (dp // 2, lax.rem(ctx // 2, 2), lax.rem(ctx, 2))
        self.shard = self.shard_of(self.own)
        self.at_home = self.own[0] == self.far
        self.sibling = self.device(self.own, core=1 - self.core)
        self.across = self.device(self.own, far=1 - self.far)

    def shard_of(self, bits):
        return bits[0] * 4 + bits[1] * 2 + bits[2]

    def device(self, bits, core=None, far=None):
        core = self.core if core is None else core
        far = self.far if far is None else far
        return (bits[0] * 2 + core, far * 4 + bits[1] * 2 + bits[2])

    def flip(self, *turned, of=None):
        bits = self.own if of is None else of
        return tuple(1 - bit if index in turned else bit for index, bit in enumerate(bits))

    def next(self, bit):
        return self.device(self.flip(bit))

    def others(self):
        return [
            self.flip(*[bit for bit in BITS if code >> (2 - bit) & 1]) for code in range(1, CUBE)
        ]

    def greet(self, partners):
        barrier = pltpu.get_barrier_semaphore()
        for partner in partners:
            pl.semaphore_signal(
                barrier, inc=1, device_id=partner, device_id_type=pl.DeviceIdType.MESH
            )
        pl.semaphore_wait(barrier, len(partners))

    def peers(self):
        return [self.device(bits) for bits in self.others()]

    def same_core(self):
        beyond = [self.device(bits, far=1 - self.far) for bits in self.others() + [self.own]]
        return self.peers() + beyond


def make_send(source, target, sems, device):
    return pltpu.make_async_remote_copy(
        src_ref=source,
        dst_ref=target,
        send_sem=sems[0],
        recv_sem=sems[1],
        device_id=device,
        device_id_type=pl.DeviceIdType.MESH,
    )


def send(*operands):
    copy = make_send(*operands)
    copy.start()
    return copy


class Sems:
    def __init__(self, sent, received):
        self.sent, self.received, self.used = sent, received, 0

    def __call__(self):
        pair = (self.sent.at[self.used], self.received.at[self.used])
        self.used += 1
        return pair


def run_all(*generators):
    live = list(generators)
    while live:
        for one in list(live):
            try:
                next(one)
            except StopIteration:
                live.remove(one)


def play(script, transfers, actions):
    actions = {name: list(some) for name, some in actions.items()}
    for name in script:
        if name in actions:
            actions[name].pop(0)()
        else:
            next(transfers[name], None)
    run_all(*transfers.values())


def in_step(live):
    live = list(live)
    while live:
        for one in list(live):
            try:
                next(one)
            except StopIteration:
                live.remove(one)
        yield


ORDERS = ((0, 1, 2), (1, 2, 0), (2, 0, 1))
ORDERS_Z_FIRST = ((1, 0, 2), (1, 2, 0))


def gather_cube(here, place_of, order, sems, source=None):
    a, b, c = order
    to = lambda bits, bit: send(place_of(bits), place_of(bits), sems(), here.next(bit))
    from_a, from_b = here.flip(a), here.flip(b)
    own = place_of(here.own)
    pairs = [sems() for _ in order]
    first = lambda block: [
        make_send(block, own, pair, here.next(bit)) for pair, bit in zip(pairs, order)
    ]
    a0, b0, c0 = first(own)
    if source is None:
        for copy in (a0, b0, c0):
            copy.start()
    else:

        @pl.when(here.at_home)
        def _():
            for copy in first(source):
                copy.start()

        yield
        yield

        @pl.when(jnp.logical_not(here.at_home))
        def _():
            for copy in (a0, b0, c0):
                copy.start()

    yield
    a0.wait_recv()
    b1, c1 = to(from_a, b), to(from_a, c)
    yield
    b0.wait_recv()
    c2 = to(from_b, c)
    yield
    b1.wait_recv()
    c3 = to(here.flip(a, b), c)
    yield
    for copy in (c0, c1, c2, c3):
        copy.wait_recv()
    for copy in (a0, b0, b1, c0, c1, c2, c3):
        copy.wait_send()


def gather_cube_parts(here, place_of, size, orders, sems, source=None):
    step = size // len(orders)
    live = []
    for index, order in enumerate(orders):
        part = pl.ds(index * step, step)
        live.append(
            gather_cube(
                here,
                functools.partial(place_of, part=part),
                order,
                sems,
                None if source is None else source.at[:, part],
            )
        )
    return in_step(live)


def total_of(*refs):
    total = refs[0][...].astype(F32)
    for ref in refs[1:]:
        total = total + ref[...].astype(F32)
    return total


PAIRS = (((0, 1, 2), (0, 1)), ((1, 2), (0, 2)), ((0,), (2,)), ((1,), ()))


class ReduceStream:
    def __init__(self, here, part_of, slots, out, order, sems):
        self.here, self.part_of, self.slots, self.out = here, part_of, slots, out
        c, b, a = self.order = order
        self.first = [(c, b, a), (c, b), (c, a), (c,)]
        self.copies = [None] * (CUBE - 1)
        self.sems = [sems() for _ in range(CUBE - 1)]
        self.made = set()

    def send(self, turned, slot, bit):
        self.copies[slot] = send(
            self.part_of(self.here.flip(*turned)),
            self.slots(slot),
            self.sems[slot],
            self.here.next(bit),
        )

    def add(self, turned, *slots):
        for slot in slots:
            self.copies[slot].wait_recv()
        spot = self.part_of(self.here.flip(*turned))
        spot[...] = total_of(spot, *[self.slots(slot) for slot in slots]).astype(BF16)

    def after(self, pair):
        c, b, a = self.order
        before = set(self.made)
        self.made |= {frozenset(turned) for turned in PAIRS[pair]}
        for slot, turned in enumerate(self.first):
            if frozenset(turned) in self.made - before:
                self.send(turned, slot, c)
        if self.copies[4] is None and self.copies[0] is not None and frozenset((b, a)) in self.made:
            self.add((b, a), 0)
            self.send((b, a), 4, b)
        if self.copies[5] is None and self.copies[1] is not None and frozenset((b,)) in self.made:
            self.add((b,), 1)
            self.send((b,), 5, b)

    def finish(self):
        _, b, a = self.order
        self.add((a,), 2, 4)
        self.send((a,), 6, a)
        yield
        for slot in (3, 5, 6):
            self.copies[slot].wait_recv()
        self.out[...] = total_of(
            self.part_of(self.here.own), self.slots(3), self.slots(5), self.slots(6)
        )
        yield
        for copy in self.copies:
            copy.wait_send()


def reductions(here, part, slots, out, orders, sems):
    width = out.shape[1] // len(orders)
    return [
        ReduceStream(
            here,
            lambda bits, columns=columns: part.at[here.shard_of(bits), :, columns],
            lambda slot, columns=columns: slots.at[slot, :, columns],
            out.at[:, columns],
            order,
            sems,
        )
        for columns, order in [
            (pl.ds(index * width, width), order) for index, order in enumerate(orders)
        ]
    ]


def swap_home(here, source, target, relay, local_sem, sems, beyond=None):
    beyond = target if beyond is None else beyond
    half = source.shape[1] // 2
    left, right = pl.ds(0, half), pl.ds(half, half)
    there = here.device(here.flip(0), far=1 - here.far)
    local = pltpu.make_async_copy(source, target, local_sem)
    straight = make_send(source.at[:, left], beyond.at[:, left], sems(), there)
    aside = make_send(source.at[:, right], relay, sems(), here.next(0))
    onward = make_send(relay, target.at[:, right], sems(), here.across)

    @pl.when(here.at_home)
    def _():
        local.start()

    @pl.when(jnp.logical_not(here.at_home))
    def _():
        aside.start()
        straight.start()

    yield

    @pl.when(here.at_home)
    def _():
        aside.wait_recv()
        onward.start()

    yield

    @pl.when(here.at_home)
    def _():
        local.wait()

    @pl.when(jnp.logical_not(here.at_home))
    def _():
        straight.wait_recv()
        onward.wait_recv()
        straight.wait_send()
        aside.wait_send()

    yield

    @pl.when(here.at_home)
    def _():
        onward.wait_send()


def spread(here, place_of, sems, ready=()):
    for copy in ready:
        copy.wait()
    over = send(place_of(here.far), place_of(here.far), sems(), here.across)
    beside = send(place_of(here.far), place_of(here.far), sems(), here.sibling)
    yield
    over.wait_recv()
    last = send(place_of(1 - here.far), place_of(1 - here.far), sems(), here.sibling)
    yield
    beside.wait_recv()
    last.wait_recv()
    for copy in (over, beside, last):
        copy.wait_send()


def gather_columns(here, chunks, target, local_sem, sems):
    x, z, y = here.own
    place = target.at[x, here.core, here.far, z, y]
    local = pltpu.make_async_copy(chunks.at[here.shard], place, local_sem)
    local.start()
    copies = [
        send(chunks.at[here.shard_of(bits)], place, sems(), here.device(bits))
        for bits in here.others()
    ]
    yield
    yield from spread(
        here, lambda far: target.at[:, here.core, far], sems, copies + [local]
    )


ANY = pl.BlockSpec(memory_space=pltpu.MemorySpace.HBM)
VMEM = pl.BlockSpec(memory_space=pltpu.MemorySpace.VMEM)
VMEM_BYTES = 62 * 2**20


def params(collective_id):
    return pltpu.CompilerParams(
        collective_id=collective_id, has_side_effects=True, vmem_limit_bytes=VMEM_BYTES
    )


def dma_sems(count):
    return [pltpu.SemaphoreType.DMA((count,)), pltpu.SemaphoreType.DMA((count,))]


def half_blocks(block):
    return pltpu.VMEM((block[0], block[1] // 2), BF16)


QUERY_TILE = 256
SCRIPT = (
    "xqgxhxqxcoxdxqcxogcqxo1c1o1chgo1c1oaobadoabagbha",
    "PPbbbocPPgdgdhhAAAAGfBBfBBGjGisjiss",
    "Npp2222f3t3t3t3t4kijt4wkwttrrNvnvrrnrrruvnkijfuwkjuwu",
)
ORDERS_SPARE_Z = ((1, 0, 2), (1, 2, 0), (0, 1, 2), (2, 1, 0))
ORDERS_Z_LAST = ((0, 2, 1), (2, 0, 1))
ORDERS_ALL = ORDERS + ((0, 2, 1), (1, 0, 2), (2, 1, 0))
FRONT_ORDERS = dict(x=ORDERS_ALL, c=ORDERS_SPARE_Z, o=ORDERS_SPARE_Z, a=ORDERS_ALL)
BACK_ORDERS = dict(r=ORDERS_ALL, t=ORDERS_ALL, s=ORDERS)
NT = (((1,), (1,)), ((), ()))
TN = (((0,), (0,)), ((), ()))


def dot(left, right):
    return jnp.dot(left, right, preferred_element_type=F32)


def dot_nt(left, right):
    return lax.dot_general(left, right, NT, preferred_element_type=F32)


def dot_tn(left, right):
    return lax.dot_general(left, right, TN, preferred_element_type=F32)


def rotate(head, cosine, sine):
    return head * cosine + pltpu.roll(head, HALF_LANES, 1) * sine


def scores_of(keys, queries):
    count = keys.shape[0] - QUERY_TILE
    parts = []
    if count > 0:
        parts.append(dot_nt(keys[:count], queries) * HEAD_SIZE**-0.5)
    last = dot_nt(keys[count:], queries) * HEAD_SIZE**-0.5
    key = lax.broadcasted_iota(jnp.int32, last.shape, 0)
    query = lax.broadcasted_iota(jnp.int32, last.shape, 1)
    parts.append(jnp.where(key <= query, last, MASK_FILL))
    return parts


def attend_tile(q, k, v_t, o_t, ob, lse, group, tile):
    rows = pl.ds(tile * QUERY_TILE, QUERY_TILE)
    count = (tile + 1) * QUERY_TILE
    parts = scores_of(k[:count, :], q[group, rows, :])
    top = jnp.max(parts[-1], axis=0, keepdims=True)
    for part in parts[:-1]:
        top = jnp.maximum(top, jnp.max(part, axis=0, keepdims=True))
    total = jnp.zeros_like(top)
    result = None
    first = 0
    for part in parts:
        expo = jnp.exp(part - top)
        total = total + jnp.sum(expo, axis=0, keepdims=True)
        added = dot(v_t[:, first : first + part.shape[0]], expo.astype(BF16))
        result = added if result is None else result + added
        first += part.shape[0]
    result = result / total
    o_t[group, :, rows] = result
    ob[group * HEAD_SIZE : (group + 1) * HEAD_SIZE, rows] = result[:HEAD_SIZE].astype(BF16)
    lse[group, :, rows] = top + jnp.log(total)


def spaced(head):
    half = HEAD_SIZE // 2
    gap = jnp.zeros((head.shape[0], HALF_LANES - half), head.dtype)
    return jnp.concatenate([head[:, :half], gap, head[:, half:], gap], axis=1)


def packed(head):
    half = HEAD_SIZE // 2
    return jnp.concatenate([head[:, :half], head[:, HALF_LANES : HALF_LANES + half]], axis=1)


def as_column(row):
    size = row.shape[1]
    same = lax.broadcasted_iota(jnp.int32, (size, size), 0) == lax.broadcasted_iota(
        jnp.int32, (size, size), 1
    )
    return jnp.sum(jnp.where(same, row, 0.0), axis=1, keepdims=True)


def cut_projections(w_query, key_weight, value_weight, gain_attn, gain_ffn, chunks):
    query, key, value = (ref[...].astype(F32) for ref in (w_query, key_weight, value_weight))
    rows = query.shape[0]
    gains = [as_column(ref[...].astype(F32)) for ref in (gain_attn, gain_ffn)]
    gap = jnp.zeros((rows, HEAD_LANES - HEAD_SIZE - 2), F32)
    head = lambda weight, index: weight[:, index * HEAD_SIZE : (index + 1) * HEAD_SIZE]
    for shard in range(CUBE):
        parts = [
            spaced(head(query, 2 * shard)),
            spaced(head(query, 2 * shard + 1)),
            spaced(head(key, shard)),
            jnp.concatenate([head(value, shard), *gains, gap], axis=1),
        ]
        chunks[shard] = jnp.concatenate(parts, axis=1).astype(BF16)


def hidden_lanes(shard, part, lanes):
    x, zy = divmod(shard, 4)
    first = (x * 16 + part * 4 + zy) * lanes
    return slice(first, first + lanes)


def chunk_lanes(part, lanes):
    first = (part // 2 * 4 + part % 2) * lanes
    return slice(first, first + lanes), slice(first + 2 * lanes, first + 3 * lanes)


def cut_hidden(w_gate, w_up, chunks, half):
    lanes = chunks.shape[2] // 8
    for shard in range(CUBE):
        for part in (2 * half, 2 * half + 1):
            place = hidden_lanes(shard, part, lanes)
            gate, up = chunk_lanes(part, lanes)
            chunks[shard, :, gate] = w_gate[:, place]
            chunks[shard, :, up] = w_up[:, place]


def norm_after_attention(shards, own, x_all, ob_all, w_o, gains, y1_own):
    _, block_rows, width = x_all.shape
    rows = pl.ds(shards[0] * block_rows, len(shards) * block_rows)
    ob_t = ob_all[:, :, rows].reshape(width, len(shards) * block_rows)
    x = x_all[pl.ds(shards[0], len(shards))].reshape(len(shards) * block_rows, width)
    y1 = x.astype(F32) + dot_tn(ob_t, w_o[...].reshape(width, width))
    inv_root = lax.rsqrt(jnp.mean(y1 * y1, axis=-1, keepdims=True) + NORM_EPS)
    h2 = (y1 * inv_root * gains[1:2, :]).astype(BF16)
    for index, shard in enumerate(shards):
        block = slice(index * block_rows, (index + 1) * block_rows)
        x_all[shard] = h2[block]

        @pl.when(own == shard)
        def _():
            y1_own[...] = y1[block]


def feed_forward(half, shards, h2_all, ct_all, w_gu, w_d, hidden, d_gu, out_part, dh2_part):
    _, block_rows, width = h2_all.shape
    share = d_gu.shape[1] // 4
    pair = lambda ref: jnp.concatenate([ref[shard] for shard in shards], axis=0)
    rows_of = [
        pl.ds(pl.multiple_of(shard * block_rows, block_rows), block_rows) for shard in shards
    ]
    both = pl.ds(half * 2 * share, 2 * share)
    weight = w_gu[:, :, :, :, :, :, both].reshape(width, 2 * share)
    gate_up = dot(pair(h2_all), weight)
    gate, up = gate_up[:, :share], gate_up[:, share:]
    sig = 1.0 / (1.0 + jnp.exp(-gate))
    silu = gate * sig
    kept = (silu * up).astype(BF16)
    down = w_d[0, half].reshape(share, width)
    d_hidden = dot_nt(pair(ct_all), down)
    d_gate = (d_hidden * up * sig * (1.0 + gate * (1.0 - sig))).astype(BF16)
    d_up = (d_hidden * silu).astype(BF16)
    d_both = jnp.concatenate([d_gate, d_up], axis=1)
    dh2 = dot_nt(d_both, weight)
    out = dot(kept, down)
    for index, (shard, rows) in enumerate(zip(shards, rows_of)):
        block = slice(index * block_rows, (index + 1) * block_rows)
        hidden[rows, pl.ds(half * share, share)] = kept[block]
        d_gu[rows, both] = d_both[block]
        for total, added in ((dh2_part, dh2), (out_part, out)):
            more = added[block]
            if half == 1:
                more = more + total[shard].astype(F32)
            total[shard] = more.astype(BF16)


def attend_back_tile(q, k, k_t, v, do_t, o_t, lse, dk, dv, group, tile):
    rows = pl.ds(tile * QUERY_TILE, QUERY_TILE)
    count = (tile + 1) * QUERY_TILE
    q_rows = q[group, rows, :]
    do_rows = do_t[group * HEAD_SIZE : (group + 1) * HEAD_SIZE, rows]
    do_rows = jnp.concatenate(
        [do_rows, jnp.zeros((HEAD_LANES - HEAD_SIZE, QUERY_TILE), BF16)], axis=0
    )
    delta = jnp.sum(do_rows.astype(F32) * o_t[group, :, rows], axis=0, keepdims=True)
    log_total = lse[group, :, rows]
    dq_t = None
    first = 0
    for part in scores_of(k[:count, :], q_rows):
        keys = slice(first, first + part.shape[0])
        probs = jnp.exp(part - log_total)
        d_probs = dot(v[keys, :], do_rows)
        d_scores = (probs * (d_probs - delta)).astype(BF16)
        dv[keys, :] += dot_nt(probs.astype(BF16), do_rows)
        dk[keys, :] += dot(d_scores, q_rows)
        added = dot(k_t[:, keys], d_scores)
        dq_t = added if dq_t is None else dq_t + added
        first += part.shape[0]
    return jnp.transpose(dq_t) * HEAD_SIZE**-0.5


def add_rows(total, more, piece):
    if len(total.shape) == 5:
        for z in range(2):
            for y in range(2):
                add_rows(total.at[:, z, y], more.at[:, z, y], piece)
        return

    def body(index, carry):
        rows = pl.ds(pl.multiple_of(index * piece, piece), piece)
        for block in range(total.shape[0]):
            total[block, rows, :] = total_of(
                total.at[block, rows, :], more.at[block, rows, :]
            ).astype(BF16)
        return carry

    lax.fori_loop(0, total.shape[1] // piece, body, 0)


def reduce_copies(here, part, beside, over, sems, piece):
    core, far = here.core, here.far
    first = send(part.at[:, 1 - core, 1 - far], beside.at[0], sems(), here.sibling)
    second = send(part.at[:, 1 - core, far], beside.at[1], sems(), here.sibling)
    yield
    first.wait_recv()
    add_rows(part.at[:, core, 1 - far], beside.at[0], piece)
    third = send(part.at[:, core, 1 - far], over, sems(), here.across)
    second.wait_recv()
    add_rows(part.at[:, core, far], beside.at[1], piece)
    yield
    third.wait_recv()
    add_rows(part.at[:, core, far], over, piece)
    for copy in (first, second, third):
        copy.wait_send()


def scatter_columns(here, part, beside, over, out, local_sem, sems):
    rows = out.shape[1]
    yield from reduce_copies(here, part, beside, over, sems, rows)

    def source(bits):
        return part.at[bits[0], here.core, here.far, bits[1], bits[2]]

    local = pltpu.make_async_copy(source(here.own), out.at[here.shard], local_sem)
    local.start()
    copies = [
        send(source(bits), out.at[here.shard], sems(), here.device(bits)) for bits in here.others()
    ]
    yield
    for copy in copies + [local]:
        copy.wait()


def copy_slots(shape):
    rest = (shape[0], *shape[3:])
    return [pltpu.VMEM((2, *rest), BF16), pltpu.VMEM(rest, BF16)]


def norm_back_rows(grad_normed, rows, gain):
    inv_root = lax.rsqrt(jnp.mean(rows * rows, axis=-1, keepdims=True) + NORM_EPS)
    grad_gain, grad_rows = norm_back(grad_normed, rows, inv_root, gain)
    return grad_gain.reshape(1, -1), grad_rows


def sum_everywhere(here, total, slots, sems):
    peers = here.same_core()
    copies = [send(total, slots.at[index], sems(), device) for index, device in enumerate(peers)]
    yield
    for copy in copies:
        copy.wait()
    total[...] += jnp.sum(slots[: len(peers)], axis=0)
    beside = send(total, slots.at[len(peers)], sems(), here.sibling)
    yield
    beside.wait()
    total[...] += slots[len(peers)]


def layer_kernel(
    tokens, cotangent, w_query, key_weight, value_weight, gain_attn, gain_ffn, w_gate, w_up, down, out,
    cosine, sine,
    output_home, grad_home, gu_rows_too, down_sum, qkv_rows, out_rows, gain_out, gu_rows,
    w_qkv, w_gu, w_d, w_o, x_all, ct_all, ob_all, h1, q, k, v, v_t, o_t, lse, gains, x_own, ct_own, y1_own,
    hidden, d_gu, out_part, dh2_part, dh2, slots, x_relay, ct_relay, qkv, gate_up,
    gu_beside, gu_over, gu_beside_too, gu_over_too, down_beside, down_over, qkv_beside, qkv_over,
    wo_part, wo_beside, wo_over, gain_sums, gain_slots, d_middle, pairs, columns, k_t, dk, dv, out_sum,
    own_rows, local, sent, got,
):
    here = Here()
    sems = Sems(sent, got)
    here.greet(here.same_core() + [here.sibling])
    out_slots, dh1_part, dh1, d_qkv = ct_all, x_all, dh2, hidden
    x, z, y = here.own
    width = tokens.shape[1]
    block_rows = tokens.shape[0]
    seq_rows = CUBE * block_rows

    def swapped(source, target, relay, local_sem, orders):
        swap = swap_home(
            here,
            source,
            target.at[here.shard],
            relay,
            local_sem,
            sems,
            target.at[here.shard_of(here.flip(0))],
        )
        gather = gather_cube_parts(
            here,
            lambda bits, part: target.at[here.shard_of(bits), :, part],
            width,
            orders,
            sems,
            source,
        )
        for _ in range(3):
            next(swap)
            next(gather)
            yield
        run_all(swap)
        yield from gather

    def out_gather():
        mine = w_o.at[x, here.core, here.far, z, y]
        kept = pltpu.make_async_copy(out, mine, local.at[3])
        kept.start()
        over = send(out, mine, sems(), here.across)
        yield
        kept.wait()
        over.wait()
        yield from gather_cube_parts(
            here,
            lambda bits, part: w_o.at[bits[0], here.core, :, bits[1], bits[2], :, part],
            width,
            FRONT_ORDERS["o"],
            sems,
        )
        beside = send(w_o.at[:, here.core], w_o.at[:, here.core], sems(), here.sibling)
        yield
        beside.wait()

    def down_gather():
        kept = pltpu.make_async_copy(down, w_d.at[0, here.core, here.far], local.at[2])
        kept.start()
        yield from spread(here, lambda far: w_d.at[0, here.core, far], sems, [kept])

    def qkv_gather():
        cut_projections(w_query, key_weight, value_weight, gain_attn, gain_ffn, qkv)
        yield from gather_columns(here, qkv, w_qkv, local.at[4], sems)

    ff_share = w_gu.shape[6] // 2
    halves = [pl.ds(half * ff_share, ff_share) for half in range(2)]

    def gate_up_gather(half):
        cut_hidden(w_gate, w_up, gate_up, half)
        yield from gather_columns(
            here,
            gate_up.at[:, :, halves[half]],
            w_gu.at[:, :, :, :, :, :, halves[half]],
            local.at[5 + half],
            sems,
        )

    transfers = dict(
        x=swapped(tokens, x_all, x_relay, local.at[0], FRONT_ORDERS["x"]),
        q=qkv_gather(),
        g=gate_up_gather(0),
        h=gate_up_gather(1),
        o=out_gather(),
        d=down_gather(),
        c=swapped(cotangent, ct_all, ct_relay, local.at[1], FRONT_ORDERS["c"]),
    )
    ob = ob_all.at[here.shard]
    turns = [[here.shard_of(here.flip(*bits)) for bits in turned] for turned in PAIRS]

    def norm():
        turned = jnp.transpose(
            w_qkv[:, :, :, :, :, :, 3 * HEAD_LANES :].astype(F32).reshape(width, HEAD_LANES)
        )
        gains[...] = turned[HEAD_SIZE : HEAD_SIZE + 8]
        x_own[...] = x_all[here.shard]

        def norm_block(index, carry):
            rows = x_all[index].astype(F32)
            inv_root = lax.rsqrt(jnp.mean(rows * rows, axis=-1, keepdims=True) + NORM_EPS)
            place = pl.ds(pl.multiple_of(index * block_rows, block_rows), block_rows)
            h1[place, :] = (rows * inv_root * gains[0:1, :]).astype(BF16)
            return carry

        lax.fori_loop(0, CUBE, norm_block, 0)

    def project():
        def project_tile(index, carry):
            rows = pl.ds(pl.multiple_of(index * QUERY_TILE, QUERY_TILE), QUERY_TILE)
            raw = dot(h1[rows, :], w_qkv[...].reshape(width, SHARE))
            cos_rows, sin_rows = cosine[rows, :], sine[rows, :]
            heads = [raw[:, lane : lane + HEAD_LANES] for lane in range(0, SHARE, HEAD_LANES)]
            q[0, rows, :] = rotate(heads[0], cos_rows, sin_rows).astype(BF16)
            q[1, rows, :] = rotate(heads[1], cos_rows, sin_rows).astype(BF16)
            k[rows, :] = rotate(heads[2], cos_rows, sin_rows).astype(BF16)
            v[rows, :] = heads[3].astype(BF16)
            v_t[:, rows] = jnp.transpose(heads[3]).astype(BF16)
            return carry

        lax.fori_loop(0, seq_rows // QUERY_TILE, project_tile, 0)

    def attend(*tiles):
        for tile in tiles:
            for group in range(2):
                attend_tile(q, k, v_t, o_t, ob, lse, group, tile)
        if tiles[-1] % 2 == 1:
            lanes = pl.ds((tiles[-1] - 1) * QUERY_TILE, 2 * QUERY_TILE)
            transfers["ab"[tiles[-1] // 2]] = gather_cube_parts(
                here,
                lambda bits, part: ob_all.at[here.shard_of(bits), part, lanes],
                ob.shape[0],
                FRONT_ORDERS["a"],
                sems,
            )

    def normed_pair(pair):
        norm_after_attention(
            (2 * pair, 2 * pair + 1), here.shard, x_all, ob_all, w_o, gains, y1_own
        )

    bind = functools.partial
    streams = reductions(here, dh2_part, slots, dh2, BACK_ORDERS["s"], sems)

    def feed(half, pair):
        if half == 0 and pair == 0:
            ct_own[...] = ct_all[here.shard]
        feed_forward(
            half, turns[pair], x_all, ct_all, w_gu, w_d, hidden, d_gu, out_part, dh2_part
        )
        if half == 1:
            for stream in streams:
                stream.after(pair)

    def gate_up_grad(half):
        def quarter(index, carry):
            lanes = pl.ds(pl.multiple_of(index * 4 * HEAD_SIZE, 4 * HEAD_SIZE), 4 * HEAD_SIZE)
            left = x_all[:, :, lanes].reshape(seq_rows, 4 * HEAD_SIZE)
            grad = dot_tn(left, d_gu[:, halves[half]]).astype(BF16)
            place = w_gu.at[index // 2, lax.rem(index, 2), :, :, :, :, halves[half]]
            place[...] = grad.reshape(place.shape)
            return carry

        lax.fori_loop(0, 4, quarter, 0)

    def down_grad():
        def quarter(index, carry):
            lanes = pl.ds(pl.multiple_of(index * HEAD_LANES, HEAD_LANES), HEAD_LANES)
            grad = dot_tn(hidden[:, lanes], ct_all[...].reshape(seq_rows, width)).astype(BF16)
            w_d[0, index // 2, lax.rem(index, 2)] = grad
            return carry

        lax.fori_loop(0, 4, quarter, 0)

    weight_rows = out.shape[0]
    share = 2 * HEAD_SIZE

    def gate_up_reduce(half, beside, over, rows):
        yield from scatter_columns(
            here,
            w_gu.at[:, :, :, :, :, :, halves[half]],
            beside,
            over,
            rows,
            local.at[7 + half],
            sems,
        )

    def down_reduce():
        yield from reduce_copies(here, w_d, down_beside, down_over, sems, 32)
        down_sum[...] = w_d[0, here.core, here.far]

    def to_heads():
        rows = pl.ds(pl.multiple_of(here.shard * block_rows, block_rows), block_rows)
        place = columns.at[:, :, rows]
        mine = pltpu.make_async_copy(pairs.at[here.shard], place, local.at[9])
        mine.start()
        copies = [
            send(pairs.at[here.shard_of(bits)], place, sems(), here.device(bits))
            for bits in here.others()
        ]
        yield
        for copy in copies + [mine]:
            copy.wait()

    def reduce_rows(part, slots, out, orders):
        streams = reductions(here, part, slots, out, orders, sems)
        for pair in range(len(PAIRS)):
            for stream in streams:
                stream.after(pair)
            yield
        yield from in_step([stream.finish() for stream in streams])

    def output_reduce():
        yield from reduce_rows(out_part, out_slots, out_sum, BACK_ORDERS["r"])

    def output_swap():
        own_rows[0] = (y1_own[...] + out_sum[...]).astype(BF16)
        yield from swap_home(here, own_rows.at[0], output_home, ct_relay, local.at[12], sems)

    transfers.update(
        f=gate_up_reduce(0, gu_beside, gu_over, gu_rows),
        s=in_step([stream.finish() for stream in streams]),
        i=gate_up_reduce(1, gu_beside_too, gu_over_too, gu_rows_too),
        j=down_reduce(),
        p=to_heads(),
        r=output_reduce(),
        t=reduce_rows(dh1_part, slots, dh1, BACK_ORDERS["t"]),
        k=scatter_columns(here, w_qkv, qkv_beside, qkv_over, qkv_rows, local.at[10], sems),
        w=scatter_columns(here, wo_part, wo_beside, wo_over, out_rows, local.at[11], sems),
        u=output_swap(),
        v=swap_home(here, own_rows.at[1], grad_home, x_relay, local.at[13], sems),
        n=sum_everywhere(here, gain_sums, gain_slots, sems),
    )

    def norm_two():
        grad_gain, grad_rows = norm_back_rows(dh2[...], y1_own[...], gains[1:2, :])
        gain_sums[...] = jnp.zeros_like(gain_sums)
        gain_sums[1:2, :] = grad_gain
        d_middle[...] = ct_own[...].astype(F32) + grad_rows
        da = d_middle[...].astype(BF16)
        pairs[:, 0] = dot_nt(w_o[...].reshape(width, width), da).astype(BF16).reshape(CUBE, share, block_rows)
        pairs[:, 1] = jnp.transpose(d_middle[...]).astype(BF16).reshape(CUBE, share, block_rows)

    def norm_one():
        grad_gain, grad_rows = norm_back_rows(dh1[...], x_own[...].astype(F32), gains[0:1, :])
        gain_sums[0:1, :] = grad_gain
        own_rows[1] = (d_middle[...] + grad_rows).astype(BF16)

    def attention(tile):
        if tile == 0:
            k_t[...] = jnp.transpose(k[...].astype(F32)).astype(BF16)
            dk[...] = jnp.zeros_like(dk)
            dv[...] = jnp.zeros_like(dv)
        rows = pl.ds(tile * QUERY_TILE, QUERY_TILE)
        for group in range(2):
            dq = attend_back_tile(q, k, k_t, v, columns.at[0], o_t, lse, dk, dv, group, tile)
            d_qkv[rows, group * HEAD_LANES : (group + 1) * HEAD_LANES] = rotate(
                dq, cosine[rows, :], -sine[rows, :]
            ).astype(BF16)
        if rows.start + rows.size == seq_rows:
            d_qkv[:, 2 * HEAD_LANES : 3 * HEAD_LANES] = rotate(
                dk[...] * HEAD_SIZE**-0.5, cosine[...], -sine[...]
            ).astype(BF16)
            d_qkv[:, 3 * HEAD_LANES :] = dv[...].astype(BF16)

    def pair_back(pair):
        shards = [here.shard_of(here.flip(*bits)) for bits in PAIRS[pair]]
        some = jnp.concatenate(
            [
                d_qkv[pl.ds(pl.multiple_of(shard * block_rows, block_rows), block_rows), :]
                for shard in shards
            ],
            axis=0,
        )
        rows = dot_nt(some, w_qkv[...].reshape(width, SHARE)).astype(BF16)
        for index, shard in enumerate(shards):
            dh1_part[shard] = rows[index * block_rows : (index + 1) * block_rows]

    def qkv_grad():

        def quarter(index, carry):
            lanes = pl.ds(pl.multiple_of(index * 4 * HEAD_SIZE, 4 * HEAD_SIZE), 4 * HEAD_SIZE)
            grad = dot_tn(h1[:, lanes], d_qkv[...]).astype(BF16)
            w_qkv[index // 2, lax.rem(index, 2)] = grad.reshape(w_qkv.shape[2:])
            return carry

        lax.fori_loop(0, 4, quarter, 0)

    def out_grad():
        for index in range(4):
            left = ob_all[2 * index : 2 * index + 2].reshape(2 * share, seq_rows)
            grad = dot_nt(left, columns[1]).astype(BF16)
            grad = jnp.concatenate(
                [grad, jnp.zeros((2 * share, wo_part.shape[6] - share), BF16)], axis=1
            )
            wo_part[index // 2, index % 2] = grad.reshape(wo_part.shape[2:])

    bind = functools.partial
    everyone = range(len(PAIRS))
    play(
        "".join(SCRIPT),
        transfers,
        {
            "1": [norm, project, bind(attend, 0), bind(attend, 1), bind(attend, 2, 3)],
            "P": [bind(normed_pair, pair) for pair in everyone],
            "A": [bind(feed, 0, pair) for pair in everyone],
            "B": [bind(feed, 1, pair) for pair in everyone],
            "G": [bind(gate_up_grad, 0), down_grad, bind(gate_up_grad, 1)],
            "N": [norm_two, norm_one],
            "2": [bind(attention, tile) for tile in range(seq_rows // QUERY_TILE)],
            "3": [bind(pair_back, pair) for pair in everyone],
            "4": [qkv_grad, out_grad],
        },
    )
    rank = here.device(here.own)
    rank = rank[0] * CUBE + rank[1]
    sums = jnp.concatenate([gain_sums[...], jnp.zeros((6, width), F32)], axis=0)
    gain_out[...] = pltpu.roll(sums, lax.rem(width - rank * weight_rows, width), 1)[:, :HEAD_LANES]


def layer(tokens, cotangent, w_query, key_weight, value_weight, gain_attn, gain_ffn, w_gate, w_up, down,
          out, cosine, sine):
    operands = (
        tokens, cotangent, w_query, key_weight, value_weight, gain_attn, gain_ffn, w_gate, w_up, down, out,
        cosine, sine,
    )
    rows, width = tokens.shape
    weight_rows = out.shape[0]
    seq_rows = CUBE * rows
    share = 2 * HEAD_SIZE
    ff_share = 4 * down.shape[0]
    by_row = lambda lanes: (2, 2, 2, 2, 2, weight_rows, lanes)
    low = lambda *dims: pltpu.VMEM(dims, BF16)
    wide = lambda *dims: pltpu.VMEM(dims, F32)
    home = lambda *dims: jax.ShapeDtypeStruct(dims, BF16)
    outs = (
        home(rows, width),
        home(rows, width),
        home(CUBE, weight_rows, ff_share),
        home(*down.shape),
        home(CUBE, weight_rows, SHARE),
        home(CUBE, weight_rows, 2 * HEAD_LANES),
        jax.ShapeDtypeStruct((8, HEAD_LANES), F32),
        home(CUBE, weight_rows, ff_share),
    )
    return pl.pallas_call(
        layer_kernel,
        out_shape=outs,
        in_specs=[VMEM] * len(operands),
        out_specs=(VMEM,) * len(outs),
        scratch_shapes=[
            low(*by_row(SHARE)),
            low(*by_row(2 * ff_share)),
            low(1, 2, 2, *down.shape),
            low(*by_row(width)),
            low(CUBE, rows, width),
            low(CUBE, rows, width),
            low(CUBE, share, seq_rows),
            low(seq_rows, width),
            low(2, seq_rows, HEAD_LANES),
            low(seq_rows, HEAD_LANES),
            low(seq_rows, HEAD_LANES),
            low(HEAD_LANES, seq_rows),
            wide(2, HEAD_LANES, seq_rows),
            wide(2, 1, seq_rows),
            wide(8, width),
            low(rows, width),
            low(rows, width),
            wide(rows, width),
            low(seq_rows, ff_share),
            low(seq_rows, 2 * ff_share),
            low(CUBE, rows, width),
            low(CUBE, rows, width),
            wide(rows, width),
            low(CUBE - 1, rows, width),
            half_blocks(tokens.shape),
            half_blocks(tokens.shape),
            low(CUBE, weight_rows, SHARE),
            low(CUBE, weight_rows, 2 * ff_share),
            *copy_slots(by_row(ff_share)),
            *copy_slots(by_row(ff_share)),
            *copy_slots((1, 2, 2, *down.shape)),
            *copy_slots(by_row(SHARE)),
            low(*by_row(2 * HEAD_LANES)),
            *copy_slots(by_row(2 * HEAD_LANES)),
            wide(2, width),
            wide(2 * CUBE, 2, width),
            wide(rows, width),
            low(CUBE, 2, share, rows),
            low(2, share, seq_rows),
            low(HEAD_LANES, seq_rows),
            wide(seq_rows, HEAD_LANES),
            wide(seq_rows, HEAD_LANES),
            wide(rows, width),
            low(2, rows, width),
            pltpu.SemaphoreType.DMA((14,)),
        ]
        + dma_sems(500),
        compiler_params=params(1),
        name="layer",
    )(*operands)


def finish_kernel(
    output_home, grad_home, gu_rows_too, down_sum, qkv_rows, out_rows, gains, gu_rows,
    output, grad, gate, up, down, query, key, value, out, gain_one, gain_two,
):
    output[...] = output_home[...]
    grad[...] = grad_home[...].astype(F32)
    down[...] = down_sum[...].astype(F32)
    lanes = gu_rows.shape[2] // 4
    for shard in range(CUBE):
        for part in range(4):
            place = hidden_lanes(shard, part, lanes)
            gate_lanes, up_lanes = chunk_lanes(part % 2, lanes)
            rows = (gu_rows, gu_rows_too)[part // 2]
            gate[:, place] = rows[shard, :, gate_lanes].astype(F32)
            up[:, place] = rows[shard, :, up_lanes].astype(F32)
    heads = [
        [
            qkv_rows[shard, :, index * HEAD_LANES : (index + 1) * HEAD_LANES].astype(F32)
            for index in range(4)
        ]
        for shard in range(CUBE)
    ]
    query[...] = jnp.concatenate([packed(head) for some in heads for head in some[:2]], axis=1)
    key[...] = jnp.concatenate([packed(some[2]) for some in heads], axis=1)
    value[...] = jnp.concatenate([some[3][:, :HEAD_SIZE] for some in heads], axis=1)
    out[...] = jnp.concatenate(
        [out_rows[shard, :, : 2 * HEAD_SIZE].astype(F32) for shard in range(CUBE)], axis=1
    )
    gain_one[...] = gains[0, : gain_one.shape[0]]
    gain_two[...] = gains[1, : gain_two.shape[0]]


def finish(parts, ff_width):
    rows, width = parts[0].shape
    weight_rows = parts[2].shape[1]
    out = lambda *dims: jax.ShapeDtypeStruct(dims, F32)
    outs = (
        jax.ShapeDtypeStruct((rows, width), BF16),
        out(rows, width),
        out(weight_rows, ff_width),
        out(weight_rows, ff_width),
        out(*parts[3].shape),
        out(weight_rows, width),
        out(weight_rows, width // 2),
        out(weight_rows, width // 2),
        out(weight_rows, width),
        out(weight_rows),
        out(weight_rows),
    )
    return pl.pallas_call(
        finish_kernel,
        out_shape=outs,
        in_specs=[VMEM] * len(parts),
        out_specs=(VMEM,) * len(outs),
        compiler_params=pltpu.CompilerParams(vmem_limit_bytes=VMEM_BYTES),
        name="finish",
    )(*parts)


def spaced_tables(row_count):
    half = HEAD_SIZE // 2
    frequency = np.float32(ROPE_THETA) ** (-np.arange(half, dtype=np.float32) * 2.0 / HEAD_SIZE)
    angles = np.arange(row_count, dtype=np.float32)[:, None] * frequency.astype(np.float32)[None, :]
    pad = ((0, 0), (0, HALF_LANES - half))
    cosine, sine = np.pad(np.cos(angles), pad), np.pad(np.sin(angles), pad)
    return (
        jnp.asarray(np.concatenate([cosine, cosine], axis=1), F32),
        jnp.asarray(np.concatenate([-sine, sine], axis=1), F32),
    )


def split_layer(
    tokens,
    cotangent,
    gain_attn,
    w_query,
    key_weight,
    value_weight,
    w_out,
    gain_ffn,
    w_gate,
    w_up,
    w_down,
):
    block_rows = tokens.shape[0]
    cosine, sine = spaced_tables(block_rows * CUBE)
    parts = layer(
        tokens, cotangent, w_query, key_weight, value_weight, gain_attn[None], gain_ffn[None], w_gate, w_up,
        w_down, w_out, cosine, sine,
    )
    output, grad, gate, up, down, query, key, value, out, gain_one, gain_two = finish(
        parts, w_gate.shape[1]
    )
    return (output, grad, gain_one, query, key, value, out, gain_two, gate, up, down)


def solution(mesh):
    heads_split = mesh.shape["dp"] == 4 and mesh.shape["ctx"] == KEY_VALUE_HEADS
    return jax.shard_map(
        split_layer if heads_split else blockwise_layer,
        mesh=mesh,
        in_specs=(
            P(("dp", "ctx"), None),
            P(("dp", "ctx"), None),
            P(("dp", "ctx")),
            P(("dp", "ctx"), None),
            P(("dp", "ctx"), None),
            P(("dp", "ctx"), None),
            P(("dp", "ctx"), None),
            P(("dp", "ctx")),
            P(("dp", "ctx"), None),
            P(("dp", "ctx"), None),
            P(("dp", "ctx"), None),
        ),
        out_specs=(
            P(("dp", "ctx"), None),
            P(("dp", "ctx"), None),
            P(("dp", "ctx")),
            P(("dp", "ctx"), None),
            P(("dp", "ctx"), None),
            P(("dp", "ctx"), None),
            P(("dp", "ctx"), None),
            P(("dp", "ctx")),
            P(("dp", "ctx"), None),
            P(("dp", "ctx"), None),
            P(("dp", "ctx"), None),
        ),
        check_vma=False,
    )
```
